32 devices in a mesh: seq: 16 (over z, y, x), head: 2 (over core).
Axes of the slice: x: 2, y: 2, z: 4, core: 2. Of those that a mesh axis runs over, the one named last changes fastest.
Arguments:
- text_rows: bfloat16 [2048, 4096], P('seq', 'head'), may hold values from -6 to 6
- picture_rows: bfloat16 [512, 4096], P('seq', 'head'), may hold values from -6 to 6
- picture_slots: int32 [512], P('seq'), may hold values from 0 to 2047, as said below
- norm_gain: float32 [4096], replicated, may hold values from 0.1 to 1.9
- w_query: bfloat16 [4096, 4096], P('seq', 'head'), may hold values from -1 to 1
- w_key: bfloat16 [4096, 1024], P('seq', 'head'), may hold values from -1 to 1
- w_value: bfloat16 [4096, 1024], P('seq', 'head'), may hold values from -0.09375 to 0.09375
- w_out: bfloat16 [4096, 4096], P('head', 'seq'), may hold values from -0.5 to 0.5
- cache_keys: bfloat16 [1024, 1024], P('seq', 'head'), may hold values from -500 to 500
- cache_values: bfloat16 [1024, 1024], P('seq', 'head'), may hold values from -6 to 6
- recompute_rows: bfloat16 [128, 4096], P('seq', 'head'), may hold values from -6 to 6
- recompute_slots: int32 [128], P('seq'), may hold values from 0 to 1023, as said below
Outputs:
- mixed: bfloat16 [2048, 4096], P('seq', 'head')
The draws below stay inside these ranges and needn't reach their ends.
Inputs may be any that keep to these rules, and one draw needn't show every extreme that they name: `picture_slots`: distinct stream positions, in runs of 256 consecutive positions, one run a tile; the first tile's run starts at position 1024 and the last tile's run ends at the stream's last position. `recompute_slots`: each aligned block b of 8 entries names distinct rows of cache rows b * 64 to (b + 1) * 64 - 1.
All inputs are finite; a program needn't handle non-finite values.
Results may differ from the reference program's by a relative error of at most 0.02.
Values may be sent and summed in bfloat16 or wider, within the bound.
No kernel may reach another device: no remote copies, remote signals or barrier semaphores. Data moves between devices by JAX's collectives and lax.ppermute only.
A program may use at most 128 MiB of HBM per device.

```python
import jax
import jax.numpy as jnp
from jax import lax

D = 4096
HEADS = 32
KV_HEADS = 8
HD = 128
PIC_RUN = 256
CACHE_DEV = 64
REC_DEV = 8
STREAM = 2048
PICS = 512
CACHE = 1024
RECOMP = 128


def place_runs(key, count, seg_start, seg_len):
    spare = seg_len - count * PIC_RUN
    offsets = jnp.sort(jax.random.randint(key, (count,), 0, spare + 1))
    return (seg_start + offsets + PIC_RUN * jnp.arange(count, dtype=jnp.int32)).astype(jnp.int32)


def draw_picture_slots(key, part):
    tiles = PICS // PIC_RUN
    middle = STREAM // 2
    inner = tiles - 2
    before = inner // 2
    after = inner - before
    first_runs = place_runs(jax.random.fold_in(key, 3), before, 0, middle)
    second_runs = place_runs(jax.random.fold_in(key, 4), after, middle + PIC_RUN, STREAM - middle - 2 * PIC_RUN)
    starts = jnp.concatenate([jnp.array([middle], jnp.int32), first_runs, second_runs, jnp.array([STREAM - PIC_RUN], jnp.int32)])
    return (starts[:, None] + jnp.arange(PIC_RUN, dtype=jnp.int32)[None, :]).reshape(-1).astype(jnp.int32)


def recompute_choice(key):
    blocks = RECOMP // REC_DEV
    subkeys = jax.random.split(jax.random.fold_in(key, 7), blocks)
    chosen = jax.vmap(lambda sub: jax.random.permutation(sub, CACHE_DEV)[:REC_DEV])(subkeys)
    offsets = CACHE_DEV * jnp.arange(blocks, dtype=jnp.int32)
    return (chosen.astype(jnp.int32) + offsets[:, None]).reshape(-1).astype(jnp.int32)


def draw_recompute_slots(key, part):
    return recompute_choice(key)


def weight_table(key, fan_in, columns, tag):
    raw = jax.random.normal(jax.random.fold_in(key, tag), (fan_in, columns), jnp.float32)
    return jnp.clip(raw, -6.0, 6.0) * fan_in ** (-0.5)


def draw_w_query(key, part):
    return weight_table(key, D, HEADS * HD, 21).astype(jnp.bfloat16)


def draw_w_key(key, part):
    return weight_table(key, D, KV_HEADS * HD, 22).astype(jnp.bfloat16)


def draw_picture_rows(key, part):
    noise = jnp.clip(jax.random.normal(jax.random.fold_in(key, 31), (PICS, D), jnp.float32), -6.0, 6.0)
    return noise.astype(jnp.bfloat16)


def draw_cache_keys(key, part):
    base = jnp.clip(jax.random.normal(jax.random.fold_in(key, 11), (CACHE, KV_HEADS * HD), jnp.float32), -6.0, 6.0)
    return base.astype(jnp.bfloat16)


def block_levels(stream_key, extent, cuts, low, top_value):
    def one(axis_at, shards_of):
        steps = jax.random.uniform(jax.random.fold_in(jax.random.fold_in(stream_key, 6), axis_at), (shards_of,), jnp.float32, low / len(cuts), top_value / len(cuts))
        return jnp.repeat(jnp.exp(steps), extent[axis_at] // shards_of).reshape((-1,) + (1,) * (len(extent) - axis_at - 1))

    level = one(*cuts[0])
    for cut in cuts[1:]:
        level = level * one(*cut)
    return level


def normal_values(own_key, dims, spread, reach, shards=(), kind=jnp.bfloat16):
    loudness = block_levels(own_key, dims, shards, -0.22, 0.18) if shards else 1.0
    entries = jax.random.normal(own_key, dims, jnp.float32) * spread * loudness
    return jnp.minimum(jnp.maximum(entries, -reach), reach).astype(kind)


def setup_inputs(seed: int = 0) -> dict:
    key_of = jax.random.split(jax.random.key(seed), 13)
    return {
        "text_rows": normal_values(key_of[0], (STREAM, D), 1.0, 6.0, ((0, 16), (1, 2))),
        "picture_rows": draw_picture_rows(jax.random.fold_in(key_of[12], 71), 0),
        "picture_slots": draw_picture_slots(jax.random.fold_in(key_of[12], 71), 0),
        "norm_gain": jnp.clip(1.0 + 0.18 * jax.random.normal(key_of[3], (D,), jnp.float32), 0.1, 1.9),
        "w_query": draw_w_query(jax.random.fold_in(key_of[12], 71), 0),
        "w_key": draw_w_key(jax.random.fold_in(key_of[12], 71), 0),
        "w_value": normal_values(key_of[6], (D, KV_HEADS * HD), D ** -0.5, 0.09375, ((0, 16), (1, 2))),
        "w_out": normal_values(key_of[7], (HEADS * HD, D), HD ** -0.5, 0.5, ((0, 2), (1, 16))),
        "cache_keys": draw_cache_keys(jax.random.fold_in(key_of[12], 71), 0),
        "cache_values": normal_values(key_of[9], (CACHE, KV_HEADS * HD), 1.0, 6.0, ((0, 16), (1, 2))),
        "recompute_rows": normal_values(key_of[10], (RECOMP, D), 1.0, 6.0, ((0, 16), (1, 2))),
        "recompute_slots": draw_recompute_slots(jax.random.fold_in(key_of[12], 71), 0),
    }


EPSILON = 1e-05
ROPE_BASE = 1000000.0

def rotate(values, positions):
    half = values.shape[-1] // 2
    freqs = ROPE_BASE ** (-jnp.arange(half, dtype=jnp.float32) / half)
    angles = positions[:, None] * freqs[None, :]
    cosine = jnp.cos(angles)[:, None, :]
    sine = jnp.sin(angles)[:, None, :]
    first = values[..., :half]
    second = values[..., half:]
    return jnp.concatenate([first * cosine - second * sine, second * cosine + first * sine], axis=-1)

def normalise(rows, gain):
    rows_wide = rows.astype(jnp.float32)
    squares = lax.optimization_barrier(jnp.sum(rows_wide * rows_wide, axis=1))
    return (rows_wide * lax.rsqrt(squares / D + EPSILON)[:, None] * gain[None, :]).astype(jnp.bfloat16)

def reference(text_rows, picture_rows, picture_slots, norm_gain, w_query, w_key, w_value, w_out, cache_keys, cache_values, recompute_rows, recompute_slots):
    stream = text_rows.at[picture_slots].set(picture_rows)
    normed = normalise(stream, norm_gain)
    rec_normed = normalise(recompute_rows, norm_gain)
    query = jnp.dot(normed, w_query, preferred_element_type=jnp.float32)
    key_new = jnp.dot(normed, w_key, preferred_element_type=jnp.float32)
    value_new = jnp.dot(normed, w_value, preferred_element_type=jnp.float32)
    rec_key = jnp.dot(rec_normed, w_key, preferred_element_type=jnp.float32)
    rec_value = jnp.dot(rec_normed, w_value, preferred_element_type=jnp.float32)
    stream_pos = (CACHE + jnp.arange(STREAM)).astype(jnp.float32)
    rec_pos = recompute_slots.astype(jnp.float32)
    rot_query = rotate(query.reshape(STREAM, HEADS, HD), stream_pos).astype(jnp.bfloat16).reshape(STREAM, HEADS * HD)
    rot_key = rotate(key_new.reshape(STREAM, KV_HEADS, HD), stream_pos).astype(jnp.bfloat16).reshape(STREAM, KV_HEADS * HD)
    rot_rec_key = rotate(rec_key.reshape(RECOMP, KV_HEADS, HD), rec_pos).astype(jnp.bfloat16).reshape(RECOMP, KV_HEADS * HD)
    all_keys = jnp.concatenate([cache_keys.at[recompute_slots].set(rot_rec_key), rot_key], axis=0)
    all_values = jnp.concatenate([cache_values.at[recompute_slots].set(rec_value.astype(jnp.bfloat16)), value_new.astype(jnp.bfloat16)], axis=0)
    rows_index = jnp.arange(STREAM, dtype=jnp.int32)
    cols_index = jnp.arange(CACHE + STREAM, dtype=jnp.int32)
    allowed = (cols_index[None, :] < CACHE) | (cols_index[None, :] - CACHE <= rows_index[:, None])
    group = HEADS // KV_HEADS

    def one_head(head_index):
        kv_index = head_index // group
        head_query = lax.dynamic_slice_in_dim(rot_query, head_index * HD, HD, 1)
        head_keys = lax.dynamic_slice_in_dim(all_keys, kv_index * HD, HD, 1)
        head_values = lax.dynamic_slice_in_dim(all_values, kv_index * HD, HD, 1)
        scores = jnp.dot(head_query, head_keys.T, preferred_element_type=jnp.float32) * HD ** (-0.5)
        scores = jnp.where(allowed, scores, -1e+30)
        top = lax.optimization_barrier(jnp.max(scores, axis=1, keepdims=True))
        weights = jnp.where(allowed, jnp.exp(scores - top), 0.0)
        total = lax.optimization_barrier(jnp.sum(weights, axis=1, keepdims=True))
        return jnp.dot(weights.astype(jnp.bfloat16), head_values, preferred_element_type=jnp.float32) / total
    heads_out = lax.map(one_head, jnp.arange(HEADS, dtype=jnp.int32))
    attended = jnp.transpose(heads_out, (1, 0, 2)).reshape(STREAM, HEADS * HD).astype(jnp.bfloat16)
    return jnp.dot(attended, w_out, preferred_element_type=jnp.float32).astype(jnp.bfloat16)
```

```python
import jax
import jax.numpy as jnp
from jax import lax
from jax.experimental import pallas as pl
from jax.experimental.pallas import tpu as pltpu
from jax.sharding import PartitionSpec as P

D = 4096
HD = 128


EPSILON = 1e-05
ROPE_BASE = 1000000.0
NEG_FILL = -1e30


def rotate(values, positions):
    half = values.shape[-1] // 2
    freqs = ROPE_BASE ** (-jnp.arange(half, dtype=jnp.float32) / half)
    angles = positions[:, None] * freqs[None, :]
    cosine = jnp.cos(angles)[:, None, :]
    sine = jnp.sin(angles)[:, None, :]
    first = values[..., :half]
    second = values[..., half:]
    return jnp.concatenate(
        [first * cosine - second * sine, second * cosine + first * sine], axis=-1
    )


def scaled(rows_wide, squares, gain):
    return (rows_wide * lax.rsqrt(squares / D + EPSILON)[:, None] * gain[None, :]).astype(
        jnp.bfloat16
    )


def attend(carry, key_piece, value_piece, queries, allowed):
    best, total, accum = carry
    count = key_piece.shape[0]
    kv_local = queries.shape[0]
    keys_split = key_piece.reshape(count, kv_local, HD)
    values_split = value_piece.reshape(count, kv_local, HD)
    scores = jnp.einsum(
        "kgtd,nkd->kgtn", queries, keys_split, preferred_element_type=jnp.float32
    ) * HD ** (-0.5)
    scores = jnp.where(allowed, scores, NEG_FILL)
    fresh = jnp.maximum(best, jnp.max(scores, axis=-1))
    factor = jnp.exp(best - fresh)
    weights = jnp.where(allowed, jnp.exp(scores - fresh[..., None]), 0.0)
    total = total * factor + jnp.sum(weights, axis=-1)
    accum = accum * factor[..., None] + jnp.einsum(
        "kgtn,nkd->kgtd",
        weights.astype(jnp.bfloat16),
        values_split,
        preferred_element_type=jnp.float32,
    )
    return (fresh, total, accum)


def on_device(
    text_rows,
    picture_rows,
    picture_slots,
    norm_gain,
    w_query,
    w_key,
    w_value,
    w_out,
    cache_keys,
    cache_values,
    recompute_rows,
    recompute_slots,
):
    tok_rows = text_rows.shape[0]
    rec_count = recompute_rows.shape[0]
    cache_rows = cache_keys.shape[0]
    seq_index = lax.axis_index("seq")
    local_pos = seq_index * tok_rows + jnp.arange(tok_rows, dtype=jnp.int32)
    rows_piece = lax.all_gather(picture_rows, "seq", axis=0, tiled=True)
    slots_piece = lax.all_gather(picture_slots, "seq", axis=0, tiled=True)
    select = (slots_piece[None, :] == local_pos[:, None]).astype(jnp.bfloat16)
    placed = jnp.dot(select, rows_piece, preferred_element_type=jnp.float32)
    hits = jnp.sum(select.astype(jnp.float32), axis=1)
    added, hits = (placed, hits)
    stream = jnp.where(hits[:, None] > 0.5, added, text_rows.astype(jnp.float32)).astype(
        jnp.bfloat16
    )
    slice_width = stream.shape[1]
    gain_slice = lax.dynamic_slice_in_dim(
        norm_gain, lax.axis_index("head") * slice_width, slice_width, 0
    )
    stream_wide = stream.astype(jnp.float32)
    rec_wide = recompute_rows.astype(jnp.float32)
    stream_sq, rec_sq = lax.psum(
        (jnp.sum(stream_wide * stream_wide, axis=1), jnp.sum(rec_wide * rec_wide, axis=1)), "head"
    )
    normed, rec_normed = (
        lax.all_gather(scaled(stream_wide, stream_sq, gain_slice), "head", axis=1, tiled=True),
        lax.all_gather(scaled(rec_wide, rec_sq, gain_slice), "head", axis=1, tiled=True),
    )
    stacked = jnp.concatenate([normed, rec_normed], axis=0)
    query_cols = w_query.shape[1]
    key_cols = w_key.shape[1]
    pieces = (
        lax.all_gather(w_query, "seq", axis=0, tiled=True),
        lax.all_gather(w_key, "seq", axis=0, tiled=True),
        lax.all_gather(w_value, "seq", axis=0, tiled=True),
    )
    query_all = jnp.dot(stacked, pieces[0], preferred_element_type=jnp.float32)
    key_all = jnp.dot(stacked, pieces[1], preferred_element_type=jnp.float32)
    value_all = jnp.dot(stacked, pieces[2], preferred_element_type=jnp.float32)
    cache_total = cache_rows * lax.axis_size("seq")
    stream_pos = (cache_total + local_pos).astype(jnp.float32)
    rec_pos = recompute_slots.astype(jnp.float32)
    heads_local = query_cols // HD
    kv_local = key_cols // HD
    group = heads_local // kv_local
    rot_query = rotate(query_all[:tok_rows].reshape(tok_rows, heads_local, HD), stream_pos).astype(
        jnp.bfloat16
    )
    rot_key = (
        rotate(key_all[:tok_rows].reshape(tok_rows, kv_local, HD), stream_pos)
        .astype(jnp.bfloat16)
        .reshape(tok_rows, key_cols)
    )
    values_new = value_all[:tok_rows].astype(jnp.bfloat16)
    rot_rec_key = (
        rotate(key_all[tok_rows:].reshape(rec_count, kv_local, HD), rec_pos)
        .astype(jnp.bfloat16)
        .reshape(rec_count, key_cols)
    )
    rec_values = value_all[tok_rows:].astype(jnp.bfloat16)
    local_slots = recompute_slots - seq_index * cache_rows
    select = local_slots[:, None] == jnp.arange(cache_rows, dtype=jnp.int32)[None, :]
    replaced = jnp.any(select, axis=0)[:, None]
    select_cols = select.astype(jnp.bfloat16).T
    new_keys = jnp.dot(select_cols, rot_rec_key, preferred_element_type=jnp.float32).astype(
        jnp.bfloat16
    )
    new_values = jnp.dot(select_cols, rec_values, preferred_element_type=jnp.float32).astype(
        jnp.bfloat16
    )
    cache_k = jnp.where(replaced, new_keys, cache_keys)
    cache_v = jnp.where(replaced, new_values, cache_values)
    queries = jnp.transpose(rot_query.reshape(tok_rows, kv_local, group, HD), (1, 2, 0, 3))
    carry_start = (
        jnp.full((kv_local, group, tok_rows), NEG_FILL, jnp.float32),
        jnp.zeros((kv_local, group, tok_rows), jnp.float32),
        jnp.zeros((kv_local, group, tok_rows, HD), jnp.float32),
    )
    pieces = (
        lax.all_gather(cache_k, "seq", axis=0, tiled=True),
        lax.all_gather(cache_v, "seq", axis=0, tiled=True),
    )
    allowed = jnp.ones((tok_rows, pieces[0].shape[0]), jnp.bool_)
    carry_mid = attend(carry_start, pieces[0], pieces[1], queries, allowed)
    pieces = (
        lax.all_gather(rot_key, "seq", axis=0, tiled=True),
        lax.all_gather(values_new, "seq", axis=0, tiled=True),
    )
    key_pos = jnp.arange(pieces[0].shape[0], dtype=jnp.int32)
    allowed = key_pos[None, :] <= local_pos[:, None]
    best, total, accum = attend(carry_mid, pieces[0], pieces[1], queries, allowed)
    attended = (
        jnp.transpose(accum / total[..., None], (2, 0, 1, 3))
        .reshape(tok_rows, query_cols)
        .astype(jnp.bfloat16)
    )
    partial_out = jnp.dot(
        attended,
        lax.all_gather(w_out, "seq", axis=1, tiled=True),
        preferred_element_type=jnp.float32,
    )
    return lax.psum_scatter(
        partial_out.astype(jnp.bfloat16), "head", scatter_dimension=1, tiled=True
    )


LEVELS = 4
PLANE = 4
REC_PAD = 16
TILE_RUN = 256


def permuted(value, move):
    perm = []
    for level in range(LEVELS):
        for place in range(PLANE):
            for core in range(2):
                target = move(level, place, core)
                if target is not None:
                    to_level, to_place, to_core = target
                    perm.append(
                        (
                            (level * PLANE + place) * 2 + core,
                            (to_level * PLANE + to_place) * 2 + to_core,
                        )
                    )
    return lax.ppermute(value, ("seq", "head"), perm)


def up(value, steps):
    return permuted(value, lambda z, p, c: ((z + steps) % LEVELS, p, c))


def other_core(value):
    return permuted(value, lambda z, p, c: (z, p, 1 - c))


def in_plane(piece):
    near = permuted(piece, lambda z, p, c: (z, p ^ (1 + c), c))
    far = permuted(piece, lambda z, p, c: (z, p ^ (2 - c), c))
    both = permuted(near, lambda z, p, c: (z, p ^ (2 - c), c))
    return [piece, near, far, both]


def place_of(which, place, core):
    if which == 0:
        return place
    if which == 3:
        return place ^ 3
    return place ^ (1 + core) if which == 1 else place ^ (2 - core)


def project_kernel(where_ref, *refs):
    acts = refs[:8]
    weights = refs[8:24]
    caches = refs[24:28]
    cos_ref, sin_ref, query_ref, kv_ref, x_ref = refs[28:]
    level, place, core = where_ref[0], where_ref[1], where_ref[2]
    rows = acts[0].shape[0]
    depth = weights[0].shape[0]
    width = acts[0].shape[1]
    tok = rows - REC_PAD
    mine = pl.multiple_of(core * width, width)
    others = pl.multiple_of((1 - core) * width, width)
    for k in range(LEVELS):
        x_ref[k * rows : (k + 1) * rows, pl.ds(mine, width)] = acts[2 * k][...]
        x_ref[k * rows : (k + 1) * rows, pl.ds(others, width)] = acts[2 * k + 1][...]
    total = None
    for d in range(LEVELS):
        from_level = lax.rem(level + LEVELS - d, LEVELS)
        for j in range(PLANE):
            block = from_level * PLANE + place_of(j, place, core)
            start = pl.multiple_of(block * depth, depth)
            part = jnp.dot(
                x_ref[:, pl.ds(start, depth)],
                weights[d * PLANE + j][...],
                preferred_element_type=jnp.float32,
            )
            total = part if total is None else total + part
    for k in range(LEVELS):
        at = lax.rem(level + LEVELS - k, LEVELS)
        block = total[k * rows : (k + 1) * rows]
        cosine = cos_ref[at]
        sine = sin_ref[at]

        def turned(values, cosine, sine):
            return values * cosine + pltpu.roll(values, HD // 2, 1) * sine

        for h in range(4):
            head = turned(block[:tok, h * HD : (h + 1) * HD], cosine[:tok], sine[:tok])
            query_ref[at, h] = head.astype(jnp.bfloat16)
        keys = turned(block[:, 4 * HD : 5 * HD], cosine, sine)
        values = block[:, 5 * HD : 6 * HD]
        both = jnp.concatenate([keys, values], axis=1)
        kv_ref[LEVELS * 64 // 128 + at] = both[:tok].astype(jnp.bfloat16)
        cached = caches[k][0:64, :].astype(jnp.float32)
        slots = caches[k][64:80, :].astype(jnp.int32)
        row = lax.broadcasted_iota(jnp.int32, cached.shape, 0)
        for r in range(8):
            cached = jnp.where(row == slots[r : r + 1], both[tok + r : tok + r + 1], cached)
        half = lax.rem(at, 2)
        kv_ref[at // 2, pl.ds(pl.multiple_of(half * 64, 64), 64)] = cached.astype(jnp.bfloat16)


def attend_kernel(where_ref, query_ref, kv0, kv1, kv2, kv3, out_ref):
    place, core = where_ref[1], where_ref[2]
    pieces = (kv0, kv1, kv2, kv3)
    tok = query_ref.shape[2]
    old = LEVELS // 2
    row = lax.broadcasted_iota(jnp.int32, (tok, tok), 0)
    col = lax.broadcasted_iota(jnp.int32, (tok, tok), 1)
    scale = HD ** (-0.5) * 1.4426950408889634
    for i in range(LEVELS):
        count = (old + i + 1) * tok
        queries = query_ref[i].reshape(4 * tok, HD)
        scores = []
        best = None
        for j in range(PLANE):
            theirs = place_of(j, place, core)
            keys = pieces[j][0 : old + i + 1, :, 0:HD].reshape(count, HD)
            raw = lax.dot_general(
                queries, keys, (((1,), (1,)), ((), ())), preferred_element_type=jnp.float32
            )
            if j == 0:
                allowed = col <= row
            else:
                allowed = jnp.broadcast_to(theirs, (tok, tok)) < place
            allowed = jnp.concatenate([allowed] * 4, axis=0)
            last = jnp.where(allowed, raw[:, count - tok :], NEG_FILL)
            raw = jnp.concatenate([raw[:, : count - tok], last], axis=1)
            top = jnp.max(raw, axis=1, keepdims=True)
            best = top if best is None else jnp.maximum(best, top)
            scores.append(raw)
        total, accum = 0.0, 0.0
        for j in range(PLANE):
            weights = jnp.exp2((scores[j] - best) * scale)
            total = total + jnp.sum(weights, axis=1, keepdims=True)
            values = pieces[j][0 : old + i + 1, :, HD : 2 * HD].reshape(count, HD)
            accum = accum + jnp.dot(
                weights.astype(jnp.bfloat16), values, preferred_element_type=jnp.float32
            )
        result = (accum / total).astype(jnp.bfloat16)
        for h in range(4):
            out_ref[i * tok : (i + 1) * tok, h * HD : (h + 1) * HD] = result[
                h * tok : (h + 1) * tok
            ]


def output_kernel(where_ref, attended_ref, *refs):
    weights = refs[:16]
    mine_ref, other_ref = refs[16:]
    level, place, core = where_ref[0], where_ref[1], where_ref[2]
    width = weights[0].shape[1]
    half = LEVELS * PLANE // 2
    for d in range(LEVELS):
        from_level = lax.rem(level + LEVELS - d, LEVELS)
        for j in range(PLANE):
            block = from_level * PLANE + place_of(j, place, core)
            start = pl.multiple_of(lax.rem(block, half) * width, width)
            part = jnp.dot(
                attended_ref[...], weights[d * PLANE + j][...], preferred_element_type=jnp.float32
            )

            @pl.when(block // half == core)
            def _():
                mine_ref[:, pl.ds(start, width)] = part

            @pl.when(block // half != core)
            def _():
                other_ref[:, pl.ds(start, width)] = part.astype(jnp.bfloat16)


SMEM = pl.BlockSpec(memory_space=pltpu.SMEM)
VMEM = pl.BlockSpec(memory_space=pltpu.VMEM)
PARAMS = pltpu.CompilerParams(vmem_limit_bytes=48 * 1024 * 1024)


def by_levels(
    text_rows,
    picture_rows,
    picture_slots,
    norm_gain,
    w_query,
    w_key,
    w_value,
    w_out,
    cache_keys,
    cache_values,
    recompute_rows,
    recompute_slots,
):
    seq_index = lax.axis_index("seq")
    core = lax.axis_index("head")
    level, place = seq_index // PLANE, seq_index % PLANE
    where = jnp.stack([level, place, core]).astype(jnp.int32)
    tok, width = text_rows.shape
    rec = recompute_rows.shape[0]
    cache_rows = cache_keys.shape[0]
    depth = w_query.shape[0]

    def group_of(level_at):
        q = lax.dynamic_slice_in_dim(w_query, level_at * 4 * HD, 4 * HD, 1)
        k = lax.dynamic_slice_in_dim(w_key, level_at * HD, HD, 1)
        v = lax.dynamic_slice_in_dim(w_value, level_at * HD, HD, 1)
        return jnp.concatenate([q, k, v], axis=1)

    local_slots = (recompute_slots - seq_index * cache_rows).astype(jnp.bfloat16)
    slot_rows = jnp.broadcast_to(
        jnp.pad(local_slots, (0, REC_PAD - rec))[:, None], (REC_PAD, 2 * HD)
    )

    def cache_of(level_at):
        k = lax.dynamic_slice_in_dim(cache_keys, level_at * HD, HD, 1)
        v = lax.dynamic_slice_in_dim(cache_values, level_at * HD, HD, 1)
        return jnp.concatenate([jnp.concatenate([k, v], axis=1), slot_rows], axis=0)

    def out_of(level_at):
        return lax.dynamic_slice_in_dim(w_out, level_at * 4 * HD, 4 * HD, 0)

    weights, caches = [], []
    for d in range(LEVELS):
        to_level = (level + d) % LEVELS
        piece, cached = group_of(to_level), cache_of(to_level)
        if d:
            piece, cached = up(piece, d), up(cached, d)
        caches.append(cached)
        weights += in_plane(piece)

    stream_len = tok * LEVELS * PLANE
    tile_owners = TILE_RUN // tok
    first = stream_len // 2 // tok
    last = (stream_len - TILE_RUN) // tok
    owners = [first + i for i in range(tile_owners)] + [last + i for i in range(tile_owners)]
    senders = tok // picture_rows.shape[0]
    received = []
    for k in range(senders):
        perm = [
            ((i * senders + k) * 2 + c, owner * 2 + c)
            for i, owner in enumerate(owners)
            for c in range(2)
        ]
        received.append(lax.ppermute(picture_rows, ("seq", "head"), perm))
    placed = jnp.concatenate(received, axis=0)
    is_owner = jnp.any(seq_index == jnp.array(owners, jnp.int32))
    stream = jnp.where(is_owner, placed, text_rows)

    rows = jnp.concatenate(
        [stream, recompute_rows, jnp.zeros((REC_PAD - rec, width), stream.dtype)], axis=0
    )
    wide = rows.astype(jnp.float32)
    squares = jnp.sum(wide * wide, axis=1)
    squares = squares + other_core(squares)
    gain = lax.dynamic_slice_in_dim(norm_gain, core * width, width, 0)
    normed = scaled(wide, squares, gain)

    acts, held = [], normed
    for k in range(LEVELS):
        if k:
            held = up(held, 1)
        acts += [held, other_core(held)]

    half = HD // 2
    freqs = ROPE_BASE ** (-jnp.arange(half, dtype=jnp.float32) / half)
    level_start = (jnp.arange(LEVELS, dtype=jnp.int32) * PLANE + place)[:, None]
    stream_pos = (
        cache_rows * LEVELS * PLANE + level_start * tok + jnp.arange(tok, dtype=jnp.int32)[None]
    ).astype(jnp.float32)
    order = (level - jnp.arange(LEVELS, dtype=jnp.int32)) % LEVELS
    slots = jnp.stack([c[cache_rows:, 0] for c in caches])[order].astype(jnp.float32)
    rec_pos = slots + (level_start * cache_rows).astype(jnp.float32)
    positions = jnp.concatenate([stream_pos, rec_pos], axis=1)
    angles = positions[..., None] * freqs
    cosine, sine = jnp.cos(angles), jnp.sin(angles)
    cosine = jnp.concatenate([cosine, cosine], axis=-1)
    sine = jnp.concatenate([-sine, sine], axis=-1)

    blocks = LEVELS * cache_rows // tok + LEVELS
    query, kv = pl.pallas_call(
        project_kernel,
        out_shape=(
            jax.ShapeDtypeStruct((LEVELS, 4, tok, HD), jnp.bfloat16),
            jax.ShapeDtypeStruct((blocks, tok, 2 * HD), jnp.bfloat16),
        ),
        in_specs=[SMEM] + [VMEM] * 30,
        out_specs=(VMEM, VMEM),
        scratch_shapes=[pltpu.VMEM((LEVELS * (tok + REC_PAD), 2 * width), jnp.bfloat16)],
        compiler_params=PARAMS,
        name="project",
    )(where, *acts, *weights, *caches, cosine, sine)

    attended = pl.pallas_call(
        attend_kernel,
        out_shape=jax.ShapeDtypeStruct((LEVELS * tok, 4 * HD), jnp.bfloat16),
        in_specs=[SMEM] + [VMEM] * 5,
        out_specs=VMEM,
        compiler_params=PARAMS,
        name="attend",
    )(where, query, *in_plane(kv))

    out_weights = []
    for d in range(LEVELS):
        piece = out_of((level + d) % LEVELS)
        if d:
            piece = up(piece, d)
        out_weights += in_plane(piece)
    mine, other = pl.pallas_call(
        output_kernel,
        out_shape=(
            jax.ShapeDtypeStruct((LEVELS * tok, width), jnp.float32),
            jax.ShapeDtypeStruct((LEVELS * tok, width), jnp.bfloat16),
        ),
        in_specs=[SMEM] + [VMEM] * 17,
        out_specs=(VMEM, VMEM),
        compiler_params=PARAMS,
        name="output",
    )(where, attended, *out_weights)
    summed = (mine + other_core(other).astype(jnp.float32)).reshape(LEVELS, tok, width)
    result = lax.dynamic_index_in_dim(summed, level, 0, keepdims=False)
    for d in range(1, LEVELS):
        block = lax.dynamic_index_in_dim(summed, (level + d) % LEVELS, 0, keepdims=False)
        result = result + up(block.astype(jnp.bfloat16), d).astype(jnp.float32)
    return result.astype(jnp.bfloat16)


def solution(mesh):
    def run(*args):
        kv_local = args[5].shape[1] // HD // mesh.shape["head"]
        levels_fit = (
            mesh.shape["seq"] == LEVELS * PLANE
            and mesh.shape["head"] == 2
            and kv_local == LEVELS
            and args[1].shape[0] == 2 * TILE_RUN
            and args[0].shape[0] == 2048
            and args[8].shape[0] == 1024
            and args[10].shape[0] == 128
        )
        return jax.shard_map(
            by_levels if levels_fit else on_device,
            mesh=mesh,
            in_specs=(
                P("seq", "head"),
                P("seq", "head"),
                P("seq"),
                P(),
                P("seq", "head"),
                P("seq", "head"),
                P("seq", "head"),
                P("head", "seq"),
                P("seq", "head"),
                P("seq", "head"),
                P("seq", "head"),
                P("seq"),
            ),
            out_specs=P("seq", "head"),
            check_vma=False,
        )(*args)

    return run
```

```python
import jax
import jax.numpy as jnp
from jax import lax
from jax.experimental import pallas as pl
from jax.experimental.pallas import tpu as pltpu
from jax.sharding import PartitionSpec as P

D = 4096
HD = 128


EPSILON = 1e-05
ROPE_BASE = 1000000.0
NEG_FILL = -1e30


def rotate(values, positions):
    half = values.shape[-1] // 2
    freqs = ROPE_BASE ** (-jnp.arange(half, dtype=jnp.float32) / half)
    angles = positions[:, None] * freqs[None, :]
    cosine = jnp.cos(angles)[:, None, :]
    sine = jnp.sin(angles)[:, None, :]
    first = values[..., :half]
    second = values[..., half:]
    return jnp.concatenate(
        [first * cosine - second * sine, second * cosine + first * sine], axis=-1
    )


def scaled(rows_wide, squares, gain):
    return (rows_wide * lax.rsqrt(squares / D + EPSILON)[:, None] * gain[None, :]).astype(
        jnp.bfloat16
    )


def attend(carry, key_piece, value_piece, queries, allowed):
    best, total, accum = carry
    count = key_piece.shape[0]
    kv_local = queries.shape[0]
    keys_split = key_piece.reshape(count, kv_local, HD)
    values_split = value_piece.reshape(count, kv_local, HD)
    scores = jnp.einsum(
        "kgtd,nkd->kgtn", queries, keys_split, preferred_element_type=jnp.float32
    ) * HD ** (-0.5)
    scores = jnp.where(allowed, scores, NEG_FILL)
    fresh = jnp.maximum(best, jnp.max(scores, axis=-1))
    factor = jnp.exp(best - fresh)
    weights = jnp.where(allowed, jnp.exp(scores - fresh[..., None]), 0.0)
    total = total * factor + jnp.sum(weights, axis=-1)
    accum = accum * factor[..., None] + jnp.einsum(
        "kgtn,nkd->kgtd",
        weights.astype(jnp.bfloat16),
        values_split,
        preferred_element_type=jnp.float32,
    )
    return (fresh, total, accum)


def on_device(
    text_rows,
    picture_rows,
    picture_slots,
    norm_gain,
    w_query,
    w_key,
    w_value,
    w_out,
    cache_keys,
    cache_values,
    recompute_rows,
    recompute_slots,
):
    tok_rows = text_rows.shape[0]
    rec_count = recompute_rows.shape[0]
    cache_rows = cache_keys.shape[0]
    seq_index = lax.axis_index("seq")
    local_pos = seq_index * tok_rows + jnp.arange(tok_rows, dtype=jnp.int32)
    rows_piece = lax.all_gather(picture_rows, "seq", axis=0, tiled=True)
    slots_piece = lax.all_gather(picture_slots, "seq", axis=0, tiled=True)
    select = (slots_piece[None, :] == local_pos[:, None]).astype(jnp.bfloat16)
    placed = jnp.dot(select, rows_piece, preferred_element_type=jnp.float32)
    hits = jnp.sum(select.astype(jnp.float32), axis=1)
    added, hits = (placed, hits)
    stream = jnp.where(hits[:, None] > 0.5, added, text_rows.astype(jnp.float32)).astype(
        jnp.bfloat16
    )
    slice_width = stream.shape[1]
    gain_slice = lax.dynamic_slice_in_dim(
        norm_gain, lax.axis_index("head") * slice_width, slice_width, 0
    )
    stream_wide = stream.astype(jnp.float32)
    rec_wide = recompute_rows.astype(jnp.float32)
    stream_sq, rec_sq = lax.psum(
        (jnp.sum(stream_wide * stream_wide, axis=1), jnp.sum(rec_wide * rec_wide, axis=1)), "head"
    )
    normed, rec_normed = (
        lax.all_gather(scaled(stream_wide, stream_sq, gain_slice), "head", axis=1, tiled=True),
        lax.all_gather(scaled(rec_wide, rec_sq, gain_slice), "head", axis=1, tiled=True),
    )
    stacked = jnp.concatenate([normed, rec_normed], axis=0)
    query_cols = w_query.shape[1]
    key_cols = w_key.shape[1]
    pieces = (
        lax.all_gather(w_query, "seq", axis=0, tiled=True),
        lax.all_gather(w_key, "seq", axis=0, tiled=True),
        lax.all_gather(w_value, "seq", axis=0, tiled=True),
    )
    query_all = jnp.dot(stacked, pieces[0], preferred_element_type=jnp.float32)
    key_all = jnp.dot(stacked, pieces[1], preferred_element_type=jnp.float32)
    value_all = jnp.dot(stacked, pieces[2], preferred_element_type=jnp.float32)
    cache_total = cache_rows * lax.axis_size("seq")
    stream_pos = (cache_total + local_pos).astype(jnp.float32)
    rec_pos = recompute_slots.astype(jnp.float32)
    heads_local = query_cols // HD
    kv_local = key_cols // HD
    group = heads_local // kv_local
    rot_query = rotate(query_all[:tok_rows].reshape(tok_rows, heads_local, HD), stream_pos).astype(
        jnp.bfloat16
    )
    rot_key = (
        rotate(key_all[:tok_rows].reshape(tok_rows, kv_local, HD), stream_pos)
        .astype(jnp.bfloat16)
        .reshape(tok_rows, key_cols)
    )
    values_new = value_all[:tok_rows].astype(jnp.bfloat16)
    rot_rec_key = (
        rotate(key_all[tok_rows:].reshape(rec_count, kv_local, HD), rec_pos)
        .astype(jnp.bfloat16)
        .reshape(rec_count, key_cols)
    )
    rec_values = value_all[tok_rows:].astype(jnp.bfloat16)
    local_slots = recompute_slots - seq_index * cache_rows
    select = local_slots[:, None] == jnp.arange(cache_rows, dtype=jnp.int32)[None, :]
    replaced = jnp.any(select, axis=0)[:, None]
    select_cols = select.astype(jnp.bfloat16).T
    new_keys = jnp.dot(select_cols, rot_rec_key, preferred_element_type=jnp.float32).astype(
        jnp.bfloat16
    )
    new_values = jnp.dot(select_cols, rec_values, preferred_element_type=jnp.float32).astype(
        jnp.bfloat16
    )
    cache_k = jnp.where(replaced, new_keys, cache_keys)
    cache_v = jnp.where(replaced, new_values, cache_values)
    queries = jnp.transpose(rot_query.reshape(tok_rows, kv_local, group, HD), (1, 2, 0, 3))
    carry_start = (
        jnp.full((kv_local, group, tok_rows), NEG_FILL, jnp.float32),
        jnp.zeros((kv_local, group, tok_rows), jnp.float32),
        jnp.zeros((kv_local, group, tok_rows, HD), jnp.float32),
    )
    pieces = (
        lax.all_gather(cache_k, "seq", axis=0, tiled=True),
        lax.all_gather(cache_v, "seq", axis=0, tiled=True),
    )
    allowed = jnp.ones((tok_rows, pieces[0].shape[0]), jnp.bool_)
    carry_mid = attend(carry_start, pieces[0], pieces[1], queries, allowed)
    pieces = (
        lax.all_gather(rot_key, "seq", axis=0, tiled=True),
        lax.all_gather(values_new, "seq", axis=0, tiled=True),
    )
    key_pos = jnp.arange(pieces[0].shape[0], dtype=jnp.int32)
    allowed = key_pos[None, :] <= local_pos[:, None]
    best, total, accum = attend(carry_mid, pieces[0], pieces[1], queries, allowed)
    attended = (
        jnp.transpose(accum / total[..., None], (2, 0, 1, 3))
        .reshape(tok_rows, query_cols)
        .astype(jnp.bfloat16)
    )
    partial_out = jnp.dot(
        attended,
        lax.all_gather(w_out, "seq", axis=1, tiled=True),
        preferred_element_type=jnp.float32,
    )
    return lax.psum_scatter(
        partial_out.astype(jnp.bfloat16), "head", scatter_dimension=1, tiled=True
    )


LEVELS = 4
PLANE = 4
TILE_RUN = 256
CACHED = 64
REC = 8
REC_PAD = 16


def permuted(value, move):
    perm = []
    for level in range(LEVELS):
        for place in range(PLANE):
            for core in range(2):
                target = move(level, place, core)
                if target is not None:
                    to_level, to_place, to_core = target
                    perm.append(
                        (
                            (level * PLANE + place) * 2 + core,
                            (to_level * PLANE + to_place) * 2 + to_core,
                        )
                    )
    return lax.ppermute(value, ("seq", "head"), perm)


def up(value, steps):
    return permuted(value, lambda z, p, c: ((z + steps) % LEVELS, p, c))


def other_core(value):
    return permuted(value, lambda z, p, c: (z, p, 1 - c))


def to_near(value):
    return permuted(value, lambda z, p, c: (z, p ^ (1 + c), c))


def to_far(value):
    return permuted(value, lambda z, p, c: (z, p ^ (2 - c), c))


def in_plane(pieces):
    near = to_near(pieces)
    pair = to_far(jnp.concatenate([pieces, near], axis=0))
    return pieces, near, pair


def place_of(which, place, core):
    if which == 0:
        return place
    if which == 3:
        return place ^ 3
    return place ^ (1 + core) if which == 1 else place ^ (2 - core)


def level_before(level, steps):
    return lax.rem(level + LEVELS - steps, LEVELS)


def piece_at(groups, which, steps):
    for levels, refs in groups:
        if steps in levels:
            at = levels.index(steps)
            if which < 2:
                return refs[which].at[at]
            return refs[2].at[(which - 2) * len(levels) + at]
    return None


GROUPS = ((0,), (1,), (2, 3))


def grouped(refs):
    return [(levels, refs[3 * i : 3 * i + 3]) for i, levels in enumerate(GROUPS)]


def turned(values, cosine, sine):
    return values * cosine + pltpu.roll(values, HD // 2, 1) * sine


def project_kernel(where_ref, *refs):
    acts = refs[:8]
    groups = grouped(refs[8:17])
    cos_ref, sin_ref, query_ref, kv_ref, x_ref = refs[17:]
    level, place, core = where_ref[0], where_ref[1], where_ref[2]
    rows, width = acts[0].shape
    tok = rows - REC_PAD
    depth = 2 * width // (LEVELS * PLANE)
    mine = pl.multiple_of(core * width, width)
    others = pl.multiple_of((1 - core) * width, width)
    for k in range(LEVELS):
        x_ref[k * rows : (k + 1) * rows, pl.ds(mine, width)] = acts[2 * k][...]
        x_ref[k * rows : (k + 1) * rows, pl.ds(others, width)] = acts[2 * k + 1][...]
    total = None
    for d in range(LEVELS):
        for j in range(PLANE):
            block = level_before(level, d) * PLANE + place_of(j, place, core)
            start = pl.multiple_of(block * depth, depth)
            part = jnp.dot(
                x_ref[:, pl.ds(start, depth)],
                piece_at(groups, j, d)[0:depth, :],
                preferred_element_type=jnp.float32,
            )
            total = part if total is None else total + part
    lane = lax.broadcasted_iota(jnp.int32, (REC, CACHED), 1)
    for k in range(LEVELS):
        at = level_before(level, k)
        block = total[k * rows : (k + 1) * rows]
        cosine, sine = cos_ref[at], sin_ref[at]
        for h in range(4):
            head = turned(block[:tok, h * HD : (h + 1) * HD], cosine[:tok], sine[:tok])
            query_ref[at, h] = head.astype(jnp.bfloat16)
        keys = turned(block[:tok, 4 * HD : 5 * HD], cosine[:tok], sine[:tok])
        kv_ref[at, 0:tok, 0:HD] = keys.astype(jnp.bfloat16)
        kv_ref[at, 0:tok, HD : 2 * HD] = block[:tok, 5 * HD : 6 * HD].astype(jnp.bfloat16)
        slots = piece_at(groups, 0, k)[depth : depth + REC_PAD, 4 * HD : 4 * HD + CACHED]
        chosen = (slots[0:REC].astype(jnp.int32) == lane).astype(jnp.float32)
        rec_cos, rec_sin = (
            jnp.dot(
                chosen,
                table[tok : tok + CACHED],
                preferred_element_type=jnp.float32,
                precision=lax.Precision.HIGHEST,
            )
            for table in (cosine, sine)
        )
        rec_keys = turned(block[tok : tok + REC, 4 * HD : 5 * HD], rec_cos, rec_sin)
        both = jnp.concatenate([rec_keys, block[tok : tok + REC, 5 * HD : 6 * HD]], axis=1)
        both = jnp.concatenate([both, jnp.zeros_like(both)], axis=0)
        kv_ref[at, tok : tok + REC_PAD, :] = both.astype(jnp.bfloat16)


def attend_kernel(where_ref, query_ref, *refs):
    kv_mine, kv_near, kv_pair = refs[:3]
    groups = grouped(refs[3:12])
    out_ref, cache_ref = refs[12:]
    level, place, core = where_ref[0], where_ref[1], where_ref[2]
    kvs = (kv_mine.at[0], kv_near.at[0], kv_pair.at[0], kv_pair.at[1])
    tok = query_ref.shape[2]
    line = lax.broadcasted_iota(jnp.int32, (CACHED, 2 * HD), 0)
    for j in range(PLANE):
        for d in range(LEVELS):
            at = level_before(level, d)
            piece = piece_at(groups, j, d)
            slots = piece[0:REC_PAD, 4 * HD : 6 * HD].astype(jnp.int32)
            cached = jnp.concatenate(
                [piece[:, 0 : 2 * HD], piece[:, 2 * HD : 4 * HD]], axis=0
            ).astype(jnp.float32)
            fresh = kvs[j][at, tok : tok + REC_PAD, :].astype(jnp.float32)
            for r in range(REC):
                cached = jnp.where(line == slots[r : r + 1], fresh[r : r + 1], cached)
            cache_ref[j, d * CACHED : (d + 1) * CACHED, :] = cached.astype(jnp.bfloat16)
    row = lax.broadcasted_iota(jnp.int32, (tok, tok), 0)
    col = lax.broadcasted_iota(jnp.int32, (tok, tok), 1)
    scale = HD ** (-0.5) * 1.4426950408889634

    def scores_of(queries, keys):
        return lax.dot_general(
            queries, keys, (((1,), (1,)), ((), ())), preferred_element_type=jnp.float32
        )

    for i in range(LEVELS):
        queries = query_ref[i].reshape(4 * tok, HD)
        scores, values = [], []
        for j in range(PLANE):
            scores.append(scores_of(queries, cache_ref[j, :, 0:HD]))
            values.append(cache_ref[j, :, HD : 2 * HD])
            if i:
                scores.append(scores_of(queries, kvs[j][0:i, 0:tok, 0:HD].reshape(i * tok, HD)))
                values.append(kvs[j][0:i, 0:tok, HD : 2 * HD].reshape(i * tok, HD))
            raw = scores_of(queries, kvs[j][i, 0:tok, 0:HD])
            if j == 0:
                allowed = col <= row
            else:
                allowed = jnp.broadcast_to(place_of(j, place, core), (tok, tok)) < place
            scores.append(jnp.where(jnp.concatenate([allowed] * 4, axis=0), raw, NEG_FILL))
            values.append(kvs[j][i, 0:tok, HD : 2 * HD])
        best = jnp.max(scores[0], axis=1, keepdims=True)
        for raw in scores[1:]:
            best = jnp.maximum(best, jnp.max(raw, axis=1, keepdims=True))
        total, accum = 0.0, 0.0
        for raw, value in zip(scores, values):
            weights = jnp.exp2((raw - best) * scale)
            total = total + jnp.sum(weights, axis=1, keepdims=True)
            accum = accum + jnp.dot(
                weights.astype(jnp.bfloat16), value, preferred_element_type=jnp.float32
            )
        result = (accum / total).astype(jnp.bfloat16)
        for h in range(4):
            out_ref[i * tok : (i + 1) * tok, h * HD : (h + 1) * HD] = result[
                h * tok : (h + 1) * tok
            ]


def output_kernel(where_ref, *refs):
    heads = refs[:LEVELS]
    w_mine, w_near, w_pair, mine_ref, other_ref = refs[LEVELS:]
    weights = (w_mine.at[0], w_near.at[0], w_pair.at[0], w_pair.at[1])
    level, place, core = where_ref[0], where_ref[1], where_ref[2]
    depth = heads[0].shape[1]
    width = w_mine.shape[2]
    part_rows = mine_ref.shape[1]
    for j in range(PLANE):
        total = None
        for k in range(LEVELS):
            start = pl.multiple_of(level_before(level, k) * depth, depth)
            part = jnp.dot(
                heads[k][...],
                weights[j][pl.ds(start, depth), :],
                preferred_element_type=jnp.float32,
            )
            total = part if total is None else total + part
        to = pl.multiple_of(place_of(j, place, core) * width, width)
        split = total.reshape(LEVELS, 2, part_rows, width)
        first, second = split[:, 0], split[:, 1]
        mine_ref[:, :, pl.ds(to, width)] = jnp.where(core == 0, first, second)
        other_ref[:, :, pl.ds(to, width)] = jnp.where(core == 0, second, first).astype(jnp.bfloat16)


SMEM = pl.BlockSpec(memory_space=pltpu.SMEM)
VMEM = pl.BlockSpec(memory_space=pltpu.VMEM)
PARAMS = pltpu.CompilerParams(vmem_limit_bytes=48 * 1024 * 1024)


def by_levels(
    text_rows,
    picture_rows,
    picture_slots,
    norm_gain,
    w_query,
    w_key,
    w_value,
    w_out,
    cache_keys,
    cache_values,
    recompute_rows,
    recompute_slots,
):
    seq_index = lax.axis_index("seq")
    core = lax.axis_index("head")
    level, place = seq_index // PLANE, seq_index % PLANE
    where = jnp.stack([level, place, core]).astype(jnp.int32)
    tok, width = text_rows.shape
    depth = w_query.shape[0]

    stream_len = tok * LEVELS * PLANE
    tile_owners = TILE_RUN // tok
    first = stream_len // 2 // tok
    last = (stream_len - TILE_RUN) // tok
    owners = [first + i for i in range(tile_owners)] + [last + i for i in range(tile_owners)]
    senders = tok // picture_rows.shape[0]
    received = []
    for k in range(senders):
        perm = [
            ((i * senders + k) * 2 + c, owner * 2 + c)
            for i, owner in enumerate(owners)
            for c in range(2)
        ]
        received.append(lax.ppermute(picture_rows, ("seq", "head"), perm))
    placed = jnp.concatenate(received, axis=0)
    is_owner = jnp.any(seq_index == jnp.array(owners, jnp.int32))
    stream = jnp.where(is_owner, placed, text_rows)

    slots = (recompute_slots - seq_index * CACHED).astype(jnp.bfloat16)
    slot_rows = jnp.broadcast_to(
        jnp.pad(slots, (0, CACHED // 2 - REC))[:, None], (CACHED // 2, 2 * HD)
    )

    def piece_for(to_level):
        q = lax.dynamic_slice_in_dim(w_query, to_level * 4 * HD, 4 * HD, 1)
        k, v, old_k, old_v = (
            lax.dynamic_slice_in_dim(a, to_level * HD, HD, 1)
            for a in (w_key, w_value, cache_keys, cache_values)
        )
        old = jnp.concatenate([old_k, old_v], axis=1)
        half = CACHED // 2
        old = jnp.concatenate([old[:half], old[half:], slot_rows], axis=1)
        return jnp.concatenate([jnp.concatenate([q, k, v], axis=1), old], axis=0)[None]

    pieces = [piece_for((level + d) % LEVELS) for d in range(LEVELS)]
    moved = [up(piece, d) if d else piece for d, piece in enumerate(pieces)]
    gathered = []
    for levels in GROUPS:
        group = [moved[d] for d in levels]
        gathered += in_plane(group[0] if len(group) == 1 else jnp.concatenate(group, axis=0))

    rows = jnp.concatenate(
        [stream, recompute_rows, jnp.zeros((REC_PAD - REC, width), stream.dtype)], axis=0
    )
    wide = rows.astype(jnp.float32)
    squares = jnp.sum(wide * wide, axis=1)
    squares = squares + other_core(squares)
    gain = lax.dynamic_slice_in_dim(norm_gain, core * width, width, 0)
    held = scaled(wide, squares, gain)
    acts = []
    for k in range(LEVELS):
        if k:
            held = up(held, 1)
        acts += [held, other_core(held)]

    half = HD // 2
    freqs = ROPE_BASE ** (-jnp.arange(half, dtype=jnp.float32) / half)
    blocks = (jnp.arange(LEVELS, dtype=jnp.int32) * PLANE + place)[:, None]
    stream_pos = (
        CACHED * LEVELS * PLANE + blocks * tok + jnp.arange(tok, dtype=jnp.int32)[None]
    ).astype(jnp.float32)
    cache_pos = (blocks * CACHED + jnp.arange(CACHED, dtype=jnp.int32)[None]).astype(jnp.float32)
    angles = jnp.concatenate([stream_pos, cache_pos], axis=1)[..., None] * freqs
    cosine, sine = jnp.cos(angles), jnp.sin(angles)
    cosine = jnp.concatenate([cosine, cosine], axis=-1)
    sine = jnp.concatenate([-sine, sine], axis=-1)

    query, kv = pl.pallas_call(
        project_kernel,
        out_shape=(
            jax.ShapeDtypeStruct((LEVELS, 4, tok, HD), jnp.bfloat16),
            jax.ShapeDtypeStruct((LEVELS, tok + REC_PAD, 2 * HD), jnp.bfloat16),
        ),
        in_specs=[SMEM] + [VMEM] * 19,
        out_specs=(VMEM, VMEM),
        scratch_shapes=[pltpu.VMEM((LEVELS * (tok + REC_PAD), 2 * width), jnp.bfloat16)],
        compiler_params=PARAMS,
        name="project",
    )(where, *acts, *gathered, cosine, sine)

    kv_mine, kv_near, kv_pair = in_plane(kv[None])
    old_rows = [
        pl.BlockSpec(
            (a.shape[0], CACHED // 2, a.shape[2]), lambda i: (0, depth // (CACHED // 2), 0)
        )
        for a in gathered
    ]

    def whole(shape):
        return pl.BlockSpec(shape, lambda i: (0,) * len(shape))

    attended = pl.pallas_call(
        attend_kernel,
        grid=(1,),
        out_shape=jax.ShapeDtypeStruct((LEVELS * tok, 4 * HD), jnp.bfloat16),
        in_specs=[SMEM]
        + [whole(a.shape) for a in (query, kv_mine, kv_near, kv_pair)]
        + old_rows,
        out_specs=whole((LEVELS * tok, 4 * HD)),
        scratch_shapes=[pltpu.VMEM((PLANE, LEVELS * CACHED, 2 * HD), jnp.bfloat16)],
        compiler_params=PARAMS,
        name="attend",
    )(where, query, kv_mine, kv_near, kv_pair, *gathered)

    w_out, kv_pair = lax.optimization_barrier((w_out, kv_pair))
    out_weights = in_plane(w_out[None])
    heads = [attended]
    for k in range(1, LEVELS):
        heads.append(up(heads[-1], 1))
    part = tok // 2
    wide_cols = PLANE * w_out.shape[1]
    mine, other = pl.pallas_call(
        output_kernel,
        out_shape=(
            jax.ShapeDtypeStruct((LEVELS, part, wide_cols), jnp.float32),
            jax.ShapeDtypeStruct((LEVELS, part, wide_cols), jnp.bfloat16),
        ),
        in_specs=[SMEM] + [VMEM] * (LEVELS + 3),
        out_specs=(VMEM, VMEM),
        compiler_params=PARAMS,
        name="output",
    )(where, *heads, *out_weights)
    summed = (mine + other_core(other).astype(jnp.float32)).astype(jnp.bfloat16)
    columns = []
    for d in range(LEVELS):
        block = lax.dynamic_index_in_dim(summed, (level + d) % LEVELS, 0, keepdims=False)
        columns.append(up(block, d) if d else block)
    by_level = jnp.stack(columns)[(level - jnp.arange(LEVELS, dtype=jnp.int32)) % LEVELS]
    halves = by_level.reshape(2, LEVELS // 2, part, wide_cols)
    keep = lax.dynamic_index_in_dim(halves, core, 0, keepdims=False)
    give = lax.dynamic_index_in_dim(halves, 1 - core, 0, keepdims=False)
    got = other_core(give)
    top = jnp.where(core == 0, keep, got)
    low = jnp.where(core == 0, got, keep)
    both = jnp.stack([top, low])
    return jnp.transpose(both, (0, 2, 1, 3)).reshape(tok, width)


def solution(mesh):
    def run(*args):
        kv_local = args[5].shape[1] // HD // mesh.shape["head"]
        levels_fit = (
            mesh.shape["seq"] == LEVELS * PLANE
            and mesh.shape["head"] == 2
            and kv_local == LEVELS
            and args[1].shape[0] == 2 * TILE_RUN
            and args[0].shape[0] == 2048
            and args[8].shape[0] == LEVELS * PLANE * CACHED
            and args[10].shape[0] == LEVELS * PLANE * REC
        )
        return jax.shard_map(
            by_levels if levels_fit else on_device,
            mesh=mesh,
            in_specs=(
                P("seq", "head"),
                P("seq", "head"),
                P("seq"),
                P(),
                P("seq", "head"),
                P("seq", "head"),
                P("seq", "head"),
                P("head", "seq"),
                P("seq", "head"),
                P("seq", "head"),
                P("seq", "head"),
                P("seq"),
            ),
            out_specs=P("seq", "head"),
            check_vma=False,
        )(*args)

    return run
```

```python
import functools

import jax
import jax.numpy as jnp
from jax import lax
from jax.experimental import pallas as pl
from jax.experimental.pallas import tpu as pltpu
from jax.sharding import PartitionSpec as P

D = 4096
HD = 128


EPSILON = 1e-05
ROPE_BASE = 1000000.0
NEG_FILL = -1e30


def rotate(values, positions):
    half = values.shape[-1] // 2
    freqs = ROPE_BASE ** (-jnp.arange(half, dtype=jnp.float32) / half)
    angles = positions[:, None] * freqs[None, :]
    cosine = jnp.cos(angles)[:, None, :]
    sine = jnp.sin(angles)[:, None, :]
    first = values[..., :half]
    second = values[..., half:]
    return jnp.concatenate(
        [first * cosine - second * sine, second * cosine + first * sine], axis=-1
    )


def scaled(rows_wide, squares, gain):
    return (rows_wide * lax.rsqrt(squares / D + EPSILON)[:, None] * gain[None, :]).astype(
        jnp.bfloat16
    )


def attend(carry, key_piece, value_piece, queries, allowed):
    best, total, accum = carry
    count = key_piece.shape[0]
    kv_local = queries.shape[0]
    keys_split = key_piece.reshape(count, kv_local, HD)
    values_split = value_piece.reshape(count, kv_local, HD)
    scores = jnp.einsum(
        "kgtd,nkd->kgtn", queries, keys_split, preferred_element_type=jnp.float32
    ) * HD ** (-0.5)
    scores = jnp.where(allowed, scores, NEG_FILL)
    fresh = jnp.maximum(best, jnp.max(scores, axis=-1))
    factor = jnp.exp(best - fresh)
    weights = jnp.where(allowed, jnp.exp(scores - fresh[..., None]), 0.0)
    total = total * factor + jnp.sum(weights, axis=-1)
    accum = accum * factor[..., None] + jnp.einsum(
        "kgtn,nkd->kgtd",
        weights.astype(jnp.bfloat16),
        values_split,
        preferred_element_type=jnp.float32,
    )
    return (fresh, total, accum)


def on_device(
    text_rows,
    picture_rows,
    picture_slots,
    norm_gain,
    w_query,
    w_key,
    w_value,
    w_out,
    cache_keys,
    cache_values,
    recompute_rows,
    recompute_slots,
):
    tok_rows = text_rows.shape[0]
    rec_count = recompute_rows.shape[0]
    cache_rows = cache_keys.shape[0]
    seq_index = lax.axis_index("seq")
    local_pos = seq_index * tok_rows + jnp.arange(tok_rows, dtype=jnp.int32)
    rows_piece = lax.all_gather(picture_rows, "seq", axis=0, tiled=True)
    slots_piece = lax.all_gather(picture_slots, "seq", axis=0, tiled=True)
    select = (slots_piece[None, :] == local_pos[:, None]).astype(jnp.bfloat16)
    placed = jnp.dot(select, rows_piece, preferred_element_type=jnp.float32)
    hits = jnp.sum(select.astype(jnp.float32), axis=1)
    added, hits = (placed, hits)
    stream = jnp.where(hits[:, None] > 0.5, added, text_rows.astype(jnp.float32)).astype(
        jnp.bfloat16
    )
    slice_width = stream.shape[1]
    gain_slice = lax.dynamic_slice_in_dim(
        norm_gain, lax.axis_index("head") * slice_width, slice_width, 0
    )
    stream_wide = stream.astype(jnp.float32)
    rec_wide = recompute_rows.astype(jnp.float32)
    stream_sq, rec_sq = lax.psum(
        (jnp.sum(stream_wide * stream_wide, axis=1), jnp.sum(rec_wide * rec_wide, axis=1)), "head"
    )
    normed, rec_normed = (
        lax.all_gather(scaled(stream_wide, stream_sq, gain_slice), "head", axis=1, tiled=True),
        lax.all_gather(scaled(rec_wide, rec_sq, gain_slice), "head", axis=1, tiled=True),
    )
    stacked = jnp.concatenate([normed, rec_normed], axis=0)
    query_cols = w_query.shape[1]
    key_cols = w_key.shape[1]
    pieces = (
        lax.all_gather(w_query, "seq", axis=0, tiled=True),
        lax.all_gather(w_key, "seq", axis=0, tiled=True),
        lax.all_gather(w_value, "seq", axis=0, tiled=True),
    )
    query_all = jnp.dot(stacked, pieces[0], preferred_element_type=jnp.float32)
    key_all = jnp.dot(stacked, pieces[1], preferred_element_type=jnp.float32)
    value_all = jnp.dot(stacked, pieces[2], preferred_element_type=jnp.float32)
    cache_total = cache_rows * lax.axis_size("seq")
    stream_pos = (cache_total + local_pos).astype(jnp.float32)
    rec_pos = recompute_slots.astype(jnp.float32)
    heads_local = query_cols // HD
    kv_local = key_cols // HD
    group = heads_local // kv_local
    rot_query = rotate(query_all[:tok_rows].reshape(tok_rows, heads_local, HD), stream_pos).astype(
        jnp.bfloat16
    )
    rot_key = (
        rotate(key_all[:tok_rows].reshape(tok_rows, kv_local, HD), stream_pos)
        .astype(jnp.bfloat16)
        .reshape(tok_rows, key_cols)
    )
    values_new = value_all[:tok_rows].astype(jnp.bfloat16)
    rot_rec_key = (
        rotate(key_all[tok_rows:].reshape(rec_count, kv_local, HD), rec_pos)
        .astype(jnp.bfloat16)
        .reshape(rec_count, key_cols)
    )
    rec_values = value_all[tok_rows:].astype(jnp.bfloat16)
    local_slots = recompute_slots - seq_index * cache_rows
    select = local_slots[:, None] == jnp.arange(cache_rows, dtype=jnp.int32)[None, :]
    replaced = jnp.any(select, axis=0)[:, None]
    select_cols = select.astype(jnp.bfloat16).T
    new_keys = jnp.dot(select_cols, rot_rec_key, preferred_element_type=jnp.float32).astype(
        jnp.bfloat16
    )
    new_values = jnp.dot(select_cols, rec_values, preferred_element_type=jnp.float32).astype(
        jnp.bfloat16
    )
    cache_k = jnp.where(replaced, new_keys, cache_keys)
    cache_v = jnp.where(replaced, new_values, cache_values)
    queries = jnp.transpose(rot_query.reshape(tok_rows, kv_local, group, HD), (1, 2, 0, 3))
    carry_start = (
        jnp.full((kv_local, group, tok_rows), NEG_FILL, jnp.float32),
        jnp.zeros((kv_local, group, tok_rows), jnp.float32),
        jnp.zeros((kv_local, group, tok_rows, HD), jnp.float32),
    )
    pieces = (
        lax.all_gather(cache_k, "seq", axis=0, tiled=True),
        lax.all_gather(cache_v, "seq", axis=0, tiled=True),
    )
    allowed = jnp.ones((tok_rows, pieces[0].shape[0]), jnp.bool_)
    carry_mid = attend(carry_start, pieces[0], pieces[1], queries, allowed)
    pieces = (
        lax.all_gather(rot_key, "seq", axis=0, tiled=True),
        lax.all_gather(values_new, "seq", axis=0, tiled=True),
    )
    key_pos = jnp.arange(pieces[0].shape[0], dtype=jnp.int32)
    allowed = key_pos[None, :] <= local_pos[:, None]
    best, total, accum = attend(carry_mid, pieces[0], pieces[1], queries, allowed)
    attended = (
        jnp.transpose(accum / total[..., None], (2, 0, 1, 3))
        .reshape(tok_rows, query_cols)
        .astype(jnp.bfloat16)
    )
    partial_out = jnp.dot(
        attended,
        lax.all_gather(w_out, "seq", axis=1, tiled=True),
        preferred_element_type=jnp.float32,
    )
    return lax.psum_scatter(
        partial_out.astype(jnp.bfloat16), "head", scatter_dimension=1, tiled=True
    )


LEVELS = 4
PLANE = 4
TILE_RUN = 256
CACHED = 64
REC = 8
REC_PAD = 16


def permuted(value, move):
    perm = []
    for level in range(LEVELS):
        for place in range(PLANE):
            for core in range(2):
                target = move(level, place, core)
                if target is not None:
                    to_level, to_place, to_core = target
                    perm.append(
                        (
                            (level * PLANE + place) * 2 + core,
                            (to_level * PLANE + to_place) * 2 + to_core,
                        )
                    )
    return lax.ppermute(value, ("seq", "head"), perm)


def up(value, steps):
    return permuted(value, lambda z, p, c: ((z + steps) % LEVELS, p, c))


def climb(value, hop):
    return permuted(value, lambda z, p, c: (z + 1, p, c) if hop - 1 <= z < LEVELS - 1 else None)


def descend(value, hop):
    return permuted(value, lambda z, p, c: (z - 1, p, c) if 0 < z <= LEVELS - hop else None)


def other_core(value):
    return permuted(value, lambda z, p, c: (z, p, 1 - c))


def to_near(value):
    return permuted(value, lambda z, p, c: (z, p ^ (1 + c), c))


def to_far(value):
    return permuted(value, lambda z, p, c: (z, p ^ (2 - c), c))


def in_plane(pieces):
    near = to_near(pieces)
    pair = to_far(jnp.concatenate([pieces, near], axis=0))
    return pieces, near, pair


def place_of(which, place, core):
    if which == 0:
        return place
    if which == 3:
        return place ^ 3
    return place ^ (1 + core) if which == 1 else place ^ (2 - core)


def level_before(level, steps):
    return lax.rem(level + LEVELS - steps, LEVELS)


GATHERED = 10
PIECES = {
    0: ((0, 0), (1, 0), (2, 0), (2, 1)),
    1: ((3, 0), (4, 0), (5, 0), (5, 1)),
    2: ((7, 0), (8, 0), (9, 0), (9, 1)),
    3: ((3, 1), (4, 1), (6, 0), (6, 1)),
}


def piece_at(refs, which, steps):
    array, index = PIECES[steps][which]
    return refs[array].at[index]


def turned(values, cosine, sine):
    return values * cosine + pltpu.roll(values, HD // 2, 1) * sine


def norm_kernel(where_ref, mine_ref, other_ref, gain_ref, *out_refs):
    out_ref = out_refs[-1]
    core = where_ref[2]
    width = mine_ref.shape[1]
    mine = mine_ref[...].astype(jnp.float32)
    other = other_ref[...].astype(jnp.float32)
    squares = jnp.sum(mine * mine + other * other, axis=1, keepdims=True)
    factor = lax.rsqrt(squares / D + EPSILON)
    for values, at in ((mine, core), (other, 1 - core)):
        to = pl.multiple_of(at * width, width)
        out_ref[:, pl.ds(to, width)] = (values * factor * gain_ref[:, pl.ds(to, width)]).astype(
            jnp.bfloat16
        )


def products(where_ref, x_ref, groups, depth):
    level, place, core = where_ref[0], where_ref[1], where_ref[2]
    total = None
    for d in range(LEVELS):
        for j in range(PLANE):
            block = level_before(level, d) * PLANE + place_of(j, place, core)
            start = pl.multiple_of(block * depth, depth)
            part = jnp.dot(
                x_ref[:, pl.ds(start, depth)],
                piece_at(groups, j, d)[0:depth, :],
                preferred_element_type=jnp.float32,
            )
            total = part if total is None else total + part
    return total


def keys_kernel(where_ref, x_ref, *refs):
    groups = refs[:GATHERED]
    slot_refs = refs[GATHERED : GATHERED + 3]
    cos_ref, sin_ref, kv_ref = refs[GATHERED + 3 :]
    depth = refs[0].shape[1] - CACHED // 2
    total = products(where_ref, x_ref, groups, depth)
    rows = total.shape[0] // LEVELS
    tok = rows - REC_PAD
    lane = lax.broadcasted_iota(jnp.int32, (REC, CACHED), 1)
    for k in range(LEVELS):
        at = where_ref[3 + k]
        block = total[k * rows : (k + 1) * rows]
        cosine, sine = cos_ref[at], sin_ref[at]
        kv_ref[0, at, 0:tok, 0:HD] = turned(block[:tok, 0:HD], cosine[:tok], sine[:tok]).astype(
            jnp.bfloat16
        )
        kv_ref[0, at, 0:tok, HD : 2 * HD] = block[:tok, HD : 2 * HD].astype(jnp.bfloat16)
        before = level_before(where_ref[0], at)
        slots = jnp.where(
            before == 0,
            slot_refs[0][0, 0:REC_PAD, 0:CACHED].astype(jnp.float32),
            jnp.where(
                before == 2,
                slot_refs[2][0, 0:REC_PAD, 0:CACHED].astype(jnp.float32),
                slot_refs[1][before // 2, 0:REC_PAD, 0:CACHED].astype(jnp.float32),
            ),
        )
        chosen = (slots[0:REC].astype(jnp.int32) == lane).astype(jnp.float32)
        rec_cos, rec_sin = (
            jnp.dot(
                chosen,
                table[tok : tok + CACHED],
                preferred_element_type=jnp.float32,
                precision=lax.Precision.HIGHEST,
            )
            for table in (cosine, sine)
        )
        rec_keys = turned(block[tok : tok + REC, 0:HD], rec_cos, rec_sin)
        both = jnp.concatenate([rec_keys, block[tok : tok + REC, HD : 2 * HD]], axis=1)
        both = jnp.concatenate([both, jnp.zeros_like(both)], axis=0)
        kv_ref[0, at, tok : tok + REC_PAD, :] = both.astype(jnp.bfloat16)


def queries_kernel(where_ref, x_ref, *refs):
    groups = refs[:GATHERED]
    cos_ref, sin_ref, query_ref = refs[GATHERED:]
    depth = refs[0].shape[1] - CACHED // 2
    total = products(where_ref, x_ref, groups, depth)
    rows = total.shape[0] // LEVELS
    tok = rows - REC_PAD
    for k in range(LEVELS):
        at = where_ref[3 + k]
        cosine, sine = cos_ref[at][:tok], sin_ref[at][:tok]
        for h in range(4):
            head = total[k * rows : k * rows + tok, h * HD : (h + 1) * HD]
            query_ref[at, h] = turned(head, cosine, sine).astype(jnp.bfloat16)


def attend_kernel(where_ref, query_ref, *refs):
    kvs = [ref.at[0] for ref in refs[:4]]
    groups = refs[4 : 4 + GATHERED]
    out_ref, cache_ref = refs[4 + GATHERED :]
    level, place, core = where_ref[0], where_ref[1], where_ref[2]
    tok = query_ref.shape[2]
    line = lax.broadcasted_iota(jnp.int32, (CACHED, 2 * HD), 0)
    for j in range(PLANE):
        for d in range(LEVELS):
            at = level_before(level, d)
            piece = piece_at(groups, j, d)
            slots = piece[0:REC_PAD, 4 * HD : 6 * HD].astype(jnp.int32)
            cached = jnp.concatenate(
                [piece[:, 0 : 2 * HD], piece[:, 2 * HD : 4 * HD]], axis=0
            ).astype(jnp.float32)
            fresh = kvs[j][at, tok : tok + REC_PAD, :].astype(jnp.float32)
            for r in range(REC):
                cached = jnp.where(line == slots[r : r + 1], fresh[r : r + 1], cached)
            cache_ref[j, d * CACHED : (d + 1) * CACHED, :] = cached.astype(jnp.bfloat16)
    row = lax.broadcasted_iota(jnp.int32, (tok, tok), 0)
    col = lax.broadcasted_iota(jnp.int32, (tok, tok), 1)
    scale = HD ** (-0.5) * 1.4426950408889634

    def scores_of(queries, keys):
        return lax.dot_general(
            queries, keys, (((1,), (1,)), ((), ())), preferred_element_type=jnp.float32
        )

    for i in range(LEVELS):
        queries = query_ref[i].reshape(4 * tok, HD)
        scores, values = [], []
        for j in range(PLANE):
            scores.append(scores_of(queries, cache_ref[j, :, 0:HD]))
            values.append(cache_ref[j, :, HD : 2 * HD])
            if i:
                scores.append(scores_of(queries, kvs[j][0:i, 0:tok, 0:HD].reshape(i * tok, HD)))
                values.append(kvs[j][0:i, 0:tok, HD : 2 * HD].reshape(i * tok, HD))
            raw = scores_of(queries, kvs[j][i, 0:tok, 0:HD])
            if j == 0:
                allowed = col <= row
            else:
                allowed = jnp.broadcast_to(place_of(j, place, core), (tok, tok)) < place
            scores.append(jnp.where(jnp.concatenate([allowed] * 4, axis=0), raw, NEG_FILL))
            values.append(kvs[j][i, 0:tok, HD : 2 * HD])
        best = jnp.max(scores[0], axis=1, keepdims=True)
        for raw in scores[1:]:
            best = jnp.maximum(best, jnp.max(raw, axis=1, keepdims=True))
        total, accum = 0.0, 0.0
        for raw, value in zip(scores, values):
            weights = jnp.exp2((raw - best) * scale)
            total = total + jnp.sum(weights, axis=1, keepdims=True)
            accum = accum + jnp.dot(
                weights.astype(jnp.bfloat16), value, preferred_element_type=jnp.float32
            )
        result = (accum / total).astype(jnp.bfloat16)
        for h in range(4):
            out_ref[i * tok : (i + 1) * tok, h * HD : (h + 1) * HD] = result[
                h * tok : (h + 1) * tok
            ]


def output_kernel(where_ref, *refs):
    heads = refs[:LEVELS]
    w_mine, w_near, w_pair, mine_ref, other_ref = refs[LEVELS:]
    weights = (w_mine.at[0], w_near.at[0], w_pair.at[0], w_pair.at[1])
    level, place, core = where_ref[0], where_ref[1], where_ref[2]
    depth = heads[0].shape[1]
    width = w_mine.shape[2]
    part_rows = mine_ref.shape[1]
    for j in range(PLANE):
        total = None
        for k in range(LEVELS):
            start = pl.multiple_of(level_before(level, k) * depth, depth)
            part = jnp.dot(
                heads[k][...],
                weights[j][pl.ds(start, depth), :],
                preferred_element_type=jnp.float32,
            )
            total = part if total is None else total + part
        to = pl.multiple_of(place_of(j, place, core) * width, width)
        split = total.reshape(LEVELS, 2, part_rows, width)
        first, second = split[:, 0], split[:, 1]
        mine_ref[:, :, pl.ds(to, width)] = jnp.where(core == 0, first, second)
        other_ref[:, :, pl.ds(to, width)] = jnp.where(core == 0, second, first).astype(jnp.bfloat16)


SMEM = pl.BlockSpec(memory_space=pltpu.SMEM)
VMEM = pl.BlockSpec(memory_space=pltpu.VMEM)
PARAMS = pltpu.CompilerParams(vmem_limit_bytes=48 * 1024 * 1024)


def by_levels(
    text_rows,
    picture_rows,
    picture_slots,
    norm_gain,
    w_query,
    w_key,
    w_value,
    w_out,
    cache_keys,
    cache_values,
    recompute_rows,
    recompute_slots,
):
    seq_index = lax.axis_index("seq")
    core = lax.axis_index("head")
    level, place = seq_index // PLANE, seq_index % PLANE
    blocks_at = jnp.stack(
        [
            level,
            jnp.where(level == 0, 1, level - 1),
            jnp.where(level < 2, 2, jnp.where(level == 2, 3, 1)),
            jnp.where(level < 2, 3, 0),
        ]
    )
    where = jnp.concatenate([jnp.stack([level, place, core]), blocks_at]).astype(jnp.int32)
    tok, width = text_rows.shape
    depth = w_query.shape[0]

    stream_len = tok * LEVELS * PLANE
    tile_owners = TILE_RUN // tok
    first = stream_len // 2 // tok
    last = (stream_len - TILE_RUN) // tok
    owners = [first + i for i in range(tile_owners)] + [last + i for i in range(tile_owners)]
    next_pictures = permuted(picture_rows, lambda z, p, c: (z, p ^ 1, c))
    pair = jnp.concatenate([picture_rows, next_pictures], axis=0)

    def to_owner(z, p, c, place):
        return (owners[z] // PLANE, owners[z] % PLANE, c) if p == place else None

    placed = jnp.concatenate(
        [permuted(pair, functools.partial(to_owner, place=place)) for place in (0, 2)], axis=0
    )
    is_owner = jnp.any(seq_index == jnp.array(owners, jnp.int32))
    stream = jnp.where(is_owner, placed, text_rows)

    slots = (recompute_slots - seq_index * CACHED).astype(jnp.bfloat16)
    slot_rows = jnp.broadcast_to(
        jnp.pad(slots, (0, CACHED // 2 - REC))[:, None], (CACHED // 2, 2 * HD)
    )

    def piece_for(to_level):
        q = lax.dynamic_slice_in_dim(w_query, to_level * 4 * HD, 4 * HD, 1)
        k, v, old_k, old_v = (
            lax.dynamic_slice_in_dim(a, to_level * HD, HD, 1)
            for a in (w_key, w_value, cache_keys, cache_values)
        )
        old = jnp.concatenate([old_k, old_v], axis=1)
        half = CACHED // 2
        old = jnp.concatenate([old[:half], old[half:], slot_rows], axis=1)
        return jnp.concatenate([jnp.concatenate([q, k, v], axis=1), old], axis=0)[None]

    def whole(shape):
        return pl.BlockSpec(shape, lambda i: (0,) * len(shape))

    block_rows = tok + REC_PAD

    def normalise(normed, k, block, other):
        return pl.pallas_call(
            norm_kernel,
            grid=(1,),
            out_shape=jax.ShapeDtypeStruct((LEVELS * block_rows, 2 * width), jnp.bfloat16),
            in_specs=[SMEM, *(whole((block_rows, width)),) * 2, whole((1, 2 * width))]
            + [pl.BlockSpec(memory_space=pl.ANY)] * (k > 0),
            out_specs=pl.BlockSpec((block_rows, 2 * width), lambda i: (k, 0)),
            input_output_aliases={4: 0} if k else {},
            compiler_params=PARAMS,
            name="norm",
        )(where, block, other, norm_gain[None], *([normed] if k else []))

    pieces = [piece_for((level + d) % LEVELS) for d in range(LEVELS)]
    rows = jnp.concatenate(
        [stream, recompute_rows, jnp.zeros((REC_PAD - REC, width), stream.dtype)], axis=0
    )
    near0 = to_near(pieces[0])
    z1, z2, z3 = (up(pieces[d], d) for d in (1, 2, 3))
    rows, near0, z1, z3 = lax.optimization_barrier((rows, near0, z1, z3))
    far0 = to_far(jnp.concatenate([pieces[0], near0], axis=0))
    z13 = jnp.concatenate([z1, z3], axis=0)
    near13 = to_near(z13)
    u1, d1 = climb(rows, 1), descend(rows, 1)
    u1, d1, near13, far0, z2 = lax.optimization_barrier((u1, d1, near13, far0, z2))
    far1 = to_far(jnp.concatenate([z1, near13[0:1]], axis=0))
    near2 = to_near(z2)
    u2, d2 = climb(u1, 2), descend(d1, 2)
    normed = normalise(None, 0, rows, other_core(rows))
    block1 = jnp.where(level == 0, d1, u1)
    other1 = other_core(block1)
    u2, d2, normed, other1, far1, near2 = lax.optimization_barrier(
        (u2, d2, normed, other1, far1, near2)
    )
    far3 = to_far(jnp.concatenate([z3, near13[1:2]], axis=0))
    far2 = to_far(jnp.concatenate([z2, near2], axis=0))
    u3, d3 = climb(u2, 3), descend(d2, 3)
    normed = normalise(normed, 1, block1, other1)
    block2 = jnp.where(level == 0, d2, jnp.where(level == 3, u2, d1))
    normed = normalise(normed, 2, block2, other_core(block2))
    u3, d3, normed, far3 = lax.optimization_barrier((u3, d3, normed, far3))
    gathered = [pieces[0], near0, far0, z13, near13, far1, far3, z2, near2, far2]
    block3 = jnp.where(level == 0, d3, jnp.where(level == 3, u3, jnp.where(level == 1, d2, u2)))
    normed = normalise(normed, 3, block3, other_core(block3))

    half = HD // 2
    freqs = ROPE_BASE ** (-jnp.arange(half, dtype=jnp.float32) / half)
    blocks = (jnp.arange(LEVELS, dtype=jnp.int32) * PLANE + place)[:, None]
    stream_pos = (
        CACHED * LEVELS * PLANE + blocks * tok + jnp.arange(tok, dtype=jnp.int32)[None]
    ).astype(jnp.float32)
    cache_pos = (blocks * CACHED + jnp.arange(CACHED, dtype=jnp.int32)[None]).astype(jnp.float32)
    angles = jnp.concatenate([stream_pos, cache_pos], axis=1)[..., None] * freqs
    cosine, sine = jnp.cos(angles), jnp.sin(angles)
    cosine = jnp.concatenate([cosine, cosine], axis=-1)
    sine = jnp.concatenate([-sine, sine], axis=-1)

    def lanes(a, width, at):
        return pl.BlockSpec((*a.shape[:2], width), lambda i: (0, 0, at))

    def old_rows(a, width, at):
        return pl.BlockSpec(
            (a.shape[0], CACHED // 2, width), lambda i: (0, depth // (CACHED // 2), at)
        )

    tables = [whole(cosine.shape)] * 2
    kv = pl.pallas_call(
        keys_kernel,
        grid=(1,),
        out_shape=jax.ShapeDtypeStruct((1, LEVELS, block_rows, 2 * HD), jnp.bfloat16),
        in_specs=[SMEM, whole(normed.shape)]
        + [lanes(a, 2 * HD, 2) for a in gathered]
        + [old_rows(gathered[i], 2 * HD, 2) for i in (0, 3, 7)]
        + tables,
        out_specs=whole((1, LEVELS, block_rows, 2 * HD)),
        compiler_params=PARAMS,
        name="keys",
    )(where, normed, *gathered, gathered[0], gathered[3], gathered[7], cosine, sine)
    kv_near, kv_far = to_near(kv), to_far(kv)
    kv_both = to_far(kv_near)
    query = pl.pallas_call(
        queries_kernel,
        grid=(1,),
        out_shape=jax.ShapeDtypeStruct((LEVELS, 4, tok, HD), jnp.bfloat16),
        in_specs=[SMEM, whole(normed.shape)] + [lanes(a, 4 * HD, 0) for a in gathered] + tables,
        out_specs=whole((LEVELS, 4, tok, HD)),
        compiler_params=PARAMS,
        name="queries",
    )(where, normed, *gathered, cosine, sine)

    w_out, kv_both, kv_far, query = lax.optimization_barrier(
        (w_out[None], kv_both, kv_far, query)
    )
    w_near = to_near(w_out)
    kvs = (kv, kv_near, kv_far, kv_both)
    attended = pl.pallas_call(
        attend_kernel,
        grid=(1,),
        out_shape=jax.ShapeDtypeStruct((LEVELS * tok, 4 * HD), jnp.bfloat16),
        in_specs=[SMEM, whole(query.shape)]
        + [whole(kv.shape)] * 4
        + [old_rows(a, 6 * HD, 0) for a in gathered],
        out_specs=whole((LEVELS * tok, 4 * HD)),
        scratch_shapes=[pltpu.VMEM((PLANE, LEVELS * CACHED, 2 * HD), jnp.bfloat16)],
        compiler_params=PARAMS,
        name="attend",
    )(where, query, *kvs, *gathered)

    heads = [attended]
    for k in range(1, LEVELS):
        heads.append(up(heads[-1], 1))
        if k == 1:
            w_near, heads[1] = lax.optimization_barrier((w_near, heads[1]))
    out_weights = [w_out, w_near, to_far(jnp.concatenate([w_out, w_near], axis=0))]
    part = tok // 2
    wide_cols = PLANE * w_out.shape[2]
    mine, other = pl.pallas_call(
        output_kernel,
        out_shape=(
            jax.ShapeDtypeStruct((LEVELS, part, wide_cols), jnp.float32),
            jax.ShapeDtypeStruct((LEVELS, part, wide_cols), jnp.bfloat16),
        ),
        in_specs=[SMEM] + [VMEM] * (LEVELS + 3),
        out_specs=(VMEM, VMEM),
        compiler_params=PARAMS,
        name="output",
    )(where, *heads, *out_weights)
    summed = (mine + other_core(other).astype(jnp.float32)).astype(jnp.bfloat16)
    source = (level % 2) * 2 + core
    received = []
    for e in range(LEVELS):
        block = lax.dynamic_index_in_dim(summed, (source + e) % LEVELS, 0, keepdims=False)
        received.append(
            permuted(
                block,
                lambda z, p, c, e=e: (((z % 2) * 2 + c + e) % LEVELS, p, z // 2),
            )
        )
    by_source = jnp.stack(received)[(level - jnp.arange(LEVELS, dtype=jnp.int32)) % LEVELS]
    by_source = by_source.reshape(2, 2, part, wide_cols)
    return jnp.transpose(by_source, (1, 2, 0, 3)).reshape(tok, width)


def solution(mesh):
    def run(*args):
        kv_local = args[5].shape[1] // HD // mesh.shape["head"]
        levels_fit = (
            mesh.shape["seq"] == LEVELS * PLANE
            and mesh.shape["head"] == 2
            and kv_local == LEVELS
            and args[1].shape[0] == 2 * TILE_RUN
            and args[0].shape[0] == 2048
            and args[8].shape[0] == LEVELS * PLANE * CACHED
            and args[10].shape[0] == LEVELS * PLANE * REC
        )
        return jax.shard_map(
            by_levels if levels_fit else on_device,
            mesh=mesh,
            in_specs=(
                P("seq", "head"),
                P("seq", "head"),
                P("seq"),
                P(),
                P("seq", "head"),
                P("seq", "head"),
                P("seq", "head"),
                P("head", "seq"),
                P("seq", "head"),
                P("seq", "head"),
                P("seq", "head"),
                P("seq"),
            ),
            out_specs=P("seq", "head"),
            check_vma=False,
        )(*args)

    return run
```

```python
import jax
import jax.numpy as jnp
from jax import lax
from jax.experimental import pallas as pl
from jax.experimental.pallas import tpu as pltpu
from jax.sharding import PartitionSpec as P

D = 4096
HD = 128


EPSILON = 1e-05
ROPE_BASE = 1000000.0
NEG_FILL = -1e30


def rotate(values, positions):
    half = values.shape[-1] // 2
    freqs = ROPE_BASE ** (-jnp.arange(half, dtype=jnp.float32) / half)
    angles = positions[:, None] * freqs[None, :]
    cosine = jnp.cos(angles)[:, None, :]
    sine = jnp.sin(angles)[:, None, :]
    first = values[..., :half]
    second = values[..., half:]
    return jnp.concatenate(
        [first * cosine - second * sine, second * cosine + first * sine], axis=-1
    )


def scaled(rows_wide, squares, gain):
    return (rows_wide * lax.rsqrt(squares / D + EPSILON)[:, None] * gain[None, :]).astype(
        jnp.bfloat16
    )


def attend(carry, key_piece, value_piece, queries, allowed):
    best, total, accum = carry
    count = key_piece.shape[0]
    kv_local = queries.shape[0]
    keys_split = key_piece.reshape(count, kv_local, HD)
    values_split = value_piece.reshape(count, kv_local, HD)
    scores = jnp.einsum(
        "kgtd,nkd->kgtn", queries, keys_split, preferred_element_type=jnp.float32
    ) * HD ** (-0.5)
    scores = jnp.where(allowed, scores, NEG_FILL)
    fresh = jnp.maximum(best, jnp.max(scores, axis=-1))
    factor = jnp.exp(best - fresh)
    weights = jnp.where(allowed, jnp.exp(scores - fresh[..., None]), 0.0)
    total = total * factor + jnp.sum(weights, axis=-1)
    accum = accum * factor[..., None] + jnp.einsum(
        "kgtn,nkd->kgtd",
        weights.astype(jnp.bfloat16),
        values_split,
        preferred_element_type=jnp.float32,
    )
    return (fresh, total, accum)


def on_device(
    text_rows,
    picture_rows,
    picture_slots,
    norm_gain,
    w_query,
    w_key,
    w_value,
    w_out,
    cache_keys,
    cache_values,
    recompute_rows,
    recompute_slots,
):
    tok_rows = text_rows.shape[0]
    rec_count = recompute_rows.shape[0]
    cache_rows = cache_keys.shape[0]
    seq_index = lax.axis_index("seq")
    local_pos = seq_index * tok_rows + jnp.arange(tok_rows, dtype=jnp.int32)
    rows_piece = lax.all_gather(picture_rows, "seq", axis=0, tiled=True)
    slots_piece = lax.all_gather(picture_slots, "seq", axis=0, tiled=True)
    select = (slots_piece[None, :] == local_pos[:, None]).astype(jnp.bfloat16)
    placed = jnp.dot(select, rows_piece, preferred_element_type=jnp.float32)
    hits = jnp.sum(select.astype(jnp.float32), axis=1)
    added, hits = (placed, hits)
    stream = jnp.where(hits[:, None] > 0.5, added, text_rows.astype(jnp.float32)).astype(
        jnp.bfloat16
    )
    slice_width = stream.shape[1]
    gain_slice = lax.dynamic_slice_in_dim(
        norm_gain, lax.axis_index("head") * slice_width, slice_width, 0
    )
    stream_wide = stream.astype(jnp.float32)
    rec_wide = recompute_rows.astype(jnp.float32)
    stream_sq, rec_sq = lax.psum(
        (jnp.sum(stream_wide * stream_wide, axis=1), jnp.sum(rec_wide * rec_wide, axis=1)), "head"
    )
    normed, rec_normed = (
        lax.all_gather(scaled(stream_wide, stream_sq, gain_slice), "head", axis=1, tiled=True),
        lax.all_gather(scaled(rec_wide, rec_sq, gain_slice), "head", axis=1, tiled=True),
    )
    stacked = jnp.concatenate([normed, rec_normed], axis=0)
    query_cols = w_query.shape[1]
    key_cols = w_key.shape[1]
    pieces = (
        lax.all_gather(w_query, "seq", axis=0, tiled=True),
        lax.all_gather(w_key, "seq", axis=0, tiled=True),
        lax.all_gather(w_value, "seq", axis=0, tiled=True),
    )
    query_all = jnp.dot(stacked, pieces[0], preferred_element_type=jnp.float32)
    key_all = jnp.dot(stacked, pieces[1], preferred_element_type=jnp.float32)
    value_all = jnp.dot(stacked, pieces[2], preferred_element_type=jnp.float32)
    cache_total = cache_rows * lax.axis_size("seq")
    stream_pos = (cache_total + local_pos).astype(jnp.float32)
    rec_pos = recompute_slots.astype(jnp.float32)
    heads_local = query_cols // HD
    kv_local = key_cols // HD
    group = heads_local // kv_local
    rot_query = rotate(query_all[:tok_rows].reshape(tok_rows, heads_local, HD), stream_pos).astype(
        jnp.bfloat16
    )
    rot_key = (
        rotate(key_all[:tok_rows].reshape(tok_rows, kv_local, HD), stream_pos)
        .astype(jnp.bfloat16)
        .reshape(tok_rows, key_cols)
    )
    values_new = value_all[:tok_rows].astype(jnp.bfloat16)
    rot_rec_key = (
        rotate(key_all[tok_rows:].reshape(rec_count, kv_local, HD), rec_pos)
        .astype(jnp.bfloat16)
        .reshape(rec_count, key_cols)
    )
    rec_values = value_all[tok_rows:].astype(jnp.bfloat16)
    local_slots = recompute_slots - seq_index * cache_rows
    select = local_slots[:, None] == jnp.arange(cache_rows, dtype=jnp.int32)[None, :]
    replaced = jnp.any(select, axis=0)[:, None]
    select_cols = select.astype(jnp.bfloat16).T
    new_keys = jnp.dot(select_cols, rot_rec_key, preferred_element_type=jnp.float32).astype(
        jnp.bfloat16
    )
    new_values = jnp.dot(select_cols, rec_values, preferred_element_type=jnp.float32).astype(
        jnp.bfloat16
    )
    cache_k = jnp.where(replaced, new_keys, cache_keys)
    cache_v = jnp.where(replaced, new_values, cache_values)
    queries = jnp.transpose(rot_query.reshape(tok_rows, kv_local, group, HD), (1, 2, 0, 3))
    carry_start = (
        jnp.full((kv_local, group, tok_rows), NEG_FILL, jnp.float32),
        jnp.zeros((kv_local, group, tok_rows), jnp.float32),
        jnp.zeros((kv_local, group, tok_rows, HD), jnp.float32),
    )
    pieces = (
        lax.all_gather(cache_k, "seq", axis=0, tiled=True),
        lax.all_gather(cache_v, "seq", axis=0, tiled=True),
    )
    allowed = jnp.ones((tok_rows, pieces[0].shape[0]), jnp.bool_)
    carry_mid = attend(carry_start, pieces[0], pieces[1], queries, allowed)
    pieces = (
        lax.all_gather(rot_key, "seq", axis=0, tiled=True),
        lax.all_gather(values_new, "seq", axis=0, tiled=True),
    )
    key_pos = jnp.arange(pieces[0].shape[0], dtype=jnp.int32)
    allowed = key_pos[None, :] <= local_pos[:, None]
    best, total, accum = attend(carry_mid, pieces[0], pieces[1], queries, allowed)
    attended = (
        jnp.transpose(accum / total[..., None], (2, 0, 1, 3))
        .reshape(tok_rows, query_cols)
        .astype(jnp.bfloat16)
    )
    partial_out = jnp.dot(
        attended,
        lax.all_gather(w_out, "seq", axis=1, tiled=True),
        preferred_element_type=jnp.float32,
    )
    return lax.psum_scatter(
        partial_out.astype(jnp.bfloat16), "head", scatter_dimension=1, tiled=True
    )


LEVELS = 4
PLANE = 4
TILE_RUN = 256
CACHED = 64
REC = 8
REC_PAD = 16


def permuted(value, move):
    perm = []
    for level in range(LEVELS):
        for place in range(PLANE):
            for core in range(2):
                target = move(level, place, core)
                if target is not None:
                    to_level, to_place, to_core = target
                    perm.append(
                        (
                            (level * PLANE + place) * 2 + core,
                            (to_level * PLANE + to_place) * 2 + to_core,
                        )
                    )
    return lax.ppermute(value, ("seq", "head"), perm)


def across(value, bit):
    return permuted(value, lambda z, p, c: (z ^ bit, p, c))


def up(value, steps):
    return permuted(value, lambda z, p, c: ((z + steps) % LEVELS, p, c))


def other_core(value):
    return permuted(value, lambda z, p, c: (z, p, 1 - c))


def to_near(value):
    return permuted(value, lambda z, p, c: (z, p ^ (1 + c), c))


def to_far(value):
    return permuted(value, lambda z, p, c: (z, p ^ (2 - c), c))


def place_of(which, place, core):
    if which == 0:
        return place
    if which == 3:
        return place ^ 3
    return place ^ (1 + core) if which == 1 else place ^ (2 - core)


def turned(values, cosine, sine):
    return values * cosine + pltpu.roll(values, HD // 2, 1) * sine


def products(where_ref, x_refs, pieces):
    level, place, core = where_ref[0], where_ref[1], where_ref[2]
    totals = [None] * len(x_refs)
    for i in range(2):
        for j in range(PLANE):
            depth = pieces[i][j].shape[0]
            block = lax.rem(level + i, 2) * PLANE + place_of(j, place, core)
            start = pl.multiple_of(block * depth, depth)
            weights = pieces[i][j][...]
            for r, x_ref in enumerate(x_refs):
                part = jnp.dot(
                    x_ref[:, pl.ds(start, depth)], weights, preferred_element_type=jnp.float32
                )
                totals[r] = part if totals[r] is None else totals[r] + part
    return totals


def keys_part_kernel(where_ref, x0, x1, own, near, far, old0, old1, keep_ref, send_ref):
    pieces = [[own.at[i], near.at[i], far.at[i], far.at[2 + i]] for i in range(2)]
    rows = x0.shape[0]
    width = 2 * HD
    for r, total in enumerate(products(where_ref, (x0, x1), pieces)):
        keep_ref[r * rows : (r + 1) * rows] = total[:, :width]
        send_ref[r * rows : (r + 1) * rows] = total[:, width:].astype(jnp.bfloat16)
    at = 2 * rows
    for old in (old0, old1):
        send_ref[at : at + CACHED + REC_PAD] = old[:, width:]
        at += CACHED + REC_PAD


def keys_join_kernel(where_ref, keep_ref, got_ref, old0, old1, cos_ref, sin_ref, kv_ref, sum_ref):
    level = where_ref[0]
    rows = sum_ref.shape[0]
    block = rows // LEVELS
    tok = block - REC_PAD
    width = 2 * HD
    sum_ref[...] = keep_ref[...] + got_ref[0:rows].astype(jnp.float32)
    first = where_ref[3]
    span = CACHED + REC_PAD
    for n in range(LEVELS):
        at = jnp.bitwise_xor(level, n)
        start = pl.multiple_of(lax.rem(first + n, LEVELS) * block, 16)
        cosine, sine = cos_ref[at], sin_ref[at]
        fresh = sum_ref[pl.ds(start, tok), :]
        kv_ref[2 + at, :, 0:HD] = turned(fresh[:, :HD], cosine[:tok], sine[:tok]).astype(
            jnp.bfloat16
        )
        kv_ref[2 + at, :, HD:width] = fresh[:, HD:].astype(jnp.bfloat16)
        if n < 2:
            old = (old0, old1)[n][:, 0:width].astype(jnp.float32)
        else:
            old = got_ref[rows + (n - 2) * span : rows + (n - 1) * span].astype(jnp.float32)
        slots = old[CACHED : CACHED + REC].astype(jnp.int32)
        rec = sum_ref[pl.ds(pl.multiple_of(start + tok, 16), REC_PAD), :]
        line = lax.broadcasted_iota(jnp.int32, (CACHED, width), 0)
        found = jnp.zeros((CACHED, width), jnp.float32)
        hit = jnp.zeros((CACHED, width), jnp.int32)
        for r in range(REC):
            same = line == slots[r : r + 1]
            found = jnp.where(same, rec[r : r + 1], found)
            hit = jnp.where(same, 1, hit)
        keys = turned(found[:, :HD], cosine[tok : tok + CACHED], sine[tok : tok + CACHED])
        found = jnp.concatenate([keys, found[:, HD:]], axis=1)
        line_at = pl.multiple_of(lax.rem(at, 2) * CACHED, CACHED)
        kv_ref[at // 2, pl.ds(line_at, CACHED), :] = jnp.where(
            hit == 1, found, old[:CACHED]
        ).astype(jnp.bfloat16)


def queries_part_kernel(where_ref, x0, x1, *refs):
    pieces = []
    for own, near, far in (refs[0:3], refs[3:6]):
        pieces.append([own.at[0], near.at[0], far.at[0], far.at[1]])
    keep_ref, send_ref = refs[6:]
    block = x0.shape[0] // 2
    tok = block - REC_PAD
    width = 4 * HD
    for r, total in enumerate(products(where_ref, (x0, x1), pieces)):
        for k in range(2):
            fresh = total[k * block : k * block + tok]
            keep_ref[2 * r + k] = fresh[:, :width]
            send_ref[2 * r + k] = fresh[:, width:].astype(jnp.bfloat16)


def attend_kernel(
    where_ref, keep_ref, got_ref, cos_ref, sin_ref, kv0, kv1, kv2, kv3, out_ref, query_ref
):
    level, place, core = where_ref[0], where_ref[1], where_ref[2]
    pieces = (kv0, kv1, kv2, kv3)
    tok = keep_ref.shape[1]
    old = LEVELS // 2
    for n in range(LEVELS):
        at = jnp.bitwise_xor(level, n)
        block = lax.rem(where_ref[3] + n, LEVELS)
        total = keep_ref[block] + got_ref[block].astype(jnp.float32)
        cosine, sine = cos_ref[at][:tok], sin_ref[at][:tok]
        for h in range(4):
            head = turned(total[:, h * HD : (h + 1) * HD], cosine, sine)
            query_ref[at, h] = head.astype(jnp.bfloat16)
    row = lax.broadcasted_iota(jnp.int32, (tok, tok), 0)
    col = lax.broadcasted_iota(jnp.int32, (tok, tok), 1)
    scale = HD ** (-0.5) * 1.4426950408889634
    for i in range(LEVELS):
        count = (old + i + 1) * tok
        queries = query_ref[i].reshape(4 * tok, HD)
        scores = []
        best = None
        for j in range(PLANE):
            keys = pieces[j][0 : old + i + 1, :, 0:HD].reshape(count, HD)
            raw = lax.dot_general(
                queries, keys, (((1,), (1,)), ((), ())), preferred_element_type=jnp.float32
            )
            if j == 0:
                allowed = col <= row
            else:
                allowed = jnp.broadcast_to(place_of(j, place, core), (tok, tok)) < place
            allowed = jnp.concatenate([allowed] * 4, axis=0)
            last = jnp.where(allowed, raw[:, count - tok :], NEG_FILL)
            raw = jnp.concatenate([raw[:, : count - tok], last], axis=1)
            top = jnp.max(raw, axis=1, keepdims=True)
            best = top if best is None else jnp.maximum(best, top)
            scores.append(raw)
        total, accum = 0.0, 0.0
        for j in range(PLANE):
            weights = jnp.exp2((scores[j] - best) * scale)
            total = total + jnp.sum(weights, axis=1, keepdims=True)
            values = pieces[j][0 : old + i + 1, :, HD : 2 * HD].reshape(count, HD)
            accum = accum + jnp.dot(
                weights.astype(jnp.bfloat16), values, preferred_element_type=jnp.float32
            )
        result = (accum / total).astype(jnp.bfloat16)
        for h in range(4):
            out_ref[i * tok : (i + 1) * tok, h * HD : (h + 1) * HD] = result[
                h * tok : (h + 1) * tok
            ]


def output_kernel(where_ref, own_ref, next_ref, w_own, w_near, w_far, mine_ref, other_ref):
    level, place, core = where_ref[0], where_ref[1], where_ref[2]
    depth = own_ref.shape[1]
    width = w_own.shape[2]
    start = pl.multiple_of(lax.rem(level, 2) * depth, depth)
    start_next = pl.multiple_of(lax.rem(level + 1, 2) * depth, depth)
    for i in range(2):
        for j in range(PLANE):
            weights = (w_own.at[i], w_near.at[i], w_far.at[i], w_far.at[2 + i])[j]
            part = jnp.dot(
                own_ref[...], weights[pl.ds(start, depth), :], preferred_element_type=jnp.float32
            ) + jnp.dot(
                next_ref[...],
                weights[pl.ds(start_next, depth), :],
                preferred_element_type=jnp.float32,
            )
            to = pl.multiple_of(place_of(j, place, core) * width, width)
            mine = (core == level // 2) if i == 0 else (core != level // 2)

            @pl.when(mine)
            def _():
                mine_ref[:, pl.ds(to, width)] = part

            @pl.when(jnp.logical_not(mine))
            def _():
                other_ref[:, pl.ds(to, width)] = part.astype(jnp.bfloat16)


SMEM = pl.BlockSpec(memory_space=pltpu.SMEM)
VMEM = pl.BlockSpec(memory_space=pltpu.VMEM)
PARAMS = pltpu.CompilerParams(vmem_limit_bytes=48 * 1024 * 1024)


def shaped(shape, dtype=jnp.bfloat16):
    return jax.ShapeDtypeStruct(shape, dtype)


def by_levels(
    text_rows,
    picture_rows,
    picture_slots,
    norm_gain,
    w_query,
    w_key,
    w_value,
    w_out,
    cache_keys,
    cache_values,
    recompute_rows,
    recompute_slots,
):
    seq_index = lax.axis_index("seq")
    core = lax.axis_index("head")
    level, place = seq_index // PLANE, seq_index % PLANE
    half_at = level // 2
    own_first = core == half_at
    where = jnp.stack([level, place, core, jnp.where(own_first, 0, 2)]).astype(jnp.int32)
    tok, width = text_rows.shape
    block_rows = tok + REC_PAD

    stream_len = tok * LEVELS * PLANE
    tile_owners = TILE_RUN // tok
    first = stream_len // 2 // tok
    last = (stream_len - TILE_RUN) // tok
    owners = [first + i for i in range(tile_owners)] + [last + i for i in range(tile_owners)]
    received = []
    for k in range(PLANE):

        def to_owner(z, p, c, k=k):
            return (owners[z] // PLANE, owners[z] % PLANE, c) if p == k else None

        received.append(permuted(picture_rows, to_owner))
    placed = jnp.concatenate(received, axis=0)
    is_owner = jnp.any(seq_index == jnp.array(owners, jnp.int32))
    stream = jnp.where(is_owner, placed, text_rows)

    slots = (recompute_slots - seq_index * CACHED).astype(jnp.bfloat16)
    slot_rows = jnp.broadcast_to(jnp.pad(slots, (0, REC_PAD - REC))[:, None], (REC_PAD, 4 * HD))

    def columns(array, size, at):
        return lax.dynamic_slice_in_dim(array, at * size, size, 1)

    def key_piece(to_level):
        def pair(k, v):
            return [columns(a, HD, at) for at in (to_level, to_level ^ 2) for a in (k, v)]

        weights = jnp.concatenate(pair(w_key, w_value), axis=1)
        old = jnp.concatenate(pair(cache_keys, cache_values), axis=1)
        return jnp.concatenate([weights, old, slot_rows], axis=0)

    def query_piece(to_level):
        return jnp.concatenate(
            [columns(w_query, 4 * HD, at) for at in (to_level, to_level ^ 2)], axis=1
        )[None]

    depth = w_query.shape[0]
    key_own = key_piece(level)
    key_next = across(key_piece(level ^ 1), 1)
    query_own = query_piece(level)
    query_next = across(query_piece(level ^ 1), 1)
    query_near = to_near(query_own)

    rows = jnp.concatenate(
        [stream, recompute_rows, jnp.zeros((REC_PAD - REC, width), stream.dtype)], axis=0
    )
    wide = rows.astype(jnp.float32)
    squares = lax.psum(jnp.sum(wide * wide, axis=1), "head")
    normed = scaled(wide, squares, lax.dynamic_slice_in_dim(norm_gain, core * width, width, 0))

    normed, key_next, query_near = lax.optimization_barrier((normed, key_next, query_near))
    query_far = to_far(jnp.concatenate([query_own, query_near], axis=0))
    keys = jnp.stack([key_own[:depth], key_next[:depth]])
    old_own, old_next = key_own[depth:], key_next[depth:]
    crossed = permuted(normed, lambda z, p, c: (z ^ 2, p, 1 - c) if c == 1 - z // 2 else None)
    crossed, query_far, query_next = lax.optimization_barrier((crossed, query_far, query_next))
    keys_near = to_near(keys)
    held = jnp.where(own_first, normed, crossed)
    next_rows = across(held, 1)
    next_rows, keys_near = lax.optimization_barrier((next_rows, keys_near))
    keys_far = to_far(jnp.concatenate([keys, keys_near], axis=0))
    rows_mine = jnp.concatenate([held, next_rows], axis=0)
    rows_other = other_core(rows_mine)
    rows_other, keys_far = lax.optimization_barrier((rows_other, keys_far))
    next_near = to_near(query_next)
    next_far = to_far(jnp.concatenate([query_next, next_near], axis=0))

    out_rows = w_out.shape[0] // 2
    out_own, out_give = (
        lax.dynamic_slice_in_dim(w_out, at * out_rows, out_rows, 0) for at in (half_at, 1 - half_at)
    )
    out_got = across(out_give, 2)

    half = HD // 2
    freqs = ROPE_BASE ** (-jnp.arange(half, dtype=jnp.float32) / half)
    blocks = (jnp.arange(LEVELS, dtype=jnp.int32) * PLANE + place)[:, None]
    stream_pos = (
        CACHED * LEVELS * PLANE + blocks * tok + jnp.arange(tok, dtype=jnp.int32)[None]
    ).astype(jnp.float32)
    cache_pos = (blocks * CACHED + jnp.arange(CACHED, dtype=jnp.int32)[None]).astype(jnp.float32)
    angles = jnp.concatenate([stream_pos, cache_pos], axis=1)[..., None] * freqs
    cosine, sine = jnp.cos(angles), jnp.sin(angles)
    cosine = jnp.concatenate([cosine, cosine], axis=-1)
    sine = jnp.concatenate([-sine, sine], axis=-1)

    all_rows = LEVELS * block_rows
    keep, send = pl.pallas_call(
        keys_part_kernel,
        out_shape=(
            shaped((all_rows, 2 * HD), jnp.float32),
            shaped((all_rows + 2 * (CACHED + REC_PAD), 2 * HD)),
        ),
        in_specs=[SMEM] + [VMEM] * 7,
        out_specs=(VMEM, VMEM),
        compiler_params=PARAMS,
        name="keys_part",
    )(where, rows_mine, rows_other, keys, keys_near, keys_far, old_own, old_next)
    send, rows_after, out_got = lax.optimization_barrier((send, rows_mine, out_got))
    q_keep, q_send = pl.pallas_call(
        queries_part_kernel,
        out_shape=(
            shaped((LEVELS, tok, 4 * HD), jnp.float32),
            shaped((LEVELS, tok, 4 * HD)),
        ),
        in_specs=[SMEM] + [VMEM] * 8,
        out_specs=(VMEM, VMEM),
        compiler_params=PARAMS,
        name="queries_part",
    )(
        where,
        rows_after,
        rows_other,
        query_own,
        query_near,
        query_far,
        query_next,
        next_near,
        next_far,
    )
    got_keys, q_send = lax.optimization_barrier((across(send, 2), q_send))
    kv = pl.pallas_call(
        keys_join_kernel,
        out_shape=shaped((LEVELS // 2 + LEVELS, tok, 2 * HD)),
        in_specs=[SMEM] + [VMEM] * 6,
        out_specs=VMEM,
        scratch_shapes=[pltpu.VMEM((all_rows, 2 * HD), jnp.float32)],
        compiler_params=PARAMS,
        name="keys_join",
    )(where, keep, got_keys, old_own, old_next, cosine, sine)
    kv_near, kv_far = to_near(kv), to_far(kv)
    kv_both = to_far(kv_near)

    out_pair = jnp.stack([out_own, out_got])
    out_pair, kv_near = lax.optimization_barrier((out_pair, kv_near))
    out_near, got_queries = lax.optimization_barrier((to_near(out_pair), across(q_send, 2)))
    out_far = to_far(jnp.concatenate([out_pair, out_near], axis=0))
    attended = pl.pallas_call(
        attend_kernel,
        out_shape=shaped((LEVELS * tok, 4 * HD)),
        in_specs=[SMEM] + [VMEM] * 8,
        out_specs=VMEM,
        scratch_shapes=[pltpu.VMEM((LEVELS, 4, tok, HD), jnp.bfloat16)],
        compiler_params=PARAMS,
        name="attend",
    )(where, q_keep, got_queries, cosine, sine, kv, kv_near, kv_far, kv_both)

    wide_cols = PLANE * w_out.shape[1]
    mine, other = pl.pallas_call(
        output_kernel,
        out_shape=(
            shaped((LEVELS * tok, wide_cols), jnp.float32),
            shaped((LEVELS * tok, wide_cols)),
        ),
        in_specs=[SMEM] + [VMEM] * 5,
        out_specs=(VMEM, VMEM),
        compiler_params=PARAMS,
        name="output",
    )(where, attended, across(attended, 1), out_pair, out_near, out_far)
    summed = (mine + other_core(other).astype(jnp.float32)).reshape(LEVELS, tok, wide_cols)

    def block_for(steps):
        return lax.dynamic_index_in_dim(summed, (level + steps) % LEVELS, 0, keepdims=False)

    second, first, third = (up(block_for(d).astype(jnp.bfloat16), d) for d in (2, 1, 3))
    same = (block_for(0) + second.astype(jnp.float32)).astype(jnp.bfloat16)
    cross = (first.astype(jnp.float32) + third.astype(jnp.float32)).astype(jnp.bfloat16)
    even = level % 2 == 0
    return jnp.concatenate([jnp.where(even, same, cross), jnp.where(even, cross, same)], axis=1)


def solution(mesh):
    def run(*args):
        kv_local = args[5].shape[1] // HD // mesh.shape["head"]
        levels_fit = (
            mesh.shape["seq"] == LEVELS * PLANE
            and mesh.shape["head"] == 2
            and kv_local == LEVELS
            and args[1].shape[0] == 2 * TILE_RUN
            and args[0].shape[0] == 2048
            and args[8].shape[0] == LEVELS * PLANE * CACHED
            and args[10].shape[0] == LEVELS * PLANE * REC
        )
        return jax.shard_map(
            by_levels if levels_fit else on_device,
            mesh=mesh,
            in_specs=(
                P("seq", "head"),
                P("seq", "head"),
                P("seq"),
                P(),
                P("seq", "head"),
                P("seq", "head"),
                P("seq", "head"),
                P("head", "seq"),
                P("seq", "head"),
                P("seq", "head"),
                P("seq", "head"),
                P("seq"),
            ),
            out_specs=P("seq", "head"),
            check_vma=False,
        )(*args)

    return run
```

```python
import jax
import jax.numpy as jnp
from jax import lax
from jax.experimental import pallas as pl
from jax.experimental.pallas import tpu as pltpu
from jax.sharding import PartitionSpec as P

D = 4096
HD = 128


EPSILON = 1e-05
ROPE_BASE = 1000000.0
NEG_FILL = -1e30


def rotate(values, positions):
    half = values.shape[-1] // 2
    freqs = ROPE_BASE ** (-jnp.arange(half, dtype=jnp.float32) / half)
    angles = positions[:, None] * freqs[None, :]
    cosine = jnp.cos(angles)[:, None, :]
    sine = jnp.sin(angles)[:, None, :]
    first = values[..., :half]
    second = values[..., half:]
    return jnp.concatenate(
        [first * cosine - second * sine, second * cosine + first * sine], axis=-1
    )


def scaled(rows_wide, squares, gain):
    return (rows_wide * lax.rsqrt(squares / D + EPSILON)[:, None] * gain[None, :]).astype(
        jnp.bfloat16
    )


def attend(carry, key_piece, value_piece, queries, allowed):
    best, total, accum = carry
    count = key_piece.shape[0]
    kv_local = queries.shape[0]
    keys_split = key_piece.reshape(count, kv_local, HD)
    values_split = value_piece.reshape(count, kv_local, HD)
    scores = jnp.einsum(
        "kgtd,nkd->kgtn", queries, keys_split, preferred_element_type=jnp.float32
    ) * HD ** (-0.5)
    scores = jnp.where(allowed, scores, NEG_FILL)
    fresh = jnp.maximum(best, jnp.max(scores, axis=-1))
    factor = jnp.exp(best - fresh)
    weights = jnp.where(allowed, jnp.exp(scores - fresh[..., None]), 0.0)
    total = total * factor + jnp.sum(weights, axis=-1)
    accum = accum * factor[..., None] + jnp.einsum(
        "kgtn,nkd->kgtd",
        weights.astype(jnp.bfloat16),
        values_split,
        preferred_element_type=jnp.float32,
    )
    return (fresh, total, accum)


def on_device(
    text_rows,
    picture_rows,
    picture_slots,
    norm_gain,
    w_query,
    w_key,
    w_value,
    w_out,
    cache_keys,
    cache_values,
    recompute_rows,
    recompute_slots,
):
    tok_rows = text_rows.shape[0]
    rec_count = recompute_rows.shape[0]
    cache_rows = cache_keys.shape[0]
    seq_index = lax.axis_index("seq")
    local_pos = seq_index * tok_rows + jnp.arange(tok_rows, dtype=jnp.int32)
    rows_piece = lax.all_gather(picture_rows, "seq", axis=0, tiled=True)
    slots_piece = lax.all_gather(picture_slots, "seq", axis=0, tiled=True)
    select = (slots_piece[None, :] == local_pos[:, None]).astype(jnp.bfloat16)
    placed = jnp.dot(select, rows_piece, preferred_element_type=jnp.float32)
    hits = jnp.sum(select.astype(jnp.float32), axis=1)
    added, hits = (placed, hits)
    stream = jnp.where(hits[:, None] > 0.5, added, text_rows.astype(jnp.float32)).astype(
        jnp.bfloat16
    )
    slice_width = stream.shape[1]
    gain_slice = lax.dynamic_slice_in_dim(
        norm_gain, lax.axis_index("head") * slice_width, slice_width, 0
    )
    stream_wide = stream.astype(jnp.float32)
    rec_wide = recompute_rows.astype(jnp.float32)
    stream_sq, rec_sq = lax.psum(
        (jnp.sum(stream_wide * stream_wide, axis=1), jnp.sum(rec_wide * rec_wide, axis=1)), "head"
    )
    normed, rec_normed = (
        lax.all_gather(scaled(stream_wide, stream_sq, gain_slice), "head", axis=1, tiled=True),
        lax.all_gather(scaled(rec_wide, rec_sq, gain_slice), "head", axis=1, tiled=True),
    )
    stacked = jnp.concatenate([normed, rec_normed], axis=0)
    query_cols = w_query.shape[1]
    key_cols = w_key.shape[1]
    pieces = (
        lax.all_gather(w_query, "seq", axis=0, tiled=True),
        lax.all_gather(w_key, "seq", axis=0, tiled=True),
        lax.all_gather(w_value, "seq", axis=0, tiled=True),
    )
    query_all = jnp.dot(stacked, pieces[0], preferred_element_type=jnp.float32)
    key_all = jnp.dot(stacked, pieces[1], preferred_element_type=jnp.float32)
    value_all = jnp.dot(stacked, pieces[2], preferred_element_type=jnp.float32)
    cache_total = cache_rows * lax.axis_size("seq")
    stream_pos = (cache_total + local_pos).astype(jnp.float32)
    rec_pos = recompute_slots.astype(jnp.float32)
    heads_local = query_cols // HD
    kv_local = key_cols // HD
    group = heads_local // kv_local
    rot_query = rotate(query_all[:tok_rows].reshape(tok_rows, heads_local, HD), stream_pos).astype(
        jnp.bfloat16
    )
    rot_key = (
        rotate(key_all[:tok_rows].reshape(tok_rows, kv_local, HD), stream_pos)
        .astype(jnp.bfloat16)
        .reshape(tok_rows, key_cols)
    )
    values_new = value_all[:tok_rows].astype(jnp.bfloat16)
    rot_rec_key = (
        rotate(key_all[tok_rows:].reshape(rec_count, kv_local, HD), rec_pos)
        .astype(jnp.bfloat16)
        .reshape(rec_count, key_cols)
    )
    rec_values = value_all[tok_rows:].astype(jnp.bfloat16)
    local_slots = recompute_slots - seq_index * cache_rows
    select = local_slots[:, None] == jnp.arange(cache_rows, dtype=jnp.int32)[None, :]
    replaced = jnp.any(select, axis=0)[:, None]
    select_cols = select.astype(jnp.bfloat16).T
    new_keys = jnp.dot(select_cols, rot_rec_key, preferred_element_type=jnp.float32).astype(
        jnp.bfloat16
    )
    new_values = jnp.dot(select_cols, rec_values, preferred_element_type=jnp.float32).astype(
        jnp.bfloat16
    )
    cache_k = jnp.where(replaced, new_keys, cache_keys)
    cache_v = jnp.where(replaced, new_values, cache_values)
    queries = jnp.transpose(rot_query.reshape(tok_rows, kv_local, group, HD), (1, 2, 0, 3))
    carry_start = (
        jnp.full((kv_local, group, tok_rows), NEG_FILL, jnp.float32),
        jnp.zeros((kv_local, group, tok_rows), jnp.float32),
        jnp.zeros((kv_local, group, tok_rows, HD), jnp.float32),
    )
    pieces = (
        lax.all_gather(cache_k, "seq", axis=0, tiled=True),
        lax.all_gather(cache_v, "seq", axis=0, tiled=True),
    )
    allowed = jnp.ones((tok_rows, pieces[0].shape[0]), jnp.bool_)
    carry_mid = attend(carry_start, pieces[0], pieces[1], queries, allowed)
    pieces = (
        lax.all_gather(rot_key, "seq", axis=0, tiled=True),
        lax.all_gather(values_new, "seq", axis=0, tiled=True),
    )
    key_pos = jnp.arange(pieces[0].shape[0], dtype=jnp.int32)
    allowed = key_pos[None, :] <= local_pos[:, None]
    best, total, accum = attend(carry_mid, pieces[0], pieces[1], queries, allowed)
    attended = (
        jnp.transpose(accum / total[..., None], (2, 0, 1, 3))
        .reshape(tok_rows, query_cols)
        .astype(jnp.bfloat16)
    )
    partial_out = jnp.dot(
        attended,
        lax.all_gather(w_out, "seq", axis=1, tiled=True),
        preferred_element_type=jnp.float32,
    )
    return lax.psum_scatter(
        partial_out.astype(jnp.bfloat16), "head", scatter_dimension=1, tiled=True
    )


LEVELS = 4
PLANE = 4
TILE_RUN = 256
CACHED = 64
REC = 8
REC_PAD = 16


def permuted(value, move):
    perm = []
    for level in range(LEVELS):
        for place in range(PLANE):
            for core in range(2):
                target = move(level, place, core)
                if target is not None:
                    to_level, to_place, to_core = target
                    perm.append(
                        (
                            (level * PLANE + place) * 2 + core,
                            (to_level * PLANE + to_place) * 2 + to_core,
                        )
                    )
    return lax.ppermute(value, ("seq", "head"), perm)


def across(value, bit):
    return permuted(value, lambda z, p, c: (z ^ bit, p, c))


def up(value, steps):
    return permuted(value, lambda z, p, c: ((z + steps) % LEVELS, p, c))


def other_core(value):
    return permuted(value, lambda z, p, c: (z, p, 1 - c))


def to_near(value):
    return permuted(value, lambda z, p, c: (z, p ^ (1 + c), c))


def to_far(value):
    return permuted(value, lambda z, p, c: (z, p ^ (2 - c), c))


def place_of(which, place, core):
    if which == 0:
        return place
    if which == 3:
        return place ^ 3
    return place ^ (1 + core) if which == 1 else place ^ (2 - core)


def turned(values, cosine, sine):
    return values * cosine + pltpu.roll(values, HD // 2, 1) * sine


def products(where_ref, x_refs, pieces):
    level, place, core = where_ref[0], where_ref[1], where_ref[2]
    totals = [None] * len(x_refs)
    for i in range(2):
        for j in range(PLANE):
            depth = pieces[i][j].shape[0]
            block = lax.rem(level + i, 2) * PLANE + place_of(j, place, core)
            start = pl.multiple_of(block * depth, depth)
            weights = pieces[i][j][...]
            for r, x_ref in enumerate(x_refs):
                part = jnp.dot(
                    x_ref[:, pl.ds(start, depth)], weights, preferred_element_type=jnp.float32
                )
                totals[r] = part if totals[r] is None else totals[r] + part
    return totals


def keys_part_kernel(where_ref, x0, x1, own, near, far, old0, old1, keep_ref, send_ref):
    pieces = [[own.at[i], near.at[i], far.at[i], far.at[2 + i]] for i in range(2)]
    rows = x0.shape[0]
    width = 2 * HD
    for r, total in enumerate(products(where_ref, (x0, x1), pieces)):
        keep_ref[r * rows : (r + 1) * rows] = total[:, :width]
        send_ref[r * rows : (r + 1) * rows] = total[:, width:].astype(jnp.bfloat16)
    at = 2 * rows
    for old in (old0, old1):
        send_ref[at : at + CACHED + REC_PAD] = old[:, width:]
        at += CACHED + REC_PAD


def keys_join_kernel(where_ref, keep_ref, got_ref, old0, old1, cos_ref, sin_ref, kv_ref, sum_ref):
    level = where_ref[0]
    rows = sum_ref.shape[0]
    block = rows // LEVELS
    tok = block - REC_PAD
    width = 2 * HD
    sum_ref[...] = keep_ref[...] + got_ref[0:rows].astype(jnp.float32)
    first = where_ref[3]
    span = CACHED + REC_PAD
    for n in range(LEVELS):
        at = jnp.bitwise_xor(level, n)
        start = pl.multiple_of(lax.rem(first + n, LEVELS) * block, 16)
        cosine, sine = cos_ref[at], sin_ref[at]
        fresh = sum_ref[pl.ds(start, tok), :]
        kv_ref[2 + at, :, 0:HD] = turned(fresh[:, :HD], cosine[:tok], sine[:tok]).astype(
            jnp.bfloat16
        )
        kv_ref[2 + at, :, HD:width] = fresh[:, HD:].astype(jnp.bfloat16)
        if n < 2:
            old = (old0, old1)[n][:, 0:width].astype(jnp.float32)
        else:
            old = got_ref[rows + (n - 2) * span : rows + (n - 1) * span].astype(jnp.float32)
        slots = old[CACHED : CACHED + REC].astype(jnp.int32)
        rec = sum_ref[pl.ds(pl.multiple_of(start + tok, 16), REC_PAD), :]
        line = lax.broadcasted_iota(jnp.int32, (CACHED, width), 0)
        found = jnp.zeros((CACHED, width), jnp.float32)
        hit = jnp.zeros((CACHED, width), jnp.int32)
        for r in range(REC):
            same = line == slots[r : r + 1]
            found = jnp.where(same, rec[r : r + 1], found)
            hit = jnp.where(same, 1, hit)
        keys = turned(found[:, :HD], cosine[tok : tok + CACHED], sine[tok : tok + CACHED])
        found = jnp.concatenate([keys, found[:, HD:]], axis=1)
        line_at = pl.multiple_of(lax.rem(at, 2) * CACHED, CACHED)
        kv_ref[at // 2, pl.ds(line_at, CACHED), :] = jnp.where(
            hit == 1, found, old[:CACHED]
        ).astype(jnp.bfloat16)


def queries_part_kernel(where_ref, x0, x1, *refs):
    pieces = []
    for own, near, far in (refs[0:3], refs[3:6]):
        pieces.append([own.at[0], near.at[0], far.at[0], far.at[1]])
    keep_ref, send_ref = refs[6:]
    block = x0.shape[0] // 2
    tok = block - REC_PAD
    width = 4 * HD
    for r, total in enumerate(products(where_ref, (x0, x1), pieces)):
        for k in range(2):
            fresh = total[k * block : k * block + tok]
            keep_ref[2 * r + k] = fresh[:, :width]
            send_ref[2 * r + k] = fresh[:, width:].astype(jnp.bfloat16)


def attend_kernel(
    where_ref, keep_ref, got_ref, cos_ref, sin_ref, kv0, kv1, kv2, kv3, out_ref, query_ref
):
    level, place, core = where_ref[0], where_ref[1], where_ref[2]
    pieces = (kv0, kv1, kv2, kv3)
    tok = keep_ref.shape[1]
    old = LEVELS // 2
    for n in range(LEVELS):
        at = jnp.bitwise_xor(level, n)
        block = lax.rem(where_ref[3] + n, LEVELS)
        total = keep_ref[block] + got_ref[block].astype(jnp.float32)
        cosine, sine = cos_ref[at][:tok], sin_ref[at][:tok]
        for h in range(4):
            head = turned(total[:, h * HD : (h + 1) * HD], cosine, sine)
            query_ref[at, h] = head.astype(jnp.bfloat16)
    row = lax.broadcasted_iota(jnp.int32, (tok, tok), 0)
    col = lax.broadcasted_iota(jnp.int32, (tok, tok), 1)
    scale = HD ** (-0.5) * 1.4426950408889634
    for i in range(LEVELS):
        count = (old + i + 1) * tok
        queries = query_ref[i].reshape(4 * tok, HD)
        scores = []
        best = None
        for j in range(PLANE):
            keys = pieces[j][0 : old + i + 1, :, 0:HD].reshape(count, HD)
            raw = lax.dot_general(
                queries, keys, (((1,), (1,)), ((), ())), preferred_element_type=jnp.float32
            )
            if j == 0:
                allowed = col <= row
            else:
                allowed = jnp.broadcast_to(place_of(j, place, core), (tok, tok)) < place
            allowed = jnp.concatenate([allowed] * 4, axis=0)
            last = jnp.where(allowed, raw[:, count - tok :], NEG_FILL)
            raw = jnp.concatenate([raw[:, : count - tok], last], axis=1)
            top = jnp.max(raw, axis=1, keepdims=True)
            best = top if best is None else jnp.maximum(best, top)
            scores.append(raw)
        total, accum = 0.0, 0.0
        for j in range(PLANE):
            weights = jnp.exp2((scores[j] - best) * scale)
            total = total + jnp.sum(weights, axis=1, keepdims=True)
            values = pieces[j][0 : old + i + 1, :, HD : 2 * HD].reshape(count, HD)
            accum = accum + jnp.dot(
                weights.astype(jnp.bfloat16), values, preferred_element_type=jnp.float32
            )
        result = (accum / total).astype(jnp.bfloat16)
        for h in range(4):
            out_ref[i * tok : (i + 1) * tok, h * HD : (h + 1) * HD] = result[
                h * tok : (h + 1) * tok
            ]


def output_kernel(where_ref, own_ref, next_ref, w_own, w_near, w_far, mine_ref, other_ref):
    level, place, core = where_ref[0], where_ref[1], where_ref[2]
    depth = own_ref.shape[1]
    width = w_own.shape[2]
    start = pl.multiple_of(lax.rem(level, 2) * depth, depth)
    start_next = pl.multiple_of(lax.rem(level + 1, 2) * depth, depth)
    for i in range(2):
        for j in range(PLANE):
            weights = (w_own.at[i], w_near.at[i], w_far.at[i], w_far.at[2 + i])[j]
            part = jnp.dot(
                own_ref[...], weights[pl.ds(start, depth), :], preferred_element_type=jnp.float32
            ) + jnp.dot(
                next_ref[...],
                weights[pl.ds(start_next, depth), :],
                preferred_element_type=jnp.float32,
            )
            to = pl.multiple_of(place_of(j, place, core) * width, width)
            mine = (core == level // 2) if i == 0 else (core != level // 2)

            @pl.when(mine)
            def _():
                mine_ref[:, pl.ds(to, width)] = part

            @pl.when(jnp.logical_not(mine))
            def _():
                other_ref[:, pl.ds(to, width)] = part.astype(jnp.bfloat16)


SMEM = pl.BlockSpec(memory_space=pltpu.SMEM)
VMEM = pl.BlockSpec(memory_space=pltpu.VMEM)
PARAMS = pltpu.CompilerParams(vmem_limit_bytes=48 * 1024 * 1024)


def shaped(shape, dtype=jnp.bfloat16):
    return jax.ShapeDtypeStruct(shape, dtype)


def by_levels(
    text_rows,
    picture_rows,
    picture_slots,
    norm_gain,
    w_query,
    w_key,
    w_value,
    w_out,
    cache_keys,
    cache_values,
    recompute_rows,
    recompute_slots,
):
    seq_index = lax.axis_index("seq")
    core = lax.axis_index("head")
    level, place = seq_index // PLANE, seq_index % PLANE
    half_at = level // 2
    own_first = core == half_at
    where = jnp.stack([level, place, core, jnp.where(own_first, 0, 2)]).astype(jnp.int32)
    tok, width = text_rows.shape
    block_rows = tok + REC_PAD

    stream_len = tok * LEVELS * PLANE
    tile_owners = TILE_RUN // tok
    first = stream_len // 2 // tok
    last = (stream_len - TILE_RUN) // tok
    owners = [first + i for i in range(tile_owners)] + [last + i for i in range(tile_owners)]
    assert [owner % PLANE for owner in owners] == list(range(LEVELS))
    owner_levels = jnp.array([owner // PLANE for owner in owners], jnp.int32)

    slots = (recompute_slots - seq_index * CACHED).astype(jnp.bfloat16)
    slot_rows = jnp.broadcast_to(jnp.pad(slots, (0, REC_PAD - REC))[:, None], (REC_PAD, 4 * HD))

    def columns(array, size, at):
        return lax.dynamic_slice_in_dim(array, at * size, size, 1)

    def key_piece(to_level):
        def pair(k, v):
            return [columns(a, HD, at) for at in (to_level, to_level ^ 2) for a in (k, v)]

        weights = jnp.concatenate(pair(w_key, w_value), axis=1)
        old = jnp.concatenate(pair(cache_keys, cache_values), axis=1)
        return jnp.concatenate([weights, old, slot_rows], axis=0)

    def query_piece(to_level):
        return jnp.concatenate(
            [columns(w_query, 4 * HD, at) for at in (to_level, to_level ^ 2)], axis=1
        )[None]

    depth = w_query.shape[0]
    key_own = key_piece(level)
    key_next = across(key_piece(level ^ 1), 1)
    query_own = query_piece(level)
    query_next = across(query_piece(level ^ 1), 1)
    query_near = to_near(query_own)

    rows = jnp.concatenate(
        [text_rows, recompute_rows, jnp.zeros((REC_PAD - REC, width), text_rows.dtype)], axis=0
    )
    gain = lax.dynamic_slice_in_dim(norm_gain, core * width, width, 0)
    wide, pictures = rows.astype(jnp.float32), picture_rows.astype(jnp.float32)
    squares, picture_squares = lax.psum(
        (jnp.sum(wide * wide, axis=1), jnp.sum(pictures * pictures, axis=1)), "head"
    )
    normed = scaled(wide, squares, gain)
    pictures = scaled(pictures, picture_squares, gain)
    shown = [
        permuted(pictures, lambda z, p, c, k=k: (2 * c + (k ^ (p % 2)), z, p // 2)) for k in (0, 1)
    ]

    crossed = permuted(normed, lambda z, p, c: (z ^ 2, p, 1 - c) if c == 1 - z // 2 else None)
    crossed, key_next, query_near, *shown = lax.optimization_barrier(
        (crossed, key_next, query_near, *shown)
    )
    query_far = to_far(jnp.concatenate([query_own, query_near], axis=0))
    keys = jnp.stack([key_own[:depth], key_next[:depth]])
    old_own, old_next = key_own[depth:], key_next[depth:]
    keys_near = to_near(keys)
    held = jnp.where(own_first, normed, crossed)
    next_rows = across(held, 1)
    odd = level % 2 == 1
    shown_mine = jnp.concatenate(
        [jnp.where(odd, shown[1], shown[0]), jnp.where(odd, shown[0], shown[1])], axis=0
    )
    shown_other = other_core(shown_mine)
    next_rows, keys_near, shown_other, query_next, query_far = lax.optimization_barrier(
        (next_rows, keys_near, shown_other, query_next, query_far)
    )
    keys_far = to_far(jnp.concatenate([keys, keys_near], axis=0))
    next_near = to_near(query_next)
    shown_all = jnp.concatenate(
        [
            jnp.where(core == 0, shown_mine, shown_other),
            jnp.where(core == 0, shown_other, shown_mine),
        ],
        axis=0,
    )
    shown_at = owner_levels[place]

    def with_pictures(block, at):
        return [jnp.where(at == shown_at, shown_all, block[:tok]), block[tok:]]

    held_at = jnp.where(own_first, level, level ^ 2)
    rows_mine = jnp.concatenate(
        with_pictures(held, held_at) + with_pictures(next_rows, held_at ^ 1), axis=0
    )
    rows_other = other_core(rows_mine)
    rows_other, keys_far = lax.optimization_barrier((rows_other, keys_far))
    next_far = to_far(jnp.concatenate([query_next, next_near], axis=0))

    out_rows = w_out.shape[0] // 2
    out_own, out_give = (
        lax.dynamic_slice_in_dim(w_out, at * out_rows, out_rows, 0) for at in (half_at, 1 - half_at)
    )
    out_got = across(out_give, 2)

    half = HD // 2
    freqs = ROPE_BASE ** (-jnp.arange(half, dtype=jnp.float32) / half)
    blocks = (jnp.arange(LEVELS, dtype=jnp.int32) * PLANE + place)[:, None]
    stream_pos = (
        CACHED * LEVELS * PLANE + blocks * tok + jnp.arange(tok, dtype=jnp.int32)[None]
    ).astype(jnp.float32)
    cache_pos = (blocks * CACHED + jnp.arange(CACHED, dtype=jnp.int32)[None]).astype(jnp.float32)
    angles = jnp.concatenate([stream_pos, cache_pos], axis=1)[..., None] * freqs
    cosine, sine = jnp.cos(angles), jnp.sin(angles)
    cosine = jnp.concatenate([cosine, cosine], axis=-1)
    sine = jnp.concatenate([-sine, sine], axis=-1)

    all_rows = LEVELS * block_rows
    keep, send = pl.pallas_call(
        keys_part_kernel,
        out_shape=(
            shaped((all_rows, 2 * HD), jnp.float32),
            shaped((all_rows + 2 * (CACHED + REC_PAD), 2 * HD)),
        ),
        in_specs=[SMEM] + [VMEM] * 7,
        out_specs=(VMEM, VMEM),
        compiler_params=PARAMS,
        name="keys_part",
    )(where, rows_mine, rows_other, keys, keys_near, keys_far, old_own, old_next)
    send, rows_after, out_got = lax.optimization_barrier((send, rows_mine, out_got))
    out_pair = jnp.stack([out_own, out_got])
    out_pair, next_far = lax.optimization_barrier((out_pair, next_far))
    out_near = to_near(out_pair)
    q_keep, q_send = pl.pallas_call(
        queries_part_kernel,
        out_shape=(
            shaped((LEVELS, tok, 4 * HD), jnp.float32),
            shaped((LEVELS, tok, 4 * HD)),
        ),
        in_specs=[SMEM] + [VMEM] * 8,
        out_specs=(VMEM, VMEM),
        compiler_params=PARAMS,
        name="queries_part",
    )(
        where,
        rows_after,
        rows_other,
        query_own,
        query_near,
        query_far,
        query_next,
        next_near,
        next_far,
    )
    got_keys, q_send = lax.optimization_barrier((across(send, 2), q_send))
    kv = pl.pallas_call(
        keys_join_kernel,
        out_shape=shaped((LEVELS // 2 + LEVELS, tok, 2 * HD)),
        in_specs=[SMEM] + [VMEM] * 6,
        out_specs=VMEM,
        scratch_shapes=[pltpu.VMEM((all_rows, 2 * HD), jnp.float32)],
        compiler_params=PARAMS,
        name="keys_join",
    )(where, keep, got_keys, old_own, old_next, cosine, sine)
    kv_near, kv_far = to_near(kv), to_far(kv)
    kv_both = to_far(kv_near)

    kv_far, kv_both, out_near, got_queries = lax.optimization_barrier(
        (kv_far, kv_both, out_near, across(q_send, 2))
    )
    out_far = to_far(jnp.concatenate([out_pair, out_near], axis=0))

    attended = pl.pallas_call(
        attend_kernel,
        out_shape=shaped((LEVELS * tok, 4 * HD)),
        in_specs=[SMEM] + [VMEM] * 8,
        out_specs=VMEM,
        scratch_shapes=[pltpu.VMEM((LEVELS, 4, tok, HD), jnp.bfloat16)],
        compiler_params=PARAMS,
        name="attend",
    )(where, q_keep, got_queries, cosine, sine, kv, kv_near, kv_far, kv_both)

    wide_cols = PLANE * w_out.shape[1]
    mine, other = pl.pallas_call(
        output_kernel,
        out_shape=(
            shaped((LEVELS * tok, wide_cols), jnp.float32),
            shaped((LEVELS * tok, wide_cols)),
        ),
        in_specs=[SMEM] + [VMEM] * 5,
        out_specs=(VMEM, VMEM),
        compiler_params=PARAMS,
        name="output",
    )(where, attended, across(attended, 1), out_pair, out_near, out_far)
    summed = (mine + other_core(other).astype(jnp.float32)).reshape(LEVELS, tok, wide_cols)

    def block_for(steps):
        return lax.dynamic_index_in_dim(summed, (level + steps) % LEVELS, 0, keepdims=False)

    second, first, third = (up(block_for(d).astype(jnp.bfloat16), d) for d in (2, 1, 3))
    same = (block_for(0) + second.astype(jnp.float32)).astype(jnp.bfloat16)
    cross = (first.astype(jnp.float32) + third.astype(jnp.float32)).astype(jnp.bfloat16)
    even = level % 2 == 0
    return jnp.concatenate([jnp.where(even, same, cross), jnp.where(even, cross, same)], axis=1)


def solution(mesh):
    def run(*args):
        kv_local = args[5].shape[1] // HD // mesh.shape["head"]
        levels_fit = (
            mesh.shape["seq"] == LEVELS * PLANE
            and mesh.shape["head"] == 2
            and kv_local == LEVELS
            and args[1].shape[0] == 2 * TILE_RUN
            and args[0].shape[0] == 2048
            and args[8].shape[0] == LEVELS * PLANE * CACHED
            and args[10].shape[0] == LEVELS * PLANE * REC
        )
        return jax.shard_map(
            by_levels if levels_fit else on_device,
            mesh=mesh,
            in_specs=(
                P("seq", "head"),
                P("seq", "head"),
                P("seq"),
                P(),
                P("seq", "head"),
                P("seq", "head"),
                P("seq", "head"),
                P("head", "seq"),
                P("seq", "head"),
                P("seq", "head"),
                P("seq", "head"),
                P("seq"),
            ),
            out_specs=P("seq", "head"),
            check_vma=False,
        )(*args)

    return run
```

```python
import jax
import jax.numpy as jnp
from jax import lax
from jax.experimental import pallas as pl
from jax.experimental.pallas import tpu as pltpu
from jax.sharding import PartitionSpec as P

D = 4096
HD = 128


EPSILON = 1e-05
ROPE_BASE = 1000000.0
NEG_FILL = -1e30


def rotate(values, positions):
    half = values.shape[-1] // 2
    freqs = ROPE_BASE ** (-jnp.arange(half, dtype=jnp.float32) / half)
    angles = positions[:, None] * freqs[None, :]
    cosine = jnp.cos(angles)[:, None, :]
    sine = jnp.sin(angles)[:, None, :]
    first = values[..., :half]
    second = values[..., half:]
    return jnp.concatenate(
        [first * cosine - second * sine, second * cosine + first * sine], axis=-1
    )


def scaled(rows_wide, squares, gain):
    return (rows_wide * lax.rsqrt(squares / D + EPSILON)[:, None] * gain[None, :]).astype(
        jnp.bfloat16
    )


def attend(carry, key_piece, value_piece, queries, allowed):
    best, total, accum = carry
    count = key_piece.shape[0]
    kv_local = queries.shape[0]
    keys_split = key_piece.reshape(count, kv_local, HD)
    values_split = value_piece.reshape(count, kv_local, HD)
    scores = jnp.einsum(
        "kgtd,nkd->kgtn", queries, keys_split, preferred_element_type=jnp.float32
    ) * HD ** (-0.5)
    scores = jnp.where(allowed, scores, NEG_FILL)
    fresh = jnp.maximum(best, jnp.max(scores, axis=-1))
    factor = jnp.exp(best - fresh)
    weights = jnp.where(allowed, jnp.exp(scores - fresh[..., None]), 0.0)
    total = total * factor + jnp.sum(weights, axis=-1)
    accum = accum * factor[..., None] + jnp.einsum(
        "kgtn,nkd->kgtd",
        weights.astype(jnp.bfloat16),
        values_split,
        preferred_element_type=jnp.float32,
    )
    return (fresh, total, accum)


def on_device(
    text_rows,
    picture_rows,
    picture_slots,
    norm_gain,
    w_query,
    w_key,
    w_value,
    w_out,
    cache_keys,
    cache_values,
    recompute_rows,
    recompute_slots,
):
    tok_rows = text_rows.shape[0]
    rec_count = recompute_rows.shape[0]
    cache_rows = cache_keys.shape[0]
    seq_index = lax.axis_index("seq")
    local_pos = seq_index * tok_rows + jnp.arange(tok_rows, dtype=jnp.int32)
    rows_piece = lax.all_gather(picture_rows, "seq", axis=0, tiled=True)
    slots_piece = lax.all_gather(picture_slots, "seq", axis=0, tiled=True)
    select = (slots_piece[None, :] == local_pos[:, None]).astype(jnp.bfloat16)
    placed = jnp.dot(select, rows_piece, preferred_element_type=jnp.float32)
    hits = jnp.sum(select.astype(jnp.float32), axis=1)
    added, hits = (placed, hits)
    stream = jnp.where(hits[:, None] > 0.5, added, text_rows.astype(jnp.float32)).astype(
        jnp.bfloat16
    )
    slice_width = stream.shape[1]
    gain_slice = lax.dynamic_slice_in_dim(
        norm_gain, lax.axis_index("head") * slice_width, slice_width, 0
    )
    stream_wide = stream.astype(jnp.float32)
    rec_wide = recompute_rows.astype(jnp.float32)
    stream_sq, rec_sq = lax.psum(
        (jnp.sum(stream_wide * stream_wide, axis=1), jnp.sum(rec_wide * rec_wide, axis=1)), "head"
    )
    normed, rec_normed = (
        lax.all_gather(scaled(stream_wide, stream_sq, gain_slice), "head", axis=1, tiled=True),
        lax.all_gather(scaled(rec_wide, rec_sq, gain_slice), "head", axis=1, tiled=True),
    )
    stacked = jnp.concatenate([normed, rec_normed], axis=0)
    query_cols = w_query.shape[1]
    key_cols = w_key.shape[1]
    pieces = (
        lax.all_gather(w_query, "seq", axis=0, tiled=True),
        lax.all_gather(w_key, "seq", axis=0, tiled=True),
        lax.all_gather(w_value, "seq", axis=0, tiled=True),
    )
    query_all = jnp.dot(stacked, pieces[0], preferred_element_type=jnp.float32)
    key_all = jnp.dot(stacked, pieces[1], preferred_element_type=jnp.float32)
    value_all = jnp.dot(stacked, pieces[2], preferred_element_type=jnp.float32)
    cache_total = cache_rows * lax.axis_size("seq")
    stream_pos = (cache_total + local_pos).astype(jnp.float32)
    rec_pos = recompute_slots.astype(jnp.float32)
    heads_local = query_cols // HD
    kv_local = key_cols // HD
    group = heads_local // kv_local
    rot_query = rotate(query_all[:tok_rows].reshape(tok_rows, heads_local, HD), stream_pos).astype(
        jnp.bfloat16
    )
    rot_key = (
        rotate(key_all[:tok_rows].reshape(tok_rows, kv_local, HD), stream_pos)
        .astype(jnp.bfloat16)
        .reshape(tok_rows, key_cols)
    )
    values_new = value_all[:tok_rows].astype(jnp.bfloat16)
    rot_rec_key = (
        rotate(key_all[tok_rows:].reshape(rec_count, kv_local, HD), rec_pos)
        .astype(jnp.bfloat16)
        .reshape(rec_count, key_cols)
    )
    rec_values = value_all[tok_rows:].astype(jnp.bfloat16)
    local_slots = recompute_slots - seq_index * cache_rows
    select = local_slots[:, None] == jnp.arange(cache_rows, dtype=jnp.int32)[None, :]
    replaced = jnp.any(select, axis=0)[:, None]
    select_cols = select.astype(jnp.bfloat16).T
    new_keys = jnp.dot(select_cols, rot_rec_key, preferred_element_type=jnp.float32).astype(
        jnp.bfloat16
    )
    new_values = jnp.dot(select_cols, rec_values, preferred_element_type=jnp.float32).astype(
        jnp.bfloat16
    )
    cache_k = jnp.where(replaced, new_keys, cache_keys)
    cache_v = jnp.where(replaced, new_values, cache_values)
    queries = jnp.transpose(rot_query.reshape(tok_rows, kv_local, group, HD), (1, 2, 0, 3))
    carry_start = (
        jnp.full((kv_local, group, tok_rows), NEG_FILL, jnp.float32),
        jnp.zeros((kv_local, group, tok_rows), jnp.float32),
        jnp.zeros((kv_local, group, tok_rows, HD), jnp.float32),
    )
    pieces = (
        lax.all_gather(cache_k, "seq", axis=0, tiled=True),
        lax.all_gather(cache_v, "seq", axis=0, tiled=True),
    )
    allowed = jnp.ones((tok_rows, pieces[0].shape[0]), jnp.bool_)
    carry_mid = attend(carry_start, pieces[0], pieces[1], queries, allowed)
    pieces = (
        lax.all_gather(rot_key, "seq", axis=0, tiled=True),
        lax.all_gather(values_new, "seq", axis=0, tiled=True),
    )
    key_pos = jnp.arange(pieces[0].shape[0], dtype=jnp.int32)
    allowed = key_pos[None, :] <= local_pos[:, None]
    best, total, accum = attend(carry_mid, pieces[0], pieces[1], queries, allowed)
    attended = (
        jnp.transpose(accum / total[..., None], (2, 0, 1, 3))
        .reshape(tok_rows, query_cols)
        .astype(jnp.bfloat16)
    )
    partial_out = jnp.dot(
        attended,
        lax.all_gather(w_out, "seq", axis=1, tiled=True),
        preferred_element_type=jnp.float32,
    )
    return lax.psum_scatter(
        partial_out.astype(jnp.bfloat16), "head", scatter_dimension=1, tiled=True
    )


LEVELS = 4
PLANE = 4
TILE_RUN = 256
CACHED = 64
REC = 8
REC_PAD = 16


def permuted(value, move):
    perm = []
    for level in range(LEVELS):
        for place in range(PLANE):
            for core in range(2):
                target = move(level, place, core)
                if target is not None:
                    to_level, to_place, to_core = target
                    perm.append(
                        (
                            (level * PLANE + place) * 2 + core,
                            (to_level * PLANE + to_place) * 2 + to_core,
                        )
                    )
    return lax.ppermute(value, ("seq", "head"), perm)


def across(value, bit):
    return permuted(value, lambda z, p, c: (z ^ bit, p, c))


def up(value, steps):
    return permuted(value, lambda z, p, c: ((z + steps) % LEVELS, p, c))


def other_core(value):
    return permuted(value, lambda z, p, c: (z, p, 1 - c))


def to_near(value):
    return permuted(value, lambda z, p, c: (z, p ^ (1 + c), c))


def to_far(value):
    return permuted(value, lambda z, p, c: (z, p ^ (2 - c), c))


def place_of(which, place, core):
    if which == 0:
        return place
    if which == 3:
        return place ^ 3
    return place ^ (1 + core) if which == 1 else place ^ (2 - core)


def turned(values, cosine, sine):
    return values * cosine + pltpu.roll(values, HD // 2, 1) * sine


def products(where_ref, x_refs, pieces):
    level, place, core = where_ref[0], where_ref[1], where_ref[2]
    totals = [None] * len(x_refs)
    for i in range(2):
        for j in range(PLANE):
            depth = pieces[i][j].shape[0]
            block = lax.rem(level + i, 2) * PLANE + place_of(j, place, core)
            start = pl.multiple_of(block * depth, depth)
            weights = pieces[i][j][...]
            for r, x_ref in enumerate(x_refs):
                part = jnp.dot(
                    x_ref[:, pl.ds(start, depth)], weights, preferred_element_type=jnp.float32
                )
                totals[r] = part if totals[r] is None else totals[r] + part
    return totals


def keys_part_kernel(where_ref, x0, x1, own, near, far, old0, old1, keep_ref, send_ref):
    pieces = [[own.at[i], near.at[i], far.at[i], far.at[2 + i]] for i in range(2)]
    rows = x0.shape[0]
    width = 2 * HD
    for r, total in enumerate(products(where_ref, (x0, x1), pieces)):
        keep_ref[r * rows : (r + 1) * rows] = total[:, :width]
        send_ref[r * rows : (r + 1) * rows] = total[:, width:].astype(jnp.bfloat16)
    at = 2 * rows
    for old in (old0, old1):
        send_ref[at : at + CACHED + REC_PAD] = old[:, width:]
        at += CACHED + REC_PAD


def keys_join_kernel(where_ref, keep_ref, got_ref, old0, old1, cos_ref, sin_ref, kv_ref, sum_ref):
    level = where_ref[0]
    rows = sum_ref.shape[0]
    block = rows // LEVELS
    tok = block - REC_PAD
    width = 2 * HD
    sum_ref[...] = keep_ref[...] + got_ref[0:rows].astype(jnp.float32)
    first = where_ref[3]
    span = CACHED + REC_PAD
    for n in range(LEVELS):
        at = jnp.bitwise_xor(level, n)
        start = pl.multiple_of(lax.rem(first + n, LEVELS) * block, 16)
        cosine, sine = cos_ref[at], sin_ref[at]
        fresh = sum_ref[pl.ds(start, tok), :]
        kv_ref[2 + at, :, 0:HD] = turned(fresh[:, :HD], cosine[:tok], sine[:tok]).astype(
            jnp.bfloat16
        )
        kv_ref[2 + at, :, HD:width] = fresh[:, HD:].astype(jnp.bfloat16)
        if n < 2:
            old = (old0, old1)[n][:, 0:width].astype(jnp.float32)
        else:
            old = got_ref[rows + (n - 2) * span : rows + (n - 1) * span].astype(jnp.float32)
        slots = old[CACHED : CACHED + REC].astype(jnp.int32)
        rec = sum_ref[pl.ds(pl.multiple_of(start + tok, 16), REC_PAD), :]
        line = lax.broadcasted_iota(jnp.int32, (CACHED, width), 0)
        found = jnp.zeros((CACHED, width), jnp.float32)
        hit = jnp.zeros((CACHED, width), jnp.int32)
        for r in range(REC):
            same = line == slots[r : r + 1]
            found = jnp.where(same, rec[r : r + 1], found)
            hit = jnp.where(same, 1, hit)
        keys = turned(found[:, :HD], cosine[tok : tok + CACHED], sine[tok : tok + CACHED])
        found = jnp.concatenate([keys, found[:, HD:]], axis=1)
        line_at = pl.multiple_of(lax.rem(at, 2) * CACHED, CACHED)
        kv_ref[at // 2, pl.ds(line_at, CACHED), :] = jnp.where(
            hit == 1, found, old[:CACHED]
        ).astype(jnp.bfloat16)


def queries_part_kernel(where_ref, x0, x1, *refs):
    next_own, next_near, next_far = refs[4:7]
    pieces = [
        [ref.at[0] for ref in refs[:4]],
        [next_own.at[0], next_near.at[0], next_far.at[0], next_far.at[1]],
    ]
    keep_ref, send_ref = refs[7:]
    block = x0.shape[0] // 2
    tok = block - REC_PAD
    width = 4 * HD
    for r, total in enumerate(products(where_ref, (x0, x1), pieces)):
        for k in range(2):
            fresh = total[k * block : k * block + tok]
            keep_ref[2 * r + k] = fresh[:, :width]
            send_ref[2 * r + k] = fresh[:, width:].astype(jnp.bfloat16)


def attend_kernel(
    where_ref, keep_ref, got_ref, cos_ref, sin_ref, kv0, kv1, kv2, kv3, out_ref, query_ref
):
    level, place, core = where_ref[0], where_ref[1], where_ref[2]
    pieces = (kv0, kv1, kv2, kv3)
    tok = keep_ref.shape[1]
    old = LEVELS // 2
    for n in range(LEVELS):
        at = jnp.bitwise_xor(level, n)
        block = lax.rem(where_ref[3] + n, LEVELS)
        total = keep_ref[block] + got_ref[block].astype(jnp.float32)
        cosine, sine = cos_ref[at][:tok], sin_ref[at][:tok]
        for h in range(4):
            head = turned(total[:, h * HD : (h + 1) * HD], cosine, sine)
            query_ref[at, h] = head.astype(jnp.bfloat16)
    row = lax.broadcasted_iota(jnp.int32, (tok, tok), 0)
    col = lax.broadcasted_iota(jnp.int32, (tok, tok), 1)
    scale = HD ** (-0.5) * 1.4426950408889634
    for i in range(LEVELS):
        count = (old + i + 1) * tok
        queries = query_ref[i].reshape(4 * tok, HD)
        scores = []
        best = None
        for j in range(PLANE):
            keys = pieces[j][0 : old + i + 1, :, 0:HD].reshape(count, HD)
            raw = lax.dot_general(
                queries, keys, (((1,), (1,)), ((), ())), preferred_element_type=jnp.float32
            )
            if j == 0:
                allowed = col <= row
            else:
                allowed = jnp.broadcast_to(place_of(j, place, core), (tok, tok)) < place
            allowed = jnp.concatenate([allowed] * 4, axis=0)
            last = jnp.where(allowed, raw[:, count - tok :], NEG_FILL)
            raw = jnp.concatenate([raw[:, : count - tok], last], axis=1)
            top = jnp.max(raw, axis=1, keepdims=True)
            best = top if best is None else jnp.maximum(best, top)
            scores.append(raw)
        total, accum = 0.0, 0.0
        for j in range(PLANE):
            weights = jnp.exp2((scores[j] - best) * scale)
            total = total + jnp.sum(weights, axis=1, keepdims=True)
            values = pieces[j][0 : old + i + 1, :, HD : 2 * HD].reshape(count, HD)
            accum = accum + jnp.dot(
                weights.astype(jnp.bfloat16), values, preferred_element_type=jnp.float32
            )
        result = (accum / total).astype(jnp.bfloat16)
        for h in range(4):
            out_ref[i * tok : (i + 1) * tok, h * HD : (h + 1) * HD] = result[
                h * tok : (h + 1) * tok
            ]


def output_kernel(where_ref, own_ref, next_ref, w_own, w_near, w_far, mine_ref, other_ref, x_ref):
    level, place, core = where_ref[0], where_ref[1], where_ref[2]
    depth = own_ref.shape[1]
    width = w_own.shape[2]
    tok = mine_ref.shape[1]
    x_ref[:, pl.ds(pl.multiple_of(lax.rem(level, 2) * depth, depth), depth)] = own_ref[...]
    x_ref[:, pl.ds(pl.multiple_of(lax.rem(level + 1, 2) * depth, depth), depth)] = next_ref[...]
    swap = jnp.where(core == level // 2, 0, 1)
    for s, out_ref in enumerate((mine_ref, other_ref)):
        i = jnp.bitwise_xor(swap, s)
        for j in range(PLANE):
            weights = (w_own.at[i], w_near.at[i], w_far.at[i], w_far.at[2 + i])[j]
            part = jnp.dot(x_ref[...], weights[...], preferred_element_type=jnp.float32)
            to = pl.multiple_of(place_of(j, place, core) * width, width)
            for t in range(LEVELS):
                out_ref[lax.rem(t + LEVELS - level, LEVELS), :, pl.ds(to, width)] = part[
                    t * tok : (t + 1) * tok
                ].astype(out_ref.dtype)


SMEM = pl.BlockSpec(memory_space=pltpu.SMEM)
VMEM = pl.BlockSpec(memory_space=pltpu.VMEM)
PARAMS = pltpu.CompilerParams(vmem_limit_bytes=48 * 1024 * 1024)


def shaped(shape, dtype=jnp.bfloat16):
    return jax.ShapeDtypeStruct(shape, dtype)


def by_levels(
    text_rows,
    picture_rows,
    picture_slots,
    norm_gain,
    w_query,
    w_key,
    w_value,
    w_out,
    cache_keys,
    cache_values,
    recompute_rows,
    recompute_slots,
):
    seq_index = lax.axis_index("seq")
    core = lax.axis_index("head")
    level, place = seq_index // PLANE, seq_index % PLANE
    half_at = level // 2
    own_first = core == half_at
    where = jnp.stack([level, place, core, jnp.where(own_first, 0, 2)]).astype(jnp.int32)
    tok, width = text_rows.shape
    block_rows = tok + REC_PAD

    stream_len = tok * LEVELS * PLANE
    tile_owners = TILE_RUN // tok
    first = stream_len // 2 // tok
    last = (stream_len - TILE_RUN) // tok
    owners = [first + i for i in range(tile_owners)] + [last + i for i in range(tile_owners)]
    assert [owner % PLANE for owner in owners] == list(range(LEVELS))
    owner_levels = jnp.array([owner // PLANE for owner in owners], jnp.int32)

    slots = (recompute_slots - seq_index * CACHED).astype(jnp.bfloat16)
    slot_rows = jnp.broadcast_to(jnp.pad(slots, (0, REC_PAD - REC))[:, None], (REC_PAD, 4 * HD))

    def columns(array, size, at):
        return lax.dynamic_slice_in_dim(array, at * size, size, 1)

    def key_columns(to_level):
        def pair(k, v):
            return [columns(a, HD, at) for at in (to_level, to_level ^ 2) for a in (k, v)]

        old = jnp.concatenate(pair(cache_keys, cache_values), axis=1)
        return pair(w_key, w_value), jnp.concatenate([old, slot_rows], axis=0)

    def query_columns(to_level):
        return [columns(w_query, 4 * HD, at) for at in (to_level, to_level ^ 2)]

    depth = w_query.shape[0]
    query_own = jnp.concatenate(query_columns(level), axis=1)[None]
    query_near = to_near(query_own)
    query_far = to_far(query_own)
    own_columns, old_own = key_columns(level)
    give_columns, old_give = key_columns(level ^ 1)
    third = (CACHED + REC_PAD + 2) // 3 // 16 * 16 + 16
    old_give = jnp.pad(old_give, ((0, 3 * third - CACHED - REC_PAD), (0, 0)))
    given = jnp.concatenate(
        [
            jnp.concatenate(give_columns + query_columns(level ^ 1), axis=1),
            jnp.concatenate([old_give[i * third : (i + 1) * third] for i in range(3)], axis=1),
        ],
        axis=0,
    )
    taken = across(given, 1)

    rows = jnp.concatenate(
        [text_rows, recompute_rows, jnp.zeros((REC_PAD - REC, width), text_rows.dtype)], axis=0
    )
    gain = lax.dynamic_slice_in_dim(norm_gain, core * width, width, 0)
    wide, pictures = rows.astype(jnp.float32), picture_rows.astype(jnp.float32)
    squares, picture_squares = lax.psum(
        (jnp.sum(wide * wide, axis=1), jnp.sum(pictures * pictures, axis=1)), "head"
    )
    normed = scaled(wide, squares, gain)
    pictures = scaled(pictures, picture_squares, gain)
    shown = [
        permuted(pictures, lambda z, p, c, k=k: (2 * c + (k ^ (p % 2)), z, p // 2)) for k in (0, 1)
    ]

    out_rows = w_out.shape[0] // 2
    out_own, out_give = (
        lax.dynamic_slice_in_dim(w_out, at * out_rows, out_rows, 0) for at in (half_at, 1 - half_at)
    )
    out_half = out_rows // 2
    out_got0, out_got1 = across(out_give[:out_half], 2), across(out_give[out_half:], 2)

    crossed = permuted(normed, lambda z, p, c: (z ^ 2, p, 1 - c) if c == 1 - z // 2 else None)
    crossed, taken, query_near, query_far, *shown = lax.optimization_barrier(
        (crossed, taken, query_near, query_far, *shown)
    )
    query_both = to_far(query_near)
    key_cols = 4 * HD
    keys = jnp.stack([jnp.concatenate(own_columns, axis=1), taken[:depth, :key_cols]])
    query_next = taken[None, :depth, key_cols:]
    old_next = jnp.concatenate(
        [taken[depth:, i * key_cols : (i + 1) * key_cols] for i in range(3)], axis=0
    )[: CACHED + REC_PAD]
    held = jnp.where(own_first, normed, crossed)
    next_rows = across(held, 1)
    keys_near, next_near = to_near(keys), to_near(query_next)
    odd = level % 2 == 1
    shown_mine = jnp.concatenate(
        [jnp.where(odd, shown[1], shown[0]), jnp.where(odd, shown[0], shown[1])], axis=0
    )
    shown_other = other_core(shown_mine)
    next_rows, keys_near, shown_other, next_near, out_got0, query_both = lax.optimization_barrier(
        (next_rows, keys_near, shown_other, next_near, out_got0, query_both)
    )
    keys_far = to_far(jnp.concatenate([keys, keys_near], axis=0))
    shown_all = jnp.concatenate(
        [
            jnp.where(core == 0, shown_mine, shown_other),
            jnp.where(core == 0, shown_other, shown_mine),
        ],
        axis=0,
    )
    shown_at = owner_levels[place]

    def with_pictures(block, at):
        return [jnp.where(at == shown_at, shown_all, block[:tok]), block[tok:]]

    held_at = jnp.where(own_first, level, level ^ 2)
    rows_mine = jnp.concatenate(
        with_pictures(held, held_at) + with_pictures(next_rows, held_at ^ 1), axis=0
    )
    rows_other = other_core(rows_mine)
    rows_other, keys_far, next_near, out_got1 = lax.optimization_barrier(
        (rows_other, keys_far, next_near, out_got1)
    )
    next_far = to_far(jnp.concatenate([query_next, next_near], axis=0))

    half = HD // 2
    freqs = ROPE_BASE ** (-jnp.arange(half, dtype=jnp.float32) / half)
    blocks = (jnp.arange(LEVELS, dtype=jnp.int32) * PLANE + place)[:, None]
    stream_pos = (
        CACHED * LEVELS * PLANE + blocks * tok + jnp.arange(tok, dtype=jnp.int32)[None]
    ).astype(jnp.float32)
    cache_pos = (blocks * CACHED + jnp.arange(CACHED, dtype=jnp.int32)[None]).astype(jnp.float32)
    angles = jnp.concatenate([stream_pos, cache_pos], axis=1)[..., None] * freqs
    cosine, sine = jnp.cos(angles), jnp.sin(angles)
    cosine = jnp.concatenate([cosine, cosine], axis=-1)
    sine = jnp.concatenate([-sine, sine], axis=-1)

    all_rows = LEVELS * block_rows
    keep, send = pl.pallas_call(
        keys_part_kernel,
        out_shape=(
            shaped((all_rows, 2 * HD), jnp.float32),
            shaped((all_rows + 2 * (CACHED + REC_PAD), 2 * HD)),
        ),
        in_specs=[SMEM] + [VMEM] * 7,
        out_specs=(VMEM, VMEM),
        compiler_params=PARAMS,
        name="keys_part",
    )(where, rows_mine, rows_other, keys, keys_near, keys_far, old_own, old_next)
    send, rows_after = lax.optimization_barrier((send, rows_mine))
    out_pair = jnp.stack([out_own, jnp.concatenate([out_got0, out_got1], axis=0)])
    out_pair, next_far = lax.optimization_barrier((out_pair, next_far))
    out_near = to_near(out_pair)
    q_keep, q_send = pl.pallas_call(
        queries_part_kernel,
        out_shape=(
            shaped((LEVELS, tok, 4 * HD), jnp.float32),
            shaped((LEVELS, tok, 4 * HD)),
        ),
        in_specs=[SMEM] + [VMEM] * 9,
        out_specs=(VMEM, VMEM),
        compiler_params=PARAMS,
        name="queries_part",
    )(
        where,
        rows_after,
        rows_other,
        query_own,
        query_near,
        query_far,
        query_both,
        query_next,
        next_near,
        next_far,
    )
    got_keys, q_send = lax.optimization_barrier((across(send, 2), q_send))
    kv = pl.pallas_call(
        keys_join_kernel,
        out_shape=shaped((LEVELS // 2 + LEVELS, tok, 2 * HD)),
        in_specs=[SMEM] + [VMEM] * 6,
        out_specs=VMEM,
        scratch_shapes=[pltpu.VMEM((all_rows, 2 * HD), jnp.float32)],
        compiler_params=PARAMS,
        name="keys_join",
    )(where, keep, got_keys, old_own, old_next, cosine, sine)
    kv_near, kv_far = to_near(kv), to_far(kv)
    kv_both = to_far(kv_near)

    kv_far, kv_both, out_near, got_queries = lax.optimization_barrier(
        (kv_far, kv_both, out_near, across(q_send, 2))
    )
    out_far = to_far(jnp.concatenate([out_pair, out_near], axis=0))

    attended = pl.pallas_call(
        attend_kernel,
        out_shape=shaped((LEVELS * tok, 4 * HD)),
        in_specs=[SMEM] + [VMEM] * 8,
        out_specs=VMEM,
        scratch_shapes=[pltpu.VMEM((LEVELS, 4, tok, HD), jnp.bfloat16)],
        compiler_params=PARAMS,
        name="attend",
    )(where, q_keep, got_queries, cosine, sine, kv, kv_near, kv_far, kv_both)

    wide_cols = PLANE * w_out.shape[1]
    mine, other = pl.pallas_call(
        output_kernel,
        out_shape=(
            shaped((LEVELS, tok, wide_cols), jnp.float32),
            shaped((LEVELS, tok, wide_cols)),
        ),
        in_specs=[SMEM] + [VMEM] * 5,
        out_specs=(VMEM, VMEM),
        scratch_shapes=[pltpu.VMEM((LEVELS * tok, out_rows), jnp.bfloat16)],
        compiler_params=PARAMS,
        name="output",
    )(where, attended, across(attended, 1), out_pair, out_near, out_far)
    got = other_core(other)

    def block_for(steps):
        return mine[steps] + got[steps].astype(jnp.float32)

    second, first, third = (up(block_for(d).astype(jnp.bfloat16), d) for d in (2, 1, 3))
    same = (block_for(0) + second.astype(jnp.float32)).astype(jnp.bfloat16)
    cross = (first.astype(jnp.float32) + third.astype(jnp.float32)).astype(jnp.bfloat16)
    even = level % 2 == 0
    return jnp.concatenate([jnp.where(even, same, cross), jnp.where(even, cross, same)], axis=1)


def solution(mesh):
    def run(*args):
        kv_local = args[5].shape[1] // HD // mesh.shape["head"]
        levels_fit = (
            mesh.shape["seq"] == LEVELS * PLANE
            and mesh.shape["head"] == 2
            and kv_local == LEVELS
            and args[1].shape[0] == 2 * TILE_RUN
            and args[0].shape[0] == 2048
            and args[8].shape[0] == LEVELS * PLANE * CACHED
            and args[10].shape[0] == LEVELS * PLANE * REC
        )
        return jax.shard_map(
            by_levels if levels_fit else on_device,
            mesh=mesh,
            in_specs=(
                P("seq", "head"),
                P("seq", "head"),
                P("seq"),
                P(),
                P("seq", "head"),
                P("seq", "head"),
                P("seq", "head"),
                P("head", "seq"),
                P("seq", "head"),
                P("seq", "head"),
                P("seq", "head"),
                P("seq"),
            ),
            out_specs=P("seq", "head"),
            check_vma=False,
        )(*args)

    return run
```

```python
import jax
import jax.numpy as jnp
from jax import lax
from jax.experimental import pallas as pl
from jax.experimental.pallas import tpu as pltpu
from jax.sharding import PartitionSpec as P

D = 4096
HD = 128


EPSILON = 1e-05
ROPE_BASE = 1000000.0
NEG_FILL = -1e30


def rotate(values, positions):
    half = values.shape[-1] // 2
    freqs = ROPE_BASE ** (-jnp.arange(half, dtype=jnp.float32) / half)
    angles = positions[:, None] * freqs[None, :]
    cosine = jnp.cos(angles)[:, None, :]
    sine = jnp.sin(angles)[:, None, :]
    first = values[..., :half]
    second = values[..., half:]
    return jnp.concatenate(
        [first * cosine - second * sine, second * cosine + first * sine], axis=-1
    )


def scaled(rows_wide, squares, gain):
    return (rows_wide * lax.rsqrt(squares / D + EPSILON)[:, None] * gain[None, :]).astype(
        jnp.bfloat16
    )


def attend(carry, key_piece, value_piece, queries, allowed):
    best, total, accum = carry
    count = key_piece.shape[0]
    kv_local = queries.shape[0]
    keys_split = key_piece.reshape(count, kv_local, HD)
    values_split = value_piece.reshape(count, kv_local, HD)
    scores = jnp.einsum(
        "kgtd,nkd->kgtn", queries, keys_split, preferred_element_type=jnp.float32
    ) * HD ** (-0.5)
    scores = jnp.where(allowed, scores, NEG_FILL)
    fresh = jnp.maximum(best, jnp.max(scores, axis=-1))
    factor = jnp.exp(best - fresh)
    weights = jnp.where(allowed, jnp.exp(scores - fresh[..., None]), 0.0)
    total = total * factor + jnp.sum(weights, axis=-1)
    accum = accum * factor[..., None] + jnp.einsum(
        "kgtn,nkd->kgtd",
        weights.astype(jnp.bfloat16),
        values_split,
        preferred_element_type=jnp.float32,
    )
    return (fresh, total, accum)


def on_device(
    text_rows,
    picture_rows,
    picture_slots,
    norm_gain,
    w_query,
    w_key,
    w_value,
    w_out,
    cache_keys,
    cache_values,
    recompute_rows,
    recompute_slots,
):
    tok_rows = text_rows.shape[0]
    rec_count = recompute_rows.shape[0]
    cache_rows = cache_keys.shape[0]
    seq_index = lax.axis_index("seq")
    local_pos = seq_index * tok_rows + jnp.arange(tok_rows, dtype=jnp.int32)
    rows_piece = lax.all_gather(picture_rows, "seq", axis=0, tiled=True)
    slots_piece = lax.all_gather(picture_slots, "seq", axis=0, tiled=True)
    select = (slots_piece[None, :] == local_pos[:, None]).astype(jnp.bfloat16)
    placed = jnp.dot(select, rows_piece, preferred_element_type=jnp.float32)
    hits = jnp.sum(select.astype(jnp.float32), axis=1)
    added, hits = (placed, hits)
    stream = jnp.where(hits[:, None] > 0.5, added, text_rows.astype(jnp.float32)).astype(
        jnp.bfloat16
    )
    slice_width = stream.shape[1]
    gain_slice = lax.dynamic_slice_in_dim(
        norm_gain, lax.axis_index("head") * slice_width, slice_width, 0
    )
    stream_wide = stream.astype(jnp.float32)
    rec_wide = recompute_rows.astype(jnp.float32)
    stream_sq, rec_sq = lax.psum(
        (jnp.sum(stream_wide * stream_wide, axis=1), jnp.sum(rec_wide * rec_wide, axis=1)), "head"
    )
    normed, rec_normed = (
        lax.all_gather(scaled(stream_wide, stream_sq, gain_slice), "head", axis=1, tiled=True),
        lax.all_gather(scaled(rec_wide, rec_sq, gain_slice), "head", axis=1, tiled=True),
    )
    stacked = jnp.concatenate([normed, rec_normed], axis=0)
    query_cols = w_query.shape[1]
    key_cols = w_key.shape[1]
    pieces = (
        lax.all_gather(w_query, "seq", axis=0, tiled=True),
        lax.all_gather(w_key, "seq", axis=0, tiled=True),
        lax.all_gather(w_value, "seq", axis=0, tiled=True),
    )
    query_all = jnp.dot(stacked, pieces[0], preferred_element_type=jnp.float32)
    key_all = jnp.dot(stacked, pieces[1], preferred_element_type=jnp.float32)
    value_all = jnp.dot(stacked, pieces[2], preferred_element_type=jnp.float32)
    cache_total = cache_rows * lax.axis_size("seq")
    stream_pos = (cache_total + local_pos).astype(jnp.float32)
    rec_pos = recompute_slots.astype(jnp.float32)
    heads_local = query_cols // HD
    kv_local = key_cols // HD
    group = heads_local // kv_local
    rot_query = rotate(query_all[:tok_rows].reshape(tok_rows, heads_local, HD), stream_pos).astype(
        jnp.bfloat16
    )
    rot_key = (
        rotate(key_all[:tok_rows].reshape(tok_rows, kv_local, HD), stream_pos)
        .astype(jnp.bfloat16)
        .reshape(tok_rows, key_cols)
    )
    values_new = value_all[:tok_rows].astype(jnp.bfloat16)
    rot_rec_key = (
        rotate(key_all[tok_rows:].reshape(rec_count, kv_local, HD), rec_pos)
        .astype(jnp.bfloat16)
        .reshape(rec_count, key_cols)
    )
    rec_values = value_all[tok_rows:].astype(jnp.bfloat16)
    local_slots = recompute_slots - seq_index * cache_rows
    select = local_slots[:, None] == jnp.arange(cache_rows, dtype=jnp.int32)[None, :]
    replaced = jnp.any(select, axis=0)[:, None]
    select_cols = select.astype(jnp.bfloat16).T
    new_keys = jnp.dot(select_cols, rot_rec_key, preferred_element_type=jnp.float32).astype(
        jnp.bfloat16
    )
    new_values = jnp.dot(select_cols, rec_values, preferred_element_type=jnp.float32).astype(
        jnp.bfloat16
    )
    cache_k = jnp.where(replaced, new_keys, cache_keys)
    cache_v = jnp.where(replaced, new_values, cache_values)
    queries = jnp.transpose(rot_query.reshape(tok_rows, kv_local, group, HD), (1, 2, 0, 3))
    carry_start = (
        jnp.full((kv_local, group, tok_rows), NEG_FILL, jnp.float32),
        jnp.zeros((kv_local, group, tok_rows), jnp.float32),
        jnp.zeros((kv_local, group, tok_rows, HD), jnp.float32),
    )
    pieces = (
        lax.all_gather(cache_k, "seq", axis=0, tiled=True),
        lax.all_gather(cache_v, "seq", axis=0, tiled=True),
    )
    allowed = jnp.ones((tok_rows, pieces[0].shape[0]), jnp.bool_)
    carry_mid = attend(carry_start, pieces[0], pieces[1], queries, allowed)
    pieces = (
        lax.all_gather(rot_key, "seq", axis=0, tiled=True),
        lax.all_gather(values_new, "seq", axis=0, tiled=True),
    )
    key_pos = jnp.arange(pieces[0].shape[0], dtype=jnp.int32)
    allowed = key_pos[None, :] <= local_pos[:, None]
    best, total, accum = attend(carry_mid, pieces[0], pieces[1], queries, allowed)
    attended = (
        jnp.transpose(accum / total[..., None], (2, 0, 1, 3))
        .reshape(tok_rows, query_cols)
        .astype(jnp.bfloat16)
    )
    partial_out = jnp.dot(
        attended,
        lax.all_gather(w_out, "seq", axis=1, tiled=True),
        preferred_element_type=jnp.float32,
    )
    return lax.psum_scatter(
        partial_out.astype(jnp.bfloat16), "head", scatter_dimension=1, tiled=True
    )


LEVELS = 4
PLANE = 4
TILE_RUN = 256
CACHED = 64
REC = 8
REC_PAD = 16


def permuted(value, move):
    perm = []
    for level in range(LEVELS):
        for place in range(PLANE):
            for core in range(2):
                target = move(level, place, core)
                if target is not None:
                    to_level, to_place, to_core = target
                    perm.append(
                        (
                            (level * PLANE + place) * 2 + core,
                            (to_level * PLANE + to_place) * 2 + to_core,
                        )
                    )
    return lax.ppermute(value, ("seq", "head"), perm)


def across(value, bit):
    return permuted(value, lambda z, p, c: (z ^ bit, p, c))


def up(value, steps):
    return permuted(value, lambda z, p, c: ((z + steps) % LEVELS, p, c))


def other_core(value):
    return permuted(value, lambda z, p, c: (z, p, 1 - c))


def to_near(value):
    return permuted(value, lambda z, p, c: (z, p ^ (1 + c), c))


def to_far(value):
    return permuted(value, lambda z, p, c: (z, p ^ (2 - c), c))


def place_of(which, place, core):
    if which == 0:
        return place
    if which == 3:
        return place ^ 3
    return place ^ (1 + core) if which == 1 else place ^ (2 - core)


def turned(values, cosine, sine):
    return values * cosine + pltpu.roll(values, HD // 2, 1) * sine


def pack_kernel(where_ref, *refs):
    w_query, w_key, w_value, cache_keys, cache_values, slots = refs[:6]
    outs, sems = refs[6:10], refs[10]
    level = where_ref[0]
    depth = w_query.shape[0]
    copies = []

    def copy(source, target):
        copies.append(pltpu.make_async_copy(source, target, sems.at[len(copies)]))
        copies[-1].start()

    for n in range(2):
        keys, queries = outs[2 * n : 2 * n + 2]
        for m in range(2):
            at = jnp.bitwise_xor(level, n + 2 * m)
            small = pl.ds(pl.multiple_of(at * HD, HD), HD)
            large = pl.ds(pl.multiple_of(at * 4 * HD, 4 * HD), 4 * HD)
            for k, (new, old) in enumerate(((w_key, cache_keys), (w_value, cache_values))):
                to = pl.ds((2 * m + k) * HD, HD)
                copy(new.at[:, small], keys.at[0:depth, to])
                copy(old.at[:, small], keys.at[depth : depth + CACHED, to])
            copy(w_query.at[:, large], queries.at[0, :, pl.ds(m * 4 * HD, 4 * HD)])
        copy(slots, keys.at[depth + CACHED : depth + CACHED + REC_PAD])
    for each in copies:
        each.wait()


PACK_COPIES = 22


def assemble(where_ref, parts, x_ref):
    level, core = where_ref[0], where_ref[2]
    shown = TILE_RUN // 2 // PLANE
    rows = parts[0].shape[0] - shown
    for n, part in enumerate(parts):
        x_ref[n * rows : (n + 1) * rows] = part[0:rows]
    start = where_ref[4] * rows
    for n, part in enumerate(parts):
        which = 2 * lax.rem(level + n % 2, 2) + (core if n < 2 else 1 - core)
        to = pl.multiple_of(start + which * shown, 16)
        x_ref[pl.ds(to, shown)] = part[rows : rows + shown]


def products(where_ref, x_ref, pieces):
    level, place, core = where_ref[0], where_ref[1], where_ref[2]
    total = None
    for i in range(2):
        for j in range(PLANE):
            depth = pieces[i][j].shape[0]
            block = lax.rem(level + i, 2) * PLANE + place_of(j, place, core)
            start = pl.multiple_of(block * depth, depth)
            part = jnp.dot(
                x_ref[:, pl.ds(start, depth)],
                pieces[i][j][...],
                preferred_element_type=jnp.float32,
            )
            total = part if total is None else total + part
    return total


def keys_part_kernel(
    where_ref, x0, x1, x2, x3, own, near, far, old0, old1, keep_ref, send_ref, x_ref
):
    assemble(where_ref, (x0, x1, x2, x3), x_ref)
    pieces = [[own.at[i], near.at[i], far.at[i], far.at[2 + i]] for i in range(2)]
    width = 2 * HD
    total = products(where_ref, x_ref, pieces)
    at = total.shape[0]
    keep_ref[...] = total[:, :width]
    send_ref[0:at] = total[:, width:].astype(jnp.bfloat16)
    for old in (old0, old1):
        send_ref[at : at + CACHED + REC_PAD] = old[:, width:]
        at += CACHED + REC_PAD


def keys_join_kernel(where_ref, keep_ref, got_ref, old0, old1, cos_ref, sin_ref, kv_ref, sum_ref):
    level = where_ref[0]
    rows = sum_ref.shape[0]
    block = rows // LEVELS
    tok = block - REC_PAD
    width = 2 * HD
    sum_ref[...] = keep_ref[...] + got_ref[0:rows].astype(jnp.float32)
    first = where_ref[3]
    span = CACHED + REC_PAD
    for n in range(LEVELS):
        at = jnp.bitwise_xor(level, n)
        start = pl.multiple_of(lax.rem(first + n, LEVELS) * block, 16)
        cosine, sine = cos_ref[at], sin_ref[at]
        fresh = sum_ref[pl.ds(start, tok), :]
        kv_ref[2 + at, :, 0:HD] = turned(fresh[:, :HD], cosine[:tok], sine[:tok]).astype(
            jnp.bfloat16
        )
        kv_ref[2 + at, :, HD:width] = fresh[:, HD:].astype(jnp.bfloat16)
        if n < 2:
            old = (old0, old1)[n][:, 0:width].astype(jnp.float32)
        else:
            old = got_ref[rows + (n - 2) * span : rows + (n - 1) * span].astype(jnp.float32)
        slots = old[CACHED : CACHED + REC].astype(jnp.int32)
        rec = sum_ref[pl.ds(pl.multiple_of(start + tok, 16), REC_PAD), :]
        line = lax.broadcasted_iota(jnp.int32, (CACHED, width), 0)
        found = jnp.zeros((CACHED, width), jnp.float32)
        hit = jnp.zeros((CACHED, width), jnp.int32)
        for r in range(REC):
            same = line == slots[r : r + 1]
            found = jnp.where(same, rec[r : r + 1], found)
            hit = jnp.where(same, 1, hit)
        keys = turned(found[:, :HD], cosine[tok : tok + CACHED], sine[tok : tok + CACHED])
        found = jnp.concatenate([keys, found[:, HD:]], axis=1)
        line_at = pl.multiple_of(lax.rem(at, 2) * CACHED, CACHED)
        kv_ref[at // 2, pl.ds(line_at, CACHED), :] = jnp.where(
            hit == 1, found, old[:CACHED]
        ).astype(jnp.bfloat16)


def queries_part_kernel(where_ref, x0, x1, x2, x3, *refs):
    keep_ref, send_ref, x_ref = refs[6:]
    assemble(where_ref, (x0, x1, x2, x3), x_ref)
    pieces = [
        [own.at[0], near.at[0], far.at[0], far.at[1]] for own, near, far in (refs[0:3], refs[3:6])
    ]
    total = products(where_ref, x_ref, pieces)
    block = total.shape[0] // LEVELS
    tok = block - REC_PAD
    width = 4 * HD
    for k in range(LEVELS):
        fresh = total[k * block : k * block + tok]
        keep_ref[k] = fresh[:, :width]
        send_ref[k] = fresh[:, width:].astype(jnp.bfloat16)


def attend_kernel(
    where_ref, keep_ref, got_ref, cos_ref, sin_ref, kv0, kv1, kv2, kv3, out_ref, query_ref
):
    level, place, core = where_ref[0], where_ref[1], where_ref[2]
    pieces = (kv0, kv1, kv2, kv3)
    tok = keep_ref.shape[1]
    old = LEVELS // 2
    for n in range(LEVELS):
        at = jnp.bitwise_xor(level, n)
        block = lax.rem(where_ref[3] + n, LEVELS)
        total = keep_ref[block] + got_ref[block].astype(jnp.float32)
        cosine, sine = cos_ref[at][:tok], sin_ref[at][:tok]
        for h in range(4):
            head = turned(total[:, h * HD : (h + 1) * HD], cosine, sine)
            query_ref[at, h] = head.astype(jnp.bfloat16)
    row = lax.broadcasted_iota(jnp.int32, (tok, tok), 0)
    col = lax.broadcasted_iota(jnp.int32, (tok, tok), 1)
    scale = HD ** (-0.5) * 1.4426950408889634
    for i in range(LEVELS):
        count = (old + i + 1) * tok
        queries = query_ref[i].reshape(4 * tok, HD)
        scores = []
        best = None
        for j in range(PLANE):
            keys = pieces[j][0 : old + i + 1, :, 0:HD].reshape(count, HD)
            raw = lax.dot_general(
                queries, keys, (((1,), (1,)), ((), ())), preferred_element_type=jnp.float32
            )
            if j == 0:
                allowed = col <= row
            else:
                allowed = jnp.broadcast_to(place_of(j, place, core), (tok, tok)) < place
            allowed = jnp.concatenate([allowed] * 4, axis=0)
            last = jnp.where(allowed, raw[:, count - tok :], NEG_FILL)
            raw = jnp.concatenate([raw[:, : count - tok], last], axis=1)
            top = jnp.max(raw, axis=1, keepdims=True)
            best = top if best is None else jnp.maximum(best, top)
            scores.append(raw)
        total, accum = 0.0, 0.0
        for j in range(PLANE):
            weights = jnp.exp2((scores[j] - best) * scale)
            total = total + jnp.sum(weights, axis=1, keepdims=True)
            values = pieces[j][0 : old + i + 1, :, HD : 2 * HD].reshape(count, HD)
            accum = accum + jnp.dot(
                weights.astype(jnp.bfloat16), values, preferred_element_type=jnp.float32
            )
        result = (accum / total).astype(jnp.bfloat16)
        for h in range(4):
            out_ref[i * tok : (i + 1) * tok, h * HD : (h + 1) * HD] = result[
                h * tok : (h + 1) * tok
            ]


def output_kernel(where_ref, own_ref, next_ref, w_own, w_near, w_far, mine_ref, other_ref, x_ref):
    level, place, core = where_ref[0], where_ref[1], where_ref[2]
    depth = own_ref.shape[1]
    width = w_own.shape[2]
    tok = mine_ref.shape[1]
    x_ref[:, pl.ds(pl.multiple_of(lax.rem(level, 2) * depth, depth), depth)] = own_ref[...]
    x_ref[:, pl.ds(pl.multiple_of(lax.rem(level + 1, 2) * depth, depth), depth)] = next_ref[...]
    swap = jnp.where(core == level // 2, 0, 1)
    for s, out_ref in enumerate((mine_ref, other_ref)):
        i = jnp.bitwise_xor(swap, s)
        for j in range(PLANE):
            weights = (w_own.at[i], w_near.at[i], w_far.at[i], w_far.at[2 + i])[j]
            part = jnp.dot(x_ref[...], weights[...], preferred_element_type=jnp.float32)
            to = pl.multiple_of(place_of(j, place, core) * width, width)
            for t in range(LEVELS):
                out_ref[lax.rem(t + LEVELS - level, LEVELS), :, pl.ds(to, width)] = part[
                    t * tok : (t + 1) * tok
                ].astype(out_ref.dtype)


SMEM = pl.BlockSpec(memory_space=pltpu.SMEM)
VMEM = pl.BlockSpec(memory_space=pltpu.VMEM)
ANY = pl.BlockSpec(memory_space=pl.ANY)
PARAMS = pltpu.CompilerParams(vmem_limit_bytes=48 * 1024 * 1024)


def shaped(shape, dtype=jnp.bfloat16):
    return jax.ShapeDtypeStruct(shape, dtype)


def by_levels(
    text_rows,
    picture_rows,
    picture_slots,
    norm_gain,
    w_query,
    w_key,
    w_value,
    w_out,
    cache_keys,
    cache_values,
    recompute_rows,
    recompute_slots,
):
    seq_index = lax.axis_index("seq")
    core = lax.axis_index("head")
    level, place = seq_index // PLANE, seq_index % PLANE
    half_at = level // 2
    own_first = core == half_at
    tok, width = text_rows.shape
    block_rows = tok + REC_PAD

    stream_len = tok * LEVELS * PLANE
    tile_owners = TILE_RUN // tok
    first = stream_len // 2 // tok
    last = (stream_len - TILE_RUN) // tok
    owners = [first + i for i in range(tile_owners)] + [last + i for i in range(tile_owners)]
    assert [owner % PLANE for owner in owners] == list(range(LEVELS))
    owner_levels = jnp.array([owner // PLANE for owner in owners], jnp.int32)

    first_block = jnp.where(own_first, 0, 2)
    shown_block = (first_block + (level ^ owner_levels[place])) % LEVELS
    where = jnp.stack([level, place, core, first_block, shown_block]).astype(jnp.int32)

    slots = (recompute_slots - seq_index * CACHED).astype(jnp.bfloat16)
    slot_rows = jnp.broadcast_to(jnp.pad(slots, (0, REC_PAD - REC))[:, None], (REC_PAD, 4 * HD))
    depth = w_query.shape[0]
    key_shape = shaped((depth + CACHED + REC_PAD, 4 * HD))
    query_shape = shaped((1, depth, 8 * HD))
    key_own, query_own, key_give, query_give = pl.pallas_call(
        pack_kernel,
        out_shape=(key_shape, query_shape) * 2,
        in_specs=[SMEM] + [ANY] * 6,
        out_specs=(ANY,) * 4,
        scratch_shapes=[pltpu.SemaphoreType.DMA((PACK_COPIES,))],
        compiler_params=PARAMS,
        name="pack",
    )(where, w_query, w_key, w_value, cache_keys, cache_values, slot_rows)
    query_near = to_near(query_own)

    text_rows, key_give = lax.optimization_barrier((text_rows, key_give))
    rows = jnp.concatenate(
        [text_rows, recompute_rows, jnp.zeros((REC_PAD - REC, width), text_rows.dtype)], axis=0
    )
    gain = lax.dynamic_slice_in_dim(norm_gain, core * width, width, 0)
    wide, pictures = rows.astype(jnp.float32), picture_rows.astype(jnp.float32)
    squares, picture_squares = lax.psum(
        (jnp.sum(wide * wide, axis=1), jnp.sum(pictures * pictures, axis=1)), "head"
    )
    normed = scaled(wide, squares, gain)
    pictures = scaled(pictures, picture_squares, gain)

    out_rows = w_out.shape[0] // 2
    out_own, out_give = (
        lax.dynamic_slice_in_dim(w_out, at * out_rows, out_rows, 0) for at in (half_at, 1 - half_at)
    )
    out_half = out_rows // 2
    out_got0, out_got1 = across(out_give[:out_half], 2), across(out_give[out_half:], 2)

    crossed = permuted(normed, lambda z, p, c: (z ^ 2, p, 1 - c) if c == 1 - z // 2 else None)
    normed, pictures, query_give = lax.optimization_barrier((normed, pictures, query_give))
    shown = permuted(pictures, lambda z, p, c: (2 * c + p // 2, z, p % 2))
    query_next = across(query_give, 1)
    key_next = across(key_give, 1)
    keys = jnp.stack([key_own[:depth], key_next[:depth]])
    old_own, old_next = key_own[depth:], key_next[depth:]
    keys_near = to_near(keys)
    crossed, shown, keys_near, query_next = lax.optimization_barrier(
        (crossed, shown, keys_near, query_next)
    )
    held = jnp.concatenate([jnp.where(own_first, normed, crossed), shown], axis=0)
    next_rows = across(held, 1)
    held_other = other_core(held)
    keys_far = to_far(jnp.concatenate([keys, keys_near], axis=0))
    query_far = to_far(jnp.concatenate([query_own, query_near], axis=0))
    next_near = to_near(query_next)
    next_rows, held_other, keys_far, query_far, out_got0, next_near = lax.optimization_barrier(
        (next_rows, held_other, keys_far, query_far, out_got0, next_near)
    )
    next_other = other_core(next_rows)
    next_other, out_got1 = lax.optimization_barrier((next_other, out_got1))
    next_far = to_far(jnp.concatenate([query_next, next_near], axis=0))
    parts = (held, next_rows, held_other, next_other)

    half = HD // 2
    freqs = ROPE_BASE ** (-jnp.arange(half, dtype=jnp.float32) / half)
    blocks = (jnp.arange(LEVELS, dtype=jnp.int32) * PLANE + place)[:, None]
    stream_pos = (
        CACHED * LEVELS * PLANE + blocks * tok + jnp.arange(tok, dtype=jnp.int32)[None]
    ).astype(jnp.float32)
    cache_pos = (blocks * CACHED + jnp.arange(CACHED, dtype=jnp.int32)[None]).astype(jnp.float32)
    angles = jnp.concatenate([stream_pos, cache_pos], axis=1)[..., None] * freqs
    cosine, sine = jnp.cos(angles), jnp.sin(angles)
    cosine = jnp.concatenate([cosine, cosine], axis=-1)
    sine = jnp.concatenate([-sine, sine], axis=-1)

    all_rows = LEVELS * block_rows
    keep, send = pl.pallas_call(
        keys_part_kernel,
        out_shape=(
            shaped((all_rows, 2 * HD), jnp.float32),
            shaped((all_rows + 2 * (CACHED + REC_PAD), 2 * HD)),
        ),
        in_specs=[SMEM] + [VMEM] * 9,
        out_specs=(VMEM, VMEM),
        scratch_shapes=[pltpu.VMEM((all_rows, width), jnp.bfloat16)],
        compiler_params=PARAMS,
        name="keys_part",
    )(where, *parts, keys, keys_near, keys_far, old_own, old_next)
    send, *parts = lax.optimization_barrier((send, *parts))
    out_pair = jnp.stack([out_own, jnp.concatenate([out_got0, out_got1], axis=0)])
    out_pair, next_far = lax.optimization_barrier((out_pair, next_far))
    out_near = to_near(out_pair)
    q_keep, q_send = pl.pallas_call(
        queries_part_kernel,
        out_shape=(
            shaped((LEVELS, tok, 4 * HD), jnp.float32),
            shaped((LEVELS, tok, 4 * HD)),
        ),
        in_specs=[SMEM] + [VMEM] * 10,
        out_specs=(VMEM, VMEM),
        scratch_shapes=[pltpu.VMEM((all_rows, width), jnp.bfloat16)],
        compiler_params=PARAMS,
        name="queries_part",
    )(where, *parts, query_own, query_near, query_far, query_next, next_near, next_far)
    got_keys, q_send = lax.optimization_barrier((across(send, 2), q_send))
    kv = pl.pallas_call(
        keys_join_kernel,
        out_shape=shaped((LEVELS // 2 + LEVELS, tok, 2 * HD)),
        in_specs=[SMEM] + [VMEM] * 6,
        out_specs=VMEM,
        scratch_shapes=[pltpu.VMEM((all_rows, 2 * HD), jnp.float32)],
        compiler_params=PARAMS,
        name="keys_join",
    )(where, keep, got_keys, old_own, old_next, cosine, sine)
    kv_near, kv_far = to_near(kv), to_far(kv)
    kv_both = to_far(kv_near)

    kv_far, kv_both, out_near, got_queries = lax.optimization_barrier(
        (kv_far, kv_both, out_near, across(q_send, 2))
    )
    out_far = to_far(jnp.concatenate([out_pair, out_near], axis=0))

    attended = pl.pallas_call(
        attend_kernel,
        out_shape=shaped((LEVELS * tok, 4 * HD)),
        in_specs=[SMEM] + [VMEM] * 8,
        out_specs=VMEM,
        scratch_shapes=[pltpu.VMEM((LEVELS, 4, tok, HD), jnp.bfloat16)],
        compiler_params=PARAMS,
        name="attend",
    )(where, q_keep, got_queries, cosine, sine, kv, kv_near, kv_far, kv_both)

    wide_cols = PLANE * w_out.shape[1]
    mine, other = pl.pallas_call(
        output_kernel,
        out_shape=(
            shaped((LEVELS, tok, wide_cols), jnp.float32),
            shaped((LEVELS, tok, wide_cols)),
        ),
        in_specs=[SMEM] + [VMEM] * 5,
        out_specs=(VMEM, VMEM),
        scratch_shapes=[pltpu.VMEM((LEVELS * tok, out_rows), jnp.bfloat16)],
        compiler_params=PARAMS,
        name="output",
    )(where, attended, across(attended, 1), out_pair, out_near, out_far)
    got = other_core(other)

    def block_for(steps):
        return mine[steps] + got[steps].astype(jnp.float32)

    second, first, third = (up(block_for(d).astype(jnp.bfloat16), d) for d in (2, 1, 3))
    same = (block_for(0) + second.astype(jnp.float32)).astype(jnp.bfloat16)
    cross = (first.astype(jnp.float32) + third.astype(jnp.float32)).astype(jnp.bfloat16)
    even = level % 2 == 0
    return jnp.concatenate([jnp.where(even, same, cross), jnp.where(even, cross, same)], axis=1)


def solution(mesh):
    def run(*args):
        kv_local = args[5].shape[1] // HD // mesh.shape["head"]
        levels_fit = (
            mesh.shape["seq"] == LEVELS * PLANE
            and mesh.shape["head"] == 2
            and kv_local == LEVELS
            and args[1].shape[0] == 2 * TILE_RUN
            and args[0].shape[0] == 2048
            and args[8].shape[0] == LEVELS * PLANE * CACHED
            and args[10].shape[0] == LEVELS * PLANE * REC
        )
        return jax.shard_map(
            by_levels if levels_fit else on_device,
            mesh=mesh,
            in_specs=(
                P("seq", "head"),
                P("seq", "head"),
                P("seq"),
                P(),
                P("seq", "head"),
                P("seq", "head"),
                P("seq", "head"),
                P("head", "seq"),
                P("seq", "head"),
                P("seq", "head"),
                P("seq", "head"),
                P("seq"),
            ),
            out_specs=P("seq", "head"),
            check_vma=False,
        )(*args)

    return run
```

```python
import jax
import jax.numpy as jnp
from jax import lax
from jax.experimental import pallas as pl
from jax.experimental.pallas import tpu as pltpu
from jax.sharding import PartitionSpec as P

D = 4096
HD = 128


EPSILON = 1e-05
ROPE_BASE = 1000000.0
NEG_FILL = -1e30


def rotate(values, positions):
    half = values.shape[-1] // 2
    freqs = ROPE_BASE ** (-jnp.arange(half, dtype=jnp.float32) / half)
    angles = positions[:, None] * freqs[None, :]
    cosine = jnp.cos(angles)[:, None, :]
    sine = jnp.sin(angles)[:, None, :]
    first = values[..., :half]
    second = values[..., half:]
    return jnp.concatenate(
        [first * cosine - second * sine, second * cosine + first * sine], axis=-1
    )


def scaled(rows_wide, squares, gain):
    return (rows_wide * lax.rsqrt(squares / D + EPSILON)[:, None] * gain[None, :]).astype(
        jnp.bfloat16
    )


def attend(carry, key_piece, value_piece, queries, allowed):
    best, total, accum = carry
    count = key_piece.shape[0]
    kv_local = queries.shape[0]
    keys_split = key_piece.reshape(count, kv_local, HD)
    values_split = value_piece.reshape(count, kv_local, HD)
    scores = jnp.einsum(
        "kgtd,nkd->kgtn", queries, keys_split, preferred_element_type=jnp.float32
    ) * HD ** (-0.5)
    scores = jnp.where(allowed, scores, NEG_FILL)
    fresh = jnp.maximum(best, jnp.max(scores, axis=-1))
    factor = jnp.exp(best - fresh)
    weights = jnp.where(allowed, jnp.exp(scores - fresh[..., None]), 0.0)
    total = total * factor + jnp.sum(weights, axis=-1)
    accum = accum * factor[..., None] + jnp.einsum(
        "kgtn,nkd->kgtd",
        weights.astype(jnp.bfloat16),
        values_split,
        preferred_element_type=jnp.float32,
    )
    return (fresh, total, accum)


def on_device(
    text_rows,
    picture_rows,
    picture_slots,
    norm_gain,
    w_query,
    w_key,
    w_value,
    w_out,
    cache_keys,
    cache_values,
    recompute_rows,
    recompute_slots,
):
    tok_rows = text_rows.shape[0]
    rec_count = recompute_rows.shape[0]
    cache_rows = cache_keys.shape[0]
    seq_index = lax.axis_index("seq")
    local_pos = seq_index * tok_rows + jnp.arange(tok_rows, dtype=jnp.int32)
    rows_piece = lax.all_gather(picture_rows, "seq", axis=0, tiled=True)
    slots_piece = lax.all_gather(picture_slots, "seq", axis=0, tiled=True)
    select = (slots_piece[None, :] == local_pos[:, None]).astype(jnp.bfloat16)
    placed = jnp.dot(select, rows_piece, preferred_element_type=jnp.float32)
    hits = jnp.sum(select.astype(jnp.float32), axis=1)
    added, hits = (placed, hits)
    stream = jnp.where(hits[:, None] > 0.5, added, text_rows.astype(jnp.float32)).astype(
        jnp.bfloat16
    )
    slice_width = stream.shape[1]
    gain_slice = lax.dynamic_slice_in_dim(
        norm_gain, lax.axis_index("head") * slice_width, slice_width, 0
    )
    stream_wide = stream.astype(jnp.float32)
    rec_wide = recompute_rows.astype(jnp.float32)
    stream_sq, rec_sq = lax.psum(
        (jnp.sum(stream_wide * stream_wide, axis=1), jnp.sum(rec_wide * rec_wide, axis=1)), "head"
    )
    normed, rec_normed = (
        lax.all_gather(scaled(stream_wide, stream_sq, gain_slice), "head", axis=1, tiled=True),
        lax.all_gather(scaled(rec_wide, rec_sq, gain_slice), "head", axis=1, tiled=True),
    )
    stacked = jnp.concatenate([normed, rec_normed], axis=0)
    query_cols = w_query.shape[1]
    key_cols = w_key.shape[1]
    pieces = (
        lax.all_gather(w_query, "seq", axis=0, tiled=True),
        lax.all_gather(w_key, "seq", axis=0, tiled=True),
        lax.all_gather(w_value, "seq", axis=0, tiled=True),
    )
    query_all = jnp.dot(stacked, pieces[0], preferred_element_type=jnp.float32)
    key_all = jnp.dot(stacked, pieces[1], preferred_element_type=jnp.float32)
    value_all = jnp.dot(stacked, pieces[2], preferred_element_type=jnp.float32)
    cache_total = cache_rows * lax.axis_size("seq")
    stream_pos = (cache_total + local_pos).astype(jnp.float32)
    rec_pos = recompute_slots.astype(jnp.float32)
    heads_local = query_cols // HD
    kv_local = key_cols // HD
    group = heads_local // kv_local
    rot_query = rotate(query_all[:tok_rows].reshape(tok_rows, heads_local, HD), stream_pos).astype(
        jnp.bfloat16
    )
    rot_key = (
        rotate(key_all[:tok_rows].reshape(tok_rows, kv_local, HD), stream_pos)
        .astype(jnp.bfloat16)
        .reshape(tok_rows, key_cols)
    )
    values_new = value_all[:tok_rows].astype(jnp.bfloat16)
    rot_rec_key = (
        rotate(key_all[tok_rows:].reshape(rec_count, kv_local, HD), rec_pos)
        .astype(jnp.bfloat16)
        .reshape(rec_count, key_cols)
    )
    rec_values = value_all[tok_rows:].astype(jnp.bfloat16)
    local_slots = recompute_slots - seq_index * cache_rows
    select = local_slots[:, None] == jnp.arange(cache_rows, dtype=jnp.int32)[None, :]
    replaced = jnp.any(select, axis=0)[:, None]
    select_cols = select.astype(jnp.bfloat16).T
    new_keys = jnp.dot(select_cols, rot_rec_key, preferred_element_type=jnp.float32).astype(
        jnp.bfloat16
    )
    new_values = jnp.dot(select_cols, rec_values, preferred_element_type=jnp.float32).astype(
        jnp.bfloat16
    )
    cache_k = jnp.where(replaced, new_keys, cache_keys)
    cache_v = jnp.where(replaced, new_values, cache_values)
    queries = jnp.transpose(rot_query.reshape(tok_rows, kv_local, group, HD), (1, 2, 0, 3))
    carry_start = (
        jnp.full((kv_local, group, tok_rows), NEG_FILL, jnp.float32),
        jnp.zeros((kv_local, group, tok_rows), jnp.float32),
        jnp.zeros((kv_local, group, tok_rows, HD), jnp.float32),
    )
    pieces = (
        lax.all_gather(cache_k, "seq", axis=0, tiled=True),
        lax.all_gather(cache_v, "seq", axis=0, tiled=True),
    )
    allowed = jnp.ones((tok_rows, pieces[0].shape[0]), jnp.bool_)
    carry_mid = attend(carry_start, pieces[0], pieces[1], queries, allowed)
    pieces = (
        lax.all_gather(rot_key, "seq", axis=0, tiled=True),
        lax.all_gather(values_new, "seq", axis=0, tiled=True),
    )
    key_pos = jnp.arange(pieces[0].shape[0], dtype=jnp.int32)
    allowed = key_pos[None, :] <= local_pos[:, None]
    best, total, accum = attend(carry_mid, pieces[0], pieces[1], queries, allowed)
    attended = (
        jnp.transpose(accum / total[..., None], (2, 0, 1, 3))
        .reshape(tok_rows, query_cols)
        .astype(jnp.bfloat16)
    )
    partial_out = jnp.dot(
        attended,
        lax.all_gather(w_out, "seq", axis=1, tiled=True),
        preferred_element_type=jnp.float32,
    )
    return lax.psum_scatter(
        partial_out.astype(jnp.bfloat16), "head", scatter_dimension=1, tiled=True
    )


LEVELS = 4
PLANE = 4
TILE_RUN = 256
CACHED = 64
REC = 8
REC_PAD = 16


def permuted(value, move):
    perm = []
    for level in range(LEVELS):
        for place in range(PLANE):
            for core in range(2):
                target = move(level, place, core)
                if target is not None:
                    to_level, to_place, to_core = target
                    perm.append(
                        (
                            (level * PLANE + place) * 2 + core,
                            (to_level * PLANE + to_place) * 2 + to_core,
                        )
                    )
    return lax.ppermute(value, ("seq", "head"), perm)


def across(value, bit):
    return permuted(value, lambda z, p, c: (z ^ bit, p, c))


def up(value, steps):
    return permuted(value, lambda z, p, c: ((z + steps) % LEVELS, p, c))


def other_core(value):
    return permuted(value, lambda z, p, c: (z, p, 1 - c))


def to_near(value):
    return permuted(value, lambda z, p, c: (z, p ^ (1 + c), c))


def to_far(value):
    return permuted(value, lambda z, p, c: (z, p ^ (2 - c), c))


def place_of(which, place, core):
    if which == 0:
        return place
    if which == 3:
        return place ^ 3
    return place ^ (1 + core) if which == 1 else place ^ (2 - core)


def turned(values, cosine, sine):
    return values * cosine + pltpu.roll(values, HD // 2, 1) * sine


def pack_kernel(where_ref, *refs):
    w_query, w_key, w_value, cache_keys, cache_values, slots = refs[:6]
    outs, sems = refs[6:10], refs[10]
    level = where_ref[0]
    depth = w_query.shape[0]
    copies = []

    def copy(source, target):
        copies.append(pltpu.make_async_copy(source, target, sems.at[len(copies)]))
        copies[-1].start()

    for n in range(2):
        keys, queries = outs[2 * n : 2 * n + 2]
        for m in range(2):
            at = jnp.bitwise_xor(level, n + 2 * m)
            small = pl.ds(pl.multiple_of(at * HD, HD), HD)
            large = pl.ds(pl.multiple_of(at * 4 * HD, 4 * HD), 4 * HD)
            for k, (new, old) in enumerate(((w_key, cache_keys), (w_value, cache_values))):
                to = pl.ds((2 * m + k) * HD, HD)
                copy(new.at[:, small], keys.at[0:depth, to])
                copy(old.at[:, small], keys.at[depth : depth + CACHED, to])
            copy(w_query.at[:, large], queries.at[0, :, pl.ds(m * 4 * HD, 4 * HD)])
        copy(slots, keys.at[depth + CACHED : depth + CACHED + REC_PAD])
    for each in copies:
        each.wait()


PACK_COPIES = 22


def assemble(where_ref, parts, x_ref):
    level, core = where_ref[0], where_ref[2]
    shown = TILE_RUN // 2 // PLANE
    rows = parts[0].shape[0] - shown
    for n, part in enumerate(parts):
        x_ref[n * rows : (n + 1) * rows] = part[0:rows]
    start = where_ref[4] * rows
    for n, part in enumerate(parts):
        which = 2 * lax.rem(level + n % 2, 2) + (core if n < 2 else 1 - core)
        to = pl.multiple_of(start + which * shown, 16)
        x_ref[pl.ds(to, shown)] = part[rows : rows + shown]


def products(where_ref, x_ref, pieces):
    level, place, core = where_ref[0], where_ref[1], where_ref[2]
    total = None
    for i in range(2):
        for j in range(PLANE):
            depth = pieces[i][j].shape[0]
            block = lax.rem(level + i, 2) * PLANE + place_of(j, place, core)
            start = pl.multiple_of(block * depth, depth)
            part = jnp.dot(
                x_ref[:, pl.ds(start, depth)],
                pieces[i][j][...],
                preferred_element_type=jnp.float32,
            )
            total = part if total is None else total + part
    return total


def keys_part_kernel(
    where_ref, x0, x1, x2, x3, own, near, far, old0, old1, keep_ref, send_ref, x_ref
):
    assemble(where_ref, (x0, x1, x2, x3), x_ref)
    pieces = [[own.at[i], near.at[i], far.at[i], far.at[2 + i]] for i in range(2)]
    width = 2 * HD
    total = products(where_ref, x_ref, pieces)
    at = total.shape[0]
    keep_ref[...] = total[:, :width]
    send_ref[0:at] = total[:, width:].astype(jnp.bfloat16)
    for old in (old0, old1):
        send_ref[at : at + CACHED + REC_PAD] = old[:, width:]
        at += CACHED + REC_PAD


def keys_join_kernel(where_ref, keep_ref, got_ref, old0, old1, cos_ref, sin_ref, kv_ref, sum_ref):
    level = where_ref[0]
    rows = sum_ref.shape[0]
    block = rows // LEVELS
    tok = block - REC_PAD
    width = 2 * HD
    sum_ref[...] = keep_ref[...] + got_ref[0:rows].astype(jnp.float32)
    first = where_ref[3]
    span = CACHED + REC_PAD
    for n in range(LEVELS):
        at = jnp.bitwise_xor(level, n)
        start = pl.multiple_of(lax.rem(first + n, LEVELS) * block, 16)
        cosine, sine = cos_ref[at], sin_ref[at]
        fresh = sum_ref[pl.ds(start, tok), :]
        kv_ref[2 + at, :, 0:HD] = turned(fresh[:, :HD], cosine[:tok], sine[:tok]).astype(
            jnp.bfloat16
        )
        kv_ref[2 + at, :, HD:width] = fresh[:, HD:].astype(jnp.bfloat16)
        if n < 2:
            old = (old0, old1)[n][:, 0:width].astype(jnp.float32)
        else:
            old = got_ref[rows + (n - 2) * span : rows + (n - 1) * span].astype(jnp.float32)
        slots = old[CACHED : CACHED + REC].astype(jnp.int32)
        rec = sum_ref[pl.ds(pl.multiple_of(start + tok, 16), REC_PAD), :]
        line = lax.broadcasted_iota(jnp.int32, (CACHED, width), 0)
        found = jnp.zeros((CACHED, width), jnp.float32)
        hit = jnp.zeros((CACHED, width), jnp.int32)
        for r in range(REC):
            same = line == slots[r : r + 1]
            found = jnp.where(same, rec[r : r + 1], found)
            hit = jnp.where(same, 1, hit)
        keys = turned(found[:, :HD], cosine[tok : tok + CACHED], sine[tok : tok + CACHED])
        found = jnp.concatenate([keys, found[:, HD:]], axis=1)
        line_at = pl.multiple_of(lax.rem(at, 2) * CACHED, CACHED)
        kv_ref[at // 2, pl.ds(line_at, CACHED), :] = jnp.where(
            hit == 1, found, old[:CACHED]
        ).astype(jnp.bfloat16)


def queries_part_kernel(where_ref, x0, x1, x2, x3, *refs):
    keep_ref, send_ref, x_ref = refs[6:]
    assemble(where_ref, (x0, x1, x2, x3), x_ref)
    pieces = [
        [own.at[0], near.at[0], far.at[0], far.at[1]] for own, near, far in (refs[0:3], refs[3:6])
    ]
    total = products(where_ref, x_ref, pieces)
    block = total.shape[0] // LEVELS
    tok = block - REC_PAD
    width = 4 * HD
    for k in range(LEVELS):
        fresh = total[k * block : k * block + tok]
        keep_ref[k] = fresh[:, :width]
        send_ref[k] = fresh[:, width:].astype(jnp.bfloat16)


def attend_kernel(
    where_ref, keep_ref, got_ref, cos_ref, sin_ref, kv0, kv1, kv2, kv3, out_ref, query_ref
):
    level, place, core = where_ref[0], where_ref[1], where_ref[2]
    pieces = (kv0, kv1, kv2, kv3)
    tok = keep_ref.shape[1]
    old = LEVELS // 2
    for n in range(LEVELS):
        at = jnp.bitwise_xor(level, n)
        block = lax.rem(where_ref[3] + n, LEVELS)
        total = keep_ref[block] + got_ref[block].astype(jnp.float32)
        cosine, sine = cos_ref[at][:tok], sin_ref[at][:tok]
        for h in range(4):
            head = turned(total[:, h * HD : (h + 1) * HD], cosine, sine)
            query_ref[at, h] = head.astype(jnp.bfloat16)
    row = lax.broadcasted_iota(jnp.int32, (tok, tok), 0)
    col = lax.broadcasted_iota(jnp.int32, (tok, tok), 1)
    scale = HD ** (-0.5) * 1.4426950408889634
    for i in range(LEVELS):
        count = (old + i + 1) * tok
        queries = query_ref[i].reshape(4 * tok, HD)
        scores = []
        best = None
        for j in range(PLANE):
            keys = pieces[j][0 : old + i + 1, :, 0:HD].reshape(count, HD)
            raw = lax.dot_general(
                queries, keys, (((1,), (1,)), ((), ())), preferred_element_type=jnp.float32
            )
            if j == 0:
                allowed = col <= row
            else:
                allowed = jnp.broadcast_to(place_of(j, place, core), (tok, tok)) < place
            allowed = jnp.concatenate([allowed] * 4, axis=0)
            last = jnp.where(allowed, raw[:, count - tok :], NEG_FILL)
            raw = jnp.concatenate([raw[:, : count - tok], last], axis=1)
            top = jnp.max(raw, axis=1, keepdims=True)
            best = top if best is None else jnp.maximum(best, top)
            scores.append(raw)
        total, accum = 0.0, 0.0
        for j in range(PLANE):
            weights = jnp.exp2((scores[j] - best) * scale)
            total = total + jnp.sum(weights, axis=1, keepdims=True)
            values = pieces[j][0 : old + i + 1, :, HD : 2 * HD].reshape(count, HD)
            accum = accum + jnp.dot(
                weights.astype(jnp.bfloat16), values, preferred_element_type=jnp.float32
            )
        result = (accum / total).astype(jnp.bfloat16)
        for h in range(4):
            out_ref[i * tok : (i + 1) * tok, h * HD : (h + 1) * HD] = result[
                h * tok : (h + 1) * tok
            ]


def output_kernel(where_ref, own_ref, next_ref, w_own, w_near, w_far, mine_ref, other_ref, x_ref):
    level, place, core = where_ref[0], where_ref[1], where_ref[2]
    depth = own_ref.shape[1]
    width = w_own.shape[2]
    tok = mine_ref.shape[1]
    x_ref[:, pl.ds(pl.multiple_of(lax.rem(level, 2) * depth, depth), depth)] = own_ref[...]
    x_ref[:, pl.ds(pl.multiple_of(lax.rem(level + 1, 2) * depth, depth), depth)] = next_ref[...]
    swap = jnp.where(core == level // 2, 0, 1)
    for s, out_ref in enumerate((mine_ref, other_ref)):
        i = jnp.bitwise_xor(swap, s)
        for j in range(PLANE):
            weights = (w_own.at[i], w_near.at[i], w_far.at[i], w_far.at[2 + i])[j]
            part = jnp.dot(x_ref[...], weights[...], preferred_element_type=jnp.float32)
            to = pl.multiple_of(place_of(j, place, core) * width, width)
            for t in range(LEVELS):
                out_ref[lax.rem(t + LEVELS - level, LEVELS), :, pl.ds(to, width)] = part[
                    t * tok : (t + 1) * tok
                ].astype(out_ref.dtype)


SMEM = pl.BlockSpec(memory_space=pltpu.SMEM)
VMEM = pl.BlockSpec(memory_space=pltpu.VMEM)
HBM = pl.BlockSpec(memory_space=pltpu.MemorySpace.HBM)
PARAMS = pltpu.CompilerParams(vmem_limit_bytes=48 * 1024 * 1024)


def shaped(shape, dtype=jnp.bfloat16):
    return jax.ShapeDtypeStruct(shape, dtype)


def by_levels(
    text_rows,
    picture_rows,
    picture_slots,
    norm_gain,
    w_query,
    w_key,
    w_value,
    w_out,
    cache_keys,
    cache_values,
    recompute_rows,
    recompute_slots,
):
    seq_index = lax.axis_index("seq")
    core = lax.axis_index("head")
    level, place = seq_index // PLANE, seq_index % PLANE
    half_at = level // 2
    own_first = core == half_at
    tok, width = text_rows.shape
    block_rows = tok + REC_PAD

    stream_len = tok * LEVELS * PLANE
    tile_owners = TILE_RUN // tok
    first = stream_len // 2 // tok
    last = (stream_len - TILE_RUN) // tok
    owners = [first + i for i in range(tile_owners)] + [last + i for i in range(tile_owners)]
    assert [owner % PLANE for owner in owners] == list(range(LEVELS))
    owner_level = jnp.where(place < tile_owners, first // PLANE, last // PLANE)

    first_block = jnp.where(own_first, 0, 2)
    shown_block = (first_block + (level ^ owner_level)) % LEVELS
    where = jnp.stack([level, place, core, first_block, shown_block]).astype(jnp.int32)

    slots = (recompute_slots - seq_index * CACHED).astype(jnp.bfloat16)
    slot_rows = jnp.broadcast_to(jnp.pad(slots, (0, REC_PAD - REC))[:, None], (REC_PAD, 4 * HD))
    depth = w_query.shape[0]
    key_shape = shaped((depth + CACHED + REC_PAD, 4 * HD))
    query_shape = shaped((1, depth, 8 * HD))
    key_own, query_own, key_give, query_give = pl.pallas_call(
        pack_kernel,
        out_shape=(key_shape, query_shape) * 2,
        in_specs=[SMEM] + [HBM] * 6,
        out_specs=(HBM,) * 4,
        scratch_shapes=[pltpu.SemaphoreType.DMA((PACK_COPIES,))],
        compiler_params=PARAMS,
        name="pack",
    )(where, w_query, w_key, w_value, cache_keys, cache_values, slot_rows)
    query_near = to_near(query_own)

    rows = jnp.concatenate(
        [text_rows, recompute_rows, jnp.zeros((REC_PAD - REC, width), text_rows.dtype)], axis=0
    )
    gain = lax.dynamic_slice_in_dim(norm_gain, core * width, width, 0)
    wide, pictures = rows.astype(jnp.float32), picture_rows.astype(jnp.float32)
    squares, picture_squares = lax.psum(
        (jnp.sum(wide * wide, axis=1), jnp.sum(pictures * pictures, axis=1)), "head"
    )
    normed = scaled(wide, squares, gain)
    pictures = scaled(pictures, picture_squares, gain)

    out_rows = w_out.shape[0] // 2
    out_own, out_give = (
        lax.dynamic_slice_in_dim(w_out, at * out_rows, out_rows, 0) for at in (half_at, 1 - half_at)
    )
    out_half = out_rows // 2

    crossed = permuted(normed, lambda z, p, c: (z ^ 2, p, 1 - c) if c == 1 - z // 2 else None)
    shown = permuted(pictures, lambda z, p, c: (2 * c + p // 2, z, p % 2))
    key_next = across(key_give, 1)
    query_far = to_far(jnp.concatenate([query_own, query_near], axis=0))
    query_near, query_give = lax.optimization_barrier((query_near, query_give))
    query_next = across(query_give, 1)
    shown, key_next = lax.optimization_barrier((shown, key_next))
    keys = jnp.stack([key_own[:depth], key_next[:depth]])
    old_own, old_next = key_own[depth:], key_next[depth:]
    keys_near = to_near(keys)
    crossed, keys_near = lax.optimization_barrier((crossed, keys_near))
    held = jnp.concatenate([jnp.where(own_first, normed, crossed), shown], axis=0)
    next_rows = across(held, 1)
    held_other, out_give = lax.optimization_barrier((other_core(held), out_give))
    out_got0 = across(out_give[:out_half], 2)
    keys_far = to_far(jnp.concatenate([keys, keys_near], axis=0))
    next_near = to_near(query_next)
    next_rows, held_other, keys_far, query_far, next_near, out_got0, out_give = (
        lax.optimization_barrier(
            (next_rows, held_other, keys_far, query_far, next_near, out_got0, out_give)
        )
    )
    out_got1 = across(out_give[out_half:], 2)
    next_other = other_core(next_rows)
    parts = (held, next_rows, held_other, next_other)

    half = HD // 2
    freqs = ROPE_BASE ** (-jnp.arange(half, dtype=jnp.float32) / half)
    blocks = (jnp.arange(LEVELS, dtype=jnp.int32) * PLANE + place)[:, None]
    stream_pos = (
        CACHED * LEVELS * PLANE + blocks * tok + jnp.arange(tok, dtype=jnp.int32)[None]
    ).astype(jnp.float32)
    cache_pos = (blocks * CACHED + jnp.arange(CACHED, dtype=jnp.int32)[None]).astype(jnp.float32)
    angles = jnp.concatenate([stream_pos, cache_pos], axis=1)[..., None] * freqs
    cosine, sine = jnp.cos(angles), jnp.sin(angles)
    cosine = jnp.concatenate([cosine, cosine], axis=-1)
    sine = jnp.concatenate([-sine, sine], axis=-1)

    all_rows = LEVELS * block_rows
    keep, send = pl.pallas_call(
        keys_part_kernel,
        out_shape=(
            shaped((all_rows, 2 * HD), jnp.float32),
            shaped((all_rows + 2 * (CACHED + REC_PAD), 2 * HD)),
        ),
        in_specs=[SMEM] + [VMEM] * 9,
        out_specs=(VMEM, VMEM),
        scratch_shapes=[pltpu.VMEM((all_rows, width), jnp.bfloat16)],
        compiler_params=PARAMS,
        name="keys_part",
    )(where, *parts, keys, keys_near, keys_far, old_own, old_next)
    send, next_near, *parts = lax.optimization_barrier((send, next_near, *parts))
    next_far = to_far(jnp.concatenate([query_next, next_near], axis=0))
    q_keep, q_send = pl.pallas_call(
        queries_part_kernel,
        out_shape=(
            shaped((LEVELS, tok, 4 * HD), jnp.float32),
            shaped((LEVELS, tok, 4 * HD)),
        ),
        in_specs=[SMEM] + [VMEM] * 10,
        out_specs=(VMEM, VMEM),
        scratch_shapes=[pltpu.VMEM((all_rows, width), jnp.bfloat16)],
        compiler_params=PARAMS,
        name="queries_part",
    )(where, *parts, query_own, query_near, query_far, query_next, next_near, next_far)
    got_keys, q_send, out_got1 = lax.optimization_barrier((across(send, 2), q_send, out_got1))
    kv = pl.pallas_call(
        keys_join_kernel,
        out_shape=shaped((LEVELS // 2 + LEVELS, tok, 2 * HD)),
        in_specs=[SMEM] + [VMEM] * 6,
        out_specs=VMEM,
        scratch_shapes=[pltpu.VMEM((all_rows, 2 * HD), jnp.float32)],
        compiler_params=PARAMS,
        name="keys_join",
    )(where, keep, got_keys, old_own, old_next, cosine, sine)
    kv_near, kv_far = to_near(kv), to_far(kv)
    kv_both = permuted(kv, lambda z, p, c: (z, p ^ 3, c))

    out_pair = jnp.stack([out_own, jnp.concatenate([out_got0, out_got1], axis=0)])
    out_pair, kv_near, kv_far = lax.optimization_barrier((out_pair, kv_near, kv_far))
    out_near = to_near(out_pair)
    kv_far, kv_both, out_near, got_queries = lax.optimization_barrier(
        (kv_far, kv_both, out_near, across(q_send, 2))
    )
    out_far = to_far(jnp.concatenate([out_pair, out_near], axis=0))

    attended = pl.pallas_call(
        attend_kernel,
        out_shape=shaped((LEVELS * tok, 4 * HD)),
        in_specs=[SMEM] + [VMEM] * 8,
        out_specs=VMEM,
        scratch_shapes=[pltpu.VMEM((LEVELS, 4, tok, HD), jnp.bfloat16)],
        compiler_params=PARAMS,
        name="attend",
    )(where, q_keep, got_queries, cosine, sine, kv, kv_near, kv_far, kv_both)

    wide_cols = PLANE * w_out.shape[1]
    mine, other = pl.pallas_call(
        output_kernel,
        out_shape=(
            shaped((LEVELS, tok, wide_cols), jnp.float32),
            shaped((LEVELS, tok, wide_cols)),
        ),
        in_specs=[SMEM] + [VMEM] * 5,
        out_specs=(VMEM, VMEM),
        scratch_shapes=[pltpu.VMEM((LEVELS * tok, out_rows), jnp.bfloat16)],
        compiler_params=PARAMS,
        name="output",
    )(where, attended, across(attended, 1), out_pair, out_near, out_far)
    got = other_core(other)

    def block_for(steps):
        return mine[steps] + got[steps].astype(jnp.float32)

    second, first, third = (up(block_for(d).astype(jnp.bfloat16), d) for d in (2, 1, 3))
    same = (block_for(0) + second.astype(jnp.float32)).astype(jnp.bfloat16)
    cross = (first.astype(jnp.float32) + third.astype(jnp.float32)).astype(jnp.bfloat16)
    even = level % 2 == 0
    return jnp.concatenate([jnp.where(even, same, cross), jnp.where(even, cross, same)], axis=1)


def solution(mesh):
    def run(*args):
        kv_local = args[5].shape[1] // HD // mesh.shape["head"]
        levels_fit = (
            mesh.shape["seq"] == LEVELS * PLANE
            and mesh.shape["head"] == 2
            and kv_local == LEVELS
            and args[1].shape[0] == 2 * TILE_RUN
            and args[0].shape[0] == 2048
            and args[8].shape[0] == LEVELS * PLANE * CACHED
            and args[10].shape[0] == LEVELS * PLANE * REC
        )
        return jax.shard_map(
            by_levels if levels_fit else on_device,
            mesh=mesh,
            in_specs=(
                P("seq", "head"),
                P("seq", "head"),
                P("seq"),
                P(),
                P("seq", "head"),
                P("seq", "head"),
                P("seq", "head"),
                P("head", "seq"),
                P("seq", "head"),
                P("seq", "head"),
                P("seq", "head"),
                P("seq"),
            ),
            out_specs=P("seq", "head"),
            check_vma=False,
        )(*args)

    return run
```

```python
import jax
import jax.numpy as jnp
from jax import lax
from jax.experimental import pallas as pl
from jax.experimental.pallas import tpu as pltpu
from jax.sharding import PartitionSpec as P

D = 4096
HD = 128


EPSILON = 1e-05
ROPE_BASE = 1000000.0
NEG_FILL = -1e30


def rotate(values, positions):
    half = values.shape[-1] // 2
    freqs = ROPE_BASE ** (-jnp.arange(half, dtype=jnp.float32) / half)
    angles = positions[:, None] * freqs[None, :]
    cosine = jnp.cos(angles)[:, None, :]
    sine = jnp.sin(angles)[:, None, :]
    first = values[..., :half]
    second = values[..., half:]
    return jnp.concatenate(
        [first * cosine - second * sine, second * cosine + first * sine], axis=-1
    )


def scaled(rows_wide, squares, gain):
    return (rows_wide * lax.rsqrt(squares / D + EPSILON)[:, None] * gain[None, :]).astype(
        jnp.bfloat16
    )


def attend(carry, key_piece, value_piece, queries, allowed):
    best, total, accum = carry
    count = key_piece.shape[0]
    kv_local = queries.shape[0]
    keys_split = key_piece.reshape(count, kv_local, HD)
    values_split = value_piece.reshape(count, kv_local, HD)
    scores = jnp.einsum(
        "kgtd,nkd->kgtn", queries, keys_split, preferred_element_type=jnp.float32
    ) * HD ** (-0.5)
    scores = jnp.where(allowed, scores, NEG_FILL)
    fresh = jnp.maximum(best, jnp.max(scores, axis=-1))
    factor = jnp.exp(best - fresh)
    weights = jnp.where(allowed, jnp.exp(scores - fresh[..., None]), 0.0)
    total = total * factor + jnp.sum(weights, axis=-1)
    accum = accum * factor[..., None] + jnp.einsum(
        "kgtn,nkd->kgtd",
        weights.astype(jnp.bfloat16),
        values_split,
        preferred_element_type=jnp.float32,
    )
    return (fresh, total, accum)


def on_device(
    text_rows,
    picture_rows,
    picture_slots,
    norm_gain,
    w_query,
    w_key,
    w_value,
    w_out,
    cache_keys,
    cache_values,
    recompute_rows,
    recompute_slots,
):
    tok_rows = text_rows.shape[0]
    rec_count = recompute_rows.shape[0]
    cache_rows = cache_keys.shape[0]
    seq_index = lax.axis_index("seq")
    local_pos = seq_index * tok_rows + jnp.arange(tok_rows, dtype=jnp.int32)
    rows_piece = lax.all_gather(picture_rows, "seq", axis=0, tiled=True)
    slots_piece = lax.all_gather(picture_slots, "seq", axis=0, tiled=True)
    select = (slots_piece[None, :] == local_pos[:, None]).astype(jnp.bfloat16)
    placed = jnp.dot(select, rows_piece, preferred_element_type=jnp.float32)
    hits = jnp.sum(select.astype(jnp.float32), axis=1)
    added, hits = (placed, hits)
    stream = jnp.where(hits[:, None] > 0.5, added, text_rows.astype(jnp.float32)).astype(
        jnp.bfloat16
    )
    slice_width = stream.shape[1]
    gain_slice = lax.dynamic_slice_in_dim(
        norm_gain, lax.axis_index("head") * slice_width, slice_width, 0
    )
    stream_wide = stream.astype(jnp.float32)
    rec_wide = recompute_rows.astype(jnp.float32)
    stream_sq, rec_sq = lax.psum(
        (jnp.sum(stream_wide * stream_wide, axis=1), jnp.sum(rec_wide * rec_wide, axis=1)), "head"
    )
    normed, rec_normed = (
        lax.all_gather(scaled(stream_wide, stream_sq, gain_slice), "head", axis=1, tiled=True),
        lax.all_gather(scaled(rec_wide, rec_sq, gain_slice), "head", axis=1, tiled=True),
    )
    stacked = jnp.concatenate([normed, rec_normed], axis=0)
    query_cols = w_query.shape[1]
    key_cols = w_key.shape[1]
    pieces = (
        lax.all_gather(w_query, "seq", axis=0, tiled=True),
        lax.all_gather(w_key, "seq", axis=0, tiled=True),
        lax.all_gather(w_value, "seq", axis=0, tiled=True),
    )
    query_all = jnp.dot(stacked, pieces[0], preferred_element_type=jnp.float32)
    key_all = jnp.dot(stacked, pieces[1], preferred_element_type=jnp.float32)
    value_all = jnp.dot(stacked, pieces[2], preferred_element_type=jnp.float32)
    cache_total = cache_rows * lax.axis_size("seq")
    stream_pos = (cache_total + local_pos).astype(jnp.float32)
    rec_pos = recompute_slots.astype(jnp.float32)
    heads_local = query_cols // HD
    kv_local = key_cols // HD
    group = heads_local // kv_local
    rot_query = rotate(query_all[:tok_rows].reshape(tok_rows, heads_local, HD), stream_pos).astype(
        jnp.bfloat16
    )
    rot_key = (
        rotate(key_all[:tok_rows].reshape(tok_rows, kv_local, HD), stream_pos)
        .astype(jnp.bfloat16)
        .reshape(tok_rows, key_cols)
    )
    values_new = value_all[:tok_rows].astype(jnp.bfloat16)
    rot_rec_key = (
        rotate(key_all[tok_rows:].reshape(rec_count, kv_local, HD), rec_pos)
        .astype(jnp.bfloat16)
        .reshape(rec_count, key_cols)
    )
    rec_values = value_all[tok_rows:].astype(jnp.bfloat16)
    local_slots = recompute_slots - seq_index * cache_rows
    select = local_slots[:, None] == jnp.arange(cache_rows, dtype=jnp.int32)[None, :]
    replaced = jnp.any(select, axis=0)[:, None]
    select_cols = select.astype(jnp.bfloat16).T
    new_keys = jnp.dot(select_cols, rot_rec_key, preferred_element_type=jnp.float32).astype(
        jnp.bfloat16
    )
    new_values = jnp.dot(select_cols, rec_values, preferred_element_type=jnp.float32).astype(
        jnp.bfloat16
    )
    cache_k = jnp.where(replaced, new_keys, cache_keys)
    cache_v = jnp.where(replaced, new_values, cache_values)
    queries = jnp.transpose(rot_query.reshape(tok_rows, kv_local, group, HD), (1, 2, 0, 3))
    carry_start = (
        jnp.full((kv_local, group, tok_rows), NEG_FILL, jnp.float32),
        jnp.zeros((kv_local, group, tok_rows), jnp.float32),
        jnp.zeros((kv_local, group, tok_rows, HD), jnp.float32),
    )
    pieces = (
        lax.all_gather(cache_k, "seq", axis=0, tiled=True),
        lax.all_gather(cache_v, "seq", axis=0, tiled=True),
    )
    allowed = jnp.ones((tok_rows, pieces[0].shape[0]), jnp.bool_)
    carry_mid = attend(carry_start, pieces[0], pieces[1], queries, allowed)
    pieces = (
        lax.all_gather(rot_key, "seq", axis=0, tiled=True),
        lax.all_gather(values_new, "seq", axis=0, tiled=True),
    )
    key_pos = jnp.arange(pieces[0].shape[0], dtype=jnp.int32)
    allowed = key_pos[None, :] <= local_pos[:, None]
    best, total, accum = attend(carry_mid, pieces[0], pieces[1], queries, allowed)
    attended = (
        jnp.transpose(accum / total[..., None], (2, 0, 1, 3))
        .reshape(tok_rows, query_cols)
        .astype(jnp.bfloat16)
    )
    partial_out = jnp.dot(
        attended,
        lax.all_gather(w_out, "seq", axis=1, tiled=True),
        preferred_element_type=jnp.float32,
    )
    return lax.psum_scatter(
        partial_out.astype(jnp.bfloat16), "head", scatter_dimension=1, tiled=True
    )


LEVELS = 4
PLANE = 4
TILE_RUN = 256
CACHED = 64
REC = 8
REC_PAD = 16


def permuted(value, move):
    perm = []
    for level in range(LEVELS):
        for place in range(PLANE):
            for core in range(2):
                target = move(level, place, core)
                if target is not None:
                    to_level, to_place, to_core = target
                    perm.append(
                        (
                            (level * PLANE + place) * 2 + core,
                            (to_level * PLANE + to_place) * 2 + to_core,
                        )
                    )
    return lax.ppermute(value, ("seq", "head"), perm)


def across(value, bit):
    return permuted(value, lambda z, p, c: (z ^ bit, p, c))


def up(value, steps):
    return permuted(value, lambda z, p, c: ((z + steps) % LEVELS, p, c))


def other_core(value):
    return permuted(value, lambda z, p, c: (z, p, 1 - c))


def to_near(value):
    return permuted(value, lambda z, p, c: (z, p ^ (1 + c), c))


def to_far(value):
    return permuted(value, lambda z, p, c: (z, p ^ (2 - c), c))


def place_of(which, place, core):
    if which == 0:
        return place
    if which == 3:
        return place ^ 3
    return place ^ (1 + core) if which == 1 else place ^ (2 - core)


def turned(values, cosine, sine):
    return values * cosine + pltpu.roll(values, HD // 2, 1) * sine


def pack_kernel(where_ref, *refs):
    w_query, w_key, w_value, cache_keys, cache_values, slots = refs[:6]
    outs, sems = refs[6:10], refs[10]
    level = where_ref[0]
    depth = w_query.shape[0]
    copies = []

    def copy(source, target):
        copies.append(pltpu.make_async_copy(source, target, sems.at[len(copies)]))
        copies[-1].start()

    for n in range(2):
        keys, queries = outs[2 * n : 2 * n + 2]
        for m in range(2):
            at = jnp.bitwise_xor(level, n + 2 * m)
            small = pl.ds(pl.multiple_of(at * HD, HD), HD)
            large = pl.ds(pl.multiple_of(at * 4 * HD, 4 * HD), 4 * HD)
            for k, (new, old) in enumerate(((w_key, cache_keys), (w_value, cache_values))):
                to = pl.ds((2 * m + k) * HD, HD)
                copy(new.at[:, small], keys.at[0:depth, to])
                copy(old.at[:, small], keys.at[depth : depth + CACHED, to])
            copy(w_query.at[:, large], queries.at[0, :, pl.ds(m * 4 * HD, 4 * HD)])
        copy(slots, keys.at[depth + CACHED : depth + CACHED + REC_PAD])
    for each in copies:
        each.wait()


PACK_COPIES = 22


def assemble(where_ref, parts, x_ref):
    level, core = where_ref[0], where_ref[2]
    shown = TILE_RUN // 2 // PLANE
    rows = parts[0].shape[0] - shown
    for n, part in enumerate(parts):
        x_ref[n * rows : (n + 1) * rows] = part[0:rows]
    start = where_ref[4] * rows
    for n, part in enumerate(parts):
        which = 2 * lax.rem(level + n % 2, 2) + (core if n < 2 else 1 - core)
        to = pl.multiple_of(start + which * shown, 16)
        x_ref[pl.ds(to, shown)] = part[rows : rows + shown]


def products(where_ref, x_ref, pieces):
    level, place, core = where_ref[0], where_ref[1], where_ref[2]
    total = None
    for i in range(2):
        for j in range(PLANE):
            depth = pieces[i][j].shape[0]
            block = lax.rem(level + i, 2) * PLANE + place_of(j, place, core)
            start = pl.multiple_of(block * depth, depth)
            part = jnp.dot(
                x_ref[:, pl.ds(start, depth)],
                pieces[i][j][...],
                preferred_element_type=jnp.float32,
            )
            total = part if total is None else total + part
    return total


def keys_part_kernel(
    where_ref, x0, x1, x2, x3, own, near, far, old0, old1, keep_ref, send_ref, x_ref
):
    assemble(where_ref, (x0, x1, x2, x3), x_ref)
    pieces = [[own.at[i], near.at[i], far.at[i], far.at[2 + i]] for i in range(2)]
    width = 2 * HD
    total = products(where_ref, x_ref, pieces)
    at = total.shape[0]
    keep_ref[...] = total[:, :width]
    send_ref[0:at] = total[:, width:].astype(jnp.bfloat16)
    for old in (old0, old1):
        send_ref[at : at + CACHED + REC_PAD] = old[:, width:]
        at += CACHED + REC_PAD


def keys_join_kernel(where_ref, keep_ref, got_ref, old0, old1, cos_ref, sin_ref, kv_ref, sum_ref):
    level = where_ref[0]
    rows = sum_ref.shape[0]
    block = rows // LEVELS
    tok = block - REC_PAD
    width = 2 * HD
    sum_ref[...] = keep_ref[...] + got_ref[0:rows].astype(jnp.float32)
    first = where_ref[3]
    span = CACHED + REC_PAD
    for n in range(LEVELS):
        at = jnp.bitwise_xor(level, n)
        start = pl.multiple_of(lax.rem(first + n, LEVELS) * block, 16)
        cosine, sine = cos_ref[at], sin_ref[at]
        fresh = sum_ref[pl.ds(start, tok), :]
        kv_ref[2 + at, :, 0:HD] = turned(fresh[:, :HD], cosine[:tok], sine[:tok]).astype(
            jnp.bfloat16
        )
        kv_ref[2 + at, :, HD:width] = fresh[:, HD:].astype(jnp.bfloat16)
        if n < 2:
            old = (old0, old1)[n][:, 0:width].astype(jnp.float32)
        else:
            old = got_ref[rows + (n - 2) * span : rows + (n - 1) * span].astype(jnp.float32)
        slots = old[CACHED : CACHED + REC].astype(jnp.int32)
        rec = sum_ref[pl.ds(pl.multiple_of(start + tok, 16), REC_PAD), :]
        line = lax.broadcasted_iota(jnp.int32, (CACHED, width), 0)
        found = jnp.zeros((CACHED, width), jnp.float32)
        hit = jnp.zeros((CACHED, width), jnp.int32)
        for r in range(REC):
            same = line == slots[r : r + 1]
            found = jnp.where(same, rec[r : r + 1], found)
            hit = jnp.where(same, 1, hit)
        keys = turned(found[:, :HD], cosine[tok : tok + CACHED], sine[tok : tok + CACHED])
        found = jnp.concatenate([keys, found[:, HD:]], axis=1)
        line_at = pl.multiple_of(lax.rem(at, 2) * CACHED, CACHED)
        kv_ref[at // 2, pl.ds(line_at, CACHED), :] = jnp.where(
            hit == 1, found, old[:CACHED]
        ).astype(jnp.bfloat16)


def queries_part_kernel(where_ref, x0, x1, x2, x3, *refs):
    keep_ref, send_ref, x_ref = refs[6:]
    assemble(where_ref, (x0, x1, x2, x3), x_ref)
    pieces = [
        [own.at[0], near.at[0], far.at[0], far.at[1]] for own, near, far in (refs[0:3], refs[3:6])
    ]
    total = products(where_ref, x_ref, pieces)
    block = total.shape[0] // LEVELS
    tok = block - REC_PAD
    width = 4 * HD
    for k in range(LEVELS):
        fresh = total[k * block : k * block + tok]
        keep_ref[k] = fresh[:, :width]
        send_ref[k] = fresh[:, width:].astype(jnp.bfloat16)


def attend_kernel(
    where_ref, keep_ref, got_ref, cos_ref, sin_ref, kv0, kv1, kv2, kv3, out_ref, query_ref
):
    level, place, core = where_ref[0], where_ref[1], where_ref[2]
    pieces = (kv0, kv1, kv2, kv3)
    tok = keep_ref.shape[1]
    old = LEVELS // 2
    for n in range(LEVELS):
        at = jnp.bitwise_xor(level, n)
        block = lax.rem(where_ref[3] + n, LEVELS)
        total = keep_ref[block] + got_ref[block].astype(jnp.float32)
        cosine, sine = cos_ref[at][:tok], sin_ref[at][:tok]
        for h in range(4):
            head = turned(total[:, h * HD : (h + 1) * HD], cosine, sine)
            query_ref[at, h] = head.astype(jnp.bfloat16)
    row = lax.broadcasted_iota(jnp.int32, (tok, tok), 0)
    col = lax.broadcasted_iota(jnp.int32, (tok, tok), 1)
    scale = HD ** (-0.5) * 1.4426950408889634
    for i in range(LEVELS):
        count = (old + i + 1) * tok
        queries = query_ref[i].reshape(4 * tok, HD)
        scores = []
        best = None
        for j in range(PLANE):
            keys = pieces[j][0 : old + i + 1, :, 0:HD].reshape(count, HD)
            raw = lax.dot_general(
                queries, keys, (((1,), (1,)), ((), ())), preferred_element_type=jnp.float32
            )
            if j == 0:
                allowed = col <= row
            else:
                allowed = jnp.broadcast_to(place_of(j, place, core), (tok, tok)) < place
            allowed = jnp.concatenate([allowed] * 4, axis=0)
            last = jnp.where(allowed, raw[:, count - tok :], NEG_FILL)
            raw = jnp.concatenate([raw[:, : count - tok], last], axis=1)
            top = jnp.max(raw, axis=1, keepdims=True)
            best = top if best is None else jnp.maximum(best, top)
            scores.append(raw)
        total, accum = 0.0, 0.0
        for j in range(PLANE):
            weights = jnp.exp2((scores[j] - best) * scale)
            total = total + jnp.sum(weights, axis=1, keepdims=True)
            values = pieces[j][0 : old + i + 1, :, HD : 2 * HD].reshape(count, HD)
            accum = accum + jnp.dot(
                weights.astype(jnp.bfloat16), values, preferred_element_type=jnp.float32
            )
        result = (accum / total).astype(jnp.bfloat16)
        for h in range(4):
            out_ref[i * tok : (i + 1) * tok, h * HD : (h + 1) * HD] = result[
                h * tok : (h + 1) * tok
            ]


def output_kernel(where_ref, own_ref, next_ref, w_own, w_near, w_far, mine_ref, other_ref, x_ref):
    level, place, core = where_ref[0], where_ref[1], where_ref[2]
    depth = own_ref.shape[1]
    width = w_own.shape[2]
    tok = mine_ref.shape[1]
    x_ref[:, pl.ds(pl.multiple_of(lax.rem(level, 2) * depth, depth), depth)] = own_ref[...]
    x_ref[:, pl.ds(pl.multiple_of(lax.rem(level + 1, 2) * depth, depth), depth)] = next_ref[...]
    swap = jnp.where(core == level // 2, 0, 1)
    for s, out_ref in enumerate((mine_ref, other_ref)):
        i = jnp.bitwise_xor(swap, s)
        for j in range(PLANE):
            weights = (w_own.at[i], w_near.at[i], w_far.at[i], w_far.at[2 + i])[j]
            part = jnp.dot(x_ref[...], weights[...], preferred_element_type=jnp.float32)
            to = pl.multiple_of(place_of(j, place, core) * width, width)
            for t in range(LEVELS):
                out_ref[lax.rem(t + LEVELS - level, LEVELS), :, pl.ds(to, width)] = part[
                    t * tok : (t + 1) * tok
                ].astype(out_ref.dtype)


SMEM = pl.BlockSpec(memory_space=pltpu.SMEM)
VMEM = pl.BlockSpec(memory_space=pltpu.VMEM)
HBM = pl.BlockSpec(memory_space=pltpu.MemorySpace.HBM)
PARAMS = pltpu.CompilerParams(vmem_limit_bytes=48 * 1024 * 1024)


def shaped(shape, dtype=jnp.bfloat16):
    return jax.ShapeDtypeStruct(shape, dtype)


def by_levels(
    text_rows,
    picture_rows,
    picture_slots,
    norm_gain,
    w_query,
    w_key,
    w_value,
    w_out,
    cache_keys,
    cache_values,
    recompute_rows,
    recompute_slots,
):
    seq_index = lax.axis_index("seq")
    core = lax.axis_index("head")
    level, place = seq_index // PLANE, seq_index % PLANE
    half_at = level // 2
    own_first = core == half_at
    tok, width = text_rows.shape
    block_rows = tok + REC_PAD

    stream_len = tok * LEVELS * PLANE
    tile_owners = TILE_RUN // tok
    first = stream_len // 2 // tok
    last = (stream_len - TILE_RUN) // tok
    owners = [first + i for i in range(tile_owners)] + [last + i for i in range(tile_owners)]
    assert [owner % PLANE for owner in owners] == list(range(LEVELS))
    owner_level = jnp.where(place < tile_owners, first // PLANE, last // PLANE)

    first_block = jnp.where(own_first, 0, 2)
    shown_block = (first_block + (level ^ owner_level)) % LEVELS
    where = jnp.stack([level, place, core, first_block, shown_block]).astype(jnp.int32)

    slots = (recompute_slots - seq_index * CACHED).astype(jnp.bfloat16)
    slot_rows = jnp.broadcast_to(jnp.pad(slots, (0, REC_PAD - REC))[:, None], (REC_PAD, 4 * HD))
    depth = w_query.shape[0]
    key_shape = shaped((depth + CACHED + REC_PAD, 4 * HD))
    query_shape = shaped((1, depth, 8 * HD))
    key_own, query_own, key_give, query_give = pl.pallas_call(
        pack_kernel,
        out_shape=(key_shape, query_shape) * 2,
        in_specs=[SMEM] + [HBM] * 6,
        out_specs=(HBM,) * 4,
        scratch_shapes=[pltpu.SemaphoreType.DMA((PACK_COPIES,))],
        compiler_params=PARAMS,
        name="pack",
    )(where, w_query, w_key, w_value, cache_keys, cache_values, slot_rows)
    query_near = to_near(query_own)

    rows = jnp.concatenate(
        [text_rows, recompute_rows, jnp.zeros((REC_PAD - REC, width), text_rows.dtype)], axis=0
    )
    gain = lax.dynamic_slice_in_dim(norm_gain, core * width, width, 0)
    wide, pictures = rows.astype(jnp.float32), picture_rows.astype(jnp.float32)
    squares, picture_squares = lax.psum(
        (jnp.sum(wide * wide, axis=1), jnp.sum(pictures * pictures, axis=1)), "head"
    )
    normed = scaled(wide, squares, gain)
    pictures = scaled(pictures, picture_squares, gain)

    out_rows = w_out.shape[0] // 2
    out_own, out_give = (
        lax.dynamic_slice_in_dim(w_out, at * out_rows, out_rows, 0) for at in (half_at, 1 - half_at)
    )
    out_half = out_rows // 2

    crossed = permuted(normed, lambda z, p, c: (z ^ 2, p, 1 - c) if c == 1 - z // 2 else None)
    shown = permuted(pictures, lambda z, p, c: (2 * c + p // 2, z, p % 2))
    key_next = across(key_give, 1)
    query_far = to_far(jnp.concatenate([query_own, query_near], axis=0))
    query_near, query_give = lax.optimization_barrier((query_near, query_give))
    query_next = across(query_give, 1)
    shown, key_next = lax.optimization_barrier((shown, key_next))
    keys = jnp.stack([key_own[:depth], key_next[:depth]])
    old_own, old_next = key_own[depth:], key_next[depth:]
    keys_near = to_near(keys)
    crossed, shown = lax.optimization_barrier((crossed, shown))
    held = jnp.concatenate([jnp.where(own_first, normed, crossed), shown], axis=0)
    next_rows = across(held, 1)
    held_other, out_give, keys_near = lax.optimization_barrier(
        (other_core(held), out_give, keys_near)
    )
    out_got0 = across(out_give[:out_half], 2)
    keys_far = to_far(jnp.concatenate([keys, keys_near], axis=0))
    next_near = to_near(query_next)
    next_rows, held_other, keys_far, query_far, next_near, out_got0, out_give = (
        lax.optimization_barrier(
            (next_rows, held_other, keys_far, query_far, next_near, out_got0, out_give)
        )
    )
    out_got1 = across(out_give[out_half:], 2)
    next_far = to_far(jnp.concatenate([query_next, next_near], axis=0))
    next_other = other_core(next_rows)
    next_other, out_got1 = lax.optimization_barrier((next_other, out_got1))
    parts = (held, next_rows, held_other, next_other)

    half = HD // 2
    freqs = ROPE_BASE ** (-jnp.arange(half, dtype=jnp.float32) / half)
    blocks = (jnp.arange(LEVELS, dtype=jnp.int32) * PLANE + place)[:, None]
    stream_pos = (
        CACHED * LEVELS * PLANE + blocks * tok + jnp.arange(tok, dtype=jnp.int32)[None]
    ).astype(jnp.float32)
    cache_pos = (blocks * CACHED + jnp.arange(CACHED, dtype=jnp.int32)[None]).astype(jnp.float32)
    angles = jnp.concatenate([stream_pos, cache_pos], axis=1)[..., None] * freqs
    cosine, sine = jnp.cos(angles), jnp.sin(angles)
    cosine = jnp.concatenate([cosine, cosine], axis=-1)
    sine = jnp.concatenate([-sine, sine], axis=-1)

    all_rows = LEVELS * block_rows
    keep, send = pl.pallas_call(
        keys_part_kernel,
        out_shape=(
            shaped((all_rows, 2 * HD), jnp.float32),
            shaped((all_rows + 2 * (CACHED + REC_PAD), 2 * HD)),
        ),
        in_specs=[SMEM] + [VMEM] * 9,
        out_specs=(VMEM, VMEM),
        scratch_shapes=[pltpu.VMEM((all_rows, width), jnp.bfloat16)],
        compiler_params=PARAMS,
        name="keys_part",
    )(where, *parts, keys, keys_near, keys_far, old_own, old_next)
    send, *parts = lax.optimization_barrier((send, *parts))
    out_pair = jnp.stack([out_own, jnp.concatenate([out_got0, out_got1], axis=0)])
    out_pair, next_far = lax.optimization_barrier((out_pair, next_far))
    out_near = to_near(out_pair)
    q_keep, q_send = pl.pallas_call(
        queries_part_kernel,
        out_shape=(
            shaped((LEVELS, tok, 4 * HD), jnp.float32),
            shaped((LEVELS, tok, 4 * HD)),
        ),
        in_specs=[SMEM] + [VMEM] * 10,
        out_specs=(VMEM, VMEM),
        scratch_shapes=[pltpu.VMEM((all_rows, width), jnp.bfloat16)],
        compiler_params=PARAMS,
        name="queries_part",
    )(where, *parts, query_own, query_near, query_far, query_next, next_near, next_far)
    got_keys, q_send = lax.optimization_barrier((across(send, 2), q_send))
    kv = pl.pallas_call(
        keys_join_kernel,
        out_shape=shaped((LEVELS // 2 + LEVELS, tok, 2 * HD)),
        in_specs=[SMEM] + [VMEM] * 6,
        out_specs=VMEM,
        scratch_shapes=[pltpu.VMEM((all_rows, 2 * HD), jnp.float32)],
        compiler_params=PARAMS,
        name="keys_join",
    )(where, keep, got_keys, old_own, old_next, cosine, sine)
    kv_near, kv_far = to_near(kv), to_far(kv)
    kv_both = permuted(kv, lambda z, p, c: (z, p ^ 3, c))

    kv_near, kv_far, kv_both, out_near, got_queries = lax.optimization_barrier(
        (kv_near, kv_far, kv_both, out_near, across(q_send, 2))
    )
    out_far = to_far(jnp.concatenate([out_pair, out_near], axis=0))

    attended = pl.pallas_call(
        attend_kernel,
        out_shape=shaped((LEVELS * tok, 4 * HD)),
        in_specs=[SMEM] + [VMEM] * 8,
        out_specs=VMEM,
        scratch_shapes=[pltpu.VMEM((LEVELS, 4, tok, HD), jnp.bfloat16)],
        compiler_params=PARAMS,
        name="attend",
    )(where, q_keep, got_queries, cosine, sine, kv, kv_near, kv_far, kv_both)

    wide_cols = PLANE * w_out.shape[1]
    mine, other = pl.pallas_call(
        output_kernel,
        out_shape=(
            shaped((LEVELS, tok, wide_cols), jnp.float32),
            shaped((LEVELS, tok, wide_cols)),
        ),
        in_specs=[SMEM] + [VMEM] * 5,
        out_specs=(VMEM, VMEM),
        scratch_shapes=[pltpu.VMEM((LEVELS * tok, out_rows), jnp.bfloat16)],
        compiler_params=PARAMS,
        name="output",
    )(where, attended, across(attended, 1), out_pair, out_near, out_far)
    got = other_core(other)

    def block_for(steps):
        return mine[steps] + got[steps].astype(jnp.float32)

    second, first, third = (up(block_for(d).astype(jnp.bfloat16), d) for d in (2, 1, 3))
    same = (block_for(0) + second.astype(jnp.float32)).astype(jnp.bfloat16)
    cross = (first.astype(jnp.float32) + third.astype(jnp.float32)).astype(jnp.bfloat16)
    even = level % 2 == 0
    return jnp.concatenate([jnp.where(even, same, cross), jnp.where(even, cross, same)], axis=1)


def solution(mesh):
    def run(*args):
        kv_local = args[5].shape[1] // HD // mesh.shape["head"]
        levels_fit = (
            mesh.shape["seq"] == LEVELS * PLANE
            and mesh.shape["head"] == 2
            and kv_local == LEVELS
            and args[1].shape[0] == 2 * TILE_RUN
            and args[0].shape[0] == 2048
            and args[8].shape[0] == LEVELS * PLANE * CACHED
            and args[10].shape[0] == LEVELS * PLANE * REC
        )
        return jax.shard_map(
            by_levels if levels_fit else on_device,
            mesh=mesh,
            in_specs=(
                P("seq", "head"),
                P("seq", "head"),
                P("seq"),
                P(),
                P("seq", "head"),
                P("seq", "head"),
                P("seq", "head"),
                P("head", "seq"),
                P("seq", "head"),
                P("seq", "head"),
                P("seq", "head"),
                P("seq"),
            ),
            out_specs=P("seq", "head"),
            check_vma=False,
        )(*args)

    return run
```

```python
import functools

import jax
import jax.numpy as jnp
from jax import lax
from jax.experimental import pallas as pl
from jax.experimental.pallas import tpu as pltpu
from jax.sharding import PartitionSpec as P

D = 4096
HD = 128


EPSILON = 1e-05
ROPE_BASE = 1000000.0
NEG_FILL = -1e30


def rotate(values, positions):
    half = values.shape[-1] // 2
    freqs = ROPE_BASE ** (-jnp.arange(half, dtype=jnp.float32) / half)
    angles = positions[:, None] * freqs[None, :]
    cosine = jnp.cos(angles)[:, None, :]
    sine = jnp.sin(angles)[:, None, :]
    first = values[..., :half]
    second = values[..., half:]
    return jnp.concatenate(
        [first * cosine - second * sine, second * cosine + first * sine], axis=-1
    )


def scaled(rows_wide, squares, gain):
    return (rows_wide * lax.rsqrt(squares / D + EPSILON)[:, None] * gain[None, :]).astype(
        jnp.bfloat16
    )


def attend(carry, key_piece, value_piece, queries, allowed):
    best, total, accum = carry
    count = key_piece.shape[0]
    kv_local = queries.shape[0]
    keys_split = key_piece.reshape(count, kv_local, HD)
    values_split = value_piece.reshape(count, kv_local, HD)
    scores = jnp.einsum(
        "kgtd,nkd->kgtn", queries, keys_split, preferred_element_type=jnp.float32
    ) * HD ** (-0.5)
    scores = jnp.where(allowed, scores, NEG_FILL)
    fresh = jnp.maximum(best, jnp.max(scores, axis=-1))
    factor = jnp.exp(best - fresh)
    weights = jnp.where(allowed, jnp.exp(scores - fresh[..., None]), 0.0)
    total = total * factor + jnp.sum(weights, axis=-1)
    accum = accum * factor[..., None] + jnp.einsum(
        "kgtn,nkd->kgtd",
        weights.astype(jnp.bfloat16),
        values_split,
        preferred_element_type=jnp.float32,
    )
    return (fresh, total, accum)


def on_device(
    text_rows,
    picture_rows,
    picture_slots,
    norm_gain,
    w_query,
    w_key,
    w_value,
    w_out,
    cache_keys,
    cache_values,
    recompute_rows,
    recompute_slots,
):
    tok_rows = text_rows.shape[0]
    rec_count = recompute_rows.shape[0]
    cache_rows = cache_keys.shape[0]
    seq_index = lax.axis_index("seq")
    local_pos = seq_index * tok_rows + jnp.arange(tok_rows, dtype=jnp.int32)
    rows_piece = lax.all_gather(picture_rows, "seq", axis=0, tiled=True)
    slots_piece = lax.all_gather(picture_slots, "seq", axis=0, tiled=True)
    select = (slots_piece[None, :] == local_pos[:, None]).astype(jnp.bfloat16)
    placed = jnp.dot(select, rows_piece, preferred_element_type=jnp.float32)
    hits = jnp.sum(select.astype(jnp.float32), axis=1)
    added, hits = (placed, hits)
    stream = jnp.where(hits[:, None] > 0.5, added, text_rows.astype(jnp.float32)).astype(
        jnp.bfloat16
    )
    slice_width = stream.shape[1]
    gain_slice = lax.dynamic_slice_in_dim(
        norm_gain, lax.axis_index("head") * slice_width, slice_width, 0
    )
    stream_wide = stream.astype(jnp.float32)
    rec_wide = recompute_rows.astype(jnp.float32)
    stream_sq, rec_sq = lax.psum(
        (jnp.sum(stream_wide * stream_wide, axis=1), jnp.sum(rec_wide * rec_wide, axis=1)), "head"
    )
    normed, rec_normed = (
        lax.all_gather(scaled(stream_wide, stream_sq, gain_slice), "head", axis=1, tiled=True),
        lax.all_gather(scaled(rec_wide, rec_sq, gain_slice), "head", axis=1, tiled=True),
    )
    stacked = jnp.concatenate([normed, rec_normed], axis=0)
    query_cols = w_query.shape[1]
    key_cols = w_key.shape[1]
    pieces = (
        lax.all_gather(w_query, "seq", axis=0, tiled=True),
        lax.all_gather(w_key, "seq", axis=0, tiled=True),
        lax.all_gather(w_value, "seq", axis=0, tiled=True),
    )
    query_all = jnp.dot(stacked, pieces[0], preferred_element_type=jnp.float32)
    key_all = jnp.dot(stacked, pieces[1], preferred_element_type=jnp.float32)
    value_all = jnp.dot(stacked, pieces[2], preferred_element_type=jnp.float32)
    cache_total = cache_rows * lax.axis_size("seq")
    stream_pos = (cache_total + local_pos).astype(jnp.float32)
    rec_pos = recompute_slots.astype(jnp.float32)
    heads_local = query_cols // HD
    kv_local = key_cols // HD
    group = heads_local // kv_local
    rot_query = rotate(query_all[:tok_rows].reshape(tok_rows, heads_local, HD), stream_pos).astype(
        jnp.bfloat16
    )
    rot_key = (
        rotate(key_all[:tok_rows].reshape(tok_rows, kv_local, HD), stream_pos)
        .astype(jnp.bfloat16)
        .reshape(tok_rows, key_cols)
    )
    values_new = value_all[:tok_rows].astype(jnp.bfloat16)
    rot_rec_key = (
        rotate(key_all[tok_rows:].reshape(rec_count, kv_local, HD), rec_pos)
        .astype(jnp.bfloat16)
        .reshape(rec_count, key_cols)
    )
    rec_values = value_all[tok_rows:].astype(jnp.bfloat16)
    local_slots = recompute_slots - seq_index * cache_rows
    select = local_slots[:, None] == jnp.arange(cache_rows, dtype=jnp.int32)[None, :]
    replaced = jnp.any(select, axis=0)[:, None]
    select_cols = select.astype(jnp.bfloat16).T
    new_keys = jnp.dot(select_cols, rot_rec_key, preferred_element_type=jnp.float32).astype(
        jnp.bfloat16
    )
    new_values = jnp.dot(select_cols, rec_values, preferred_element_type=jnp.float32).astype(
        jnp.bfloat16
    )
    cache_k = jnp.where(replaced, new_keys, cache_keys)
    cache_v = jnp.where(replaced, new_values, cache_values)
    queries = jnp.transpose(rot_query.reshape(tok_rows, kv_local, group, HD), (1, 2, 0, 3))
    carry_start = (
        jnp.full((kv_local, group, tok_rows), NEG_FILL, jnp.float32),
        jnp.zeros((kv_local, group, tok_rows), jnp.float32),
        jnp.zeros((kv_local, group, tok_rows, HD), jnp.float32),
    )
    pieces = (
        lax.all_gather(cache_k, "seq", axis=0, tiled=True),
        lax.all_gather(cache_v, "seq", axis=0, tiled=True),
    )
    allowed = jnp.ones((tok_rows, pieces[0].shape[0]), jnp.bool_)
    carry_mid = attend(carry_start, pieces[0], pieces[1], queries, allowed)
    pieces = (
        lax.all_gather(rot_key, "seq", axis=0, tiled=True),
        lax.all_gather(values_new, "seq", axis=0, tiled=True),
    )
    key_pos = jnp.arange(pieces[0].shape[0], dtype=jnp.int32)
    allowed = key_pos[None, :] <= local_pos[:, None]
    best, total, accum = attend(carry_mid, pieces[0], pieces[1], queries, allowed)
    attended = (
        jnp.transpose(accum / total[..., None], (2, 0, 1, 3))
        .reshape(tok_rows, query_cols)
        .astype(jnp.bfloat16)
    )
    partial_out = jnp.dot(
        attended,
        lax.all_gather(w_out, "seq", axis=1, tiled=True),
        preferred_element_type=jnp.float32,
    )
    return lax.psum_scatter(
        partial_out.astype(jnp.bfloat16), "head", scatter_dimension=1, tiled=True
    )


LEVELS = 4
PLANE = 4
TILE_RUN = 256
CACHED = 64
REC = 8
REC_PAD = 16


def permuted(value, move):
    perm = []
    for level in range(LEVELS):
        for place in range(PLANE):
            for core in range(2):
                target = move(level, place, core)
                if target is not None:
                    to_level, to_place, to_core = target
                    perm.append(
                        (
                            (level * PLANE + place) * 2 + core,
                            (to_level * PLANE + to_place) * 2 + to_core,
                        )
                    )
    return lax.ppermute(value, ("seq", "head"), perm)


def across(value, bit):
    return permuted(value, lambda z, p, c: (z ^ bit, p, c))


def up(value, steps):
    return permuted(value, lambda z, p, c: ((z + steps) % LEVELS, p, c))


def other_core(value):
    return permuted(value, lambda z, p, c: (z, p, 1 - c))


def to_near(value):
    return permuted(value, lambda z, p, c: (z, p ^ (1 + c), c))


def to_far(value):
    return permuted(value, lambda z, p, c: (z, p ^ (2 - c), c))


def place_of(which, place, core):
    if which == 0:
        return place
    if which == 3:
        return place ^ 3
    return place ^ (1 + core) if which == 1 else place ^ (2 - core)


def turned(values, cosine, sine):
    return values * cosine + pltpu.roll(values, HD // 2, 1) * sine


def pack_kernel(where_ref, *refs):
    w_query, w_key, w_value, cache_keys, cache_values, slots = refs[:6]
    outs, sems = refs[6:10], refs[10]
    level = where_ref[0]
    depth = w_query.shape[0]
    copies = []

    def copy(source, target):
        copies.append(pltpu.make_async_copy(source, target, sems.at[len(copies)]))
        copies[-1].start()

    for n in range(2):
        keys, queries = outs[2 * n : 2 * n + 2]
        for m in range(2):
            at = jnp.bitwise_xor(level, n + 2 * m)
            small = pl.ds(pl.multiple_of(at * HD, HD), HD)
            large = pl.ds(pl.multiple_of(at * 4 * HD, 4 * HD), 4 * HD)
            for k, (new, old) in enumerate(((w_key, cache_keys), (w_value, cache_values))):
                to = pl.ds((2 * m + k) * HD, HD)
                copy(new.at[:, small], keys.at[0:depth, to])
                copy(old.at[:, small], keys.at[depth : depth + CACHED, to])
            copy(w_query.at[:, large], queries.at[0, :, pl.ds(m * 4 * HD, 4 * HD)])
        copy(slots, keys.at[depth + CACHED : depth + CACHED + REC_PAD])
    for each in copies:
        each.wait()


PACK_COPIES = 22


def assemble(where_ref, parts, x_ref):
    level, core = where_ref[0], where_ref[2]
    shown = TILE_RUN // 2 // PLANE
    rows = parts[0].shape[0] - shown
    for n, part in enumerate(parts):
        x_ref[n * rows : (n + 1) * rows] = part[0:rows]
    start = where_ref[4] * rows
    for n, part in enumerate(parts):
        which = 2 * lax.rem(level + n % 2, 2) + (core if n < 2 else 1 - core)
        to = pl.multiple_of(start + which * shown, 16)
        x_ref[pl.ds(to, shown)] = part[rows : rows + shown]


def products(where_ref, x_ref, pieces):
    level, place, core = where_ref[0], where_ref[1], where_ref[2]
    total = None
    for i in range(2):
        for j in range(PLANE):
            depth = pieces[i][j].shape[0]
            block = lax.rem(level + i, 2) * PLANE + place_of(j, place, core)
            start = pl.multiple_of(block * depth, depth)
            part = jnp.dot(
                x_ref[:, pl.ds(start, depth)],
                pieces[i][j][...],
                preferred_element_type=jnp.float32,
            )
            total = part if total is None else total + part
    return total


def keys_part_kernel(
    where_ref, x0, x1, x2, x3, own, near, far, old0, old1, keep_ref, send_ref, x_ref
):
    assemble(where_ref, (x0, x1, x2, x3), x_ref)
    pieces = [[own.at[i], near.at[i], far.at[i], far.at[2 + i]] for i in range(2)]
    width = 2 * HD
    total = products(where_ref, x_ref, pieces)
    at = total.shape[0]
    keep_ref[...] = total[:, :width]
    send_ref[0:at] = total[:, width:].astype(jnp.bfloat16)
    for old in (old0, old1):
        send_ref[at : at + CACHED + REC_PAD] = old[:, width:]
        at += CACHED + REC_PAD


def keys_join_kernel(where_ref, keep_ref, got_ref, old0, old1, cos_ref, sin_ref, kv_ref, sum_ref):
    level = where_ref[0]
    rows = sum_ref.shape[0]
    block = rows // LEVELS
    tok = block - REC_PAD
    width = 2 * HD
    sum_ref[...] = keep_ref[...] + got_ref[0:rows].astype(jnp.float32)
    first = where_ref[3]
    span = CACHED + REC_PAD
    for n in range(LEVELS):
        at = jnp.bitwise_xor(level, n)
        start = pl.multiple_of(lax.rem(first + n, LEVELS) * block, 16)
        cosine, sine = cos_ref[at], sin_ref[at]
        fresh = sum_ref[pl.ds(start, tok), :]
        kv_ref[2 + at, :, 0:HD] = turned(fresh[:, :HD], cosine[:tok], sine[:tok]).astype(
            jnp.bfloat16
        )
        kv_ref[2 + at, :, HD:width] = fresh[:, HD:].astype(jnp.bfloat16)
        if n < 2:
            old = (old0, old1)[n][:, 0:width].astype(jnp.float32)
        else:
            old = got_ref[rows + (n - 2) * span : rows + (n - 1) * span].astype(jnp.float32)
        slots = old[CACHED : CACHED + REC].astype(jnp.int32)
        rec = sum_ref[pl.ds(pl.multiple_of(start + tok, 16), REC_PAD), :]
        line = lax.broadcasted_iota(jnp.int32, (CACHED, width), 0)
        found = jnp.zeros((CACHED, width), jnp.float32)
        hit = jnp.zeros((CACHED, width), jnp.int32)
        for r in range(REC):
            same = line == slots[r : r + 1]
            found = jnp.where(same, rec[r : r + 1], found)
            hit = jnp.where(same, 1, hit)
        keys = turned(found[:, :HD], cosine[tok : tok + CACHED], sine[tok : tok + CACHED])
        found = jnp.concatenate([keys, found[:, HD:]], axis=1)
        line_at = pl.multiple_of(lax.rem(at, 2) * CACHED, CACHED)
        kv_ref[at // 2, pl.ds(line_at, CACHED), :] = jnp.where(
            hit == 1, found, old[:CACHED]
        ).astype(jnp.bfloat16)


def queries_part_kernel(where_ref, x0, x1, x2, x3, *refs):
    keep_refs, send_ref, x_ref = refs[6:8], refs[8], refs[9]
    assemble(where_ref, (x0, x1, x2, x3), x_ref)
    pieces = [
        [own.at[0], near.at[0], far.at[0], far.at[1]] for own, near, far in (refs[0:3], refs[3:6])
    ]
    total = products(where_ref, x_ref, pieces)
    block = total.shape[0] // LEVELS
    tok = block - REC_PAD
    width = 2 * HD
    for k in range(LEVELS):
        fresh = total[k * block : k * block + tok]
        for n in range(2):
            keep_refs[n][k] = fresh[:, n * width : (n + 1) * width]
            send_ref[n, k] = fresh[:, (2 + n) * width : (3 + n) * width].astype(jnp.bfloat16)


def attend_kernel(
    pair, where_ref, keep_ref, got_ref, cos_ref, sin_ref, kv0, kv1, kv2, kv3, out_ref, query_ref
):
    level, place, core = where_ref[0], where_ref[1], where_ref[2]
    pieces = (kv0, kv1, kv2, kv3)
    tok = keep_ref.shape[1]
    old = LEVELS // 2
    heads = query_ref.shape[1]
    for n in range(LEVELS):
        at = jnp.bitwise_xor(level, n)
        block = lax.rem(where_ref[3] + n, LEVELS)
        total = keep_ref[block] + got_ref[pair, block].astype(jnp.float32)
        cosine, sine = cos_ref[at][:tok], sin_ref[at][:tok]
        for h in range(heads):
            head = turned(total[:, h * HD : (h + 1) * HD], cosine, sine)
            query_ref[at, h] = head.astype(jnp.bfloat16)
    row = lax.broadcasted_iota(jnp.int32, (tok, tok), 0)
    col = lax.broadcasted_iota(jnp.int32, (tok, tok), 1)
    scale = HD ** (-0.5) * 1.4426950408889634
    for i in range(LEVELS):
        count = (old + i + 1) * tok
        queries = query_ref[i].reshape(heads * tok, HD)
        scores = []
        best = None
        for j in range(PLANE):
            keys = pieces[j][0 : old + i + 1, :, 0:HD].reshape(count, HD)
            raw = lax.dot_general(
                queries, keys, (((1,), (1,)), ((), ())), preferred_element_type=jnp.float32
            )
            if j == 0:
                allowed = col <= row
            else:
                allowed = jnp.broadcast_to(place_of(j, place, core), (tok, tok)) < place
            allowed = jnp.concatenate([allowed] * heads, axis=0)
            last = jnp.where(allowed, raw[:, count - tok :], NEG_FILL)
            raw = jnp.concatenate([raw[:, : count - tok], last], axis=1)
            top = jnp.max(raw, axis=1, keepdims=True)
            best = top if best is None else jnp.maximum(best, top)
            scores.append(raw)
        total, accum = 0.0, 0.0
        for j in range(PLANE):
            weights = jnp.exp2((scores[j] - best) * scale)
            total = total + jnp.sum(weights, axis=1, keepdims=True)
            values = pieces[j][0 : old + i + 1, :, HD : 2 * HD].reshape(count, HD)
            accum = accum + jnp.dot(
                weights.astype(jnp.bfloat16), values, preferred_element_type=jnp.float32
            )
        result = (accum / total).astype(jnp.bfloat16)
        for h in range(heads):
            out_ref[i * tok : (i + 1) * tok, h * HD : (h + 1) * HD] = result[
                h * tok : (h + 1) * tok
            ]


def output_kernel(where_ref, *refs):
    heads, weights, (mine_ref, other_ref, x_ref) = refs[:4], refs[4:-3], refs[-3:]
    level, core = where_ref[0], where_ref[2]
    depth = heads[0].shape[1]
    width = weights[0].shape[2]
    tok = mine_ref.shape[1]
    for n, ref in enumerate(heads):
        at = 2 * lax.rem(level + n // 2, 2) + n % 2
        x_ref[:, pl.ds(pl.multiple_of(at * depth, depth), depth)] = ref[...]
    swap = jnp.where(core == level // 2, 0, 1)
    for s, out_ref in enumerate((mine_ref, other_ref)):
        i = jnp.bitwise_xor(swap, s)
        for j, piece in enumerate(weights):
            slot = (0, 2, 1, 3)[j] if s else j
            part = jnp.dot(x_ref[...], piece[i], preferred_element_type=jnp.float32)
            for t in range(LEVELS):
                out_ref[
                    lax.rem(t + LEVELS - level, LEVELS), :, slot * width : (slot + 1) * width
                ] = part[t * tok : (t + 1) * tok].astype(out_ref.dtype)


def finish_kernel(where_ref, own, first, second, third, out_ref):
    level, place, core = where_ref[0], where_ref[1], where_ref[2]
    half = out_ref.shape[1] // 2
    width = half // PLANE
    sums = (
        own[...] + second[...].astype(jnp.float32),
        first[...].astype(jnp.float32) + third[...].astype(jnp.float32),
    )
    for steps, total in enumerate(sums):
        for j in range(PLANE):
            at = lax.rem(level + steps, 2) * half + place_of(j, place, core) * width
            out_ref[:, pl.ds(pl.multiple_of(at, width), width)] = total[
                :, j * width : (j + 1) * width
            ].astype(out_ref.dtype)


SMEM = pl.BlockSpec(memory_space=pltpu.SMEM)
VMEM = pl.BlockSpec(memory_space=pltpu.VMEM)
HBM = pl.BlockSpec(memory_space=pltpu.MemorySpace.HBM)
PARAMS = pltpu.CompilerParams(vmem_limit_bytes=48 * 1024 * 1024)


def shaped(shape, dtype=jnp.bfloat16):
    return jax.ShapeDtypeStruct(shape, dtype)


def by_levels(
    text_rows,
    picture_rows,
    picture_slots,
    norm_gain,
    w_query,
    w_key,
    w_value,
    w_out,
    cache_keys,
    cache_values,
    recompute_rows,
    recompute_slots,
):
    seq_index = lax.axis_index("seq")
    core = lax.axis_index("head")
    level, place = seq_index // PLANE, seq_index % PLANE
    half_at = level // 2
    own_first = core == half_at
    tok, width = text_rows.shape
    block_rows = tok + REC_PAD

    stream_len = tok * LEVELS * PLANE
    tile_owners = TILE_RUN // tok
    first = stream_len // 2 // tok
    last = (stream_len - TILE_RUN) // tok
    owners = [first + i for i in range(tile_owners)] + [last + i for i in range(tile_owners)]
    assert [owner % PLANE for owner in owners] == list(range(LEVELS))
    owner_level = jnp.where(place < tile_owners, first // PLANE, last // PLANE)

    first_block = jnp.where(own_first, 0, 2)
    shown_block = (first_block + (level ^ owner_level)) % LEVELS
    where = jnp.stack([level, place, core, first_block, shown_block]).astype(jnp.int32)

    slots = (recompute_slots - seq_index * CACHED).astype(jnp.bfloat16)
    slot_rows = jnp.broadcast_to(jnp.pad(slots, (0, REC_PAD - REC))[:, None], (REC_PAD, 4 * HD))
    depth = w_query.shape[0]
    key_shape = shaped((depth + CACHED + REC_PAD, 4 * HD))
    query_shape = shaped((1, depth, 8 * HD))
    key_own, query_own, key_give, query_give = pl.pallas_call(
        pack_kernel,
        out_shape=(key_shape, query_shape) * 2,
        in_specs=[SMEM] + [HBM] * 6,
        out_specs=(HBM,) * 4,
        scratch_shapes=[pltpu.SemaphoreType.DMA((PACK_COPIES,))],
        compiler_params=PARAMS,
        name="pack",
    )(where, w_query, w_key, w_value, cache_keys, cache_values, slot_rows)
    query_near = to_near(query_own)

    rows = jnp.concatenate(
        [text_rows, recompute_rows, jnp.zeros((REC_PAD - REC, width), text_rows.dtype)], axis=0
    )
    gain = lax.dynamic_slice_in_dim(norm_gain, core * width, width, 0)
    wide, pictures = rows.astype(jnp.float32), picture_rows.astype(jnp.float32)
    squares, picture_squares = lax.psum(
        (jnp.sum(wide * wide, axis=1), jnp.sum(pictures * pictures, axis=1)), "head"
    )
    normed = scaled(wide, squares, gain)
    pictures = scaled(pictures, picture_squares, gain)

    out_rows = w_out.shape[0] // 2
    out_own, out_give = (
        lax.dynamic_slice_in_dim(w_out, at * out_rows, out_rows, 0) for at in (half_at, 1 - half_at)
    )

    crossed = permuted(normed, lambda z, p, c: (z ^ 2, p, 1 - c) if c == 1 - z // 2 else None)
    shown = permuted(pictures, lambda z, p, c: (2 * c + p // 2, z, p % 2))
    key_next = across(key_give, 1)
    query_far = to_far(jnp.concatenate([query_own, query_near], axis=0))
    query_near, query_give = lax.optimization_barrier((query_near, query_give))
    query_next = across(query_give, 1)
    shown, key_next = lax.optimization_barrier((shown, key_next))
    keys = jnp.stack([key_own[:depth], key_next[:depth]])
    old_own, old_next = key_own[depth:], key_next[depth:]
    keys_near = to_near(keys)
    crossed, shown, out_give = lax.optimization_barrier((crossed, shown, out_give))
    held = jnp.concatenate([jnp.where(own_first, normed, crossed), shown], axis=0)
    next_rows = across(held, 1)
    held_other = other_core(held)
    next_other = other_core(next_rows)
    out_got = across(out_give, 2)
    keys_far = to_far(jnp.concatenate([keys, keys_near], axis=0))
    next_near = to_near(query_next)
    next_other, keys_far, query_far, next_near, out_got = lax.optimization_barrier(
        (next_other, keys_far, query_far, next_near, out_got)
    )
    next_far = to_far(jnp.concatenate([query_next, next_near], axis=0))
    parts = (held, next_rows, held_other, next_other)

    half = HD // 2
    freqs = ROPE_BASE ** (-jnp.arange(half, dtype=jnp.float32) / half)
    blocks = (jnp.arange(LEVELS, dtype=jnp.int32) * PLANE + place)[:, None]
    stream_pos = (
        CACHED * LEVELS * PLANE + blocks * tok + jnp.arange(tok, dtype=jnp.int32)[None]
    ).astype(jnp.float32)
    cache_pos = (blocks * CACHED + jnp.arange(CACHED, dtype=jnp.int32)[None]).astype(jnp.float32)
    angles = jnp.concatenate([stream_pos, cache_pos], axis=1)[..., None] * freqs
    cosine, sine = jnp.cos(angles), jnp.sin(angles)
    cosine = jnp.concatenate([cosine, cosine], axis=-1)
    sine = jnp.concatenate([-sine, sine], axis=-1)

    all_rows = LEVELS * block_rows
    keep, send = pl.pallas_call(
        keys_part_kernel,
        out_shape=(
            shaped((all_rows, 2 * HD), jnp.float32),
            shaped((all_rows + 2 * (CACHED + REC_PAD), 2 * HD)),
        ),
        in_specs=[SMEM] + [VMEM] * 9,
        out_specs=(VMEM, VMEM),
        scratch_shapes=[pltpu.VMEM((all_rows, width), jnp.bfloat16)],
        compiler_params=PARAMS,
        name="keys_part",
    )(where, *parts, keys, keys_near, keys_far, old_own, old_next)
    send, out_got, *parts = lax.optimization_barrier((send, out_got, *parts))
    out_pair = jnp.stack([out_own, out_got])
    out_pair, next_far = lax.optimization_barrier((out_pair, next_far))
    out_near = to_near(out_pair)
    *q_keep, q_send = pl.pallas_call(
        queries_part_kernel,
        out_shape=(shaped((LEVELS, tok, 2 * HD), jnp.float32),) * 2
        + (shaped((2, LEVELS, tok, 2 * HD)),),
        in_specs=[SMEM] + [VMEM] * 10,
        out_specs=(VMEM,) * 3,
        scratch_shapes=[pltpu.VMEM((all_rows, width), jnp.bfloat16)],
        compiler_params=PARAMS,
        name="queries_part",
    )(where, *parts, query_own, query_near, query_far, query_next, next_near, next_far)
    got_keys, q_send = lax.optimization_barrier((across(send, 2), q_send))
    kv = pl.pallas_call(
        keys_join_kernel,
        out_shape=shaped((LEVELS // 2 + LEVELS, tok, 2 * HD)),
        in_specs=[SMEM] + [VMEM] * 6,
        out_specs=VMEM,
        scratch_shapes=[pltpu.VMEM((all_rows, 2 * HD), jnp.float32)],
        compiler_params=PARAMS,
        name="keys_join",
    )(where, keep, got_keys, old_own, old_next, cosine, sine)
    kv_near, kv_far = to_near(kv), to_far(kv)
    kv_both = permuted(kv, lambda z, p, c: (z, p ^ 3, c))

    kv_near, kv_far, kv_both, out_near, out_pair, got_queries = lax.optimization_barrier(
        (kv_near, kv_far, kv_both, out_near, out_pair, across(q_send, 2))
    )
    out_far, out_both = to_far(out_pair), to_far(out_near)

    attended = [
        pl.pallas_call(
            functools.partial(attend_kernel, pair),
            out_shape=shaped((LEVELS * tok, 2 * HD)),
            in_specs=[SMEM] + [VMEM] * 8,
            out_specs=VMEM,
            scratch_shapes=[pltpu.VMEM((LEVELS, 2, tok, HD), jnp.bfloat16)],
            compiler_params=PARAMS,
            name="attend",
        )(where, q_keep[pair], got_queries, cosine, sine, kv, kv_near, kv_far, kv_both)
        for pair in range(2)
    ]
    attended += [across(each, 1) for each in attended]

    wide_cols = PLANE * w_out.shape[1]
    mine, other = pl.pallas_call(
        output_kernel,
        out_shape=(
            shaped((LEVELS, tok, wide_cols), jnp.float32),
            shaped((LEVELS, tok, wide_cols)),
        ),
        in_specs=[SMEM] + [VMEM] * 8,
        out_specs=(VMEM, VMEM),
        scratch_shapes=[pltpu.VMEM((LEVELS * tok, out_rows), jnp.bfloat16)],
        compiler_params=PARAMS,
        name="output",
    )(where, *attended, out_pair, out_near, out_far, out_both)
    got = other_core(other)
    block = [mine[d] + got[d].astype(jnp.float32) for d in range(LEVELS)]
    shares = [up(block[d].astype(jnp.bfloat16), d) for d in range(1, LEVELS)]
    return pl.pallas_call(
        finish_kernel,
        out_shape=shaped((tok, width)),
        in_specs=[SMEM] + [VMEM] * 4,
        out_specs=VMEM,
        compiler_params=PARAMS,
        name="finish",
    )(where, block[0], *shares)


def solution(mesh):
    def run(*args):
        kv_local = args[5].shape[1] // HD // mesh.shape["head"]
        levels_fit = (
            mesh.shape["seq"] == LEVELS * PLANE
            and mesh.shape["head"] == 2
            and kv_local == LEVELS
            and args[1].shape[0] == 2 * TILE_RUN
            and args[0].shape[0] == 2048
            and args[8].shape[0] == LEVELS * PLANE * CACHED
            and args[10].shape[0] == LEVELS * PLANE * REC
        )
        return jax.shard_map(
            by_levels if levels_fit else on_device,
            mesh=mesh,
            in_specs=(
                P("seq", "head"),
                P("seq", "head"),
                P("seq"),
                P(),
                P("seq", "head"),
                P("seq", "head"),
                P("seq", "head"),
                P("head", "seq"),
                P("seq", "head"),
                P("seq", "head"),
                P("seq", "head"),
                P("seq"),
            ),
            out_specs=P("seq", "head"),
            check_vma=False,
        )(*args)

    return run
```

```python
import functools

import jax
import jax.numpy as jnp
from jax import lax
from jax.experimental import pallas as pl
from jax.experimental.pallas import tpu as pltpu
from jax.sharding import PartitionSpec as P

D = 4096
HD = 128


EPSILON = 1e-05
ROPE_BASE = 1000000.0
NEG_FILL = -1e30


def rotate(values, positions):
    half = values.shape[-1] // 2
    freqs = ROPE_BASE ** (-jnp.arange(half, dtype=jnp.float32) / half)
    angles = positions[:, None] * freqs[None, :]
    cosine = jnp.cos(angles)[:, None, :]
    sine = jnp.sin(angles)[:, None, :]
    first = values[..., :half]
    second = values[..., half:]
    return jnp.concatenate(
        [first * cosine - second * sine, second * cosine + first * sine], axis=-1
    )


def scaled(rows_wide, squares, gain):
    return (rows_wide * lax.rsqrt(squares / D + EPSILON)[:, None] * gain[None, :]).astype(
        jnp.bfloat16
    )


def attend(carry, key_piece, value_piece, queries, allowed):
    best, total, accum = carry
    count = key_piece.shape[0]
    kv_local = queries.shape[0]
    keys_split = key_piece.reshape(count, kv_local, HD)
    values_split = value_piece.reshape(count, kv_local, HD)
    scores = jnp.einsum(
        "kgtd,nkd->kgtn", queries, keys_split, preferred_element_type=jnp.float32
    ) * HD ** (-0.5)
    scores = jnp.where(allowed, scores, NEG_FILL)
    fresh = jnp.maximum(best, jnp.max(scores, axis=-1))
    factor = jnp.exp(best - fresh)
    weights = jnp.where(allowed, jnp.exp(scores - fresh[..., None]), 0.0)
    total = total * factor + jnp.sum(weights, axis=-1)
    accum = accum * factor[..., None] + jnp.einsum(
        "kgtn,nkd->kgtd",
        weights.astype(jnp.bfloat16),
        values_split,
        preferred_element_type=jnp.float32,
    )
    return (fresh, total, accum)


def on_device(
    text_rows,
    picture_rows,
    picture_slots,
    norm_gain,
    w_query,
    w_key,
    w_value,
    w_out,
    cache_keys,
    cache_values,
    recompute_rows,
    recompute_slots,
):
    tok_rows = text_rows.shape[0]
    rec_count = recompute_rows.shape[0]
    cache_rows = cache_keys.shape[0]
    seq_index = lax.axis_index("seq")
    local_pos = seq_index * tok_rows + jnp.arange(tok_rows, dtype=jnp.int32)
    rows_piece = lax.all_gather(picture_rows, "seq", axis=0, tiled=True)
    slots_piece = lax.all_gather(picture_slots, "seq", axis=0, tiled=True)
    select = (slots_piece[None, :] == local_pos[:, None]).astype(jnp.bfloat16)
    placed = jnp.dot(select, rows_piece, preferred_element_type=jnp.float32)
    hits = jnp.sum(select.astype(jnp.float32), axis=1)
    added, hits = (placed, hits)
    stream = jnp.where(hits[:, None] > 0.5, added, text_rows.astype(jnp.float32)).astype(
        jnp.bfloat16
    )
    slice_width = stream.shape[1]
    gain_slice = lax.dynamic_slice_in_dim(
        norm_gain, lax.axis_index("head") * slice_width, slice_width, 0
    )
    stream_wide = stream.astype(jnp.float32)
    rec_wide = recompute_rows.astype(jnp.float32)
    stream_sq, rec_sq = lax.psum(
        (jnp.sum(stream_wide * stream_wide, axis=1), jnp.sum(rec_wide * rec_wide, axis=1)), "head"
    )
    normed, rec_normed = (
        lax.all_gather(scaled(stream_wide, stream_sq, gain_slice), "head", axis=1, tiled=True),
        lax.all_gather(scaled(rec_wide, rec_sq, gain_slice), "head", axis=1, tiled=True),
    )
    stacked = jnp.concatenate([normed, rec_normed], axis=0)
    query_cols = w_query.shape[1]
    key_cols = w_key.shape[1]
    pieces = (
        lax.all_gather(w_query, "seq", axis=0, tiled=True),
        lax.all_gather(w_key, "seq", axis=0, tiled=True),
        lax.all_gather(w_value, "seq", axis=0, tiled=True),
    )
    query_all = jnp.dot(stacked, pieces[0], preferred_element_type=jnp.float32)
    key_all = jnp.dot(stacked, pieces[1], preferred_element_type=jnp.float32)
    value_all = jnp.dot(stacked, pieces[2], preferred_element_type=jnp.float32)
    cache_total = cache_rows * lax.axis_size("seq")
    stream_pos = (cache_total + local_pos).astype(jnp.float32)
    rec_pos = recompute_slots.astype(jnp.float32)
    heads_local = query_cols // HD
    kv_local = key_cols // HD
    group = heads_local // kv_local
    rot_query = rotate(query_all[:tok_rows].reshape(tok_rows, heads_local, HD), stream_pos).astype(
        jnp.bfloat16
    )
    rot_key = (
        rotate(key_all[:tok_rows].reshape(tok_rows, kv_local, HD), stream_pos)
        .astype(jnp.bfloat16)
        .reshape(tok_rows, key_cols)
    )
    values_new = value_all[:tok_rows].astype(jnp.bfloat16)
    rot_rec_key = (
        rotate(key_all[tok_rows:].reshape(rec_count, kv_local, HD), rec_pos)
        .astype(jnp.bfloat16)
        .reshape(rec_count, key_cols)
    )
    rec_values = value_all[tok_rows:].astype(jnp.bfloat16)
    local_slots = recompute_slots - seq_index * cache_rows
    select = local_slots[:, None] == jnp.arange(cache_rows, dtype=jnp.int32)[None, :]
    replaced = jnp.any(select, axis=0)[:, None]
    select_cols = select.astype(jnp.bfloat16).T
    new_keys = jnp.dot(select_cols, rot_rec_key, preferred_element_type=jnp.float32).astype(
        jnp.bfloat16
    )
    new_values = jnp.dot(select_cols, rec_values, preferred_element_type=jnp.float32).astype(
        jnp.bfloat16
    )
    cache_k = jnp.where(replaced, new_keys, cache_keys)
    cache_v = jnp.where(replaced, new_values, cache_values)
    queries = jnp.transpose(rot_query.reshape(tok_rows, kv_local, group, HD), (1, 2, 0, 3))
    carry_start = (
        jnp.full((kv_local, group, tok_rows), NEG_FILL, jnp.float32),
        jnp.zeros((kv_local, group, tok_rows), jnp.float32),
        jnp.zeros((kv_local, group, tok_rows, HD), jnp.float32),
    )
    pieces = (
        lax.all_gather(cache_k, "seq", axis=0, tiled=True),
        lax.all_gather(cache_v, "seq", axis=0, tiled=True),
    )
    allowed = jnp.ones((tok_rows, pieces[0].shape[0]), jnp.bool_)
    carry_mid = attend(carry_start, pieces[0], pieces[1], queries, allowed)
    pieces = (
        lax.all_gather(rot_key, "seq", axis=0, tiled=True),
        lax.all_gather(values_new, "seq", axis=0, tiled=True),
    )
    key_pos = jnp.arange(pieces[0].shape[0], dtype=jnp.int32)
    allowed = key_pos[None, :] <= local_pos[:, None]
    best, total, accum = attend(carry_mid, pieces[0], pieces[1], queries, allowed)
    attended = (
        jnp.transpose(accum / total[..., None], (2, 0, 1, 3))
        .reshape(tok_rows, query_cols)
        .astype(jnp.bfloat16)
    )
    partial_out = jnp.dot(
        attended,
        lax.all_gather(w_out, "seq", axis=1, tiled=True),
        preferred_element_type=jnp.float32,
    )
    return lax.psum_scatter(
        partial_out.astype(jnp.bfloat16), "head", scatter_dimension=1, tiled=True
    )


LEVELS = 4
PLANE = 4
TILE_RUN = 256
CACHED = 64
REC = 8
REC_PAD = 16


def permuted(value, move):
    perm = []
    for level in range(LEVELS):
        for place in range(PLANE):
            for core in range(2):
                target = move(level, place, core)
                if target is not None:
                    to_level, to_place, to_core = target
                    perm.append(
                        (
                            (level * PLANE + place) * 2 + core,
                            (to_level * PLANE + to_place) * 2 + to_core,
                        )
                    )
    return lax.ppermute(value, ("seq", "head"), perm)


def across(value, bit):
    return permuted(value, lambda z, p, c: (z ^ bit, p, c))


def up(value, steps):
    return permuted(value, lambda z, p, c: ((z + steps) % LEVELS, p, c))


def other_core(value):
    return permuted(value, lambda z, p, c: (z, p, 1 - c))


def to_near(value):
    return permuted(value, lambda z, p, c: (z, p ^ (1 + c), c))


def to_far(value):
    return permuted(value, lambda z, p, c: (z, p ^ (2 - c), c))


def place_of(which, place, core):
    if which == 0:
        return place
    if which == 3:
        return place ^ 3
    return place ^ (1 + core) if which == 1 else place ^ (2 - core)


def turned(values, cosine, sine):
    return values * cosine + pltpu.roll(values, HD // 2, 1) * sine


def pack_kernel(where_ref, *refs):
    w_key, w_value, cache_keys, cache_values, slots = refs[:5]
    outs, sems = refs[5:7], refs[7]
    level = where_ref[0]
    depth = w_key.shape[0]
    copies = []

    def copy(source, target):
        copies.append(pltpu.make_async_copy(source, target, sems.at[len(copies)]))
        copies[-1].start()

    for n in range(2):
        keys = outs[n]
        for m in range(2):
            at = jnp.bitwise_xor(level, n + 2 * m)
            small = pl.ds(pl.multiple_of(at * HD, HD), HD)
            for k, (new, old) in enumerate(((w_key, cache_keys), (w_value, cache_values))):
                to = pl.ds((2 * m + k) * HD, HD)
                copy(new.at[:, small], keys.at[0:depth, to])
                copy(old.at[:, small], keys.at[depth : depth + CACHED, to])
        copy(slots, keys.at[depth + CACHED : depth + CACHED + REC_PAD])
    for each in copies:
        each.wait()


PACK_COPIES = 18


def assemble(where_ref, parts, x_ref):
    level, core = where_ref[0], where_ref[2]
    shown = TILE_RUN // 2 // PLANE
    rows = parts[0].shape[0] - shown
    for n, part in enumerate(parts):
        x_ref[n * rows : (n + 1) * rows] = part[0:rows]
    start = where_ref[4] * rows
    for n, part in enumerate(parts):
        which = 2 * lax.rem(level + n % 2, 2) + (core if n < 2 else 1 - core)
        to = pl.multiple_of(start + which * shown, 16)
        x_ref[pl.ds(to, shown)] = part[rows : rows + shown]


def products(where_ref, x_ref, pieces):
    level, place, core = where_ref[0], where_ref[1], where_ref[2]
    total = None
    for i in range(2):
        for j in range(PLANE):
            depth = pieces[i][j].shape[0]
            block = lax.rem(level + i, 2) * PLANE + place_of(j, place, core)
            start = pl.multiple_of(block * depth, depth)
            part = jnp.dot(
                x_ref[:, pl.ds(start, depth)],
                pieces[i][j][...],
                preferred_element_type=jnp.float32,
            )
            total = part if total is None else total + part
    return total


def keys_part_kernel(
    where_ref, x0, x1, x2, x3, own, near, far, old0, old1, keep_ref, send_ref, x_ref
):
    assemble(where_ref, (x0, x1, x2, x3), x_ref)
    pieces = [[own.at[i], near.at[i], far.at[i], far.at[2 + i]] for i in range(2)]
    width = 2 * HD
    total = products(where_ref, x_ref, pieces)
    at = total.shape[0]
    keep_ref[...] = total[:, :width]
    send_ref[0:at] = total[:, width:].astype(jnp.bfloat16)
    for old in (old0, old1):
        send_ref[at : at + CACHED + REC_PAD] = old[:, width:]
        at += CACHED + REC_PAD


def keys_join_kernel(where_ref, keep_ref, got_ref, old0, old1, cos_ref, sin_ref, kv_ref, sum_ref):
    level = where_ref[0]
    rows = sum_ref.shape[0]
    block = rows // LEVELS
    tok = block - REC_PAD
    width = 2 * HD
    sum_ref[...] = keep_ref[...] + got_ref[0:rows].astype(jnp.float32)
    first = where_ref[3]
    span = CACHED + REC_PAD
    for n in range(LEVELS):
        at = jnp.bitwise_xor(level, n)
        start = pl.multiple_of(lax.rem(first + n, LEVELS) * block, 16)
        cosine, sine = cos_ref[at], sin_ref[at]
        fresh = sum_ref[pl.ds(start, tok), :]
        kv_ref[2 + at, :, 0:HD] = turned(fresh[:, :HD], cosine[:tok], sine[:tok]).astype(
            jnp.bfloat16
        )
        kv_ref[2 + at, :, HD:width] = fresh[:, HD:].astype(jnp.bfloat16)
        if n < 2:
            old = (old0, old1)[n][:, 0:width].astype(jnp.float32)
        else:
            old = got_ref[rows + (n - 2) * span : rows + (n - 1) * span].astype(jnp.float32)
        slots = old[CACHED : CACHED + REC].astype(jnp.int32)
        rec = sum_ref[pl.ds(pl.multiple_of(start + tok, 16), REC_PAD), :]
        line = lax.broadcasted_iota(jnp.int32, (CACHED, width), 0)
        found = jnp.zeros((CACHED, width), jnp.float32)
        hit = jnp.zeros((CACHED, width), jnp.int32)
        for r in range(REC):
            same = line == slots[r : r + 1]
            found = jnp.where(same, rec[r : r + 1], found)
            hit = jnp.where(same, 1, hit)
        keys = turned(found[:, :HD], cosine[tok : tok + CACHED], sine[tok : tok + CACHED])
        found = jnp.concatenate([keys, found[:, HD:]], axis=1)
        line_at = pl.multiple_of(lax.rem(at, 2) * CACHED, CACHED)
        kv_ref[at // 2, pl.ds(line_at, CACHED), :] = jnp.where(
            hit == 1, found, old[:CACHED]
        ).astype(jnp.bfloat16)


def queries_part_kernel(where_ref, x0, x1, x2, x3, *refs):
    weights, outs, x_ref = refs[:4], refs[4:8], refs[8]
    level, place, core = where_ref[0], where_ref[1], where_ref[2]
    assemble(where_ref, (x0, x1, x2, x3), x_ref)
    depth = weights[0].shape[0]
    width = 4 * HD
    block = x_ref.shape[0] // LEVELS
    tok = block - REC_PAD
    for m, out_ref in zip((0, 2, 1, 3), outs):
        group = pl.ds(pl.multiple_of(jnp.bitwise_xor(level, m) * width, width), width)
        total = None
        for j in range(PLANE):
            at = lax.rem(level, 2) * PLANE + place_of(j, place, core)
            part = jnp.dot(
                x_ref[:, pl.ds(pl.multiple_of(at * depth, depth), depth)],
                weights[j][:, group],
                preferred_element_type=jnp.float32,
            )
            total = part if total is None else total + part
        for k in range(LEVELS):
            at = jnp.bitwise_xor(level, lax.rem(k + LEVELS - where_ref[3], LEVELS))
            out_ref[at] = total[k * block : k * block + tok].astype(out_ref.dtype)


def attend_kernel(
    pair, where_ref, keep_ref, near_ref, got_ref, cos_ref, sin_ref, kv0, kv1, kv2, kv3, out_ref, query_ref
):
    level, place, core = where_ref[0], where_ref[1], where_ref[2]
    pieces = (kv0, kv1, kv2, kv3)
    tok = keep_ref.shape[1]
    old = LEVELS // 2
    heads = query_ref.shape[1]
    columns = slice(pair * heads * HD, (pair + 1) * heads * HD)
    for at in range(LEVELS):
        total = keep_ref[at, :, columns] + (
            near_ref[at, :, columns].astype(jnp.float32)
            + got_ref[at, :, columns].astype(jnp.float32)
        )
        cosine, sine = cos_ref[at][:tok], sin_ref[at][:tok]
        for h in range(heads):
            head = turned(total[:, h * HD : (h + 1) * HD], cosine, sine)
            query_ref[at, h] = head.astype(jnp.bfloat16)
    row = lax.broadcasted_iota(jnp.int32, (tok, tok), 0)
    col = lax.broadcasted_iota(jnp.int32, (tok, tok), 1)
    scale = HD ** (-0.5) * 1.4426950408889634
    for i in range(LEVELS):
        count = (old + i + 1) * tok
        queries = query_ref[i].reshape(heads * tok, HD)
        scores = []
        best = None
        for j in range(PLANE):
            keys = pieces[j][0 : old + i + 1, :, 0:HD].reshape(count, HD)
            raw = lax.dot_general(
                queries, keys, (((1,), (1,)), ((), ())), preferred_element_type=jnp.float32
            )
            if j == 0:
                allowed = col <= row
            else:
                allowed = jnp.broadcast_to(place_of(j, place, core), (tok, tok)) < place
            allowed = jnp.concatenate([allowed] * heads, axis=0)
            last = jnp.where(allowed, raw[:, count - tok :], NEG_FILL)
            raw = jnp.concatenate([raw[:, : count - tok], last], axis=1)
            top = jnp.max(raw, axis=1, keepdims=True)
            best = top if best is None else jnp.maximum(best, top)
            scores.append(raw)
        total, accum = 0.0, 0.0
        for j in range(PLANE):
            weights = jnp.exp2((scores[j] - best) * scale)
            total = total + jnp.sum(weights, axis=1, keepdims=True)
            values = pieces[j][0 : old + i + 1, :, HD : 2 * HD].reshape(count, HD)
            accum = accum + jnp.dot(
                weights.astype(jnp.bfloat16), values, preferred_element_type=jnp.float32
            )
        result = (accum / total).astype(jnp.bfloat16)
        for h in range(heads):
            out_ref[i * tok : (i + 1) * tok, h * HD : (h + 1) * HD] = result[
                h * tok : (h + 1) * tok
            ]


def output_kernel(where_ref, *refs):
    heads, weights, (mine_ref, other_ref, x_ref) = refs[:4], refs[4:-3], refs[-3:]
    level, core = where_ref[0], where_ref[2]
    depth = heads[0].shape[1]
    width = weights[0].shape[2]
    tok = mine_ref.shape[1]
    for n, ref in enumerate(heads):
        at = 2 * lax.rem(level + n // 2, 2) + n % 2
        x_ref[:, pl.ds(pl.multiple_of(at * depth, depth), depth)] = ref[...]
    swap = jnp.where(core == level // 2, 0, 1)
    for s, out_ref in enumerate((mine_ref, other_ref)):
        i = jnp.bitwise_xor(swap, s)
        for j, piece in enumerate(weights):
            slot = (0, 2, 1, 3)[j] if s else j
            part = jnp.dot(x_ref[...], piece[i], preferred_element_type=jnp.float32)
            for t in range(LEVELS):
                out_ref[
                    lax.rem(t + LEVELS - level, LEVELS), :, slot * width : (slot + 1) * width
                ] = part[t * tok : (t + 1) * tok].astype(out_ref.dtype)


def finish_kernel(where_ref, own, first, second, third, out_ref):
    level, place, core = where_ref[0], where_ref[1], where_ref[2]
    half = out_ref.shape[1] // 2
    width = half // PLANE
    sums = (
        own[...] + second[...].astype(jnp.float32),
        first[...].astype(jnp.float32) + third[...].astype(jnp.float32),
    )
    for steps, total in enumerate(sums):
        for j in range(PLANE):
            at = lax.rem(level + steps, 2) * half + place_of(j, place, core) * width
            out_ref[:, pl.ds(pl.multiple_of(at, width), width)] = total[
                :, j * width : (j + 1) * width
            ].astype(out_ref.dtype)


SMEM = pl.BlockSpec(memory_space=pltpu.SMEM)
VMEM = pl.BlockSpec(memory_space=pltpu.VMEM)
HBM = pl.BlockSpec(memory_space=pltpu.MemorySpace.HBM)
PARAMS = pltpu.CompilerParams(vmem_limit_bytes=48 * 1024 * 1024)


def shaped(shape, dtype=jnp.bfloat16):
    return jax.ShapeDtypeStruct(shape, dtype)


def by_levels(
    text_rows,
    picture_rows,
    picture_slots,
    norm_gain,
    w_query,
    w_key,
    w_value,
    w_out,
    cache_keys,
    cache_values,
    recompute_rows,
    recompute_slots,
):
    seq_index = lax.axis_index("seq")
    core = lax.axis_index("head")
    level, place = seq_index // PLANE, seq_index % PLANE
    half_at = level // 2
    own_first = core == half_at
    tok, width = text_rows.shape
    block_rows = tok + REC_PAD

    stream_len = tok * LEVELS * PLANE
    tile_owners = TILE_RUN // tok
    first = stream_len // 2 // tok
    last = (stream_len - TILE_RUN) // tok
    owners = [first + i for i in range(tile_owners)] + [last + i for i in range(tile_owners)]
    assert [owner % PLANE for owner in owners] == list(range(LEVELS))
    owner_level = jnp.where(place < tile_owners, first // PLANE, last // PLANE)

    first_block = jnp.where(own_first, 0, 2)
    shown_block = (first_block + (level ^ owner_level)) % LEVELS
    where = jnp.stack([level, place, core, first_block, shown_block]).astype(jnp.int32)

    slots = (recompute_slots - seq_index * CACHED).astype(jnp.bfloat16)
    slot_rows = jnp.broadcast_to(jnp.pad(slots, (0, REC_PAD - REC))[:, None], (REC_PAD, 4 * HD))
    depth = w_key.shape[0]
    key_own, key_give = pl.pallas_call(
        pack_kernel,
        out_shape=(shaped((depth + CACHED + REC_PAD, 4 * HD)),) * 2,
        in_specs=[SMEM] + [HBM] * 5,
        out_specs=(HBM,) * 2,
        scratch_shapes=[pltpu.SemaphoreType.DMA((PACK_COPIES,))],
        compiler_params=PARAMS,
        name="pack",
    )(where, w_key, w_value, cache_keys, cache_values, slot_rows)

    rows = jnp.concatenate(
        [text_rows, recompute_rows, jnp.zeros((REC_PAD - REC, width), text_rows.dtype)], axis=0
    )
    gain = lax.dynamic_slice_in_dim(norm_gain, core * width, width, 0)
    wide, pictures = rows.astype(jnp.float32), picture_rows.astype(jnp.float32)
    squares, picture_squares = lax.psum(
        (jnp.sum(wide * wide, axis=1), jnp.sum(pictures * pictures, axis=1)), "head"
    )
    normed = scaled(wide, squares, gain)
    pictures = scaled(pictures, picture_squares, gain)

    out_rows = w_out.shape[0] // 2
    out_own, out_give = (
        lax.dynamic_slice_in_dim(w_out, at * out_rows, out_rows, 0) for at in (half_at, 1 - half_at)
    )

    crossed = permuted(normed, lambda z, p, c: (z ^ 2, p, 1 - c) if c == 1 - z // 2 else None)
    shown = permuted(pictures, lambda z, p, c: (2 * c + p // 2, z, p % 2))
    key_next = across(key_give, 1)
    query_near, query_far = to_near(w_query), to_far(w_query)
    query_both = to_far(query_near)
    shown, key_next = lax.optimization_barrier((shown, key_next))
    keys = jnp.stack([key_own[:depth], key_next[:depth]])
    old_own, old_next = key_own[depth:], key_next[depth:]
    keys_near = to_near(keys)
    crossed, shown, out_give = lax.optimization_barrier((crossed, shown, out_give))
    held = jnp.concatenate([jnp.where(own_first, normed, crossed), shown], axis=0)
    next_rows = across(held, 1)
    held_other = other_core(held)
    next_other = other_core(next_rows)
    out_got = across(out_give, 2)
    keys_far = to_far(jnp.concatenate([keys, keys_near], axis=0))
    next_other, held_other, keys_far, query_far, query_both, out_got = lax.optimization_barrier(
        (next_other, held_other, keys_far, query_far, query_both, out_got)
    )
    parts = (held, next_rows, held_other, next_other)

    half = HD // 2
    freqs = ROPE_BASE ** (-jnp.arange(half, dtype=jnp.float32) / half)
    blocks = (jnp.arange(LEVELS, dtype=jnp.int32) * PLANE + place)[:, None]
    stream_pos = (
        CACHED * LEVELS * PLANE + blocks * tok + jnp.arange(tok, dtype=jnp.int32)[None]
    ).astype(jnp.float32)
    cache_pos = (blocks * CACHED + jnp.arange(CACHED, dtype=jnp.int32)[None]).astype(jnp.float32)
    angles = jnp.concatenate([stream_pos, cache_pos], axis=1)[..., None] * freqs
    cosine, sine = jnp.cos(angles), jnp.sin(angles)
    cosine = jnp.concatenate([cosine, cosine], axis=-1)
    sine = jnp.concatenate([-sine, sine], axis=-1)

    all_rows = LEVELS * block_rows
    keep, send = pl.pallas_call(
        keys_part_kernel,
        out_shape=(
            shaped((all_rows, 2 * HD), jnp.float32),
            shaped((all_rows + 2 * (CACHED + REC_PAD), 2 * HD)),
        ),
        in_specs=[SMEM] + [VMEM] * 9,
        out_specs=(VMEM, VMEM),
        scratch_shapes=[pltpu.VMEM((all_rows, width), jnp.bfloat16)],
        compiler_params=PARAMS,
        name="keys_part",
    )(where, *parts, keys, keys_near, keys_far, old_own, old_next)
    send, *parts = lax.optimization_barrier((send, *parts))
    group_shape = (LEVELS, tok, 4 * HD)
    q_keep, q_keep2, q_send, q_send2 = pl.pallas_call(
        queries_part_kernel,
        out_shape=(shaped(group_shape, jnp.float32),) * 2 + (shaped(group_shape),) * 2,
        in_specs=[SMEM] + [VMEM] * 8,
        out_specs=(VMEM,) * 4,
        scratch_shapes=[pltpu.VMEM((all_rows, width), jnp.bfloat16)],
        compiler_params=PARAMS,
        name="queries_part",
    )(where, *parts, w_query, query_near, query_far, query_both)
    got_near2 = across(q_send2, 1)
    got_near = across(q_send, 1)
    got_queries = across((q_keep2 + got_near2.astype(jnp.float32)).astype(jnp.bfloat16), 2)
    out_pair = jnp.stack([out_own, out_got])
    out_pair, q_send2 = lax.optimization_barrier((out_pair, q_send2))
    out_near = to_near(out_pair)
    got_keys, q_send2 = lax.optimization_barrier((across(send, 2), q_send2))
    kv = pl.pallas_call(
        keys_join_kernel,
        out_shape=shaped((LEVELS // 2 + LEVELS, tok, 2 * HD)),
        in_specs=[SMEM] + [VMEM] * 6,
        out_specs=VMEM,
        scratch_shapes=[pltpu.VMEM((all_rows, 2 * HD), jnp.float32)],
        compiler_params=PARAMS,
        name="keys_join",
    )(where, keep, got_keys, old_own, old_next, cosine, sine)
    kv_near, kv_far = to_near(kv), to_far(kv)
    kv_both = permuted(kv, lambda z, p, c: (z, p ^ 3, c))

    kv_near, kv_far, kv_both, out_near, out_pair, got_queries = lax.optimization_barrier(
        (kv_near, kv_far, kv_both, out_near, out_pair, got_queries)
    )
    out_far, out_both = to_far(out_pair), to_far(out_near)

    attended = [
        pl.pallas_call(
            functools.partial(attend_kernel, pair),
            out_shape=shaped((LEVELS * tok, 2 * HD)),
            in_specs=[SMEM] + [VMEM] * 9,
            out_specs=VMEM,
            scratch_shapes=[pltpu.VMEM((LEVELS, 2, tok, HD), jnp.bfloat16)],
            compiler_params=PARAMS,
            cost_estimate=pl.CostEstimate(
                flops=4_000_000_000, bytes_accessed=4_000_000, transcendentals=2_400_000
            ),
            name="attend",
        )(where, q_keep, got_near, got_queries, cosine, sine, kv, kv_near, kv_far, kv_both)
        for pair in range(2)
    ]
    attended += [across(each, 1) for each in attended]

    wide_cols = PLANE * w_out.shape[1]
    mine, other = pl.pallas_call(
        output_kernel,
        out_shape=(
            shaped((LEVELS, tok, wide_cols), jnp.float32),
            shaped((LEVELS, tok, wide_cols)),
        ),
        in_specs=[SMEM] + [VMEM] * 8,
        out_specs=(VMEM, VMEM),
        scratch_shapes=[pltpu.VMEM((LEVELS * tok, out_rows), jnp.bfloat16)],
        compiler_params=PARAMS,
        name="output",
    )(where, *attended, out_pair, out_near, out_far, out_both)
    got = other_core(other)
    block = [mine[d] + got[d].astype(jnp.float32) for d in range(LEVELS)]
    shares = [up(block[d].astype(jnp.bfloat16), d) for d in range(1, LEVELS)]
    return pl.pallas_call(
        finish_kernel,
        out_shape=shaped((tok, width)),
        in_specs=[SMEM] + [VMEM] * 4,
        out_specs=VMEM,
        compiler_params=PARAMS,
        name="finish",
    )(where, block[0], *shares)


def solution(mesh):
    def run(*args):
        kv_local = args[5].shape[1] // HD // mesh.shape["head"]
        levels_fit = (
            mesh.shape["seq"] == LEVELS * PLANE
            and mesh.shape["head"] == 2
            and kv_local == LEVELS
            and args[1].shape[0] == 2 * TILE_RUN
            and args[0].shape[0] == 2048
            and args[8].shape[0] == LEVELS * PLANE * CACHED
            and args[10].shape[0] == LEVELS * PLANE * REC
        )
        return jax.shard_map(
            by_levels if levels_fit else on_device,
            mesh=mesh,
            in_specs=(
                P("seq", "head"),
                P("seq", "head"),
                P("seq"),
                P(),
                P("seq", "head"),
                P("seq", "head"),
                P("seq", "head"),
                P("head", "seq"),
                P("seq", "head"),
                P("seq", "head"),
                P("seq", "head"),
                P("seq"),
            ),
            out_specs=P("seq", "head"),
            check_vma=False,
        )(*args)

    return run
```

```python
import functools

import jax
import jax.numpy as jnp
from jax import lax
from jax.experimental import pallas as pl
from jax.experimental.pallas import tpu as pltpu
from jax.sharding import PartitionSpec as P

D = 4096
HD = 128


EPSILON = 1e-05
ROPE_BASE = 1000000.0
NEG_FILL = -1e30


def rotate(values, positions):
    half = values.shape[-1] // 2
    freqs = ROPE_BASE ** (-jnp.arange(half, dtype=jnp.float32) / half)
    angles = positions[:, None] * freqs[None, :]
    cosine = jnp.cos(angles)[:, None, :]
    sine = jnp.sin(angles)[:, None, :]
    first = values[..., :half]
    second = values[..., half:]
    return jnp.concatenate(
        [first * cosine - second * sine, second * cosine + first * sine], axis=-1
    )


def scaled(rows_wide, squares, gain):
    return (rows_wide * lax.rsqrt(squares / D + EPSILON)[:, None] * gain[None, :]).astype(
        jnp.bfloat16
    )


def attend(carry, key_piece, value_piece, queries, allowed):
    best, total, accum = carry
    count = key_piece.shape[0]
    kv_local = queries.shape[0]
    keys_split = key_piece.reshape(count, kv_local, HD)
    values_split = value_piece.reshape(count, kv_local, HD)
    scores = jnp.einsum(
        "kgtd,nkd->kgtn", queries, keys_split, preferred_element_type=jnp.float32
    ) * HD ** (-0.5)
    scores = jnp.where(allowed, scores, NEG_FILL)
    fresh = jnp.maximum(best, jnp.max(scores, axis=-1))
    factor = jnp.exp(best - fresh)
    weights = jnp.where(allowed, jnp.exp(scores - fresh[..., None]), 0.0)
    total = total * factor + jnp.sum(weights, axis=-1)
    accum = accum * factor[..., None] + jnp.einsum(
        "kgtn,nkd->kgtd",
        weights.astype(jnp.bfloat16),
        values_split,
        preferred_element_type=jnp.float32,
    )
    return (fresh, total, accum)


def on_device(
    text_rows,
    picture_rows,
    picture_slots,
    norm_gain,
    w_query,
    w_key,
    w_value,
    w_out,
    cache_keys,
    cache_values,
    recompute_rows,
    recompute_slots,
):
    tok_rows = text_rows.shape[0]
    rec_count = recompute_rows.shape[0]
    cache_rows = cache_keys.shape[0]
    seq_index = lax.axis_index("seq")
    local_pos = seq_index * tok_rows + jnp.arange(tok_rows, dtype=jnp.int32)
    rows_piece = lax.all_gather(picture_rows, "seq", axis=0, tiled=True)
    slots_piece = lax.all_gather(picture_slots, "seq", axis=0, tiled=True)
    select = (slots_piece[None, :] == local_pos[:, None]).astype(jnp.bfloat16)
    placed = jnp.dot(select, rows_piece, preferred_element_type=jnp.float32)
    hits = jnp.sum(select.astype(jnp.float32), axis=1)
    added, hits = (placed, hits)
    stream = jnp.where(hits[:, None] > 0.5, added, text_rows.astype(jnp.float32)).astype(
        jnp.bfloat16
    )
    slice_width = stream.shape[1]
    gain_slice = lax.dynamic_slice_in_dim(
        norm_gain, lax.axis_index("head") * slice_width, slice_width, 0
    )
    stream_wide = stream.astype(jnp.float32)
    rec_wide = recompute_rows.astype(jnp.float32)
    stream_sq, rec_sq = lax.psum(
        (jnp.sum(stream_wide * stream_wide, axis=1), jnp.sum(rec_wide * rec_wide, axis=1)), "head"
    )
    normed, rec_normed = (
        lax.all_gather(scaled(stream_wide, stream_sq, gain_slice), "head", axis=1, tiled=True),
        lax.all_gather(scaled(rec_wide, rec_sq, gain_slice), "head", axis=1, tiled=True),
    )
    stacked = jnp.concatenate([normed, rec_normed], axis=0)
    query_cols = w_query.shape[1]
    key_cols = w_key.shape[1]
    pieces = (
        lax.all_gather(w_query, "seq", axis=0, tiled=True),
        lax.all_gather(w_key, "seq", axis=0, tiled=True),
        lax.all_gather(w_value, "seq", axis=0, tiled=True),
    )
    query_all = jnp.dot(stacked, pieces[0], preferred_element_type=jnp.float32)
    key_all = jnp.dot(stacked, pieces[1], preferred_element_type=jnp.float32)
    value_all = jnp.dot(stacked, pieces[2], preferred_element_type=jnp.float32)
    cache_total = cache_rows * lax.axis_size("seq")
    stream_pos = (cache_total + local_pos).astype(jnp.float32)
    rec_pos = recompute_slots.astype(jnp.float32)
    heads_local = query_cols // HD
    kv_local = key_cols // HD
    group = heads_local // kv_local
    rot_query = rotate(query_all[:tok_rows].reshape(tok_rows, heads_local, HD), stream_pos).astype(
        jnp.bfloat16
    )
    rot_key = (
        rotate(key_all[:tok_rows].reshape(tok_rows, kv_local, HD), stream_pos)
        .astype(jnp.bfloat16)
        .reshape(tok_rows, key_cols)
    )
    values_new = value_all[:tok_rows].astype(jnp.bfloat16)
    rot_rec_key = (
        rotate(key_all[tok_rows:].reshape(rec_count, kv_local, HD), rec_pos)
        .astype(jnp.bfloat16)
        .reshape(rec_count, key_cols)
    )
    rec_values = value_all[tok_rows:].astype(jnp.bfloat16)
    local_slots = recompute_slots - seq_index * cache_rows
    select = local_slots[:, None] == jnp.arange(cache_rows, dtype=jnp.int32)[None, :]
    replaced = jnp.any(select, axis=0)[:, None]
    select_cols = select.astype(jnp.bfloat16).T
    new_keys = jnp.dot(select_cols, rot_rec_key, preferred_element_type=jnp.float32).astype(
        jnp.bfloat16
    )
    new_values = jnp.dot(select_cols, rec_values, preferred_element_type=jnp.float32).astype(
        jnp.bfloat16
    )
    cache_k = jnp.where(replaced, new_keys, cache_keys)
    cache_v = jnp.where(replaced, new_values, cache_values)
    queries = jnp.transpose(rot_query.reshape(tok_rows, kv_local, group, HD), (1, 2, 0, 3))
    carry_start = (
        jnp.full((kv_local, group, tok_rows), NEG_FILL, jnp.float32),
        jnp.zeros((kv_local, group, tok_rows), jnp.float32),
        jnp.zeros((kv_local, group, tok_rows, HD), jnp.float32),
    )
    pieces = (
        lax.all_gather(cache_k, "seq", axis=0, tiled=True),
        lax.all_gather(cache_v, "seq", axis=0, tiled=True),
    )
    allowed = jnp.ones((tok_rows, pieces[0].shape[0]), jnp.bool_)
    carry_mid = attend(carry_start, pieces[0], pieces[1], queries, allowed)
    pieces = (
        lax.all_gather(rot_key, "seq", axis=0, tiled=True),
        lax.all_gather(values_new, "seq", axis=0, tiled=True),
    )
    key_pos = jnp.arange(pieces[0].shape[0], dtype=jnp.int32)
    allowed = key_pos[None, :] <= local_pos[:, None]
    best, total, accum = attend(carry_mid, pieces[0], pieces[1], queries, allowed)
    attended = (
        jnp.transpose(accum / total[..., None], (2, 0, 1, 3))
        .reshape(tok_rows, query_cols)
        .astype(jnp.bfloat16)
    )
    partial_out = jnp.dot(
        attended,
        lax.all_gather(w_out, "seq", axis=1, tiled=True),
        preferred_element_type=jnp.float32,
    )
    return lax.psum_scatter(
        partial_out.astype(jnp.bfloat16), "head", scatter_dimension=1, tiled=True
    )


LEVELS = 4
PLANE = 4
TILE_RUN = 256
CACHED = 64
REC = 8
REC_PAD = 16


def permuted(value, move):
    perm = []
    for level in range(LEVELS):
        for place in range(PLANE):
            for core in range(2):
                target = move(level, place, core)
                if target is not None:
                    to_level, to_place, to_core = target
                    perm.append(
                        (
                            (level * PLANE + place) * 2 + core,
                            (to_level * PLANE + to_place) * 2 + to_core,
                        )
                    )
    return lax.ppermute(value, ("seq", "head"), perm)


def across(value, bit):
    return permuted(value, lambda z, p, c: (z ^ bit, p, c))


def up(value, steps):
    return permuted(value, lambda z, p, c: ((z + steps) % LEVELS, p, c))


def other_core(value):
    return permuted(value, lambda z, p, c: (z, p, 1 - c))


def to_near(value):
    return permuted(value, lambda z, p, c: (z, p ^ (1 + c), c))


def to_far(value):
    return permuted(value, lambda z, p, c: (z, p ^ (2 - c), c))


def place_of(which, place, core):
    if which == 0:
        return place
    if which == 3:
        return place ^ 3
    return place ^ (1 + core) if which == 1 else place ^ (2 - core)


def turned(values, cosine, sine):
    return values * cosine + pltpu.roll(values, HD // 2, 1) * sine


def pack_kernel(where_ref, *refs):
    w_key, w_value, cache_keys, cache_values, slots = refs[:5]
    outs, sems = refs[5:7], refs[7]
    level = where_ref[0]
    depth = w_key.shape[0]
    copies = []

    def copy(source, target):
        copies.append(pltpu.make_async_copy(source, target, sems.at[len(copies)]))
        copies[-1].start()

    for n in range(2):
        keys = outs[n]
        for m in range(2):
            at = jnp.bitwise_xor(level, n + 2 * m)
            small = pl.ds(pl.multiple_of(at * HD, HD), HD)
            for k, (new, old) in enumerate(((w_key, cache_keys), (w_value, cache_values))):
                to = pl.ds((2 * m + k) * HD, HD)
                copy(new.at[:, small], keys.at[0:depth, to])
                copy(old.at[:, small], keys.at[depth : depth + CACHED, to])
        copy(slots, keys.at[depth + CACHED : depth + CACHED + REC_PAD])
    for each in copies:
        each.wait()


PACK_COPIES = 18


def assemble(where_ref, parts, x_ref):
    level, core = where_ref[0], where_ref[2]
    shown = TILE_RUN // 2 // PLANE
    rows = parts[0].shape[0] - shown
    for n, part in enumerate(parts):
        x_ref[n * rows : (n + 1) * rows] = part[0:rows]
    start = where_ref[4] * rows
    for n, part in enumerate(parts):
        which = 2 * lax.rem(level + n % 2, 2) + (core if n < 2 else 1 - core)
        to = pl.multiple_of(start + which * shown, 16)
        x_ref[pl.ds(to, shown)] = part[rows : rows + shown]


def products(where_ref, x_ref, pieces):
    level, place, core = where_ref[0], where_ref[1], where_ref[2]
    total = None
    for i in range(2):
        for j in range(PLANE):
            depth = pieces[i][j].shape[0]
            block = lax.rem(level + i, 2) * PLANE + place_of(j, place, core)
            start = pl.multiple_of(block * depth, depth)
            part = jnp.dot(
                x_ref[:, pl.ds(start, depth)],
                pieces[i][j][...],
                preferred_element_type=jnp.float32,
            )
            total = part if total is None else total + part
    return total


def keys_part_kernel(
    where_ref, x0, x1, x2, x3, own, near, far, old0, old1, keep_ref, send_ref, x_ref
):
    assemble(where_ref, (x0, x1, x2, x3), x_ref)
    pieces = [[own.at[i], near.at[i], far.at[i], far.at[2 + i]] for i in range(2)]
    width = 2 * HD
    total = products(where_ref, x_ref, pieces)
    at = total.shape[0]
    keep_ref[...] = total[:, :width]
    send_ref[0:at] = total[:, width:].astype(jnp.bfloat16)
    for old in (old0, old1):
        send_ref[at : at + CACHED + REC_PAD] = old[:, width:]
        at += CACHED + REC_PAD


def keys_join_kernel(where_ref, keep_ref, got_ref, old0, old1, cos_ref, sin_ref, kv_ref, sum_ref):
    level = where_ref[0]
    rows = sum_ref.shape[0]
    block = rows // LEVELS
    tok = block - REC_PAD
    width = 2 * HD
    sum_ref[...] = keep_ref[...] + got_ref[0:rows].astype(jnp.float32)
    first = where_ref[3]
    span = CACHED + REC_PAD
    for n in range(LEVELS):
        at = jnp.bitwise_xor(level, n)
        start = pl.multiple_of(lax.rem(first + n, LEVELS) * block, 16)
        cosine, sine = cos_ref[at], sin_ref[at]
        fresh = sum_ref[pl.ds(start, tok), :]
        kv_ref[2 + at, :, 0:HD] = turned(fresh[:, :HD], cosine[:tok], sine[:tok]).astype(
            jnp.bfloat16
        )
        kv_ref[2 + at, :, HD:width] = fresh[:, HD:].astype(jnp.bfloat16)
        if n < 2:
            old = (old0, old1)[n][:, 0:width].astype(jnp.float32)
        else:
            old = got_ref[rows + (n - 2) * span : rows + (n - 1) * span].astype(jnp.float32)
        slots = old[CACHED : CACHED + REC].astype(jnp.int32)
        rec = sum_ref[pl.ds(pl.multiple_of(start + tok, 16), REC_PAD), :]
        line = lax.broadcasted_iota(jnp.int32, (CACHED, width), 0)
        found = jnp.zeros((CACHED, width), jnp.float32)
        hit = jnp.zeros((CACHED, width), jnp.int32)
        for r in range(REC):
            same = line == slots[r : r + 1]
            found = jnp.where(same, rec[r : r + 1], found)
            hit = jnp.where(same, 1, hit)
        keys = turned(found[:, :HD], cosine[tok : tok + CACHED], sine[tok : tok + CACHED])
        found = jnp.concatenate([keys, found[:, HD:]], axis=1)
        line_at = pl.multiple_of(lax.rem(at, 2) * CACHED, CACHED)
        kv_ref[at // 2, pl.ds(line_at, CACHED), :] = jnp.where(
            hit == 1, found, old[:CACHED]
        ).astype(jnp.bfloat16)


def queries_part_kernel(where_ref, x0, x1, x2, x3, *refs):
    weights, outs, x_ref = refs[:4], refs[4:8], refs[8]
    level, place, core = where_ref[0], where_ref[1], where_ref[2]
    assemble(where_ref, (x0, x1, x2, x3), x_ref)
    depth = weights[0].shape[0]
    width = 4 * HD
    block = x_ref.shape[0] // LEVELS
    tok = block - REC_PAD
    for m, out_ref in zip((0, 2, 1, 3), outs):
        group = pl.ds(pl.multiple_of(jnp.bitwise_xor(level, m) * width, width), width)
        total = None
        for j in range(PLANE):
            at = lax.rem(level, 2) * PLANE + place_of(j, place, core)
            part = jnp.dot(
                x_ref[:, pl.ds(pl.multiple_of(at * depth, depth), depth)],
                weights[j][:, group],
                preferred_element_type=jnp.float32,
            )
            total = part if total is None else total + part
        for k in range(LEVELS):
            at = jnp.bitwise_xor(level, lax.rem(k + LEVELS - where_ref[3], LEVELS))
            out_ref[at] = total[k * block : k * block + tok].astype(out_ref.dtype)


def attend_kernel(
    pair, where_ref, keep_ref, near_ref, got_ref, cos_ref, sin_ref, kv0, kv1, kv2, kv3, out_ref, query_ref
):
    level, place, core = where_ref[0], where_ref[1], where_ref[2]
    pieces = (kv0, kv1, kv2, kv3)
    tok = keep_ref.shape[1]
    old = LEVELS // 2
    heads = query_ref.shape[1]
    columns = slice(pair * heads * HD, (pair + 1) * heads * HD)
    for at in range(LEVELS):
        total = keep_ref[at, :, columns] + (
            near_ref[at, :, columns].astype(jnp.float32)
            + got_ref[at, :, columns].astype(jnp.float32)
        )
        cosine, sine = cos_ref[at][:tok], sin_ref[at][:tok]
        for h in range(heads):
            head = turned(total[:, h * HD : (h + 1) * HD], cosine, sine)
            query_ref[at, h] = head.astype(jnp.bfloat16)
    row = lax.broadcasted_iota(jnp.int32, (tok, tok), 0)
    col = lax.broadcasted_iota(jnp.int32, (tok, tok), 1)
    scale = HD ** (-0.5) * 1.4426950408889634
    for i in range(LEVELS):
        count = (old + i + 1) * tok
        queries = query_ref[i].reshape(heads * tok, HD)
        scores = []
        best = None
        for j in range(PLANE):
            keys = pieces[j][0 : old + i + 1, :, 0:HD].reshape(count, HD)
            raw = lax.dot_general(
                queries, keys, (((1,), (1,)), ((), ())), preferred_element_type=jnp.float32
            )
            if j == 0:
                allowed = col <= row
            else:
                allowed = jnp.broadcast_to(place_of(j, place, core), (tok, tok)) < place
            allowed = jnp.concatenate([allowed] * heads, axis=0)
            last = jnp.where(allowed, raw[:, count - tok :], NEG_FILL)
            raw = jnp.concatenate([raw[:, : count - tok], last], axis=1)
            top = jnp.max(raw, axis=1, keepdims=True)
            best = top if best is None else jnp.maximum(best, top)
            scores.append(raw)
        total, accum = 0.0, 0.0
        for j in range(PLANE):
            weights = jnp.exp2((scores[j] - best) * scale)
            total = total + jnp.sum(weights, axis=1, keepdims=True)
            values = pieces[j][0 : old + i + 1, :, HD : 2 * HD].reshape(count, HD)
            accum = accum + jnp.dot(
                weights.astype(jnp.bfloat16), values, preferred_element_type=jnp.float32
            )
        result = (accum / total).astype(jnp.bfloat16)
        for h in range(heads):
            out_ref[i * tok : (i + 1) * tok, h * HD : (h + 1) * HD] = result[
                h * tok : (h + 1) * tok
            ]


def output_kernel(where_ref, *refs):
    heads, weights, (mine_ref, other_ref, x_ref) = refs[:4], refs[4:-3], refs[-3:]
    level, core = where_ref[0], where_ref[2]
    depth = heads[0].shape[1]
    width = weights[0].shape[2]
    tok = mine_ref.shape[1]
    for n, ref in enumerate(heads):
        at = 2 * lax.rem(level + n // 2, 2) + n % 2
        x_ref[:, pl.ds(pl.multiple_of(at * depth, depth), depth)] = ref[...]
    swap = jnp.where(core == level // 2, 0, 1)
    for s, out_ref in enumerate((mine_ref, other_ref)):
        i = jnp.bitwise_xor(swap, s)
        for j, piece in enumerate(weights):
            slot = (0, 2, 1, 3)[j] if s else j
            part = jnp.dot(x_ref[...], piece[i], preferred_element_type=jnp.float32)
            for t in range(LEVELS):
                out_ref[
                    lax.rem(t + LEVELS - level, LEVELS), :, slot * width : (slot + 1) * width
                ] = part[t * tok : (t + 1) * tok].astype(out_ref.dtype)


def finish_kernel(where_ref, own, first, second, third, out_ref):
    level, place, core = where_ref[0], where_ref[1], where_ref[2]
    half = out_ref.shape[1] // 2
    width = half // PLANE
    sums = (
        own[...] + second[...].astype(jnp.float32),
        first[...].astype(jnp.float32) + third[...].astype(jnp.float32),
    )
    for steps, total in enumerate(sums):
        for j in range(PLANE):
            at = lax.rem(level + steps, 2) * half + place_of(j, place, core) * width
            out_ref[:, pl.ds(pl.multiple_of(at, width), width)] = total[
                :, j * width : (j + 1) * width
            ].astype(out_ref.dtype)


SMEM = pl.BlockSpec(memory_space=pltpu.SMEM)
VMEM = pl.BlockSpec(memory_space=pltpu.VMEM)
HBM = pl.BlockSpec(memory_space=pltpu.MemorySpace.HBM)
PARAMS = pltpu.CompilerParams(vmem_limit_bytes=48 * 1024 * 1024)


def shaped(shape, dtype=jnp.bfloat16):
    return jax.ShapeDtypeStruct(shape, dtype)


def by_levels(
    text_rows,
    picture_rows,
    picture_slots,
    norm_gain,
    w_query,
    w_key,
    w_value,
    w_out,
    cache_keys,
    cache_values,
    recompute_rows,
    recompute_slots,
):
    seq_index = lax.axis_index("seq")
    core = lax.axis_index("head")
    level, place = seq_index // PLANE, seq_index % PLANE
    half_at = level // 2
    own_first = core == half_at
    tok, width = text_rows.shape
    block_rows = tok + REC_PAD

    stream_len = tok * LEVELS * PLANE
    tile_owners = TILE_RUN // tok
    first = stream_len // 2 // tok
    last = (stream_len - TILE_RUN) // tok
    owners = [first + i for i in range(tile_owners)] + [last + i for i in range(tile_owners)]
    assert [owner % PLANE for owner in owners] == list(range(LEVELS))
    owner_level = jnp.where(place < tile_owners, first // PLANE, last // PLANE)

    first_block = jnp.where(own_first, 0, 2)
    shown_block = (first_block + (level ^ owner_level)) % LEVELS
    where = jnp.stack([level, place, core, first_block, shown_block]).astype(jnp.int32)

    slots = (recompute_slots - seq_index * CACHED).astype(jnp.bfloat16)
    slot_rows = jnp.broadcast_to(jnp.pad(slots, (0, REC_PAD - REC))[:, None], (REC_PAD, 4 * HD))
    depth = w_key.shape[0]
    key_own, key_give = pl.pallas_call(
        pack_kernel,
        out_shape=(shaped((depth + CACHED + REC_PAD, 4 * HD)),) * 2,
        in_specs=[SMEM] + [HBM] * 5,
        out_specs=(HBM,) * 2,
        scratch_shapes=[pltpu.SemaphoreType.DMA((PACK_COPIES,))],
        compiler_params=PARAMS,
        name="pack",
    )(where, w_key, w_value, cache_keys, cache_values, slot_rows)

    rows = jnp.concatenate(
        [text_rows, recompute_rows, jnp.zeros((REC_PAD - REC, width), text_rows.dtype)], axis=0
    )
    gain = lax.dynamic_slice_in_dim(norm_gain, core * width, width, 0)
    wide, pictures = rows.astype(jnp.float32), picture_rows.astype(jnp.float32)
    squares, picture_squares = lax.psum(
        (jnp.sum(wide * wide, axis=1), jnp.sum(pictures * pictures, axis=1)), "head"
    )
    normed = scaled(wide, squares, gain)
    pictures = scaled(pictures, picture_squares, gain)

    out_rows = w_out.shape[0] // 2
    out_own, out_give = (
        lax.dynamic_slice_in_dim(w_out, at * out_rows, out_rows, 0) for at in (half_at, 1 - half_at)
    )

    crossed = permuted(normed, lambda z, p, c: (z ^ 2, p, 1 - c) if c == 1 - z // 2 else None)
    shown = permuted(pictures, lambda z, p, c: (2 * c + p // 2, z, p % 2))
    key_next = across(key_give, 1)
    query_near, query_far = to_near(w_query), to_far(w_query)
    query_near, query_far = lax.optimization_barrier((query_near, query_far))
    query_both = to_far(query_near)
    shown, key_next = lax.optimization_barrier((shown, key_next))
    keys = jnp.stack([key_own[:depth], key_next[:depth]])
    old_own, old_next = key_own[depth:], key_next[depth:]
    keys_near = to_near(keys)
    crossed, shown, out_give = lax.optimization_barrier((crossed, shown, out_give))
    held = jnp.concatenate([jnp.where(own_first, normed, crossed), shown], axis=0)
    next_rows = across(held, 1)
    held_other = other_core(held)
    out_half = out_rows // 2
    out_got0 = across(out_give[:out_half], 2)
    out_got1 = across(out_give[out_half:], 2)
    next_rows, out_got0 = lax.optimization_barrier((next_rows, out_got0))
    next_other = other_core(next_rows)
    keys_far = to_far(jnp.concatenate([keys, keys_near], axis=0))
    next_other, held_other, keys_far, query_both, out_got1 = lax.optimization_barrier(
        (next_other, held_other, keys_far, query_both, out_got1)
    )
    parts = (held, next_rows, held_other, next_other)

    half = HD // 2
    freqs = ROPE_BASE ** (-jnp.arange(half, dtype=jnp.float32) / half)
    blocks = (jnp.arange(LEVELS, dtype=jnp.int32) * PLANE + place)[:, None]
    stream_pos = (
        CACHED * LEVELS * PLANE + blocks * tok + jnp.arange(tok, dtype=jnp.int32)[None]
    ).astype(jnp.float32)
    cache_pos = (blocks * CACHED + jnp.arange(CACHED, dtype=jnp.int32)[None]).astype(jnp.float32)
    angles = jnp.concatenate([stream_pos, cache_pos], axis=1)[..., None] * freqs
    cosine, sine = jnp.cos(angles), jnp.sin(angles)
    cosine = jnp.concatenate([cosine, cosine], axis=-1)
    sine = jnp.concatenate([-sine, sine], axis=-1)

    all_rows = LEVELS * block_rows
    keep, send = pl.pallas_call(
        keys_part_kernel,
        out_shape=(
            shaped((all_rows, 2 * HD), jnp.float32),
            shaped((all_rows + 2 * (CACHED + REC_PAD), 2 * HD)),
        ),
        in_specs=[SMEM] + [VMEM] * 9,
        out_specs=(VMEM, VMEM),
        scratch_shapes=[pltpu.VMEM((all_rows, width), jnp.bfloat16)],
        compiler_params=PARAMS,
        cost_estimate=pl.CostEstimate(
            flops=3_000_000_000, bytes_accessed=4_000_000, transcendentals=0
        ),
        name="keys_part",
    )(where, *parts, keys, keys_near, keys_far, old_own, old_next)
    send, *parts = lax.optimization_barrier((send, *parts))
    group_shape = (LEVELS, tok, 4 * HD)
    q_keep, q_keep2, q_send, q_send2 = pl.pallas_call(
        queries_part_kernel,
        out_shape=(shaped(group_shape, jnp.float32),) * 2 + (shaped(group_shape),) * 2,
        in_specs=[SMEM] + [VMEM] * 8,
        out_specs=(VMEM,) * 4,
        scratch_shapes=[pltpu.VMEM((all_rows, width), jnp.bfloat16)],
        compiler_params=PARAMS,
        cost_estimate=pl.CostEstimate(
            flops=5_000_000_000, bytes_accessed=4_000_000, transcendentals=0
        ),
        name="queries_part",
    )(where, *parts, w_query, query_near, query_far, query_both)
    got_near2 = across(q_send2, 1)
    got_near = across(q_send, 1)
    got_queries = across((q_keep2 + got_near2.astype(jnp.float32)).astype(jnp.bfloat16), 2)
    out_pair = jnp.stack([out_own, jnp.concatenate([out_got0, out_got1], axis=0)])
    out_pair, q_send2 = lax.optimization_barrier((out_pair, q_send2))
    out_near = to_near(out_pair)
    got_keys, q_send2 = lax.optimization_barrier((across(send, 2), q_send2))
    kv = pl.pallas_call(
        keys_join_kernel,
        out_shape=shaped((LEVELS // 2 + LEVELS, tok, 2 * HD)),
        in_specs=[SMEM] + [VMEM] * 6,
        out_specs=VMEM,
        scratch_shapes=[pltpu.VMEM((all_rows, 2 * HD), jnp.float32)],
        compiler_params=PARAMS,
        cost_estimate=pl.CostEstimate(
            flops=12_000_000_000, bytes_accessed=4_000_000, transcendentals=0
        ),
        name="keys_join",
    )(where, keep, got_keys, old_own, old_next, cosine, sine)
    kv_near, kv_far = to_near(kv), to_far(kv)
    kv_both = permuted(kv, lambda z, p, c: (z, p ^ 3, c))

    kv_near, kv_far, kv_both, out_near, out_pair, got_queries = lax.optimization_barrier(
        (kv_near, kv_far, kv_both, out_near, out_pair, got_queries)
    )
    out_far, out_both = to_far(out_pair), to_far(out_near)

    attended = [
        pl.pallas_call(
            functools.partial(attend_kernel, pair),
            out_shape=shaped((LEVELS * tok, 2 * HD)),
            in_specs=[SMEM] + [VMEM] * 9,
            out_specs=VMEM,
            scratch_shapes=[pltpu.VMEM((LEVELS, 2, tok, HD), jnp.bfloat16)],
            compiler_params=PARAMS,
            cost_estimate=pl.CostEstimate(
                flops=4_000_000_000, bytes_accessed=4_000_000, transcendentals=2_400_000
            ),
            name="attend",
        )(where, q_keep, got_near, got_queries, cosine, sine, kv, kv_near, kv_far, kv_both)
        for pair in range(2)
    ]
    attended += [across(each, 1) for each in attended]

    wide_cols = PLANE * w_out.shape[1]
    mine, other = pl.pallas_call(
        output_kernel,
        out_shape=(
            shaped((LEVELS, tok, wide_cols), jnp.float32),
            shaped((LEVELS, tok, wide_cols)),
        ),
        in_specs=[SMEM] + [VMEM] * 8,
        out_specs=(VMEM, VMEM),
        scratch_shapes=[pltpu.VMEM((LEVELS * tok, out_rows), jnp.bfloat16)],
        compiler_params=PARAMS,
        cost_estimate=pl.CostEstimate(
            flops=5_000_000_000, bytes_accessed=4_000_000, transcendentals=0
        ),
        name="output",
    )(where, *attended, out_pair, out_near, out_far, out_both)
    got = other_core(other)
    block = [mine[d] + got[d].astype(jnp.float32) for d in range(LEVELS)]
    shares = [up(block[d].astype(jnp.bfloat16), d) for d in range(1, LEVELS)]
    return pl.pallas_call(
        finish_kernel,
        out_shape=shaped((tok, width)),
        in_specs=[SMEM] + [VMEM] * 4,
        out_specs=VMEM,
        compiler_params=PARAMS,
        name="finish",
    )(where, block[0], *shares)


def solution(mesh):
    def run(*args):
        kv_local = args[5].shape[1] // HD // mesh.shape["head"]
        levels_fit = (
            mesh.shape["seq"] == LEVELS * PLANE
            and mesh.shape["head"] == 2
            and kv_local == LEVELS
            and args[1].shape[0] == 2 * TILE_RUN
            and args[0].shape[0] == 2048
            and args[8].shape[0] == LEVELS * PLANE * CACHED
            and args[10].shape[0] == LEVELS * PLANE * REC
        )
        return jax.shard_map(
            by_levels if levels_fit else on_device,
            mesh=mesh,
            in_specs=(
                P("seq", "head"),
                P("seq", "head"),
                P("seq"),
                P(),
                P("seq", "head"),
                P("seq", "head"),
                P("seq", "head"),
                P("head", "seq"),
                P("seq", "head"),
                P("seq", "head"),
                P("seq", "head"),
                P("seq"),
            ),
            out_specs=P("seq", "head"),
            check_vma=False,
        )(*args)

    return run
```

```python
import functools

import jax
import jax.numpy as jnp
from jax import lax
from jax.experimental import pallas as pl
from jax.experimental.pallas import tpu as pltpu
from jax.sharding import PartitionSpec as P

D = 4096
HD = 128


EPSILON = 1e-05
ROPE_BASE = 1000000.0
NEG_FILL = -1e30


def rotate(values, positions):
    half = values.shape[-1] // 2
    freqs = ROPE_BASE ** (-jnp.arange(half, dtype=jnp.float32) / half)
    angles = positions[:, None] * freqs[None, :]
    cosine = jnp.cos(angles)[:, None, :]
    sine = jnp.sin(angles)[:, None, :]
    first = values[..., :half]
    second = values[..., half:]
    return jnp.concatenate(
        [first * cosine - second * sine, second * cosine + first * sine], axis=-1
    )


def scaled(rows_wide, squares, gain):
    return (rows_wide * lax.rsqrt(squares / D + EPSILON)[:, None] * gain[None, :]).astype(
        jnp.bfloat16
    )


def attend(carry, key_piece, value_piece, queries, allowed):
    best, total, accum = carry
    count = key_piece.shape[0]
    kv_local = queries.shape[0]
    keys_split = key_piece.reshape(count, kv_local, HD)
    values_split = value_piece.reshape(count, kv_local, HD)
    scores = jnp.einsum(
        "kgtd,nkd->kgtn", queries, keys_split, preferred_element_type=jnp.float32
    ) * HD ** (-0.5)
    scores = jnp.where(allowed, scores, NEG_FILL)
    fresh = jnp.maximum(best, jnp.max(scores, axis=-1))
    factor = jnp.exp(best - fresh)
    weights = jnp.where(allowed, jnp.exp(scores - fresh[..., None]), 0.0)
    total = total * factor + jnp.sum(weights, axis=-1)
    accum = accum * factor[..., None] + jnp.einsum(
        "kgtn,nkd->kgtd",
        weights.astype(jnp.bfloat16),
        values_split,
        preferred_element_type=jnp.float32,
    )
    return (fresh, total, accum)


def on_device(
    text_rows,
    picture_rows,
    picture_slots,
    norm_gain,
    w_query,
    w_key,
    w_value,
    w_out,
    cache_keys,
    cache_values,
    recompute_rows,
    recompute_slots,
):
    tok_rows = text_rows.shape[0]
    rec_count = recompute_rows.shape[0]
    cache_rows = cache_keys.shape[0]
    seq_index = lax.axis_index("seq")
    local_pos = seq_index * tok_rows + jnp.arange(tok_rows, dtype=jnp.int32)
    rows_piece = lax.all_gather(picture_rows, "seq", axis=0, tiled=True)
    slots_piece = lax.all_gather(picture_slots, "seq", axis=0, tiled=True)
    select = (slots_piece[None, :] == local_pos[:, None]).astype(jnp.bfloat16)
    placed = jnp.dot(select, rows_piece, preferred_element_type=jnp.float32)
    hits = jnp.sum(select.astype(jnp.float32), axis=1)
    added, hits = (placed, hits)
    stream = jnp.where(hits[:, None] > 0.5, added, text_rows.astype(jnp.float32)).astype(
        jnp.bfloat16
    )
    slice_width = stream.shape[1]
    gain_slice = lax.dynamic_slice_in_dim(
        norm_gain, lax.axis_index("head") * slice_width, slice_width, 0
    )
    stream_wide = stream.astype(jnp.float32)
    rec_wide = recompute_rows.astype(jnp.float32)
    stream_sq, rec_sq = lax.psum(
        (jnp.sum(stream_wide * stream_wide, axis=1), jnp.sum(rec_wide * rec_wide, axis=1)), "head"
    )
    normed, rec_normed = (
        lax.all_gather(scaled(stream_wide, stream_sq, gain_slice), "head", axis=1, tiled=True),
        lax.all_gather(scaled(rec_wide, rec_sq, gain_slice), "head", axis=1, tiled=True),
    )
    stacked = jnp.concatenate([normed, rec_normed], axis=0)
    query_cols = w_query.shape[1]
    key_cols = w_key.shape[1]
    pieces = (
        lax.all_gather(w_query, "seq", axis=0, tiled=True),
        lax.all_gather(w_key, "seq", axis=0, tiled=True),
        lax.all_gather(w_value, "seq", axis=0, tiled=True),
    )
    query_all = jnp.dot(stacked, pieces[0], preferred_element_type=jnp.float32)
    key_all = jnp.dot(stacked, pieces[1], preferred_element_type=jnp.float32)
    value_all = jnp.dot(stacked, pieces[2], preferred_element_type=jnp.float32)
    cache_total = cache_rows * lax.axis_size("seq")
    stream_pos = (cache_total + local_pos).astype(jnp.float32)
    rec_pos = recompute_slots.astype(jnp.float32)
    heads_local = query_cols // HD
    kv_local = key_cols // HD
    group = heads_local // kv_local
    rot_query = rotate(query_all[:tok_rows].reshape(tok_rows, heads_local, HD), stream_pos).astype(
        jnp.bfloat16
    )
    rot_key = (
        rotate(key_all[:tok_rows].reshape(tok_rows, kv_local, HD), stream_pos)
        .astype(jnp.bfloat16)
        .reshape(tok_rows, key_cols)
    )
    values_new = value_all[:tok_rows].astype(jnp.bfloat16)
    rot_rec_key = (
        rotate(key_all[tok_rows:].reshape(rec_count, kv_local, HD), rec_pos)
        .astype(jnp.bfloat16)
        .reshape(rec_count, key_cols)
    )
    rec_values = value_all[tok_rows:].astype(jnp.bfloat16)
    local_slots = recompute_slots - seq_index * cache_rows
    select = local_slots[:, None] == jnp.arange(cache_rows, dtype=jnp.int32)[None, :]
    replaced = jnp.any(select, axis=0)[:, None]
    select_cols = select.astype(jnp.bfloat16).T
    new_keys = jnp.dot(select_cols, rot_rec_key, preferred_element_type=jnp.float32).astype(
        jnp.bfloat16
    )
    new_values = jnp.dot(select_cols, rec_values, preferred_element_type=jnp.float32).astype(
        jnp.bfloat16
    )
    cache_k = jnp.where(replaced, new_keys, cache_keys)
    cache_v = jnp.where(replaced, new_values, cache_values)
    queries = jnp.transpose(rot_query.reshape(tok_rows, kv_local, group, HD), (1, 2, 0, 3))
    carry_start = (
        jnp.full((kv_local, group, tok_rows), NEG_FILL, jnp.float32),
        jnp.zeros((kv_local, group, tok_rows), jnp.float32),
        jnp.zeros((kv_local, group, tok_rows, HD), jnp.float32),
    )
    pieces = (
        lax.all_gather(cache_k, "seq", axis=0, tiled=True),
        lax.all_gather(cache_v, "seq", axis=0, tiled=True),
    )
    allowed = jnp.ones((tok_rows, pieces[0].shape[0]), jnp.bool_)
    carry_mid = attend(carry_start, pieces[0], pieces[1], queries, allowed)
    pieces = (
        lax.all_gather(rot_key, "seq", axis=0, tiled=True),
        lax.all_gather(values_new, "seq", axis=0, tiled=True),
    )
    key_pos = jnp.arange(pieces[0].shape[0], dtype=jnp.int32)
    allowed = key_pos[None, :] <= local_pos[:, None]
    best, total, accum = attend(carry_mid, pieces[0], pieces[1], queries, allowed)
    attended = (
        jnp.transpose(accum / total[..., None], (2, 0, 1, 3))
        .reshape(tok_rows, query_cols)
        .astype(jnp.bfloat16)
    )
    partial_out = jnp.dot(
        attended,
        lax.all_gather(w_out, "seq", axis=1, tiled=True),
        preferred_element_type=jnp.float32,
    )
    return lax.psum_scatter(
        partial_out.astype(jnp.bfloat16), "head", scatter_dimension=1, tiled=True
    )


LEVELS = 4
PLANE = 4
TILE_RUN = 256
CACHED = 64
REC = 8
REC_PAD = 16


def permuted(value, move):
    perm = []
    for level in range(LEVELS):
        for place in range(PLANE):
            for core in range(2):
                target = move(level, place, core)
                if target is not None:
                    to_level, to_place, to_core = target
                    perm.append(
                        (
                            (level * PLANE + place) * 2 + core,
                            (to_level * PLANE + to_place) * 2 + to_core,
                        )
                    )
    return lax.ppermute(value, ("seq", "head"), perm)


def across(value, bit):
    return permuted(value, lambda z, p, c: (z ^ bit, p, c))


def up(value, steps):
    return permuted(value, lambda z, p, c: ((z + steps) % LEVELS, p, c))


def other_core(value):
    return permuted(value, lambda z, p, c: (z, p, 1 - c))


def to_near(value):
    return permuted(value, lambda z, p, c: (z, p ^ (1 + c), c))


def to_far(value):
    return permuted(value, lambda z, p, c: (z, p ^ (2 - c), c))


def place_of(which, place, core):
    if which == 0:
        return place
    if which == 3:
        return place ^ 3
    return place ^ (1 + core) if which == 1 else place ^ (2 - core)


def turned(values, cosine, sine):
    return values * cosine + pltpu.roll(values, HD // 2, 1) * sine


def pack_kernel(where_ref, *refs):
    w_key, w_value, cache_keys, cache_values, slots = refs[:5]
    outs, sems = refs[5:7], refs[7]
    level = where_ref[0]
    depth = w_key.shape[0]
    copies = []

    def copy(source, target):
        copies.append(pltpu.make_async_copy(source, target, sems.at[len(copies)]))
        copies[-1].start()

    for n in range(2):
        keys = outs[n]
        for m in range(2):
            at = jnp.bitwise_xor(level, n + 2 * m)
            small = pl.ds(pl.multiple_of(at * HD, HD), HD)
            for k, (new, old) in enumerate(((w_key, cache_keys), (w_value, cache_values))):
                to = pl.ds((2 * m + k) * HD, HD)
                copy(new.at[:, small], keys.at[0:depth, to])
                copy(old.at[:, small], keys.at[depth : depth + CACHED, to])
        copy(slots, keys.at[depth + CACHED : depth + CACHED + REC_PAD])
    for each in copies:
        each.wait()


PACK_COPIES = 18


def assemble(where_ref, parts, x_ref):
    level, core = where_ref[0], where_ref[2]
    shown = TILE_RUN // 2 // PLANE
    rows = parts[0].shape[0] - shown
    for n, part in enumerate(parts):
        x_ref[n * rows : (n + 1) * rows] = part[0:rows]
    start = where_ref[4] * rows
    for n, part in enumerate(parts):
        which = 2 * lax.rem(level + n % 2, 2) + (core if n < 2 else 1 - core)
        to = pl.multiple_of(start + which * shown, 16)
        x_ref[pl.ds(to, shown)] = part[rows : rows + shown]


def products(where_ref, x_ref, pieces):
    level, place, core = where_ref[0], where_ref[1], where_ref[2]
    total = None
    for i in range(2):
        for j in range(PLANE):
            depth = pieces[i][j].shape[0]
            block = lax.rem(level + i, 2) * PLANE + place_of(j, place, core)
            start = pl.multiple_of(block * depth, depth)
            part = jnp.dot(
                x_ref[:, pl.ds(start, depth)],
                pieces[i][j][...],
                preferred_element_type=jnp.float32,
            )
            total = part if total is None else total + part
    return total


def keys_part_kernel(
    where_ref, x0, x1, x2, x3, own, near, far, old0, old1, keep_ref, send_ref, x_ref
):
    assemble(where_ref, (x0, x1, x2, x3), x_ref)
    pieces = [[own.at[i], near.at[i], far.at[i], far.at[2 + i]] for i in range(2)]
    width = 2 * HD
    total = products(where_ref, x_ref, pieces)
    at = total.shape[0]
    keep_ref[...] = total[:, :width]
    send_ref[0:at] = total[:, width:].astype(jnp.bfloat16)
    for old in (old0, old1):
        send_ref[at : at + CACHED + REC_PAD] = old[:, width:]
        at += CACHED + REC_PAD


def keys_join_kernel(where_ref, keep_ref, got_ref, old0, old1, cos_ref, sin_ref, kv_ref, sum_ref):
    level = where_ref[0]
    rows = sum_ref.shape[0]
    block = rows // LEVELS
    tok = block - REC_PAD
    width = 2 * HD
    sum_ref[...] = keep_ref[...] + got_ref[0:rows].astype(jnp.float32)
    first = where_ref[3]
    span = CACHED + REC_PAD
    for n in range(LEVELS):
        at = jnp.bitwise_xor(level, n)
        start = pl.multiple_of(lax.rem(first + n, LEVELS) * block, 16)
        cosine, sine = cos_ref[at], sin_ref[at]
        fresh = sum_ref[pl.ds(start, tok), :]
        kv_ref[2 + at, :, 0:HD] = turned(fresh[:, :HD], cosine[:tok], sine[:tok]).astype(
            jnp.bfloat16
        )
        kv_ref[2 + at, :, HD:width] = fresh[:, HD:].astype(jnp.bfloat16)
        if n < 2:
            old = (old0, old1)[n][:, 0:width].astype(jnp.float32)
        else:
            old = got_ref[rows + (n - 2) * span : rows + (n - 1) * span].astype(jnp.float32)
        slots = old[CACHED : CACHED + REC].astype(jnp.int32)
        rec = sum_ref[pl.ds(pl.multiple_of(start + tok, 16), REC_PAD), :]
        line = lax.broadcasted_iota(jnp.int32, (CACHED, width), 0)
        found = jnp.zeros((CACHED, width), jnp.float32)
        hit = jnp.zeros((CACHED, width), jnp.int32)
        for r in range(REC):
            same = line == slots[r : r + 1]
            found = jnp.where(same, rec[r : r + 1], found)
            hit = jnp.where(same, 1, hit)
        keys = turned(found[:, :HD], cosine[tok : tok + CACHED], sine[tok : tok + CACHED])
        found = jnp.concatenate([keys, found[:, HD:]], axis=1)
        line_at = pl.multiple_of(lax.rem(at, 2) * CACHED, CACHED)
        kv_ref[at // 2, pl.ds(line_at, CACHED), :] = jnp.where(
            hit == 1, found, old[:CACHED]
        ).astype(jnp.bfloat16)


def queries_part_kernel(where_ref, x0, x1, x2, x3, *refs):
    weights, outs, x_ref = refs[:4], refs[4:8], refs[8]
    level, place, core = where_ref[0], where_ref[1], where_ref[2]
    assemble(where_ref, (x0, x1, x2, x3), x_ref)
    depth = weights[0].shape[0]
    width = 4 * HD
    block = x_ref.shape[0] // LEVELS
    tok = block - REC_PAD
    for m, out_ref in zip((0, 2, 1, 3), outs):
        group = pl.ds(pl.multiple_of(jnp.bitwise_xor(level, m) * width, width), width)
        total = None
        for j in range(PLANE):
            at = lax.rem(level, 2) * PLANE + place_of(j, place, core)
            part = jnp.dot(
                x_ref[:, pl.ds(pl.multiple_of(at * depth, depth), depth)],
                weights[j][:, group],
                preferred_element_type=jnp.float32,
            )
            total = part if total is None else total + part
        for k in range(LEVELS):
            at = jnp.bitwise_xor(level, lax.rem(k + LEVELS - where_ref[3], LEVELS))
            out_ref[at] = total[k * block : k * block + tok].astype(out_ref.dtype)


def attend_kernel(
    pair, where_ref, keep_ref, near_ref, got_ref, cos_ref, sin_ref, kv0, kv1, kv2, kv3, out_ref, query_ref
):
    level, place, core = where_ref[0], where_ref[1], where_ref[2]
    pieces = (kv0, kv1, kv2, kv3)
    tok = keep_ref.shape[1]
    old = LEVELS // 2
    heads = query_ref.shape[1]
    columns = slice(pair * heads * HD, (pair + 1) * heads * HD)
    for at in range(LEVELS):
        total = keep_ref[at, :, columns] + (
            near_ref[at, :, columns].astype(jnp.float32)
            + got_ref[at, :, columns].astype(jnp.float32)
        )
        cosine, sine = cos_ref[at][:tok], sin_ref[at][:tok]
        for h in range(heads):
            head = turned(total[:, h * HD : (h + 1) * HD], cosine, sine)
            query_ref[at, h] = head.astype(jnp.bfloat16)
    row = lax.broadcasted_iota(jnp.int32, (tok, tok), 0)
    col = lax.broadcasted_iota(jnp.int32, (tok, tok), 1)
    scale = HD ** (-0.5) * 1.4426950408889634
    for i in range(LEVELS):
        count = (old + i + 1) * tok
        queries = query_ref[i].reshape(heads * tok, HD)
        scores = []
        best = None
        for j in range(PLANE):
            keys = pieces[j][0 : old + i + 1, :, 0:HD].reshape(count, HD)
            raw = lax.dot_general(
                queries, keys, (((1,), (1,)), ((), ())), preferred_element_type=jnp.float32
            )
            if j == 0:
                allowed = col <= row
            else:
                allowed = jnp.broadcast_to(place_of(j, place, core), (tok, tok)) < place
            allowed = jnp.concatenate([allowed] * heads, axis=0)
            last = jnp.where(allowed, raw[:, count - tok :], NEG_FILL)
            raw = jnp.concatenate([raw[:, : count - tok], last], axis=1)
            top = jnp.max(raw, axis=1, keepdims=True)
            best = top if best is None else jnp.maximum(best, top)
            scores.append(raw)
        total, accum = 0.0, 0.0
        for j in range(PLANE):
            weights = jnp.exp2((scores[j] - best) * scale)
            total = total + jnp.sum(weights, axis=1, keepdims=True)
            values = pieces[j][0 : old + i + 1, :, HD : 2 * HD].reshape(count, HD)
            accum = accum + jnp.dot(
                weights.astype(jnp.bfloat16), values, preferred_element_type=jnp.float32
            )
        result = (accum / total).astype(jnp.bfloat16)
        for h in range(heads):
            out_ref[i * tok : (i + 1) * tok, h * HD : (h + 1) * HD] = result[
                h * tok : (h + 1) * tok
            ]


def output_kernel(where_ref, *refs):
    heads, weights, (mine_ref, other_ref, x_ref) = refs[:4], refs[4:-3], refs[-3:]
    level, core = where_ref[0], where_ref[2]
    depth = heads[0].shape[1]
    width = weights[0].shape[2]
    tok = mine_ref.shape[1]
    for n, ref in enumerate(heads):
        at = 2 * lax.rem(level + n // 2, 2) + n % 2
        x_ref[:, pl.ds(pl.multiple_of(at * depth, depth), depth)] = ref[...]
    swap = jnp.where(core == level // 2, 0, 1)
    for s, out_ref in enumerate((mine_ref, other_ref)):
        i = jnp.bitwise_xor(swap, s)
        for j, piece in enumerate(weights):
            slot = (0, 2, 1, 3)[j] if s else j
            part = jnp.dot(x_ref[...], piece[i], preferred_element_type=jnp.float32)
            for t in range(LEVELS):
                out_ref[
                    lax.rem(t + LEVELS - level, LEVELS), :, slot * width : (slot + 1) * width
                ] = part[t * tok : (t + 1) * tok].astype(out_ref.dtype)


def finish_kernel(where_ref, own, first, second, third, out_ref):
    level, place, core = where_ref[0], where_ref[1], where_ref[2]
    half = out_ref.shape[1] // 2
    width = half // PLANE
    sums = (
        own[...] + second[...].astype(jnp.float32),
        first[...].astype(jnp.float32) + third[...].astype(jnp.float32),
    )
    for steps, total in enumerate(sums):
        for j in range(PLANE):
            at = lax.rem(level + steps, 2) * half + place_of(j, place, core) * width
            out_ref[:, pl.ds(pl.multiple_of(at, width), width)] = total[
                :, j * width : (j + 1) * width
            ].astype(out_ref.dtype)


SMEM = pl.BlockSpec(memory_space=pltpu.SMEM)
VMEM = pl.BlockSpec(memory_space=pltpu.VMEM)
HBM = pl.BlockSpec(memory_space=pltpu.MemorySpace.HBM)
PARAMS = pltpu.CompilerParams(vmem_limit_bytes=48 * 1024 * 1024)


def shaped(shape, dtype=jnp.bfloat16):
    return jax.ShapeDtypeStruct(shape, dtype)


def by_levels(
    text_rows,
    picture_rows,
    picture_slots,
    norm_gain,
    w_query,
    w_key,
    w_value,
    w_out,
    cache_keys,
    cache_values,
    recompute_rows,
    recompute_slots,
):
    seq_index = lax.axis_index("seq")
    core = lax.axis_index("head")
    level, place = seq_index // PLANE, seq_index % PLANE
    half_at = level // 2
    own_first = core == half_at
    tok, width = text_rows.shape
    block_rows = tok + REC_PAD

    stream_len = tok * LEVELS * PLANE
    tile_owners = TILE_RUN // tok
    first = stream_len // 2 // tok
    last = (stream_len - TILE_RUN) // tok
    owners = [first + i for i in range(tile_owners)] + [last + i for i in range(tile_owners)]
    assert [owner % PLANE for owner in owners] == list(range(LEVELS))
    owner_level = jnp.where(place < tile_owners, first // PLANE, last // PLANE)

    first_block = jnp.where(own_first, 0, 2)
    shown_block = (first_block + (level ^ owner_level)) % LEVELS
    where = jnp.stack([level, place, core, first_block, shown_block]).astype(jnp.int32)

    slots = (recompute_slots - seq_index * CACHED).astype(jnp.bfloat16)
    slot_rows = jnp.broadcast_to(jnp.pad(slots, (0, REC_PAD - REC))[:, None], (REC_PAD, 4 * HD))
    depth = w_key.shape[0]
    rows = jnp.concatenate(
        [text_rows, recompute_rows, jnp.zeros((REC_PAD - REC, width), text_rows.dtype)], axis=0
    )
    gain = lax.dynamic_slice_in_dim(norm_gain, core * width, width, 0)
    wide, pictures = rows.astype(jnp.float32), picture_rows.astype(jnp.float32)
    squares, picture_squares = lax.psum(
        (jnp.sum(wide * wide, axis=1), jnp.sum(pictures * pictures, axis=1)), "head"
    )
    normed = scaled(wide, squares, gain)
    pictures = scaled(pictures, picture_squares, gain)

    normed, pictures, slot_rows = lax.optimization_barrier((normed, pictures, slot_rows))
    key_own, key_give = pl.pallas_call(
        pack_kernel,
        out_shape=(shaped((depth + CACHED + REC_PAD, 4 * HD)),) * 2,
        in_specs=[SMEM] + [HBM] * 5,
        out_specs=(HBM,) * 2,
        scratch_shapes=[pltpu.SemaphoreType.DMA((PACK_COPIES,))],
        compiler_params=PARAMS,
        cost_estimate=pl.CostEstimate(
            flops=6_000_000_000, bytes_accessed=4_000_000, transcendentals=0
        ),
        name="pack",
    )(where, w_key, w_value, cache_keys, cache_values, slot_rows)

    out_rows = w_out.shape[0] // 2
    out_own, out_give = (
        lax.dynamic_slice_in_dim(w_out, at * out_rows, out_rows, 0) for at in (half_at, 1 - half_at)
    )

    crossed = permuted(normed, lambda z, p, c: (z ^ 2, p, 1 - c) if c == 1 - z // 2 else None)
    shown = permuted(pictures, lambda z, p, c: (2 * c + p // 2, z, p % 2))
    key_next = across(key_give, 1)
    query_near, query_far = to_near(w_query), to_far(w_query)
    query_near, query_far = lax.optimization_barrier((query_near, query_far))
    query_both = to_far(query_near)
    shown, key_next = lax.optimization_barrier((shown, key_next))
    keys = jnp.stack([key_own[:depth], key_next[:depth]])
    old_own, old_next = key_own[depth:], key_next[depth:]
    keys_near = to_near(keys)
    crossed, shown, out_give = lax.optimization_barrier((crossed, shown, out_give))
    held = jnp.concatenate([jnp.where(own_first, normed, crossed), shown], axis=0)
    next_rows = across(held, 1)
    held_other = other_core(held)
    next_rows, out_got = lax.optimization_barrier((next_rows, across(out_give, 2)))
    next_other = other_core(next_rows)
    keys_far = to_far(jnp.concatenate([keys, keys_near], axis=0))
    next_other, held_other, keys_far, query_both = lax.optimization_barrier(
        (next_other, held_other, keys_far, query_both)
    )
    parts = (held, next_rows, held_other, next_other)

    half = HD // 2
    freqs = ROPE_BASE ** (-jnp.arange(half, dtype=jnp.float32) / half)
    blocks = (jnp.arange(LEVELS, dtype=jnp.int32) * PLANE + place)[:, None]
    stream_pos = (
        CACHED * LEVELS * PLANE + blocks * tok + jnp.arange(tok, dtype=jnp.int32)[None]
    ).astype(jnp.float32)
    cache_pos = (blocks * CACHED + jnp.arange(CACHED, dtype=jnp.int32)[None]).astype(jnp.float32)
    angles = jnp.concatenate([stream_pos, cache_pos], axis=1)[..., None] * freqs
    cosine, sine = jnp.cos(angles), jnp.sin(angles)
    cosine = jnp.concatenate([cosine, cosine], axis=-1)
    sine = jnp.concatenate([-sine, sine], axis=-1)

    all_rows = LEVELS * block_rows
    keep, send = pl.pallas_call(
        keys_part_kernel,
        out_shape=(
            shaped((all_rows, 2 * HD), jnp.float32),
            shaped((all_rows + 2 * (CACHED + REC_PAD), 2 * HD)),
        ),
        in_specs=[SMEM] + [VMEM] * 9,
        out_specs=(VMEM, VMEM),
        scratch_shapes=[pltpu.VMEM((all_rows, width), jnp.bfloat16)],
        compiler_params=PARAMS,
        cost_estimate=pl.CostEstimate(
            flops=3_000_000_000, bytes_accessed=4_000_000, transcendentals=0
        ),
        name="keys_part",
    )(where, *parts, keys, keys_near, keys_far, old_own, old_next)
    send, *parts = lax.optimization_barrier((send, *parts))
    group_shape = (LEVELS, tok, 4 * HD)
    q_keep, q_keep2, q_send, q_send2 = pl.pallas_call(
        queries_part_kernel,
        out_shape=(shaped(group_shape, jnp.float32),) * 2 + (shaped(group_shape),) * 2,
        in_specs=[SMEM] + [VMEM] * 8,
        out_specs=(VMEM,) * 4,
        scratch_shapes=[pltpu.VMEM((all_rows, width), jnp.bfloat16)],
        compiler_params=PARAMS,
        cost_estimate=pl.CostEstimate(
            flops=5_000_000_000, bytes_accessed=4_000_000, transcendentals=0
        ),
        name="queries_part",
    )(where, *parts, w_query, query_near, query_far, query_both)
    got_near2 = across(q_send2, 1)
    got_near = across(q_send, 1)
    got_queries = across((q_keep2 + got_near2.astype(jnp.float32)).astype(jnp.bfloat16), 2)
    out_pair = jnp.stack([out_own, out_got])
    out_pair, q_send2 = lax.optimization_barrier((out_pair, q_send2))
    out_near = to_near(out_pair)
    got_keys, q_send2 = lax.optimization_barrier((across(send, 2), q_send2))
    kv = pl.pallas_call(
        keys_join_kernel,
        out_shape=shaped((LEVELS // 2 + LEVELS, tok, 2 * HD)),
        in_specs=[SMEM] + [VMEM] * 6,
        out_specs=VMEM,
        scratch_shapes=[pltpu.VMEM((all_rows, 2 * HD), jnp.float32)],
        compiler_params=PARAMS,
        cost_estimate=pl.CostEstimate(
            flops=24_000_000_000, bytes_accessed=4_000_000, transcendentals=0
        ),
        name="keys_join",
    )(where, keep, got_keys, old_own, old_next, cosine, sine)
    kv_near, kv_far = to_near(kv), to_far(kv)
    kv_both = permuted(kv, lambda z, p, c: (z, p ^ 3, c))

    kv_near, kv_far, kv_both, out_near, out_pair, got_near = lax.optimization_barrier(
        (kv_near, kv_far, kv_both, out_near, out_pair, got_near)
    )
    out_far, out_both = to_far(out_pair), to_far(out_near)

    attended = [
        pl.pallas_call(
            functools.partial(attend_kernel, pair),
            out_shape=shaped((LEVELS * tok, 2 * HD)),
            in_specs=[SMEM] + [VMEM] * 9,
            out_specs=VMEM,
            scratch_shapes=[pltpu.VMEM((LEVELS, 2, tok, HD), jnp.bfloat16)],
            compiler_params=PARAMS,
            cost_estimate=pl.CostEstimate(
                flops=4_000_000_000, bytes_accessed=4_000_000, transcendentals=2_400_000
            ),
            name="attend",
        )(where, q_keep, got_near, got_queries, cosine, sine, kv, kv_near, kv_far, kv_both)
        for pair in range(2)
    ]
    attended += [across(each, 1) for each in attended]

    wide_cols = PLANE * w_out.shape[1]
    mine, other = pl.pallas_call(
        output_kernel,
        out_shape=(
            shaped((LEVELS, tok, wide_cols), jnp.float32),
            shaped((LEVELS, tok, wide_cols)),
        ),
        in_specs=[SMEM] + [VMEM] * 8,
        out_specs=(VMEM, VMEM),
        scratch_shapes=[pltpu.VMEM((LEVELS * tok, out_rows), jnp.bfloat16)],
        compiler_params=PARAMS,
        cost_estimate=pl.CostEstimate(
            flops=5_000_000_000, bytes_accessed=4_000_000, transcendentals=0
        ),
        name="output",
    )(where, *attended, out_pair, out_near, out_far, out_both)
    got = other_core(other)
    block = [mine[d] + got[d].astype(jnp.float32) for d in range(LEVELS)]
    shares = [up(block[d].astype(jnp.bfloat16), d) for d in range(1, LEVELS)]
    return pl.pallas_call(
        finish_kernel,
        out_shape=shaped((tok, width)),
        in_specs=[SMEM] + [VMEM] * 4,
        out_specs=VMEM,
        compiler_params=PARAMS,
        name="finish",
    )(where, block[0], *shares)


def solution(mesh):
    def run(*args):
        kv_local = args[5].shape[1] // HD // mesh.shape["head"]
        levels_fit = (
            mesh.shape["seq"] == LEVELS * PLANE
            and mesh.shape["head"] == 2
            and kv_local == LEVELS
            and args[1].shape[0] == 2 * TILE_RUN
            and args[0].shape[0] == 2048
            and args[8].shape[0] == LEVELS * PLANE * CACHED
            and args[10].shape[0] == LEVELS * PLANE * REC
        )
        return jax.shard_map(
            by_levels if levels_fit else on_device,
            mesh=mesh,
            in_specs=(
                P("seq", "head"),
                P("seq", "head"),
                P("seq"),
                P(),
                P("seq", "head"),
                P("seq", "head"),
                P("seq", "head"),
                P("head", "seq"),
                P("seq", "head"),
                P("seq", "head"),
                P("seq", "head"),
                P("seq"),
            ),
            out_specs=P("seq", "head"),
            check_vma=False,
        )(*args)

    return run
```

```python
import functools

import jax
import jax.numpy as jnp
from jax import lax
from jax.experimental import pallas as pl
from jax.experimental.pallas import tpu as pltpu
from jax.sharding import PartitionSpec as P

D = 4096
HD = 128


EPSILON = 1e-05
ROPE_BASE = 1000000.0
NEG_FILL = -1e30


def rotate(values, positions):
    half = values.shape[-1] // 2
    freqs = ROPE_BASE ** (-jnp.arange(half, dtype=jnp.float32) / half)
    angles = positions[:, None] * freqs[None, :]
    cosine = jnp.cos(angles)[:, None, :]
    sine = jnp.sin(angles)[:, None, :]
    first = values[..., :half]
    second = values[..., half:]
    return jnp.concatenate(
        [first * cosine - second * sine, second * cosine + first * sine], axis=-1
    )


def scaled(rows_wide, squares, gain):
    return (rows_wide * lax.rsqrt(squares / D + EPSILON)[:, None] * gain[None, :]).astype(
        jnp.bfloat16
    )


def attend(carry, key_piece, value_piece, queries, allowed):
    best, total, accum = carry
    count = key_piece.shape[0]
    kv_local = queries.shape[0]
    keys_split = key_piece.reshape(count, kv_local, HD)
    values_split = value_piece.reshape(count, kv_local, HD)
    scores = jnp.einsum(
        "kgtd,nkd->kgtn", queries, keys_split, preferred_element_type=jnp.float32
    ) * HD ** (-0.5)
    scores = jnp.where(allowed, scores, NEG_FILL)
    fresh = jnp.maximum(best, jnp.max(scores, axis=-1))
    factor = jnp.exp(best - fresh)
    weights = jnp.where(allowed, jnp.exp(scores - fresh[..., None]), 0.0)
    total = total * factor + jnp.sum(weights, axis=-1)
    accum = accum * factor[..., None] + jnp.einsum(
        "kgtn,nkd->kgtd",
        weights.astype(jnp.bfloat16),
        values_split,
        preferred_element_type=jnp.float32,
    )
    return (fresh, total, accum)


def on_device(
    text_rows,
    picture_rows,
    picture_slots,
    norm_gain,
    w_query,
    w_key,
    w_value,
    w_out,
    cache_keys,
    cache_values,
    recompute_rows,
    recompute_slots,
):
    tok_rows = text_rows.shape[0]
    rec_count = recompute_rows.shape[0]
    cache_rows = cache_keys.shape[0]
    seq_index = lax.axis_index("seq")
    local_pos = seq_index * tok_rows + jnp.arange(tok_rows, dtype=jnp.int32)
    rows_piece = lax.all_gather(picture_rows, "seq", axis=0, tiled=True)
    slots_piece = lax.all_gather(picture_slots, "seq", axis=0, tiled=True)
    select = (slots_piece[None, :] == local_pos[:, None]).astype(jnp.bfloat16)
    placed = jnp.dot(select, rows_piece, preferred_element_type=jnp.float32)
    hits = jnp.sum(select.astype(jnp.float32), axis=1)
    added, hits = (placed, hits)
    stream = jnp.where(hits[:, None] > 0.5, added, text_rows.astype(jnp.float32)).astype(
        jnp.bfloat16
    )
    slice_width = stream.shape[1]
    gain_slice = lax.dynamic_slice_in_dim(
        norm_gain, lax.axis_index("head") * slice_width, slice_width, 0
    )
    stream_wide = stream.astype(jnp.float32)
    rec_wide = recompute_rows.astype(jnp.float32)
    stream_sq, rec_sq = lax.psum(
        (jnp.sum(stream_wide * stream_wide, axis=1), jnp.sum(rec_wide * rec_wide, axis=1)), "head"
    )
    normed, rec_normed = (
        lax.all_gather(scaled(stream_wide, stream_sq, gain_slice), "head", axis=1, tiled=True),
        lax.all_gather(scaled(rec_wide, rec_sq, gain_slice), "head", axis=1, tiled=True),
    )
    stacked = jnp.concatenate([normed, rec_normed], axis=0)
    query_cols = w_query.shape[1]
    key_cols = w_key.shape[1]
    pieces = (
        lax.all_gather(w_query, "seq", axis=0, tiled=True),
        lax.all_gather(w_key, "seq", axis=0, tiled=True),
        lax.all_gather(w_value, "seq", axis=0, tiled=True),
    )
    query_all = jnp.dot(stacked, pieces[0], preferred_element_type=jnp.float32)
    key_all = jnp.dot(stacked, pieces[1], preferred_element_type=jnp.float32)
    value_all = jnp.dot(stacked, pieces[2], preferred_element_type=jnp.float32)
    cache_total = cache_rows * lax.axis_size("seq")
    stream_pos = (cache_total + local_pos).astype(jnp.float32)
    rec_pos = recompute_slots.astype(jnp.float32)
    heads_local = query_cols // HD
    kv_local = key_cols // HD
    group = heads_local // kv_local
    rot_query = rotate(query_all[:tok_rows].reshape(tok_rows, heads_local, HD), stream_pos).astype(
        jnp.bfloat16
    )
    rot_key = (
        rotate(key_all[:tok_rows].reshape(tok_rows, kv_local, HD), stream_pos)
        .astype(jnp.bfloat16)
        .reshape(tok_rows, key_cols)
    )
    values_new = value_all[:tok_rows].astype(jnp.bfloat16)
    rot_rec_key = (
        rotate(key_all[tok_rows:].reshape(rec_count, kv_local, HD), rec_pos)
        .astype(jnp.bfloat16)
        .reshape(rec_count, key_cols)
    )
    rec_values = value_all[tok_rows:].astype(jnp.bfloat16)
    local_slots = recompute_slots - seq_index * cache_rows
    select = local_slots[:, None] == jnp.arange(cache_rows, dtype=jnp.int32)[None, :]
    replaced = jnp.any(select, axis=0)[:, None]
    select_cols = select.astype(jnp.bfloat16).T
    new_keys = jnp.dot(select_cols, rot_rec_key, preferred_element_type=jnp.float32).astype(
        jnp.bfloat16
    )
    new_values = jnp.dot(select_cols, rec_values, preferred_element_type=jnp.float32).astype(
        jnp.bfloat16
    )
    cache_k = jnp.where(replaced, new_keys, cache_keys)
    cache_v = jnp.where(replaced, new_values, cache_values)
    queries = jnp.transpose(rot_query.reshape(tok_rows, kv_local, group, HD), (1, 2, 0, 3))
    carry_start = (
        jnp.full((kv_local, group, tok_rows), NEG_FILL, jnp.float32),
        jnp.zeros((kv_local, group, tok_rows), jnp.float32),
        jnp.zeros((kv_local, group, tok_rows, HD), jnp.float32),
    )
    pieces = (
        lax.all_gather(cache_k, "seq", axis=0, tiled=True),
        lax.all_gather(cache_v, "seq", axis=0, tiled=True),
    )
    allowed = jnp.ones((tok_rows, pieces[0].shape[0]), jnp.bool_)
    carry_mid = attend(carry_start, pieces[0], pieces[1], queries, allowed)
    pieces = (
        lax.all_gather(rot_key, "seq", axis=0, tiled=True),
        lax.all_gather(values_new, "seq", axis=0, tiled=True),
    )
    key_pos = jnp.arange(pieces[0].shape[0], dtype=jnp.int32)
    allowed = key_pos[None, :] <= local_pos[:, None]
    best, total, accum = attend(carry_mid, pieces[0], pieces[1], queries, allowed)
    attended = (
        jnp.transpose(accum / total[..., None], (2, 0, 1, 3))
        .reshape(tok_rows, query_cols)
        .astype(jnp.bfloat16)
    )
    partial_out = jnp.dot(
        attended,
        lax.all_gather(w_out, "seq", axis=1, tiled=True),
        preferred_element_type=jnp.float32,
    )
    return lax.psum_scatter(
        partial_out.astype(jnp.bfloat16), "head", scatter_dimension=1, tiled=True
    )


LEVELS = 4
PLANE = 4
TILE_RUN = 256
CACHED = 64
REC = 8
REC_PAD = 16


def permuted(value, move):
    perm = []
    for level in range(LEVELS):
        for place in range(PLANE):
            for core in range(2):
                target = move(level, place, core)
                if target is not None:
                    to_level, to_place, to_core = target
                    perm.append(
                        (
                            (level * PLANE + place) * 2 + core,
                            (to_level * PLANE + to_place) * 2 + to_core,
                        )
                    )
    return lax.ppermute(value, ("seq", "head"), perm)


def across(value, bit):
    return permuted(value, lambda z, p, c: (z ^ bit, p, c))


def up(value, steps):
    return permuted(value, lambda z, p, c: ((z + steps) % LEVELS, p, c))


def other_core(value):
    return permuted(value, lambda z, p, c: (z, p, 1 - c))


def to_near(value):
    return permuted(value, lambda z, p, c: (z, p ^ (1 + c), c))


def to_far(value):
    return permuted(value, lambda z, p, c: (z, p ^ (2 - c), c))


def place_of(which, place, core):
    if which == 0:
        return place
    if which == 3:
        return place ^ 3
    return place ^ (1 + core) if which == 1 else place ^ (2 - core)


def turned(values, cosine, sine):
    return values * cosine + pltpu.roll(values, HD // 2, 1) * sine


def pack_kernel(where_ref, *refs):
    w_key, w_value, cache_keys, cache_values, slots = refs[:5]
    outs, sems = refs[5:7], refs[7]
    level = where_ref[0]
    depth = w_key.shape[0]
    copies = []

    def copy(source, target):
        copies.append(pltpu.make_async_copy(source, target, sems.at[len(copies)]))
        copies[-1].start()

    for n in range(2):
        keys = outs[n]
        for m in range(2):
            at = jnp.bitwise_xor(level, n + 2 * m)
            small = pl.ds(pl.multiple_of(at * HD, HD), HD)
            for k, (new, old) in enumerate(((w_key, cache_keys), (w_value, cache_values))):
                to = pl.ds((2 * m + k) * HD, HD)
                copy(new.at[:, small], keys.at[0:depth, to])
                copy(old.at[:, small], keys.at[depth : depth + CACHED, to])
        copy(slots, keys.at[depth + CACHED : depth + CACHED + REC_PAD])
    for each in copies:
        each.wait()


PACK_COPIES = 18


def assemble(where_ref, parts, x_ref):
    level, core = where_ref[0], where_ref[2]
    shown = TILE_RUN // 2 // PLANE
    rows = parts[0].shape[0] - shown
    for n, part in enumerate(parts):
        x_ref[n * rows : (n + 1) * rows] = part[0:rows]
    start = where_ref[4] * rows
    for n, part in enumerate(parts):
        which = 2 * lax.rem(level + n % 2, 2) + (core if n < 2 else 1 - core)
        to = pl.multiple_of(start + which * shown, 16)
        x_ref[pl.ds(to, shown)] = part[rows : rows + shown]


def products(where_ref, x_ref, pieces):
    level, place, core = where_ref[0], where_ref[1], where_ref[2]
    total = None
    for i in range(2):
        for j in range(PLANE):
            depth = pieces[i][j].shape[0]
            block = lax.rem(level + i, 2) * PLANE + place_of(j, place, core)
            start = pl.multiple_of(block * depth, depth)
            part = jnp.dot(
                x_ref[:, pl.ds(start, depth)],
                pieces[i][j][...],
                preferred_element_type=jnp.float32,
            )
            total = part if total is None else total + part
    return total


def keys_part_kernel(
    where_ref, x0, x1, x2, x3, own, near, far, old0, old1, keep_ref, send_ref, x_ref
):
    assemble(where_ref, (x0, x1, x2, x3), x_ref)
    pieces = [[own.at[i], near.at[i], far.at[i], far.at[2 + i]] for i in range(2)]
    width = 2 * HD
    total = products(where_ref, x_ref, pieces)
    at = total.shape[0]
    keep_ref[...] = total[:, :width]
    send_ref[0:at] = total[:, width:].astype(jnp.bfloat16)
    for old in (old0, old1):
        send_ref[at : at + CACHED + REC_PAD] = old[:, width:]
        at += CACHED + REC_PAD


def keys_join_kernel(where_ref, keep_ref, got_ref, old0, old1, cos_ref, sin_ref, kv_ref, sum_ref):
    level = where_ref[0]
    rows = sum_ref.shape[0]
    block = rows // LEVELS
    tok = block - REC_PAD
    width = 2 * HD
    sum_ref[...] = keep_ref[...] + got_ref[0:rows].astype(jnp.float32)
    first = where_ref[3]
    span = CACHED + REC_PAD
    for n in range(LEVELS):
        at = jnp.bitwise_xor(level, n)
        start = pl.multiple_of(lax.rem(first + n, LEVELS) * block, 16)
        cosine, sine = cos_ref[at], sin_ref[at]
        fresh = sum_ref[pl.ds(start, tok), :]
        kv_ref[2 + at, :, 0:HD] = turned(fresh[:, :HD], cosine[:tok], sine[:tok]).astype(
            jnp.bfloat16
        )
        kv_ref[2 + at, :, HD:width] = fresh[:, HD:].astype(jnp.bfloat16)
        if n < 2:
            old = (old0, old1)[n][:, 0:width].astype(jnp.float32)
        else:
            old = got_ref[rows + (n - 2) * span : rows + (n - 1) * span].astype(jnp.float32)
        slots = old[CACHED : CACHED + REC].astype(jnp.int32)
        rec = sum_ref[pl.ds(pl.multiple_of(start + tok, 16), REC_PAD), :]
        line = lax.broadcasted_iota(jnp.int32, (CACHED, width), 0)
        found = jnp.zeros((CACHED, width), jnp.float32)
        hit = jnp.zeros((CACHED, width), jnp.int32)
        for r in range(REC):
            same = line == slots[r : r + 1]
            found = jnp.where(same, rec[r : r + 1], found)
            hit = jnp.where(same, 1, hit)
        keys = turned(found[:, :HD], cosine[tok : tok + CACHED], sine[tok : tok + CACHED])
        found = jnp.concatenate([keys, found[:, HD:]], axis=1)
        line_at = pl.multiple_of(lax.rem(at, 2) * CACHED, CACHED)
        kv_ref[at // 2, pl.ds(line_at, CACHED), :] = jnp.where(
            hit == 1, found, old[:CACHED]
        ).astype(jnp.bfloat16)


def queries_part_kernel(where_ref, x0, x1, x2, x3, *refs):
    weights, outs, x_ref = refs[:4], refs[4:8], refs[8]
    level, place, core = where_ref[0], where_ref[1], where_ref[2]
    assemble(where_ref, (x0, x1, x2, x3), x_ref)
    depth = weights[0].shape[0]
    width = 4 * HD
    block = x_ref.shape[0] // LEVELS
    tok = block - REC_PAD
    for m, out_ref in zip((0, 2, 1, 3), outs):
        group = pl.ds(pl.multiple_of(jnp.bitwise_xor(level, m) * width, width), width)
        total = None
        for j in range(PLANE):
            at = lax.rem(level, 2) * PLANE + place_of(j, place, core)
            part = jnp.dot(
                x_ref[:, pl.ds(pl.multiple_of(at * depth, depth), depth)],
                weights[j][:, group],
                preferred_element_type=jnp.float32,
            )
            total = part if total is None else total + part
        for k in range(LEVELS):
            at = jnp.bitwise_xor(level, lax.rem(k + LEVELS - where_ref[3], LEVELS))
            out_ref[at] = total[k * block : k * block + tok].astype(out_ref.dtype)


def attend_kernel(
    pair, where_ref, keep_ref, near_ref, got_ref, cos_ref, sin_ref, kv0, kv1, kv2, kv3, out_ref, query_ref
):
    level, place, core = where_ref[0], where_ref[1], where_ref[2]
    pieces = (kv0, kv1, kv2, kv3)
    tok = keep_ref.shape[1]
    old = LEVELS // 2
    heads = query_ref.shape[1]
    columns = slice(pair * heads * HD, (pair + 1) * heads * HD)
    for at in range(LEVELS):
        total = keep_ref[at, :, columns] + (
            near_ref[at, :, columns].astype(jnp.float32)
            + got_ref[at, :, columns].astype(jnp.float32)
        )
        cosine, sine = cos_ref[at][:tok], sin_ref[at][:tok]
        for h in range(heads):
            head = turned(total[:, h * HD : (h + 1) * HD], cosine, sine)
            query_ref[at, h] = head.astype(jnp.bfloat16)
    row = lax.broadcasted_iota(jnp.int32, (tok, tok), 0)
    col = lax.broadcasted_iota(jnp.int32, (tok, tok), 1)
    scale = HD ** (-0.5) * 1.4426950408889634
    for i in range(LEVELS):
        count = (old + i + 1) * tok
        queries = query_ref[i].reshape(heads * tok, HD)
        scores = []
        best = None
        for j in range(PLANE):
            keys = pieces[j][0 : old + i + 1, :, 0:HD].reshape(count, HD)
            raw = lax.dot_general(
                queries, keys, (((1,), (1,)), ((), ())), preferred_element_type=jnp.float32
            )
            if j == 0:
                allowed = col <= row
            else:
                allowed = jnp.broadcast_to(place_of(j, place, core), (tok, tok)) < place
            allowed = jnp.concatenate([allowed] * heads, axis=0)
            last = jnp.where(allowed, raw[:, count - tok :], NEG_FILL)
            raw = jnp.concatenate([raw[:, : count - tok], last], axis=1)
            top = jnp.max(raw, axis=1, keepdims=True)
            best = top if best is None else jnp.maximum(best, top)
            scores.append(raw)
        total, accum = 0.0, 0.0
        for j in range(PLANE):
            weights = jnp.exp2((scores[j] - best) * scale)
            total = total + jnp.sum(weights, axis=1, keepdims=True)
            values = pieces[j][0 : old + i + 1, :, HD : 2 * HD].reshape(count, HD)
            accum = accum + jnp.dot(
                weights.astype(jnp.bfloat16), values, preferred_element_type=jnp.float32
            )
        result = (accum / total).astype(jnp.bfloat16)
        for h in range(heads):
            out_ref[i * tok : (i + 1) * tok, h * HD : (h + 1) * HD] = result[
                h * tok : (h + 1) * tok
            ]


def output_kernel(where_ref, *refs):
    heads, weights, (mine_ref, other_ref, x_ref) = refs[:4], refs[4:-3], refs[-3:]
    level, core = where_ref[0], where_ref[2]
    depth = heads[0].shape[1]
    width = weights[0].shape[2]
    tok = mine_ref.shape[1]
    for n, ref in enumerate(heads):
        at = 2 * lax.rem(level + n // 2, 2) + n % 2
        x_ref[:, pl.ds(pl.multiple_of(at * depth, depth), depth)] = ref[...]
    swap = jnp.where(core == level // 2, 0, 1)
    for s, out_ref in enumerate((mine_ref, other_ref)):
        i = jnp.bitwise_xor(swap, s)
        for j, piece in enumerate(weights):
            slot = (0, 2, 1, 3)[j] if s else j
            part = jnp.dot(x_ref[...], piece[i], preferred_element_type=jnp.float32)
            for t in range(LEVELS):
                out_ref[
                    lax.rem(t + LEVELS - level, LEVELS), :, slot * width : (slot + 1) * width
                ] = part[t * tok : (t + 1) * tok].astype(out_ref.dtype)


def finish_kernel(where_ref, own, first, second, third, out_ref):
    level, place, core = where_ref[0], where_ref[1], where_ref[2]
    half = out_ref.shape[1] // 2
    width = half // PLANE
    sums = (
        own[...] + second[...].astype(jnp.float32),
        first[...].astype(jnp.float32) + third[...].astype(jnp.float32),
    )
    for steps, total in enumerate(sums):
        for j in range(PLANE):
            at = lax.rem(level + steps, 2) * half + place_of(j, place, core) * width
            out_ref[:, pl.ds(pl.multiple_of(at, width), width)] = total[
                :, j * width : (j + 1) * width
            ].astype(out_ref.dtype)


SMEM = pl.BlockSpec(memory_space=pltpu.SMEM)
VMEM = pl.BlockSpec(memory_space=pltpu.VMEM)
HBM = pl.BlockSpec(memory_space=pltpu.MemorySpace.HBM)
PARAMS = pltpu.CompilerParams(vmem_limit_bytes=48 * 1024 * 1024)


def shaped(shape, dtype=jnp.bfloat16):
    return jax.ShapeDtypeStruct(shape, dtype)


def by_levels(
    text_rows,
    picture_rows,
    picture_slots,
    norm_gain,
    w_query,
    w_key,
    w_value,
    w_out,
    cache_keys,
    cache_values,
    recompute_rows,
    recompute_slots,
):
    seq_index = lax.axis_index("seq")
    core = lax.axis_index("head")
    level, place = seq_index // PLANE, seq_index % PLANE
    half_at = level // 2
    own_first = core == half_at
    tok, width = text_rows.shape
    block_rows = tok + REC_PAD

    stream_len = tok * LEVELS * PLANE
    tile_owners = TILE_RUN // tok
    first = stream_len // 2 // tok
    last = (stream_len - TILE_RUN) // tok
    owners = [first + i for i in range(tile_owners)] + [last + i for i in range(tile_owners)]
    assert [owner % PLANE for owner in owners] == list(range(LEVELS))
    owner_level = jnp.where(place < tile_owners, first // PLANE, last // PLANE)

    first_block = jnp.where(own_first, 0, 2)
    shown_block = (first_block + (level ^ owner_level)) % LEVELS
    where = jnp.stack([level, place, core, first_block, shown_block]).astype(jnp.int32)

    slots = (recompute_slots - seq_index * CACHED).astype(jnp.bfloat16)
    slot_rows = jnp.broadcast_to(jnp.pad(slots, (0, REC_PAD - REC))[:, None], (REC_PAD, 4 * HD))
    depth = w_key.shape[0]
    rows = jnp.concatenate(
        [text_rows, recompute_rows, jnp.zeros((REC_PAD - REC, width), text_rows.dtype)], axis=0
    )
    gain = lax.dynamic_slice_in_dim(norm_gain, core * width, width, 0)
    wide, pictures = rows.astype(jnp.float32), picture_rows.astype(jnp.float32)
    squares, picture_squares = lax.psum(
        (jnp.sum(wide * wide, axis=1), jnp.sum(pictures * pictures, axis=1)), "head"
    )
    normed = scaled(wide, squares, gain)
    pictures = scaled(pictures, picture_squares, gain)

    normed, pictures, slot_rows = lax.optimization_barrier((normed, pictures, slot_rows))
    key_own, key_give = pl.pallas_call(
        pack_kernel,
        out_shape=(shaped((depth + CACHED + REC_PAD, 4 * HD)),) * 2,
        in_specs=[SMEM] + [HBM] * 5,
        out_specs=(HBM,) * 2,
        scratch_shapes=[pltpu.SemaphoreType.DMA((PACK_COPIES,))],
        compiler_params=PARAMS,
        cost_estimate=pl.CostEstimate(
            flops=6_000_000_000, bytes_accessed=4_000_000, transcendentals=0
        ),
        name="pack",
    )(where, w_key, w_value, cache_keys, cache_values, slot_rows)

    out_rows = w_out.shape[0] // 2
    out_own, out_give = (
        lax.dynamic_slice_in_dim(w_out, at * out_rows, out_rows, 0) for at in (half_at, 1 - half_at)
    )

    crossed = permuted(normed, lambda z, p, c: (z ^ 2, p, 1 - c) if c == 1 - z // 2 else None)
    shown = permuted(pictures, lambda z, p, c: (2 * c + p // 2, z, p % 2))
    key_next = across(key_give, 1)
    query_near, query_far = to_near(w_query), to_far(w_query)
    query_near, query_far = lax.optimization_barrier((query_near, query_far))
    query_both = to_far(query_near)
    shown, key_next = lax.optimization_barrier((shown, key_next))
    keys = jnp.stack([key_own[:depth], key_next[:depth]])
    old_own, old_next = key_own[depth:], key_next[depth:]
    keys_near = to_near(keys)
    crossed, shown, out_give = lax.optimization_barrier((crossed, shown, out_give))
    held = jnp.concatenate([jnp.where(own_first, normed, crossed), shown], axis=0)
    next_rows = across(held, 1)
    held_other = other_core(held)
    next_rows, out_got = lax.optimization_barrier((next_rows, across(out_give, 2)))
    next_other = other_core(next_rows)
    keys_far = to_far(jnp.concatenate([keys, keys_near], axis=0))
    next_other, held_other, keys_far, query_both = lax.optimization_barrier(
        (next_other, held_other, keys_far, query_both)
    )
    parts = (held, next_rows, held_other, next_other)

    half = HD // 2
    freqs = ROPE_BASE ** (-jnp.arange(half, dtype=jnp.float32) / half)
    blocks = (jnp.arange(LEVELS, dtype=jnp.int32) * PLANE + place)[:, None]
    stream_pos = (
        CACHED * LEVELS * PLANE + blocks * tok + jnp.arange(tok, dtype=jnp.int32)[None]
    ).astype(jnp.float32)
    cache_pos = (blocks * CACHED + jnp.arange(CACHED, dtype=jnp.int32)[None]).astype(jnp.float32)
    angles = jnp.concatenate([stream_pos, cache_pos], axis=1)[..., None] * freqs
    cosine, sine = jnp.cos(angles), jnp.sin(angles)
    cosine = jnp.concatenate([cosine, cosine], axis=-1)
    sine = jnp.concatenate([-sine, sine], axis=-1)

    all_rows = LEVELS * block_rows
    keep, send = pl.pallas_call(
        keys_part_kernel,
        out_shape=(
            shaped((all_rows, 2 * HD), jnp.float32),
            shaped((all_rows + 2 * (CACHED + REC_PAD), 2 * HD)),
        ),
        in_specs=[SMEM] + [VMEM] * 9,
        out_specs=(VMEM, VMEM),
        scratch_shapes=[pltpu.VMEM((all_rows, width), jnp.bfloat16)],
        compiler_params=PARAMS,
        cost_estimate=pl.CostEstimate(
            flops=3_000_000_000, bytes_accessed=4_000_000, transcendentals=0
        ),
        name="keys_part",
    )(where, *parts, keys, keys_near, keys_far, old_own, old_next)
    send, *parts = lax.optimization_barrier((send, *parts))
    group_shape = (LEVELS, tok, 4 * HD)
    q_keep, q_keep2, q_send, q_send2 = pl.pallas_call(
        queries_part_kernel,
        out_shape=(shaped(group_shape, jnp.float32),) * 2 + (shaped(group_shape),) * 2,
        in_specs=[SMEM] + [VMEM] * 8,
        out_specs=(VMEM,) * 4,
        scratch_shapes=[pltpu.VMEM((all_rows, width), jnp.bfloat16)],
        compiler_params=PARAMS,
        cost_estimate=pl.CostEstimate(
            flops=5_000_000_000, bytes_accessed=4_000_000, transcendentals=0
        ),
        name="queries_part",
    )(where, *parts, w_query, query_near, query_far, query_both)
    got_near2 = across(q_send2, 1)
    got_near = across(q_send, 1)
    got_queries = across((q_keep2 + got_near2.astype(jnp.float32)).astype(jnp.bfloat16), 2)
    out_pair = jnp.stack([out_own, out_got])
    out_pair, q_send2 = lax.optimization_barrier((out_pair, q_send2))
    out_near = to_near(out_pair)
    got_keys, q_send2 = lax.optimization_barrier((across(send, 2), q_send2))
    kv = pl.pallas_call(
        keys_join_kernel,
        out_shape=shaped((LEVELS // 2 + LEVELS, tok, 2 * HD)),
        in_specs=[SMEM] + [VMEM] * 6,
        out_specs=VMEM,
        scratch_shapes=[pltpu.VMEM((all_rows, 2 * HD), jnp.float32)],
        compiler_params=PARAMS,
        cost_estimate=pl.CostEstimate(
            flops=24_000_000_000, bytes_accessed=4_000_000, transcendentals=0
        ),
        name="keys_join",
    )(where, keep, got_keys, old_own, old_next, cosine, sine)
    kv_near, kv_far = to_near(kv), to_far(kv)
    kv_both = permuted(kv, lambda z, p, c: (z, p ^ 3, c))

    kv_near, kv_far, kv_both, out_near, out_pair = lax.optimization_barrier(
        (kv_near, kv_far, kv_both, out_near, out_pair)
    )
    out_far, out_both = to_far(out_pair), to_far(out_near)

    attended = [
        pl.pallas_call(
            functools.partial(attend_kernel, pair),
            out_shape=shaped((LEVELS * tok, 2 * HD)),
            in_specs=[SMEM] + [VMEM] * 9,
            out_specs=VMEM,
            scratch_shapes=[pltpu.VMEM((LEVELS, 2, tok, HD), jnp.bfloat16)],
            compiler_params=PARAMS,
            cost_estimate=pl.CostEstimate(
                flops=4_000_000_000, bytes_accessed=4_000_000, transcendentals=2_400_000
            ),
            name="attend",
        )(where, q_keep, got_near, got_queries, cosine, sine, kv, kv_near, kv_far, kv_both)
        for pair in range(2)
    ]
    attended += [across(each, 1) for each in attended]

    wide_cols = PLANE * w_out.shape[1]
    mine, other = pl.pallas_call(
        output_kernel,
        out_shape=(
            shaped((LEVELS, tok, wide_cols), jnp.float32),
            shaped((LEVELS, tok, wide_cols)),
        ),
        in_specs=[SMEM] + [VMEM] * 8,
        out_specs=(VMEM, VMEM),
        scratch_shapes=[pltpu.VMEM((LEVELS * tok, out_rows), jnp.bfloat16)],
        compiler_params=PARAMS,
        cost_estimate=pl.CostEstimate(
            flops=5_000_000_000, bytes_accessed=4_000_000, transcendentals=0
        ),
        name="output",
    )(where, *attended, out_pair, out_near, out_far, out_both)
    got = other_core(other)
    block = [mine[d] + got[d].astype(jnp.float32) for d in range(LEVELS)]
    shares = [up(block[d].astype(jnp.bfloat16), d) for d in range(1, LEVELS)]
    return pl.pallas_call(
        finish_kernel,
        out_shape=shaped((tok, width)),
        in_specs=[SMEM] + [VMEM] * 4,
        out_specs=VMEM,
        compiler_params=PARAMS,
        name="finish",
    )(where, block[0], *shares)


def solution(mesh):
    def run(*args):
        kv_local = args[5].shape[1] // HD // mesh.shape["head"]
        levels_fit = (
            mesh.shape["seq"] == LEVELS * PLANE
            and mesh.shape["head"] == 2
            and kv_local == LEVELS
            and args[1].shape[0] == 2 * TILE_RUN
            and args[0].shape[0] == 2048
            and args[8].shape[0] == LEVELS * PLANE * CACHED
            and args[10].shape[0] == LEVELS * PLANE * REC
        )
        return jax.shard_map(
            by_levels if levels_fit else on_device,
            mesh=mesh,
            in_specs=(
                P("seq", "head"),
                P("seq", "head"),
                P("seq"),
                P(),
                P("seq", "head"),
                P("seq", "head"),
                P("seq", "head"),
                P("head", "seq"),
                P("seq", "head"),
                P("seq", "head"),
                P("seq", "head"),
                P("seq"),
            ),
            out_specs=P("seq", "head"),
            check_vma=False,
        )(*args)

    return run
```

```python
import functools

import jax
import jax.numpy as jnp
from jax import lax
from jax.experimental import pallas as pl
from jax.experimental.pallas import tpu as pltpu
from jax.sharding import PartitionSpec as P

D = 4096
HD = 128


EPSILON = 1e-05
ROPE_BASE = 1000000.0
NEG_FILL = -1e30


def rotate(values, positions):
    half = values.shape[-1] // 2
    freqs = ROPE_BASE ** (-jnp.arange(half, dtype=jnp.float32) / half)
    angles = positions[:, None] * freqs[None, :]
    cosine = jnp.cos(angles)[:, None, :]
    sine = jnp.sin(angles)[:, None, :]
    first = values[..., :half]
    second = values[..., half:]
    return jnp.concatenate(
        [first * cosine - second * sine, second * cosine + first * sine], axis=-1
    )


def scaled(rows_wide, squares, gain):
    return (rows_wide * lax.rsqrt(squares / D + EPSILON)[:, None] * gain[None, :]).astype(
        jnp.bfloat16
    )


def attend(carry, key_piece, value_piece, queries, allowed):
    best, total, accum = carry
    count = key_piece.shape[0]
    kv_local = queries.shape[0]
    keys_split = key_piece.reshape(count, kv_local, HD)
    values_split = value_piece.reshape(count, kv_local, HD)
    scores = jnp.einsum(
        "kgtd,nkd->kgtn", queries, keys_split, preferred_element_type=jnp.float32
    ) * HD ** (-0.5)
    scores = jnp.where(allowed, scores, NEG_FILL)
    fresh = jnp.maximum(best, jnp.max(scores, axis=-1))
    factor = jnp.exp(best - fresh)
    weights = jnp.where(allowed, jnp.exp(scores - fresh[..., None]), 0.0)
    total = total * factor + jnp.sum(weights, axis=-1)
    accum = accum * factor[..., None] + jnp.einsum(
        "kgtn,nkd->kgtd",
        weights.astype(jnp.bfloat16),
        values_split,
        preferred_element_type=jnp.float32,
    )
    return (fresh, total, accum)


def on_device(
    text_rows,
    picture_rows,
    picture_slots,
    norm_gain,
    w_query,
    w_key,
    w_value,
    w_out,
    cache_keys,
    cache_values,
    recompute_rows,
    recompute_slots,
):
    tok_rows = text_rows.shape[0]
    rec_count = recompute_rows.shape[0]
    cache_rows = cache_keys.shape[0]
    seq_index = lax.axis_index("seq")
    local_pos = seq_index * tok_rows + jnp.arange(tok_rows, dtype=jnp.int32)
    rows_piece = lax.all_gather(picture_rows, "seq", axis=0, tiled=True)
    slots_piece = lax.all_gather(picture_slots, "seq", axis=0, tiled=True)
    select = (slots_piece[None, :] == local_pos[:, None]).astype(jnp.bfloat16)
    placed = jnp.dot(select, rows_piece, preferred_element_type=jnp.float32)
    hits = jnp.sum(select.astype(jnp.float32), axis=1)
    added, hits = (placed, hits)
    stream = jnp.where(hits[:, None] > 0.5, added, text_rows.astype(jnp.float32)).astype(
        jnp.bfloat16
    )
    slice_width = stream.shape[1]
    gain_slice = lax.dynamic_slice_in_dim(
        norm_gain, lax.axis_index("head") * slice_width, slice_width, 0
    )
    stream_wide = stream.astype(jnp.float32)
    rec_wide = recompute_rows.astype(jnp.float32)
    stream_sq, rec_sq = lax.psum(
        (jnp.sum(stream_wide * stream_wide, axis=1), jnp.sum(rec_wide * rec_wide, axis=1)), "head"
    )
    normed, rec_normed = (
        lax.all_gather(scaled(stream_wide, stream_sq, gain_slice), "head", axis=1, tiled=True),
        lax.all_gather(scaled(rec_wide, rec_sq, gain_slice), "head", axis=1, tiled=True),
    )
    stacked = jnp.concatenate([normed, rec_normed], axis=0)
    query_cols = w_query.shape[1]
    key_cols = w_key.shape[1]
    pieces = (
        lax.all_gather(w_query, "seq", axis=0, tiled=True),
        lax.all_gather(w_key, "seq", axis=0, tiled=True),
        lax.all_gather(w_value, "seq", axis=0, tiled=True),
    )
    query_all = jnp.dot(stacked, pieces[0], preferred_element_type=jnp.float32)
    key_all = jnp.dot(stacked, pieces[1], preferred_element_type=jnp.float32)
    value_all = jnp.dot(stacked, pieces[2], preferred_element_type=jnp.float32)
    cache_total = cache_rows * lax.axis_size("seq")
    stream_pos = (cache_total + local_pos).astype(jnp.float32)
    rec_pos = recompute_slots.astype(jnp.float32)
    heads_local = query_cols // HD
    kv_local = key_cols // HD
    group = heads_local // kv_local
    rot_query = rotate(query_all[:tok_rows].reshape(tok_rows, heads_local, HD), stream_pos).astype(
        jnp.bfloat16
    )
    rot_key = (
        rotate(key_all[:tok_rows].reshape(tok_rows, kv_local, HD), stream_pos)
        .astype(jnp.bfloat16)
        .reshape(tok_rows, key_cols)
    )
    values_new = value_all[:tok_rows].astype(jnp.bfloat16)
    rot_rec_key = (
        rotate(key_all[tok_rows:].reshape(rec_count, kv_local, HD), rec_pos)
        .astype(jnp.bfloat16)
        .reshape(rec_count, key_cols)
    )
    rec_values = value_all[tok_rows:].astype(jnp.bfloat16)
    local_slots = recompute_slots - seq_index * cache_rows
    select = local_slots[:, None] == jnp.arange(cache_rows, dtype=jnp.int32)[None, :]
    replaced = jnp.any(select, axis=0)[:, None]
    select_cols = select.astype(jnp.bfloat16).T
    new_keys = jnp.dot(select_cols, rot_rec_key, preferred_element_type=jnp.float32).astype(
        jnp.bfloat16
    )
    new_values = jnp.dot(select_cols, rec_values, preferred_element_type=jnp.float32).astype(
        jnp.bfloat16
    )
    cache_k = jnp.where(replaced, new_keys, cache_keys)
    cache_v = jnp.where(replaced, new_values, cache_values)
    queries = jnp.transpose(rot_query.reshape(tok_rows, kv_local, group, HD), (1, 2, 0, 3))
    carry_start = (
        jnp.full((kv_local, group, tok_rows), NEG_FILL, jnp.float32),
        jnp.zeros((kv_local, group, tok_rows), jnp.float32),
        jnp.zeros((kv_local, group, tok_rows, HD), jnp.float32),
    )
    pieces = (
        lax.all_gather(cache_k, "seq", axis=0, tiled=True),
        lax.all_gather(cache_v, "seq", axis=0, tiled=True),
    )
    allowed = jnp.ones((tok_rows, pieces[0].shape[0]), jnp.bool_)
    carry_mid = attend(carry_start, pieces[0], pieces[1], queries, allowed)
    pieces = (
        lax.all_gather(rot_key, "seq", axis=0, tiled=True),
        lax.all_gather(values_new, "seq", axis=0, tiled=True),
    )
    key_pos = jnp.arange(pieces[0].shape[0], dtype=jnp.int32)
    allowed = key_pos[None, :] <= local_pos[:, None]
    best, total, accum = attend(carry_mid, pieces[0], pieces[1], queries, allowed)
    attended = (
        jnp.transpose(accum / total[..., None], (2, 0, 1, 3))
        .reshape(tok_rows, query_cols)
        .astype(jnp.bfloat16)
    )
    partial_out = jnp.dot(
        attended,
        lax.all_gather(w_out, "seq", axis=1, tiled=True),
        preferred_element_type=jnp.float32,
    )
    return lax.psum_scatter(
        partial_out.astype(jnp.bfloat16), "head", scatter_dimension=1, tiled=True
    )


LEVELS = 4
PLANE = 4
TILE_RUN = 256
CACHED = 64
REC = 8
REC_PAD = 16


def permuted(value, move):
    perm = []
    for level in range(LEVELS):
        for place in range(PLANE):
            for core in range(2):
                target = move(level, place, core)
                if target is not None:
                    to_level, to_place, to_core = target
                    perm.append(
                        (
                            (level * PLANE + place) * 2 + core,
                            (to_level * PLANE + to_place) * 2 + to_core,
                        )
                    )
    return lax.ppermute(value, ("seq", "head"), perm)


def across(value, bit):
    return permuted(value, lambda z, p, c: (z ^ bit, p, c))


def up(value, steps):
    return permuted(value, lambda z, p, c: ((z + steps) % LEVELS, p, c))


def other_core(value):
    return permuted(value, lambda z, p, c: (z, p, 1 - c))


def to_near(value):
    return permuted(value, lambda z, p, c: (z, p ^ (1 + c), c))


def to_far(value):
    return permuted(value, lambda z, p, c: (z, p ^ (2 - c), c))


def place_of(which, place, core):
    if which == 0:
        return place
    if which == 3:
        return place ^ 3
    return place ^ (1 + core) if which == 1 else place ^ (2 - core)


def turned(values, cosine, sine):
    return values * cosine + pltpu.roll(values, HD // 2, 1) * sine


def pack_kernel(where_ref, *refs):
    w_key, w_value, cache_keys, cache_values, slots = refs[:5]
    outs, sems = refs[5:7], refs[7]
    level = where_ref[0]
    depth = w_key.shape[0]
    copies = []

    def copy(source, target):
        copies.append(pltpu.make_async_copy(source, target, sems.at[len(copies)]))
        copies[-1].start()

    for n in range(2):
        keys = outs[n]
        for m in range(2):
            at = jnp.bitwise_xor(level, n + 2 * m)
            small = pl.ds(pl.multiple_of(at * HD, HD), HD)
            for k, (new, old) in enumerate(((w_key, cache_keys), (w_value, cache_values))):
                to = pl.ds((2 * m + k) * HD, HD)
                copy(new.at[:, small], keys.at[0:depth, to])
                copy(old.at[:, small], keys.at[depth : depth + CACHED, to])
        copy(slots, keys.at[depth + CACHED : depth + CACHED + REC_PAD])
    for each in copies:
        each.wait()


PACK_COPIES = 18


def assemble(where_ref, parts, x_ref):
    level, core = where_ref[0], where_ref[2]
    shown = TILE_RUN // 2 // PLANE
    rows = parts[0].shape[0] - shown
    for n, part in enumerate(parts):
        x_ref[n * rows : (n + 1) * rows] = part[0:rows]
    start = where_ref[4] * rows
    for n, part in enumerate(parts):
        which = 2 * lax.rem(level + n % 2, 2) + (core if n < 2 else 1 - core)
        to = pl.multiple_of(start + which * shown, 16)
        x_ref[pl.ds(to, shown)] = part[rows : rows + shown]


def products(where_ref, x_ref, pieces):
    level, place, core = where_ref[0], where_ref[1], where_ref[2]
    total = None
    for i in range(2):
        for j in range(PLANE):
            depth = pieces[i][j].shape[0]
            block = lax.rem(level + i, 2) * PLANE + place_of(j, place, core)
            start = pl.multiple_of(block * depth, depth)
            part = jnp.dot(
                x_ref[:, pl.ds(start, depth)],
                pieces[i][j][...],
                preferred_element_type=jnp.float32,
            )
            total = part if total is None else total + part
    return total


def keys_part_kernel(
    where_ref, x0, x1, x2, x3, own, near, far, old0, old1, keep_ref, send_ref, x_ref
):
    assemble(where_ref, (x0, x1, x2, x3), x_ref)
    pieces = [[own.at[i], near.at[i], far.at[i], far.at[2 + i]] for i in range(2)]
    width = 2 * HD
    total = products(where_ref, x_ref, pieces)
    at = total.shape[0]
    keep_ref[...] = total[:, :width]
    send_ref[0:at] = total[:, width:].astype(jnp.bfloat16)
    for old in (old0, old1):
        send_ref[at : at + CACHED + REC_PAD] = old[:, width:]
        at += CACHED + REC_PAD


def keys_join_kernel(where_ref, keep_ref, got_ref, old0, old1, cos_ref, sin_ref, kv_ref, sum_ref):
    level = where_ref[0]
    rows = sum_ref.shape[0]
    block = rows // LEVELS
    tok = block - REC_PAD
    width = 2 * HD
    sum_ref[...] = keep_ref[...] + got_ref[0:rows].astype(jnp.float32)
    first = where_ref[3]
    span = CACHED + REC_PAD
    for n in range(LEVELS):
        at = jnp.bitwise_xor(level, n)
        start = pl.multiple_of(lax.rem(first + n, LEVELS) * block, 16)
        cosine, sine = cos_ref[at], sin_ref[at]
        fresh = sum_ref[pl.ds(start, tok), :]
        kv_ref[2 + at, :, 0:HD] = turned(fresh[:, :HD], cosine[:tok], sine[:tok]).astype(
            jnp.bfloat16
        )
        kv_ref[2 + at, :, HD:width] = fresh[:, HD:].astype(jnp.bfloat16)
        if n < 2:
            old = (old0, old1)[n][:, 0:width].astype(jnp.float32)
        else:
            old = got_ref[rows + (n - 2) * span : rows + (n - 1) * span].astype(jnp.float32)
        slots = old[CACHED : CACHED + REC].astype(jnp.int32)
        rec = sum_ref[pl.ds(pl.multiple_of(start + tok, 16), REC_PAD), :]
        line = lax.broadcasted_iota(jnp.int32, (CACHED, width), 0)
        found = jnp.zeros((CACHED, width), jnp.float32)
        hit = jnp.zeros((CACHED, width), jnp.int32)
        for r in range(REC):
            same = line == slots[r : r + 1]
            found = jnp.where(same, rec[r : r + 1], found)
            hit = jnp.where(same, 1, hit)
        keys = turned(found[:, :HD], cosine[tok : tok + CACHED], sine[tok : tok + CACHED])
        found = jnp.concatenate([keys, found[:, HD:]], axis=1)
        line_at = pl.multiple_of(lax.rem(at, 2) * CACHED, CACHED)
        kv_ref[at // 2, pl.ds(line_at, CACHED), :] = jnp.where(
            hit == 1, found, old[:CACHED]
        ).astype(jnp.bfloat16)


def queries_part_kernel(where_ref, x0, x1, x2, x3, *refs):
    weights, outs, x_ref = refs[:4], refs[4:8], refs[8]
    level, place, core = where_ref[0], where_ref[1], where_ref[2]
    assemble(where_ref, (x0, x1, x2, x3), x_ref)
    depth = weights[0].shape[0]
    width = 4 * HD
    block = x_ref.shape[0] // LEVELS
    tok = block - REC_PAD
    for m, out_ref in zip((0, 2, 1, 3), outs):
        group = pl.ds(pl.multiple_of(jnp.bitwise_xor(level, m) * width, width), width)
        total = None
        for j in range(PLANE):
            at = lax.rem(level, 2) * PLANE + place_of(j, place, core)
            part = jnp.dot(
                x_ref[:, pl.ds(pl.multiple_of(at * depth, depth), depth)],
                weights[j][:, group],
                preferred_element_type=jnp.float32,
            )
            total = part if total is None else total + part
        for k in range(LEVELS):
            at = jnp.bitwise_xor(level, lax.rem(k + LEVELS - where_ref[3], LEVELS))
            out_ref[at] = total[k * block : k * block + tok].astype(out_ref.dtype)


def attend_kernel(
    pair, where_ref, keep_ref, near_ref, got_ref, cos_ref, sin_ref, kv0, kv1, kv2, kv3, out_ref, query_ref
):
    level, place, core = where_ref[0], where_ref[1], where_ref[2]
    pieces = (kv0, kv1, kv2, kv3)
    tok = keep_ref.shape[1]
    old = LEVELS // 2
    heads = query_ref.shape[1]
    columns = slice(pair * heads * HD, (pair + 1) * heads * HD)
    for at in range(LEVELS):
        total = keep_ref[at, :, columns] + (
            near_ref[at, :, columns].astype(jnp.float32)
            + got_ref[at, :, columns].astype(jnp.float32)
        )
        cosine, sine = cos_ref[at][:tok], sin_ref[at][:tok]
        for h in range(heads):
            head = turned(total[:, h * HD : (h + 1) * HD], cosine, sine)
            query_ref[at, h] = head.astype(jnp.bfloat16)
    row = lax.broadcasted_iota(jnp.int32, (tok, tok), 0)
    col = lax.broadcasted_iota(jnp.int32, (tok, tok), 1)
    scale = HD ** (-0.5) * 1.4426950408889634
    for i in range(LEVELS):
        count = (old + i + 1) * tok
        queries = query_ref[i].reshape(heads * tok, HD)
        scores = []
        best = None
        for j in range(PLANE):
            keys = pieces[j][0 : old + i + 1, :, 0:HD].reshape(count, HD)
            raw = lax.dot_general(
                queries, keys, (((1,), (1,)), ((), ())), preferred_element_type=jnp.float32
            )
            if j == 0:
                allowed = col <= row
            else:
                allowed = jnp.broadcast_to(place_of(j, place, core), (tok, tok)) < place
            allowed = jnp.concatenate([allowed] * heads, axis=0)
            last = jnp.where(allowed, raw[:, count - tok :], NEG_FILL)
            raw = jnp.concatenate([raw[:, : count - tok], last], axis=1)
            top = jnp.max(raw, axis=1, keepdims=True)
            best = top if best is None else jnp.maximum(best, top)
            scores.append(raw)
        total, accum = 0.0, 0.0
        for j in range(PLANE):
            weights = jnp.exp2((scores[j] - best) * scale)
            total = total + jnp.sum(weights, axis=1, keepdims=True)
            values = pieces[j][0 : old + i + 1, :, HD : 2 * HD].reshape(count, HD)
            accum = accum + jnp.dot(
                weights.astype(jnp.bfloat16), values, preferred_element_type=jnp.float32
            )
        result = (accum / total).astype(jnp.bfloat16)
        for h in range(heads):
            out_ref[i * tok : (i + 1) * tok, h * HD : (h + 1) * HD] = result[
                h * tok : (h + 1) * tok
            ]


def output_kernel(where_ref, *refs):
    heads, weights, (mine_ref, other_ref, x_ref) = refs[:4], refs[4:-3], refs[-3:]
    level, core = where_ref[0], where_ref[2]
    depth = heads[0].shape[1]
    width = weights[0].shape[2]
    tok = mine_ref.shape[1]
    for n, ref in enumerate(heads):
        at = 2 * lax.rem(level + n // 2, 2) + n % 2
        x_ref[:, pl.ds(pl.multiple_of(at * depth, depth), depth)] = ref[...]
    swap = jnp.where(core == level // 2, 0, 1)
    for s, out_ref in enumerate((mine_ref, other_ref)):
        i = jnp.bitwise_xor(swap, s)
        for j, piece in enumerate(weights):
            slot = (0, 2, 1, 3)[j] if s else j
            part = jnp.dot(x_ref[...], piece[i], preferred_element_type=jnp.float32)
            for t in range(LEVELS):
                out_ref[
                    lax.rem(t + LEVELS - level, LEVELS), :, slot * width : (slot + 1) * width
                ] = part[t * tok : (t + 1) * tok].astype(out_ref.dtype)


def finish_kernel(where_ref, own, first, second, third, out_ref):
    level, place, core = where_ref[0], where_ref[1], where_ref[2]
    half = out_ref.shape[1] // 2
    width = half // PLANE
    sums = (
        own[...] + second[...].astype(jnp.float32),
        first[...].astype(jnp.float32) + third[...].astype(jnp.float32),
    )
    for steps, total in enumerate(sums):
        for j in range(PLANE):
            at = lax.rem(level + steps, 2) * half + place_of(j, place, core) * width
            out_ref[:, pl.ds(pl.multiple_of(at, width), width)] = total[
                :, j * width : (j + 1) * width
            ].astype(out_ref.dtype)


SMEM = pl.BlockSpec(memory_space=pltpu.SMEM)
VMEM = pl.BlockSpec(memory_space=pltpu.VMEM)
HBM = pl.BlockSpec(memory_space=pltpu.MemorySpace.HBM)
PARAMS = pltpu.CompilerParams(vmem_limit_bytes=48 * 1024 * 1024)


def shaped(shape, dtype=jnp.bfloat16):
    return jax.ShapeDtypeStruct(shape, dtype)


def by_levels(
    text_rows,
    picture_rows,
    picture_slots,
    norm_gain,
    w_query,
    w_key,
    w_value,
    w_out,
    cache_keys,
    cache_values,
    recompute_rows,
    recompute_slots,
):
    seq_index = lax.axis_index("seq")
    core = lax.axis_index("head")
    level, place = seq_index // PLANE, seq_index % PLANE
    half_at = level // 2
    own_first = core == half_at
    tok, width = text_rows.shape
    block_rows = tok + REC_PAD

    stream_len = tok * LEVELS * PLANE
    tile_owners = TILE_RUN // tok
    first = stream_len // 2 // tok
    last = (stream_len - TILE_RUN) // tok
    owners = [first + i for i in range(tile_owners)] + [last + i for i in range(tile_owners)]
    assert [owner % PLANE for owner in owners] == list(range(LEVELS))
    owner_level = jnp.where(place < tile_owners, first // PLANE, last // PLANE)

    first_block = jnp.where(own_first, 0, 2)
    shown_block = (first_block + (level ^ owner_level)) % LEVELS
    where = jnp.stack([level, place, core, first_block, shown_block]).astype(jnp.int32)

    slots = (recompute_slots - seq_index * CACHED).astype(jnp.bfloat16)
    slot_rows = jnp.broadcast_to(jnp.pad(slots, (0, REC_PAD - REC))[:, None], (REC_PAD, 4 * HD))
    depth = w_key.shape[0]
    rows = jnp.concatenate(
        [text_rows, recompute_rows, jnp.zeros((REC_PAD - REC, width), text_rows.dtype)], axis=0
    )
    gain = lax.dynamic_slice_in_dim(norm_gain, core * width, width, 0)
    wide, pictures = rows.astype(jnp.float32), picture_rows.astype(jnp.float32)
    squares, picture_squares = lax.psum(
        (jnp.sum(wide * wide, axis=1), jnp.sum(pictures * pictures, axis=1)), "head"
    )
    normed = scaled(wide, squares, gain)
    pictures = scaled(pictures, picture_squares, gain)

    normed, pictures, slot_rows = lax.optimization_barrier((normed, pictures, slot_rows))
    key_own, key_give = pl.pallas_call(
        pack_kernel,
        out_shape=(shaped((depth + CACHED + REC_PAD, 4 * HD)),) * 2,
        in_specs=[SMEM] + [HBM] * 5,
        out_specs=(HBM,) * 2,
        scratch_shapes=[pltpu.SemaphoreType.DMA((PACK_COPIES,))],
        compiler_params=PARAMS,
        cost_estimate=pl.CostEstimate(
            flops=6_000_000_000, bytes_accessed=4_000_000, transcendentals=0
        ),
        name="pack",
    )(where, w_key, w_value, cache_keys, cache_values, slot_rows)

    out_rows = w_out.shape[0] // 2
    out_own, out_give = (
        lax.dynamic_slice_in_dim(w_out, at * out_rows, out_rows, 0) for at in (half_at, 1 - half_at)
    )

    crossed = permuted(normed, lambda z, p, c: (z ^ 2, p, 1 - c) if c == 1 - z // 2 else None)
    shown = permuted(pictures, lambda z, p, c: (2 * c + p // 2, z, p % 2))
    key_next = across(key_give, 1)
    query_near, query_far = to_near(w_query), to_far(w_query)
    query_near, query_far = lax.optimization_barrier((query_near, query_far))
    query_both = to_far(query_near)
    shown, key_next = lax.optimization_barrier((shown, key_next))
    keys = jnp.stack([key_own[:depth], key_next[:depth]])
    old_own, old_next = key_own[depth:], key_next[depth:]
    keys_near = to_near(keys)
    crossed, shown, out_give = lax.optimization_barrier((crossed, shown, out_give))
    held = jnp.concatenate([jnp.where(own_first, normed, crossed), shown], axis=0)
    next_rows = across(held, 1)
    held_other = other_core(held)
    out_half = out_rows // 2
    next_rows, out_got0 = lax.optimization_barrier((next_rows, across(out_give[:out_half], 2)))
    out_got1 = across(out_give[out_half:], 2)
    next_other = other_core(next_rows)
    keys_far = to_far(jnp.concatenate([keys, keys_near], axis=0))
    next_other, held_other, keys_far, query_both = lax.optimization_barrier(
        (next_other, held_other, keys_far, query_both)
    )
    parts = (held, next_rows, held_other, next_other)

    half = HD // 2
    freqs = ROPE_BASE ** (-jnp.arange(half, dtype=jnp.float32) / half)
    blocks = (jnp.arange(LEVELS, dtype=jnp.int32) * PLANE + place)[:, None]
    stream_pos = (
        CACHED * LEVELS * PLANE + blocks * tok + jnp.arange(tok, dtype=jnp.int32)[None]
    ).astype(jnp.float32)
    cache_pos = (blocks * CACHED + jnp.arange(CACHED, dtype=jnp.int32)[None]).astype(jnp.float32)
    angles = jnp.concatenate([stream_pos, cache_pos], axis=1)[..., None] * freqs
    cosine, sine = jnp.cos(angles), jnp.sin(angles)
    cosine = jnp.concatenate([cosine, cosine], axis=-1)
    sine = jnp.concatenate([-sine, sine], axis=-1)

    all_rows = LEVELS * block_rows
    keep, send = pl.pallas_call(
        keys_part_kernel,
        out_shape=(
            shaped((all_rows, 2 * HD), jnp.float32),
            shaped((all_rows + 2 * (CACHED + REC_PAD), 2 * HD)),
        ),
        in_specs=[SMEM] + [VMEM] * 9,
        out_specs=(VMEM, VMEM),
        scratch_shapes=[pltpu.VMEM((all_rows, width), jnp.bfloat16)],
        compiler_params=PARAMS,
        cost_estimate=pl.CostEstimate(
            flops=3_000_000_000, bytes_accessed=4_000_000, transcendentals=0
        ),
        name="keys_part",
    )(where, *parts, keys, keys_near, keys_far, old_own, old_next)
    send, *parts = lax.optimization_barrier((send, *parts))
    group_shape = (LEVELS, tok, 4 * HD)
    q_keep, q_keep2, q_send, q_send2 = pl.pallas_call(
        queries_part_kernel,
        out_shape=(shaped(group_shape, jnp.float32),) * 2 + (shaped(group_shape),) * 2,
        in_specs=[SMEM] + [VMEM] * 8,
        out_specs=(VMEM,) * 4,
        scratch_shapes=[pltpu.VMEM((all_rows, width), jnp.bfloat16)],
        compiler_params=PARAMS,
        cost_estimate=pl.CostEstimate(
            flops=5_000_000_000, bytes_accessed=4_000_000, transcendentals=0
        ),
        name="queries_part",
    )(where, *parts, w_query, query_near, query_far, query_both)
    got_near2 = across(q_send2, 1)
    got_near = across(q_send, 1)
    got_queries = across((q_keep2 + got_near2.astype(jnp.float32)).astype(jnp.bfloat16), 2)
    out_got1, q_send2 = lax.optimization_barrier((out_got1, q_send2))
    out_pair = jnp.stack([out_own, jnp.concatenate([out_got0, out_got1], axis=0)])
    out_near = to_near(out_pair)
    got_keys, q_send2 = lax.optimization_barrier((across(send, 2), q_send2))
    kv = pl.pallas_call(
        keys_join_kernel,
        out_shape=shaped((LEVELS // 2 + LEVELS, tok, 2 * HD)),
        in_specs=[SMEM] + [VMEM] * 6,
        out_specs=VMEM,
        scratch_shapes=[pltpu.VMEM((all_rows, 2 * HD), jnp.float32)],
        compiler_params=PARAMS,
        cost_estimate=pl.CostEstimate(
            flops=24_000_000_000, bytes_accessed=4_000_000, transcendentals=0
        ),
        name="keys_join",
    )(where, keep, got_keys, old_own, old_next, cosine, sine)
    kv_near, kv_far = to_near(kv), to_far(kv)
    kv_both = permuted(kv, lambda z, p, c: (z, p ^ 3, c))

    kv_near, kv_far, kv_both, out_near, out_pair = lax.optimization_barrier(
        (kv_near, kv_far, kv_both, out_near, out_pair)
    )
    out_far, out_both = to_far(out_pair), to_far(out_near)

    attended = [
        pl.pallas_call(
            functools.partial(attend_kernel, pair),
            out_shape=shaped((LEVELS * tok, 2 * HD)),
            in_specs=[SMEM] + [VMEM] * 9,
            out_specs=VMEM,
            scratch_shapes=[pltpu.VMEM((LEVELS, 2, tok, HD), jnp.bfloat16)],
            compiler_params=PARAMS,
            cost_estimate=pl.CostEstimate(
                flops=4_000_000_000, bytes_accessed=4_000_000, transcendentals=2_400_000
            ),
            name="attend",
        )(where, q_keep, got_near, got_queries, cosine, sine, kv, kv_near, kv_far, kv_both)
        for pair in range(2)
    ]
    attended += [across(each, 1) for each in attended]

    wide_cols = PLANE * w_out.shape[1]
    mine, other = pl.pallas_call(
        output_kernel,
        out_shape=(
            shaped((LEVELS, tok, wide_cols), jnp.float32),
            shaped((LEVELS, tok, wide_cols)),
        ),
        in_specs=[SMEM] + [VMEM] * 8,
        out_specs=(VMEM, VMEM),
        scratch_shapes=[pltpu.VMEM((LEVELS * tok, out_rows), jnp.bfloat16)],
        compiler_params=PARAMS,
        cost_estimate=pl.CostEstimate(
            flops=5_000_000_000, bytes_accessed=4_000_000, transcendentals=0
        ),
        name="output",
    )(where, *attended, out_pair, out_near, out_far, out_both)
    got = other_core(other)
    block = [mine[d] + got[d].astype(jnp.float32) for d in range(LEVELS)]
    shares = [up(block[d].astype(jnp.bfloat16), d) for d in range(1, LEVELS)]
    return pl.pallas_call(
        finish_kernel,
        out_shape=shaped((tok, width)),
        in_specs=[SMEM] + [VMEM] * 4,
        out_specs=VMEM,
        compiler_params=PARAMS,
        name="finish",
    )(where, block[0], *shares)


def solution(mesh):
    def run(*args):
        kv_local = args[5].shape[1] // HD // mesh.shape["head"]
        levels_fit = (
            mesh.shape["seq"] == LEVELS * PLANE
            and mesh.shape["head"] == 2
            and kv_local == LEVELS
            and args[1].shape[0] == 2 * TILE_RUN
            and args[0].shape[0] == 2048
            and args[8].shape[0] == LEVELS * PLANE * CACHED
            and args[10].shape[0] == LEVELS * PLANE * REC
        )
        return jax.shard_map(
            by_levels if levels_fit else on_device,
            mesh=mesh,
            in_specs=(
                P("seq", "head"),
                P("seq", "head"),
                P("seq"),
                P(),
                P("seq", "head"),
                P("seq", "head"),
                P("seq", "head"),
                P("head", "seq"),
                P("seq", "head"),
                P("seq", "head"),
                P("seq", "head"),
                P("seq"),
            ),
            out_specs=P("seq", "head"),
            check_vma=False,
        )(*args)

    return run
```

```python
import functools

import jax
import jax.numpy as jnp
from jax import lax
from jax.experimental import pallas as pl
from jax.experimental.pallas import tpu as pltpu
from jax.sharding import PartitionSpec as P

D = 4096
HD = 128


EPSILON = 1e-05
ROPE_BASE = 1000000.0
NEG_FILL = -1e30


def rotate(values, positions):
    half = values.shape[-1] // 2
    freqs = ROPE_BASE ** (-jnp.arange(half, dtype=jnp.float32) / half)
    angles = positions[:, None] * freqs[None, :]
    cosine = jnp.cos(angles)[:, None, :]
    sine = jnp.sin(angles)[:, None, :]
    first = values[..., :half]
    second = values[..., half:]
    return jnp.concatenate(
        [first * cosine - second * sine, second * cosine + first * sine], axis=-1
    )


def scaled(rows_wide, squares, gain):
    return (rows_wide * lax.rsqrt(squares / D + EPSILON)[:, None] * gain[None, :]).astype(
        jnp.bfloat16
    )


def attend(carry, key_piece, value_piece, queries, allowed):
    best, total, accum = carry
    count = key_piece.shape[0]
    kv_local = queries.shape[0]
    keys_split = key_piece.reshape(count, kv_local, HD)
    values_split = value_piece.reshape(count, kv_local, HD)
    scores = jnp.einsum(
        "kgtd,nkd->kgtn", queries, keys_split, preferred_element_type=jnp.float32
    ) * HD ** (-0.5)
    scores = jnp.where(allowed, scores, NEG_FILL)
    fresh = jnp.maximum(best, jnp.max(scores, axis=-1))
    factor = jnp.exp(best - fresh)
    weights = jnp.where(allowed, jnp.exp(scores - fresh[..., None]), 0.0)
    total = total * factor + jnp.sum(weights, axis=-1)
    accum = accum * factor[..., None] + jnp.einsum(
        "kgtn,nkd->kgtd",
        weights.astype(jnp.bfloat16),
        values_split,
        preferred_element_type=jnp.float32,
    )
    return (fresh, total, accum)


def on_device(
    text_rows,
    picture_rows,
    picture_slots,
    norm_gain,
    w_query,
    w_key,
    w_value,
    w_out,
    cache_keys,
    cache_values,
    recompute_rows,
    recompute_slots,
):
    tok_rows = text_rows.shape[0]
    rec_count = recompute_rows.shape[0]
    cache_rows = cache_keys.shape[0]
    seq_index = lax.axis_index("seq")
    local_pos = seq_index * tok_rows + jnp.arange(tok_rows, dtype=jnp.int32)
    rows_piece = lax.all_gather(picture_rows, "seq", axis=0, tiled=True)
    slots_piece = lax.all_gather(picture_slots, "seq", axis=0, tiled=True)
    select = (slots_piece[None, :] == local_pos[:, None]).astype(jnp.bfloat16)
    placed = jnp.dot(select, rows_piece, preferred_element_type=jnp.float32)
    hits = jnp.sum(select.astype(jnp.float32), axis=1)
    added, hits = (placed, hits)
    stream = jnp.where(hits[:, None] > 0.5, added, text_rows.astype(jnp.float32)).astype(
        jnp.bfloat16
    )
    slice_width = stream.shape[1]
    gain_slice = lax.dynamic_slice_in_dim(
        norm_gain, lax.axis_index("head") * slice_width, slice_width, 0
    )
    stream_wide = stream.astype(jnp.float32)
    rec_wide = recompute_rows.astype(jnp.float32)
    stream_sq, rec_sq = lax.psum(
        (jnp.sum(stream_wide * stream_wide, axis=1), jnp.sum(rec_wide * rec_wide, axis=1)), "head"
    )
    normed, rec_normed = (
        lax.all_gather(scaled(stream_wide, stream_sq, gain_slice), "head", axis=1, tiled=True),
        lax.all_gather(scaled(rec_wide, rec_sq, gain_slice), "head", axis=1, tiled=True),
    )
    stacked = jnp.concatenate([normed, rec_normed], axis=0)
    query_cols = w_query.shape[1]
    key_cols = w_key.shape[1]
    pieces = (
        lax.all_gather(w_query, "seq", axis=0, tiled=True),
        lax.all_gather(w_key, "seq", axis=0, tiled=True),
        lax.all_gather(w_value, "seq", axis=0, tiled=True),
    )
    query_all = jnp.dot(stacked, pieces[0], preferred_element_type=jnp.float32)
    key_all = jnp.dot(stacked, pieces[1], preferred_element_type=jnp.float32)
    value_all = jnp.dot(stacked, pieces[2], preferred_element_type=jnp.float32)
    cache_total = cache_rows * lax.axis_size("seq")
    stream_pos = (cache_total + local_pos).astype(jnp.float32)
    rec_pos = recompute_slots.astype(jnp.float32)
    heads_local = query_cols // HD
    kv_local = key_cols // HD
    group = heads_local // kv_local
    rot_query = rotate(query_all[:tok_rows].reshape(tok_rows, heads_local, HD), stream_pos).astype(
        jnp.bfloat16
    )
    rot_key = (
        rotate(key_all[:tok_rows].reshape(tok_rows, kv_local, HD), stream_pos)
        .astype(jnp.bfloat16)
        .reshape(tok_rows, key_cols)
    )
    values_new = value_all[:tok_rows].astype(jnp.bfloat16)
    rot_rec_key = (
        rotate(key_all[tok_rows:].reshape(rec_count, kv_local, HD), rec_pos)
        .astype(jnp.bfloat16)
        .reshape(rec_count, key_cols)
    )
    rec_values = value_all[tok_rows:].astype(jnp.bfloat16)
    local_slots = recompute_slots - seq_index * cache_rows
    select = local_slots[:, None] == jnp.arange(cache_rows, dtype=jnp.int32)[None, :]
    replaced = jnp.any(select, axis=0)[:, None]
    select_cols = select.astype(jnp.bfloat16).T
    new_keys = jnp.dot(select_cols, rot_rec_key, preferred_element_type=jnp.float32).astype(
        jnp.bfloat16
    )
    new_values = jnp.dot(select_cols, rec_values, preferred_element_type=jnp.float32).astype(
        jnp.bfloat16
    )
    cache_k = jnp.where(replaced, new_keys, cache_keys)
    cache_v = jnp.where(replaced, new_values, cache_values)
    queries = jnp.transpose(rot_query.reshape(tok_rows, kv_local, group, HD), (1, 2, 0, 3))
    carry_start = (
        jnp.full((kv_local, group, tok_rows), NEG_FILL, jnp.float32),
        jnp.zeros((kv_local, group, tok_rows), jnp.float32),
        jnp.zeros((kv_local, group, tok_rows, HD), jnp.float32),
    )
    pieces = (
        lax.all_gather(cache_k, "seq", axis=0, tiled=True),
        lax.all_gather(cache_v, "seq", axis=0, tiled=True),
    )
    allowed = jnp.ones((tok_rows, pieces[0].shape[0]), jnp.bool_)
    carry_mid = attend(carry_start, pieces[0], pieces[1], queries, allowed)
    pieces = (
        lax.all_gather(rot_key, "seq", axis=0, tiled=True),
        lax.all_gather(values_new, "seq", axis=0, tiled=True),
    )
    key_pos = jnp.arange(pieces[0].shape[0], dtype=jnp.int32)
    allowed = key_pos[None, :] <= local_pos[:, None]
    best, total, accum = attend(carry_mid, pieces[0], pieces[1], queries, allowed)
    attended = (
        jnp.transpose(accum / total[..., None], (2, 0, 1, 3))
        .reshape(tok_rows, query_cols)
        .astype(jnp.bfloat16)
    )
    partial_out = jnp.dot(
        attended,
        lax.all_gather(w_out, "seq", axis=1, tiled=True),
        preferred_element_type=jnp.float32,
    )
    return lax.psum_scatter(
        partial_out.astype(jnp.bfloat16), "head", scatter_dimension=1, tiled=True
    )


LEVELS = 4
PLANE = 4
TILE_RUN = 256
CACHED = 64
REC = 8
REC_PAD = 16


def permuted(value, move):
    perm = []
    for level in range(LEVELS):
        for place in range(PLANE):
            for core in range(2):
                target = move(level, place, core)
                if target is not None:
                    to_level, to_place, to_core = target
                    perm.append(
                        (
                            (level * PLANE + place) * 2 + core,
                            (to_level * PLANE + to_place) * 2 + to_core,
                        )
                    )
    return lax.ppermute(value, ("seq", "head"), perm)


def across(value, bit):
    return permuted(value, lambda z, p, c: (z ^ bit, p, c))


def up(value, steps):
    return permuted(value, lambda z, p, c: ((z + steps) % LEVELS, p, c))


def other_core(value):
    return permuted(value, lambda z, p, c: (z, p, 1 - c))


def to_near(value):
    return permuted(value, lambda z, p, c: (z, p ^ (1 + c), c))


def to_far(value):
    return permuted(value, lambda z, p, c: (z, p ^ (2 - c), c))


def place_of(which, place, core):
    if which == 0:
        return place
    if which == 3:
        return place ^ 3
    return place ^ (1 + core) if which == 1 else place ^ (2 - core)


def turned(values, cosine, sine):
    return values * cosine + pltpu.roll(values, HD // 2, 1) * sine


def pack_kernel(where_ref, *refs):
    w_key, w_value, cache_keys, cache_values, slots = refs[:5]
    outs, sems = refs[5:7], refs[7]
    level = where_ref[0]
    depth = w_key.shape[0]
    copies = []

    def copy(source, target):
        copies.append(pltpu.make_async_copy(source, target, sems.at[len(copies)]))
        copies[-1].start()

    for n in range(2):
        keys = outs[n]
        for m in range(2):
            at = jnp.bitwise_xor(level, n + 2 * m)
            small = pl.ds(pl.multiple_of(at * HD, HD), HD)
            for k, (new, old) in enumerate(((w_key, cache_keys), (w_value, cache_values))):
                to = pl.ds((2 * m + k) * HD, HD)
                copy(new.at[:, small], keys.at[0:depth, to])
                copy(old.at[:, small], keys.at[depth : depth + CACHED, to])
        copy(slots, keys.at[depth + CACHED : depth + CACHED + REC_PAD])
    for each in copies:
        each.wait()


PACK_COPIES = 18


def assemble(where_ref, parts, x_ref):
    level, core = where_ref[0], where_ref[2]
    shown = TILE_RUN // 2 // PLANE
    rows = parts[0].shape[0] - shown
    for n, part in enumerate(parts):
        x_ref[n * rows : (n + 1) * rows] = part[0:rows]
    start = where_ref[4] * rows
    for n, part in enumerate(parts):
        which = 2 * lax.rem(level + n % 2, 2) + (core if n < 2 else 1 - core)
        to = pl.multiple_of(start + which * shown, 16)
        x_ref[pl.ds(to, shown)] = part[rows : rows + shown]


def products(where_ref, x_ref, pieces):
    level, place, core = where_ref[0], where_ref[1], where_ref[2]
    total = None
    for i in range(2):
        for j in range(PLANE):
            depth = pieces[i][j].shape[0]
            block = lax.rem(level + i, 2) * PLANE + place_of(j, place, core)
            start = pl.multiple_of(block * depth, depth)
            part = jnp.dot(
                x_ref[:, pl.ds(start, depth)],
                pieces[i][j][...],
                preferred_element_type=jnp.float32,
            )
            total = part if total is None else total + part
    return total


def keys_part_kernel(
    where_ref, x0, x1, x2, x3, own, near, far, old0, old1, keep_ref, send_ref, x_ref
):
    assemble(where_ref, (x0, x1, x2, x3), x_ref)
    pieces = [[own.at[i], near.at[i], far.at[i], far.at[2 + i]] for i in range(2)]
    width = 2 * HD
    total = products(where_ref, x_ref, pieces)
    at = total.shape[0]
    keep_ref[...] = total[:, :width]
    send_ref[0:at] = total[:, width:].astype(jnp.bfloat16)
    for old in (old0, old1):
        send_ref[at : at + CACHED + REC_PAD] = old[:, width:]
        at += CACHED + REC_PAD


def keys_join_kernel(where_ref, keep_ref, got_ref, old0, old1, cos_ref, sin_ref, kv_ref, sum_ref):
    level = where_ref[0]
    rows = sum_ref.shape[0]
    block = rows // LEVELS
    tok = block - REC_PAD
    width = 2 * HD
    sum_ref[...] = keep_ref[...] + got_ref[0:rows].astype(jnp.float32)
    first = where_ref[3]
    span = CACHED + REC_PAD
    for n in range(LEVELS):
        at = jnp.bitwise_xor(level, n)
        start = pl.multiple_of(lax.rem(first + n, LEVELS) * block, 16)
        cosine, sine = cos_ref[at], sin_ref[at]
        fresh = sum_ref[pl.ds(start, tok), :]
        kv_ref[2 + at, :, 0:HD] = turned(fresh[:, :HD], cosine[:tok], sine[:tok]).astype(
            jnp.bfloat16
        )
        kv_ref[2 + at, :, HD:width] = fresh[:, HD:].astype(jnp.bfloat16)
        if n < 2:
            old = (old0, old1)[n][:, 0:width].astype(jnp.float32)
        else:
            old = got_ref[rows + (n - 2) * span : rows + (n - 1) * span].astype(jnp.float32)
        slots = old[CACHED : CACHED + REC].astype(jnp.int32)
        rec = sum_ref[pl.ds(pl.multiple_of(start + tok, 16), REC_PAD), :]
        line = lax.broadcasted_iota(jnp.int32, (CACHED, width), 0)
        found = jnp.zeros((CACHED, width), jnp.float32)
        hit = jnp.zeros((CACHED, width), jnp.int32)
        for r in range(REC):
            same = line == slots[r : r + 1]
            found = jnp.where(same, rec[r : r + 1], found)
            hit = jnp.where(same, 1, hit)
        keys = turned(found[:, :HD], cosine[tok : tok + CACHED], sine[tok : tok + CACHED])
        found = jnp.concatenate([keys, found[:, HD:]], axis=1)
        line_at = pl.multiple_of(lax.rem(at, 2) * CACHED, CACHED)
        kv_ref[at // 2, pl.ds(line_at, CACHED), :] = jnp.where(
            hit == 1, found, old[:CACHED]
        ).astype(jnp.bfloat16)


def queries_part_kernel(where_ref, x0, x1, x2, x3, *refs):
    weights, outs, x_ref = refs[:4], refs[4:8], refs[8]
    level, place, core = where_ref[0], where_ref[1], where_ref[2]
    assemble(where_ref, (x0, x1, x2, x3), x_ref)
    depth = weights[0].shape[0]
    width = 4 * HD
    block = x_ref.shape[0] // LEVELS
    tok = block - REC_PAD
    for m, out_ref in zip((0, 2, 1, 3), outs):
        group = pl.ds(pl.multiple_of(jnp.bitwise_xor(level, m) * width, width), width)
        total = None
        for j in range(PLANE):
            at = lax.rem(level, 2) * PLANE + place_of(j, place, core)
            part = jnp.dot(
                x_ref[:, pl.ds(pl.multiple_of(at * depth, depth), depth)],
                weights[j][:, group],
                preferred_element_type=jnp.float32,
            )
            total = part if total is None else total + part
        for k in range(LEVELS):
            at = jnp.bitwise_xor(level, lax.rem(k + LEVELS - where_ref[3], LEVELS))
            out_ref[at] = total[k * block : k * block + tok].astype(out_ref.dtype)


def attend_kernel(
    pair, where_ref, keep_ref, near_ref, got_ref, cos_ref, sin_ref, kv0, kv1, kv2, kv3, out_ref, query_ref
):
    level, place, core = where_ref[0], where_ref[1], where_ref[2]
    pieces = (kv0, kv1, kv2, kv3)
    tok = keep_ref.shape[1]
    old = LEVELS // 2
    heads = query_ref.shape[1]
    columns = slice(pair * heads * HD, (pair + 1) * heads * HD)
    for at in range(LEVELS):
        total = keep_ref[at, :, columns] + (
            near_ref[at, :, columns].astype(jnp.float32)
            + got_ref[at, :, columns].astype(jnp.float32)
        )
        cosine, sine = cos_ref[at][:tok], sin_ref[at][:tok]
        for h in range(heads):
            head = turned(total[:, h * HD : (h + 1) * HD], cosine, sine)
            query_ref[at, h] = head.astype(jnp.bfloat16)
    row = lax.broadcasted_iota(jnp.int32, (tok, tok), 0)
    col = lax.broadcasted_iota(jnp.int32, (tok, tok), 1)
    scale = HD ** (-0.5) * 1.4426950408889634
    for i in range(LEVELS):
        count = (old + i + 1) * tok
        queries = query_ref[i].reshape(heads * tok, HD)
        scores = []
        best = None
        for j in range(PLANE):
            keys = pieces[j][0 : old + i + 1, :, 0:HD].reshape(count, HD)
            raw = lax.dot_general(
                queries, keys, (((1,), (1,)), ((), ())), preferred_element_type=jnp.float32
            )
            if j == 0:
                allowed = col <= row
            else:
                allowed = jnp.broadcast_to(place_of(j, place, core), (tok, tok)) < place
            allowed = jnp.concatenate([allowed] * heads, axis=0)
            last = jnp.where(allowed, raw[:, count - tok :], NEG_FILL)
            raw = jnp.concatenate([raw[:, : count - tok], last], axis=1)
            top = jnp.max(raw, axis=1, keepdims=True)
            best = top if best is None else jnp.maximum(best, top)
            scores.append(raw)
        total, accum = 0.0, 0.0
        for j in range(PLANE):
            weights = jnp.exp2((scores[j] - best) * scale)
            total = total + jnp.sum(weights, axis=1, keepdims=True)
            values = pieces[j][0 : old + i + 1, :, HD : 2 * HD].reshape(count, HD)
            accum = accum + jnp.dot(
                weights.astype(jnp.bfloat16), values, preferred_element_type=jnp.float32
            )
        result = (accum / total).astype(jnp.bfloat16)
        for h in range(heads):
            out_ref[i * tok : (i + 1) * tok, h * HD : (h + 1) * HD] = result[
                h * tok : (h + 1) * tok
            ]


def output_kernel(where_ref, *refs):
    heads, weights, (mine_ref, other_ref, x_ref) = refs[:4], refs[4:-3], refs[-3:]
    level, core = where_ref[0], where_ref[2]
    depth = heads[0].shape[1]
    width = weights[0].shape[2]
    tok = mine_ref.shape[1]
    for n, ref in enumerate(heads):
        at = 2 * lax.rem(level + n // 2, 2) + n % 2
        x_ref[:, pl.ds(pl.multiple_of(at * depth, depth), depth)] = ref[...]
    swap = jnp.where(core == level // 2, 0, 1)
    for s, out_ref in enumerate((mine_ref, other_ref)):
        i = jnp.bitwise_xor(swap, s)
        for j, piece in enumerate(weights):
            slot = (0, 2, 1, 3)[j] if s else j
            part = jnp.dot(x_ref[...], piece[i], preferred_element_type=jnp.float32)
            for t in range(LEVELS):
                out_ref[
                    lax.rem(t + LEVELS - level, LEVELS), :, slot * width : (slot + 1) * width
                ] = part[t * tok : (t + 1) * tok].astype(out_ref.dtype)


def finish_kernel(where_ref, own, first, second, third, out_ref):
    level, place, core = where_ref[0], where_ref[1], where_ref[2]
    half = out_ref.shape[1] // 2
    width = half // PLANE
    sums = (
        own[...] + second[...].astype(jnp.float32),
        first[...].astype(jnp.float32) + third[...].astype(jnp.float32),
    )
    for steps, total in enumerate(sums):
        for j in range(PLANE):
            at = lax.rem(level + steps, 2) * half + place_of(j, place, core) * width
            out_ref[:, pl.ds(pl.multiple_of(at, width), width)] = total[
                :, j * width : (j + 1) * width
            ].astype(out_ref.dtype)


SMEM = pl.BlockSpec(memory_space=pltpu.SMEM)
VMEM = pl.BlockSpec(memory_space=pltpu.VMEM)
HBM = pl.BlockSpec(memory_space=pltpu.MemorySpace.HBM)
PARAMS = pltpu.CompilerParams(vmem_limit_bytes=48 * 1024 * 1024)


def shaped(shape, dtype=jnp.bfloat16):
    return jax.ShapeDtypeStruct(shape, dtype)


def by_levels(
    text_rows,
    picture_rows,
    picture_slots,
    norm_gain,
    w_query,
    w_key,
    w_value,
    w_out,
    cache_keys,
    cache_values,
    recompute_rows,
    recompute_slots,
):
    seq_index = lax.axis_index("seq")
    core = lax.axis_index("head")
    level, place = seq_index // PLANE, seq_index % PLANE
    half_at = level // 2
    own_first = core == half_at
    tok, width = text_rows.shape
    block_rows = tok + REC_PAD

    stream_len = tok * LEVELS * PLANE
    tile_owners = TILE_RUN // tok
    first = stream_len // 2 // tok
    last = (stream_len - TILE_RUN) // tok
    owners = [first + i for i in range(tile_owners)] + [last + i for i in range(tile_owners)]
    assert [owner % PLANE for owner in owners] == list(range(LEVELS))
    owner_level = jnp.where(place < tile_owners, first // PLANE, last // PLANE)

    first_block = jnp.where(own_first, 0, 2)
    shown_block = (first_block + (level ^ owner_level)) % LEVELS
    where = jnp.stack([level, place, core, first_block, shown_block]).astype(jnp.int32)

    slots = (recompute_slots - seq_index * CACHED).astype(jnp.bfloat16)
    slot_rows = jnp.broadcast_to(jnp.pad(slots, (0, REC_PAD - REC))[:, None], (REC_PAD, 4 * HD))
    depth = w_key.shape[0]
    rows = jnp.concatenate(
        [text_rows, recompute_rows, jnp.zeros((REC_PAD - REC, width), text_rows.dtype)], axis=0
    )
    gain = lax.dynamic_slice_in_dim(norm_gain, core * width, width, 0)
    wide, pictures = rows.astype(jnp.float32), picture_rows.astype(jnp.float32)
    squares, picture_squares = lax.psum(
        (jnp.sum(wide * wide, axis=1), jnp.sum(pictures * pictures, axis=1)), "head"
    )
    normed = scaled(wide, squares, gain)
    pictures = scaled(pictures, picture_squares, gain)

    normed, pictures, slot_rows = lax.optimization_barrier((normed, pictures, slot_rows))
    key_own, key_give = pl.pallas_call(
        pack_kernel,
        out_shape=(shaped((depth + CACHED + REC_PAD, 4 * HD)),) * 2,
        in_specs=[SMEM] + [HBM] * 5,
        out_specs=(HBM,) * 2,
        scratch_shapes=[pltpu.SemaphoreType.DMA((PACK_COPIES,))],
        compiler_params=PARAMS,
        cost_estimate=pl.CostEstimate(
            flops=6_000_000_000, bytes_accessed=4_000_000, transcendentals=0
        ),
        name="pack",
    )(where, w_key, w_value, cache_keys, cache_values, slot_rows)

    out_rows = w_out.shape[0] // 2
    out_own, out_give = (
        lax.dynamic_slice_in_dim(w_out, at * out_rows, out_rows, 0) for at in (half_at, 1 - half_at)
    )

    crossed = permuted(normed, lambda z, p, c: (z ^ 2, p, 1 - c) if c == 1 - z // 2 else None)
    shown = permuted(pictures, lambda z, p, c: (2 * c + p // 2, z, p % 2))
    key_next = across(key_give, 1)
    query_near, query_far = to_near(w_query), to_far(w_query)
    shown, key_next, query_near, query_far = lax.optimization_barrier(
        (shown, key_next, query_near, query_far)
    )
    query_both = to_far(query_near)
    keys = jnp.stack([key_own[:depth], key_next[:depth]])
    old_own, old_next = key_own[depth:], key_next[depth:]
    keys_near = to_near(keys)
    crossed, shown, out_give = lax.optimization_barrier((crossed, shown, out_give))
    held = jnp.concatenate([jnp.where(own_first, normed, crossed), shown], axis=0)
    next_rows = across(held, 1)
    held_other = other_core(held)
    out_half = out_rows // 2
    next_rows, out_got0, query_both = lax.optimization_barrier(
        (next_rows, across(out_give[:out_half], 2), query_both)
    )
    out_got1 = across(out_give[out_half:], 2)
    next_other = other_core(next_rows)
    keys_far = to_far(jnp.concatenate([keys, keys_near], axis=0))
    next_other, held_other, keys_far = lax.optimization_barrier(
        (next_other, held_other, keys_far)
    )
    parts = (held, next_rows, held_other, next_other)

    half = HD // 2
    freqs = ROPE_BASE ** (-jnp.arange(half, dtype=jnp.float32) / half)
    blocks = (jnp.arange(LEVELS, dtype=jnp.int32) * PLANE + place)[:, None]
    stream_pos = (
        CACHED * LEVELS * PLANE + blocks * tok + jnp.arange(tok, dtype=jnp.int32)[None]
    ).astype(jnp.float32)
    cache_pos = (blocks * CACHED + jnp.arange(CACHED, dtype=jnp.int32)[None]).astype(jnp.float32)
    angles = jnp.concatenate([stream_pos, cache_pos], axis=1)[..., None] * freqs
    cosine, sine = jnp.cos(angles), jnp.sin(angles)
    cosine = jnp.concatenate([cosine, cosine], axis=-1)
    sine = jnp.concatenate([-sine, sine], axis=-1)

    all_rows = LEVELS * block_rows
    keep, send = pl.pallas_call(
        keys_part_kernel,
        out_shape=(
            shaped((all_rows, 2 * HD), jnp.float32),
            shaped((all_rows + 2 * (CACHED + REC_PAD), 2 * HD)),
        ),
        in_specs=[SMEM] + [VMEM] * 9,
        out_specs=(VMEM, VMEM),
        scratch_shapes=[pltpu.VMEM((all_rows, width), jnp.bfloat16)],
        compiler_params=PARAMS,
        cost_estimate=pl.CostEstimate(
            flops=3_000_000_000, bytes_accessed=4_000_000, transcendentals=0
        ),
        name="keys_part",
    )(where, *parts, keys, keys_near, keys_far, old_own, old_next)
    send, *parts = lax.optimization_barrier((send, *parts))
    group_shape = (LEVELS, tok, 4 * HD)
    q_keep, q_keep2, q_send, q_send2 = pl.pallas_call(
        queries_part_kernel,
        out_shape=(shaped(group_shape, jnp.float32),) * 2 + (shaped(group_shape),) * 2,
        in_specs=[SMEM] + [VMEM] * 8,
        out_specs=(VMEM,) * 4,
        scratch_shapes=[pltpu.VMEM((all_rows, width), jnp.bfloat16)],
        compiler_params=PARAMS,
        cost_estimate=pl.CostEstimate(
            flops=5_000_000_000, bytes_accessed=4_000_000, transcendentals=0
        ),
        name="queries_part",
    )(where, *parts, w_query, query_near, query_far, query_both)
    got_near2 = across(q_send2, 1)
    got_near = across(q_send, 1)
    got_queries = across((q_keep2 + got_near2.astype(jnp.float32)).astype(jnp.bfloat16), 2)
    out_got1, q_send2 = lax.optimization_barrier((out_got1, q_send2))
    out_pair = jnp.stack([out_own, jnp.concatenate([out_got0, out_got1], axis=0)])
    out_near = to_near(out_pair)
    got_keys, q_send2 = lax.optimization_barrier((across(send, 2), q_send2))
    kv = pl.pallas_call(
        keys_join_kernel,
        out_shape=shaped((LEVELS // 2 + LEVELS, tok, 2 * HD)),
        in_specs=[SMEM] + [VMEM] * 6,
        out_specs=VMEM,
        scratch_shapes=[pltpu.VMEM((all_rows, 2 * HD), jnp.float32)],
        compiler_params=PARAMS,
        cost_estimate=pl.CostEstimate(
            flops=24_000_000_000, bytes_accessed=4_000_000, transcendentals=0
        ),
        name="keys_join",
    )(where, keep, got_keys, old_own, old_next, cosine, sine)
    kv_near, kv_far = to_near(kv), to_far(kv)
    kv_both = permuted(kv, lambda z, p, c: (z, p ^ 3, c))

    kv_near, kv_far, kv_both, out_near, out_pair = lax.optimization_barrier(
        (kv_near, kv_far, kv_both, out_near, out_pair)
    )
    out_far, out_both = to_far(out_pair), to_far(out_near)

    attended = [
        pl.pallas_call(
            functools.partial(attend_kernel, pair),
            out_shape=shaped((LEVELS * tok, 2 * HD)),
            in_specs=[SMEM] + [VMEM] * 9,
            out_specs=VMEM,
            scratch_shapes=[pltpu.VMEM((LEVELS, 2, tok, HD), jnp.bfloat16)],
            compiler_params=PARAMS,
            cost_estimate=pl.CostEstimate(
                flops=4_000_000_000, bytes_accessed=4_000_000, transcendentals=2_400_000
            ),
            name="attend",
        )(where, q_keep, got_near, got_queries, cosine, sine, kv, kv_near, kv_far, kv_both)
        for pair in range(2)
    ]
    attended += [across(each, 1) for each in attended]

    wide_cols = PLANE * w_out.shape[1]
    mine, other = pl.pallas_call(
        output_kernel,
        out_shape=(
            shaped((LEVELS, tok, wide_cols), jnp.float32),
            shaped((LEVELS, tok, wide_cols)),
        ),
        in_specs=[SMEM] + [VMEM] * 8,
        out_specs=(VMEM, VMEM),
        scratch_shapes=[pltpu.VMEM((LEVELS * tok, out_rows), jnp.bfloat16)],
        compiler_params=PARAMS,
        cost_estimate=pl.CostEstimate(
            flops=5_000_000_000, bytes_accessed=4_000_000, transcendentals=0
        ),
        name="output",
    )(where, *attended, out_pair, out_near, out_far, out_both)
    got = other_core(other)
    block = [mine[d] + got[d].astype(jnp.float32) for d in range(LEVELS)]
    shares = [up(block[d].astype(jnp.bfloat16), d) for d in range(1, LEVELS)]
    return pl.pallas_call(
        finish_kernel,
        out_shape=shaped((tok, width)),
        in_specs=[SMEM] + [VMEM] * 4,
        out_specs=VMEM,
        compiler_params=PARAMS,
        name="finish",
    )(where, block[0], *shares)


def solution(mesh):
    def run(*args):
        kv_local = args[5].shape[1] // HD // mesh.shape["head"]
        levels_fit = (
            mesh.shape["seq"] == LEVELS * PLANE
            and mesh.shape["head"] == 2
            and kv_local == LEVELS
            and args[1].shape[0] == 2 * TILE_RUN
            and args[0].shape[0] == 2048
            and args[8].shape[0] == LEVELS * PLANE * CACHED
            and args[10].shape[0] == LEVELS * PLANE * REC
        )
        return jax.shard_map(
            by_levels if levels_fit else on_device,
            mesh=mesh,
            in_specs=(
                P("seq", "head"),
                P("seq", "head"),
                P("seq"),
                P(),
                P("seq", "head"),
                P("seq", "head"),
                P("seq", "head"),
                P("head", "seq"),
                P("seq", "head"),
                P("seq", "head"),
                P("seq", "head"),
                P("seq"),
            ),
            out_specs=P("seq", "head"),
            check_vma=False,
        )(*args)

    return run
```

```python
import functools

import jax
import jax.numpy as jnp
from jax import lax
from jax.experimental import pallas as pl
from jax.experimental.pallas import tpu as pltpu
from jax.sharding import PartitionSpec as P

D = 4096
HD = 128


EPSILON = 1e-05
ROPE_BASE = 1000000.0
NEG_FILL = -1e30


def rotate(values, positions):
    half = values.shape[-1] // 2
    freqs = ROPE_BASE ** (-jnp.arange(half, dtype=jnp.float32) / half)
    angles = positions[:, None] * freqs[None, :]
    cosine = jnp.cos(angles)[:, None, :]
    sine = jnp.sin(angles)[:, None, :]
    first = values[..., :half]
    second = values[..., half:]
    return jnp.concatenate(
        [first * cosine - second * sine, second * cosine + first * sine], axis=-1
    )


def scaled(rows_wide, squares, gain):
    return (rows_wide * lax.rsqrt(squares / D + EPSILON)[:, None] * gain[None, :]).astype(
        jnp.bfloat16
    )


def attend(carry, key_piece, value_piece, queries, allowed):
    best, total, accum = carry
    count = key_piece.shape[0]
    kv_local = queries.shape[0]
    keys_split = key_piece.reshape(count, kv_local, HD)
    values_split = value_piece.reshape(count, kv_local, HD)
    scores = jnp.einsum(
        "kgtd,nkd->kgtn", queries, keys_split, preferred_element_type=jnp.float32
    ) * HD ** (-0.5)
    scores = jnp.where(allowed, scores, NEG_FILL)
    fresh = jnp.maximum(best, jnp.max(scores, axis=-1))
    factor = jnp.exp(best - fresh)
    weights = jnp.where(allowed, jnp.exp(scores - fresh[..., None]), 0.0)
    total = total * factor + jnp.sum(weights, axis=-1)
    accum = accum * factor[..., None] + jnp.einsum(
        "kgtn,nkd->kgtd",
        weights.astype(jnp.bfloat16),
        values_split,
        preferred_element_type=jnp.float32,
    )
    return (fresh, total, accum)


def on_device(
    text_rows,
    picture_rows,
    picture_slots,
    norm_gain,
    w_query,
    w_key,
    w_value,
    w_out,
    cache_keys,
    cache_values,
    recompute_rows,
    recompute_slots,
):
    tok_rows = text_rows.shape[0]
    rec_count = recompute_rows.shape[0]
    cache_rows = cache_keys.shape[0]
    seq_index = lax.axis_index("seq")
    local_pos = seq_index * tok_rows + jnp.arange(tok_rows, dtype=jnp.int32)
    rows_piece = lax.all_gather(picture_rows, "seq", axis=0, tiled=True)
    slots_piece = lax.all_gather(picture_slots, "seq", axis=0, tiled=True)
    select = (slots_piece[None, :] == local_pos[:, None]).astype(jnp.bfloat16)
    placed = jnp.dot(select, rows_piece, preferred_element_type=jnp.float32)
    hits = jnp.sum(select.astype(jnp.float32), axis=1)
    added, hits = (placed, hits)
    stream = jnp.where(hits[:, None] > 0.5, added, text_rows.astype(jnp.float32)).astype(
        jnp.bfloat16
    )
    slice_width = stream.shape[1]
    gain_slice = lax.dynamic_slice_in_dim(
        norm_gain, lax.axis_index("head") * slice_width, slice_width, 0
    )
    stream_wide = stream.astype(jnp.float32)
    rec_wide = recompute_rows.astype(jnp.float32)
    stream_sq, rec_sq = lax.psum(
        (jnp.sum(stream_wide * stream_wide, axis=1), jnp.sum(rec_wide * rec_wide, axis=1)), "head"
    )
    normed, rec_normed = (
        lax.all_gather(scaled(stream_wide, stream_sq, gain_slice), "head", axis=1, tiled=True),
        lax.all_gather(scaled(rec_wide, rec_sq, gain_slice), "head", axis=1, tiled=True),
    )
    stacked = jnp.concatenate([normed, rec_normed], axis=0)
    query_cols = w_query.shape[1]
    key_cols = w_key.shape[1]
    pieces = (
        lax.all_gather(w_query, "seq", axis=0, tiled=True),
        lax.all_gather(w_key, "seq", axis=0, tiled=True),
        lax.all_gather(w_value, "seq", axis=0, tiled=True),
    )
    query_all = jnp.dot(stacked, pieces[0], preferred_element_type=jnp.float32)
    key_all = jnp.dot(stacked, pieces[1], preferred_element_type=jnp.float32)
    value_all = jnp.dot(stacked, pieces[2], preferred_element_type=jnp.float32)
    cache_total = cache_rows * lax.axis_size("seq")
    stream_pos = (cache_total + local_pos).astype(jnp.float32)
    rec_pos = recompute_slots.astype(jnp.float32)
    heads_local = query_cols // HD
    kv_local = key_cols // HD
    group = heads_local // kv_local
    rot_query = rotate(query_all[:tok_rows].reshape(tok_rows, heads_local, HD), stream_pos).astype(
        jnp.bfloat16
    )
    rot_key = (
        rotate(key_all[:tok_rows].reshape(tok_rows, kv_local, HD), stream_pos)
        .astype(jnp.bfloat16)
        .reshape(tok_rows, key_cols)
    )
    values_new = value_all[:tok_rows].astype(jnp.bfloat16)
    rot_rec_key = (
        rotate(key_all[tok_rows:].reshape(rec_count, kv_local, HD), rec_pos)
        .astype(jnp.bfloat16)
        .reshape(rec_count, key_cols)
    )
    rec_values = value_all[tok_rows:].astype(jnp.bfloat16)
    local_slots = recompute_slots - seq_index * cache_rows
    select = local_slots[:, None] == jnp.arange(cache_rows, dtype=jnp.int32)[None, :]
    replaced = jnp.any(select, axis=0)[:, None]
    select_cols = select.astype(jnp.bfloat16).T
    new_keys = jnp.dot(select_cols, rot_rec_key, preferred_element_type=jnp.float32).astype(
        jnp.bfloat16
    )
    new_values = jnp.dot(select_cols, rec_values, preferred_element_type=jnp.float32).astype(
        jnp.bfloat16
    )
    cache_k = jnp.where(replaced, new_keys, cache_keys)
    cache_v = jnp.where(replaced, new_values, cache_values)
    queries = jnp.transpose(rot_query.reshape(tok_rows, kv_local, group, HD), (1, 2, 0, 3))
    carry_start = (
        jnp.full((kv_local, group, tok_rows), NEG_FILL, jnp.float32),
        jnp.zeros((kv_local, group, tok_rows), jnp.float32),
        jnp.zeros((kv_local, group, tok_rows, HD), jnp.float32),
    )
    pieces = (
        lax.all_gather(cache_k, "seq", axis=0, tiled=True),
        lax.all_gather(cache_v, "seq", axis=0, tiled=True),
    )
    allowed = jnp.ones((tok_rows, pieces[0].shape[0]), jnp.bool_)
    carry_mid = attend(carry_start, pieces[0], pieces[1], queries, allowed)
    pieces = (
        lax.all_gather(rot_key, "seq", axis=0, tiled=True),
        lax.all_gather(values_new, "seq", axis=0, tiled=True),
    )
    key_pos = jnp.arange(pieces[0].shape[0], dtype=jnp.int32)
    allowed = key_pos[None, :] <= local_pos[:, None]
    best, total, accum = attend(carry_mid, pieces[0], pieces[1], queries, allowed)
    attended = (
        jnp.transpose(accum / total[..., None], (2, 0, 1, 3))
        .reshape(tok_rows, query_cols)
        .astype(jnp.bfloat16)
    )
    partial_out = jnp.dot(
        attended,
        lax.all_gather(w_out, "seq", axis=1, tiled=True),
        preferred_element_type=jnp.float32,
    )
    return lax.psum_scatter(
        partial_out.astype(jnp.bfloat16), "head", scatter_dimension=1, tiled=True
    )


LEVELS = 4
PLANE = 4
TILE_RUN = 256
CACHED = 64
REC = 8
REC_PAD = 16


def permuted(value, move):
    perm = []
    for level in range(LEVELS):
        for place in range(PLANE):
            for core in range(2):
                target = move(level, place, core)
                if target is not None:
                    to_level, to_place, to_core = target
                    perm.append(
                        (
                            (level * PLANE + place) * 2 + core,
                            (to_level * PLANE + to_place) * 2 + to_core,
                        )
                    )
    return lax.ppermute(value, ("seq", "head"), perm)


def across(value, bit):
    return permuted(value, lambda z, p, c: (z ^ bit, p, c))


def up(value, steps):
    return permuted(value, lambda z, p, c: ((z + steps) % LEVELS, p, c))


def other_core(value):
    return permuted(value, lambda z, p, c: (z, p, 1 - c))


def to_near(value):
    return permuted(value, lambda z, p, c: (z, p ^ (1 + c), c))


def to_far(value):
    return permuted(value, lambda z, p, c: (z, p ^ (2 - c), c))


def place_of(which, place, core):
    if which == 0:
        return place
    if which == 3:
        return place ^ 3
    return place ^ (1 + core) if which == 1 else place ^ (2 - core)


def turned(values, cosine, sine):
    return values * cosine + pltpu.roll(values, HD // 2, 1) * sine


def pack_kernel(where_ref, *refs):
    w_key, w_value, cache_keys, cache_values, slots = refs[:5]
    outs, sems = refs[5:7], refs[7]
    level = where_ref[0]
    depth = w_key.shape[0]
    copies = []

    def copy(source, target):
        copies.append(pltpu.make_async_copy(source, target, sems.at[len(copies)]))
        copies[-1].start()

    for n in range(2):
        keys = outs[n]
        for m in range(2):
            at = jnp.bitwise_xor(level, n + 2 * m)
            small = pl.ds(pl.multiple_of(at * HD, HD), HD)
            for k, (new, old) in enumerate(((w_key, cache_keys), (w_value, cache_values))):
                to = pl.ds((2 * m + k) * HD, HD)
                copy(new.at[:, small], keys.at[0:depth, to])
                copy(old.at[:, small], keys.at[depth : depth + CACHED, to])
        copy(slots, keys.at[depth + CACHED : depth + CACHED + REC_PAD])
    for each in copies:
        each.wait()


PACK_COPIES = 18


def assemble(where_ref, parts, x_ref):
    level, core = where_ref[0], where_ref[2]
    shown = TILE_RUN // 2 // PLANE
    rows = parts[0].shape[0] - shown
    for n, part in enumerate(parts):
        x_ref[n * rows : (n + 1) * rows] = part[0:rows]
    start = where_ref[4] * rows
    for n, part in enumerate(parts):
        which = 2 * lax.rem(level + n % 2, 2) + (core if n < 2 else 1 - core)
        to = pl.multiple_of(start + which * shown, 16)
        x_ref[pl.ds(to, shown)] = part[rows : rows + shown]


def products(where_ref, x_ref, pieces):
    level, place, core = where_ref[0], where_ref[1], where_ref[2]
    total = None
    for i in range(2):
        for j in range(PLANE):
            depth = pieces[i][j].shape[0]
            block = lax.rem(level + i, 2) * PLANE + place_of(j, place, core)
            start = pl.multiple_of(block * depth, depth)
            part = jnp.dot(
                x_ref[:, pl.ds(start, depth)],
                pieces[i][j][...],
                preferred_element_type=jnp.float32,
            )
            total = part if total is None else total + part
    return total


def keys_part_kernel(
    where_ref, x0, x1, x2, x3, own, near, far, old0, old1, keep_ref, send_ref, x_ref
):
    assemble(where_ref, (x0, x1, x2, x3), x_ref)
    pieces = [[own.at[i], near.at[i], far.at[i], far.at[2 + i]] for i in range(2)]
    width = 2 * HD
    total = products(where_ref, x_ref, pieces)
    at = total.shape[0]
    keep_ref[...] = total[:, :width]
    send_ref[0:at] = total[:, width:].astype(jnp.bfloat16)
    for old in (old0, old1):
        send_ref[at : at + CACHED + REC_PAD] = old[:, width:]
        at += CACHED + REC_PAD


def keys_join_kernel(where_ref, keep_ref, got_ref, old0, old1, cos_ref, sin_ref, kv_ref, sum_ref):
    level = where_ref[0]
    rows = sum_ref.shape[0]
    block = rows // LEVELS
    tok = block - REC_PAD
    width = 2 * HD
    sum_ref[...] = keep_ref[...] + got_ref[0:rows].astype(jnp.float32)
    first = where_ref[3]
    span = CACHED + REC_PAD
    for n in range(LEVELS):
        at = jnp.bitwise_xor(level, n)
        start = pl.multiple_of(lax.rem(first + n, LEVELS) * block, 16)
        cosine, sine = cos_ref[at], sin_ref[at]
        fresh = sum_ref[pl.ds(start, tok), :]
        kv_ref[2 + at, :, 0:HD] = turned(fresh[:, :HD], cosine[:tok], sine[:tok]).astype(
            jnp.bfloat16
        )
        kv_ref[2 + at, :, HD:width] = fresh[:, HD:].astype(jnp.bfloat16)
        if n < 2:
            old = (old0, old1)[n][:, 0:width].astype(jnp.float32)
        else:
            old = got_ref[rows + (n - 2) * span : rows + (n - 1) * span].astype(jnp.float32)
        slots = old[CACHED : CACHED + REC].astype(jnp.int32)
        rec = sum_ref[pl.ds(pl.multiple_of(start + tok, 16), REC_PAD), :]
        line = lax.broadcasted_iota(jnp.int32, (CACHED, width), 0)
        found = jnp.zeros((CACHED, width), jnp.float32)
        hit = jnp.zeros((CACHED, width), jnp.int32)
        for r in range(REC):
            same = line == slots[r : r + 1]
            found = jnp.where(same, rec[r : r + 1], found)
            hit = jnp.where(same, 1, hit)
        keys = turned(found[:, :HD], cosine[tok : tok + CACHED], sine[tok : tok + CACHED])
        found = jnp.concatenate([keys, found[:, HD:]], axis=1)
        line_at = pl.multiple_of(lax.rem(at, 2) * CACHED, CACHED)
        kv_ref[at // 2, pl.ds(line_at, CACHED), :] = jnp.where(
            hit == 1, found, old[:CACHED]
        ).astype(jnp.bfloat16)


def queries_part_kernel(where_ref, x0, x1, x2, x3, *refs):
    weights, outs, x_ref = refs[:4], refs[4:8], refs[8]
    level, place, core = where_ref[0], where_ref[1], where_ref[2]
    assemble(where_ref, (x0, x1, x2, x3), x_ref)
    depth = weights[0].shape[0]
    width = 4 * HD
    block = x_ref.shape[0] // LEVELS
    tok = block - REC_PAD
    for m, out_ref in zip((0, 2, 1, 3), outs):
        group = pl.ds(pl.multiple_of(jnp.bitwise_xor(level, m) * width, width), width)
        total = None
        for j in range(PLANE):
            at = lax.rem(level, 2) * PLANE + place_of(j, place, core)
            part = jnp.dot(
                x_ref[:, pl.ds(pl.multiple_of(at * depth, depth), depth)],
                weights[j][:, group],
                preferred_element_type=jnp.float32,
            )
            total = part if total is None else total + part
        for k in range(LEVELS):
            at = jnp.bitwise_xor(level, lax.rem(k + LEVELS - where_ref[3], LEVELS))
            out_ref[at] = total[k * block : k * block + tok].astype(out_ref.dtype)


def attend_kernel(
    pair, where_ref, keep_ref, near_ref, got_ref, cos_ref, sin_ref, kv0, kv1, kv2, kv3, out_ref, query_ref
):
    level, place, core = where_ref[0], where_ref[1], where_ref[2]
    pieces = (kv0, kv1, kv2, kv3)
    tok = keep_ref.shape[1]
    old = LEVELS // 2
    heads = query_ref.shape[1]
    columns = slice(pair * heads * HD, (pair + 1) * heads * HD)
    for at in range(LEVELS):
        total = keep_ref[at, :, columns] + (
            near_ref[at, :, columns].astype(jnp.float32)
            + got_ref[at, :, columns].astype(jnp.float32)
        )
        cosine, sine = cos_ref[at][:tok], sin_ref[at][:tok]
        for h in range(heads):
            head = turned(total[:, h * HD : (h + 1) * HD], cosine, sine)
            query_ref[at, h] = head.astype(jnp.bfloat16)
    row = lax.broadcasted_iota(jnp.int32, (tok, tok), 0)
    col = lax.broadcasted_iota(jnp.int32, (tok, tok), 1)
    scale = HD ** (-0.5) * 1.4426950408889634
    for i in range(LEVELS):
        count = (old + i + 1) * tok
        queries = query_ref[i].reshape(heads * tok, HD)
        scores = []
        best = None
        for j in range(PLANE):
            keys = pieces[j][0 : old + i + 1, :, 0:HD].reshape(count, HD)
            raw = lax.dot_general(
                queries, keys, (((1,), (1,)), ((), ())), preferred_element_type=jnp.float32
            )
            if j == 0:
                allowed = col <= row
            else:
                allowed = jnp.broadcast_to(place_of(j, place, core), (tok, tok)) < place
            allowed = jnp.concatenate([allowed] * heads, axis=0)
            last = jnp.where(allowed, raw[:, count - tok :], NEG_FILL)
            raw = jnp.concatenate([raw[:, : count - tok], last], axis=1)
            top = jnp.max(raw, axis=1, keepdims=True)
            best = top if best is None else jnp.maximum(best, top)
            scores.append(raw)
        total, accum = 0.0, 0.0
        for j in range(PLANE):
            weights = jnp.exp2((scores[j] - best) * scale)
            total = total + jnp.sum(weights, axis=1, keepdims=True)
            values = pieces[j][0 : old + i + 1, :, HD : 2 * HD].reshape(count, HD)
            accum = accum + jnp.dot(
                weights.astype(jnp.bfloat16), values, preferred_element_type=jnp.float32
            )
        result = (accum / total).astype(jnp.bfloat16)
        for h in range(heads):
            out_ref[i * tok : (i + 1) * tok, h * HD : (h + 1) * HD] = result[
                h * tok : (h + 1) * tok
            ]


def output_kernel(where_ref, *refs):
    heads, weights, (mine_ref, other_ref, x_ref) = refs[:4], refs[4:-3], refs[-3:]
    level, core = where_ref[0], where_ref[2]
    depth = heads[0].shape[1]
    width = weights[0].shape[2]
    tok = mine_ref.shape[1]
    for n, ref in enumerate(heads):
        at = 2 * lax.rem(level + n // 2, 2) + n % 2
        x_ref[:, pl.ds(pl.multiple_of(at * depth, depth), depth)] = ref[...]
    swap = jnp.where(core == level // 2, 0, 1)
    for s, out_ref in enumerate((mine_ref, other_ref)):
        i = jnp.bitwise_xor(swap, s)
        for j, piece in enumerate(weights):
            slot = (0, 2, 1, 3)[j] if s else j
            part = jnp.dot(x_ref[...], piece[i], preferred_element_type=jnp.float32)
            for t in range(LEVELS):
                out_ref[
                    lax.rem(t + LEVELS - level, LEVELS), :, slot * width : (slot + 1) * width
                ] = part[t * tok : (t + 1) * tok].astype(out_ref.dtype)


def finish_kernel(where_ref, own, first, second, third, out_ref):
    level, place, core = where_ref[0], where_ref[1], where_ref[2]
    half = out_ref.shape[1] // 2
    width = half // PLANE
    sums = (
        own[...] + second[...].astype(jnp.float32),
        first[...].astype(jnp.float32) + third[...].astype(jnp.float32),
    )
    for steps, total in enumerate(sums):
        for j in range(PLANE):
            at = lax.rem(level + steps, 2) * half + place_of(j, place, core) * width
            out_ref[:, pl.ds(pl.multiple_of(at, width), width)] = total[
                :, j * width : (j + 1) * width
            ].astype(out_ref.dtype)


SMEM = pl.BlockSpec(memory_space=pltpu.SMEM)
VMEM = pl.BlockSpec(memory_space=pltpu.VMEM)
HBM = pl.BlockSpec(memory_space=pltpu.MemorySpace.HBM)
PARAMS = pltpu.CompilerParams(vmem_limit_bytes=48 * 1024 * 1024)


def shaped(shape, dtype=jnp.bfloat16):
    return jax.ShapeDtypeStruct(shape, dtype)


def by_levels(
    text_rows,
    picture_rows,
    picture_slots,
    norm_gain,
    w_query,
    w_key,
    w_value,
    w_out,
    cache_keys,
    cache_values,
    recompute_rows,
    recompute_slots,
):
    seq_index = lax.axis_index("seq")
    core = lax.axis_index("head")
    level, place = seq_index // PLANE, seq_index % PLANE
    half_at = level // 2
    own_first = core == half_at
    tok, width = text_rows.shape
    block_rows = tok + REC_PAD

    stream_len = tok * LEVELS * PLANE
    tile_owners = TILE_RUN // tok
    first = stream_len // 2 // tok
    last = (stream_len - TILE_RUN) // tok
    owners = [first + i for i in range(tile_owners)] + [last + i for i in range(tile_owners)]
    assert [owner % PLANE for owner in owners] == list(range(LEVELS))
    owner_level = jnp.where(place < tile_owners, first // PLANE, last // PLANE)

    first_block = jnp.where(own_first, 0, 2)
    shown_block = (first_block + (level ^ owner_level)) % LEVELS
    where = jnp.stack([level, place, core, first_block, shown_block]).astype(jnp.int32)

    slots = (recompute_slots - seq_index * CACHED).astype(jnp.bfloat16)
    slot_rows = jnp.broadcast_to(jnp.pad(slots, (0, REC_PAD - REC))[:, None], (REC_PAD, 4 * HD))
    depth = w_key.shape[0]
    rows = jnp.concatenate(
        [text_rows, recompute_rows, jnp.zeros((REC_PAD - REC, width), text_rows.dtype)], axis=0
    )
    gain = lax.dynamic_slice_in_dim(norm_gain, core * width, width, 0)
    wide, pictures = rows.astype(jnp.float32), picture_rows.astype(jnp.float32)
    squares, picture_squares = lax.psum(
        (jnp.sum(wide * wide, axis=1), jnp.sum(pictures * pictures, axis=1)), "head"
    )
    normed = scaled(wide, squares, gain)
    pictures = scaled(pictures, picture_squares, gain)

    normed, pictures, slot_rows = lax.optimization_barrier((normed, pictures, slot_rows))
    key_own, key_give = pl.pallas_call(
        pack_kernel,
        out_shape=(shaped((depth + CACHED + REC_PAD, 4 * HD)),) * 2,
        in_specs=[SMEM] + [HBM] * 5,
        out_specs=(HBM,) * 2,
        scratch_shapes=[pltpu.SemaphoreType.DMA((PACK_COPIES,))],
        compiler_params=PARAMS,
        cost_estimate=pl.CostEstimate(
            flops=6_000_000_000, bytes_accessed=4_000_000, transcendentals=0
        ),
        name="pack",
    )(where, w_key, w_value, cache_keys, cache_values, slot_rows)

    out_rows = w_out.shape[0] // 2
    out_own, out_give = (
        lax.dynamic_slice_in_dim(w_out, at * out_rows, out_rows, 0) for at in (half_at, 1 - half_at)
    )

    crossed = permuted(normed, lambda z, p, c: (z ^ 2, p, 1 - c) if c == 1 - z // 2 else None)
    shown = permuted(pictures, lambda z, p, c: (2 * c + p // 2, z, p % 2))
    key_next = across(key_give, 1)
    query_near, query_far = to_near(w_query), to_far(w_query)
    shown, key_next, query_near, query_far = lax.optimization_barrier(
        (shown, key_next, query_near, query_far)
    )
    query_both = to_far(query_near)
    keys = jnp.stack([key_own[:depth], key_next[:depth]])
    old_own, old_next = key_own[depth:], key_next[depth:]
    keys_near = to_near(keys)
    crossed, shown, out_give = lax.optimization_barrier((crossed, shown, out_give))
    held = jnp.concatenate([jnp.where(own_first, normed, crossed), shown], axis=0)
    next_rows = across(held, 1)
    held_other = other_core(held)
    out_first = out_rows * 3 // 4
    next_rows, out_got0, query_both = lax.optimization_barrier(
        (next_rows, across(out_give[:out_first], 2), query_both)
    )
    out_got1 = across(out_give[out_first:], 2)
    next_other = other_core(next_rows)
    keys_far = to_far(jnp.concatenate([keys, keys_near], axis=0))
    next_other, held_other, keys_far = lax.optimization_barrier(
        (next_other, held_other, keys_far)
    )
    parts = (held, next_rows, held_other, next_other)

    half = HD // 2
    freqs = ROPE_BASE ** (-jnp.arange(half, dtype=jnp.float32) / half)
    blocks = (jnp.arange(LEVELS, dtype=jnp.int32) * PLANE + place)[:, None]
    stream_pos = (
        CACHED * LEVELS * PLANE + blocks * tok + jnp.arange(tok, dtype=jnp.int32)[None]
    ).astype(jnp.float32)
    cache_pos = (blocks * CACHED + jnp.arange(CACHED, dtype=jnp.int32)[None]).astype(jnp.float32)
    angles = jnp.concatenate([stream_pos, cache_pos], axis=1)[..., None] * freqs
    cosine, sine = jnp.cos(angles), jnp.sin(angles)
    cosine = jnp.concatenate([cosine, cosine], axis=-1)
    sine = jnp.concatenate([-sine, sine], axis=-1)

    all_rows = LEVELS * block_rows
    keep, send = pl.pallas_call(
        keys_part_kernel,
        out_shape=(
            shaped((all_rows, 2 * HD), jnp.float32),
            shaped((all_rows + 2 * (CACHED + REC_PAD), 2 * HD)),
        ),
        in_specs=[SMEM] + [VMEM] * 9,
        out_specs=(VMEM, VMEM),
        scratch_shapes=[pltpu.VMEM((all_rows, width), jnp.bfloat16)],
        compiler_params=PARAMS,
        cost_estimate=pl.CostEstimate(
            flops=3_000_000_000, bytes_accessed=4_000_000, transcendentals=0
        ),
        name="keys_part",
    )(where, *parts, keys, keys_near, keys_far, old_own, old_next)
    send, *parts = lax.optimization_barrier((send, *parts))
    group_shape = (LEVELS, tok, 4 * HD)
    q_keep, q_keep2, q_send, q_send2 = pl.pallas_call(
        queries_part_kernel,
        out_shape=(shaped(group_shape, jnp.float32),) * 2 + (shaped(group_shape),) * 2,
        in_specs=[SMEM] + [VMEM] * 8,
        out_specs=(VMEM,) * 4,
        scratch_shapes=[pltpu.VMEM((all_rows, width), jnp.bfloat16)],
        compiler_params=PARAMS,
        cost_estimate=pl.CostEstimate(
            flops=5_000_000_000, bytes_accessed=4_000_000, transcendentals=0
        ),
        name="queries_part",
    )(where, *parts, w_query, query_near, query_far, query_both)
    got_near2 = across(q_send2, 1)
    got_near = across(q_send, 1)
    got_queries = across((q_keep2 + got_near2.astype(jnp.float32)).astype(jnp.bfloat16), 2)
    out_got1, q_send2 = lax.optimization_barrier((out_got1, q_send2))
    out_pair = jnp.stack([out_own, jnp.concatenate([out_got0, out_got1], axis=0)])
    out_near = to_near(out_pair)
    got_keys, q_send2 = lax.optimization_barrier((across(send, 2), q_send2))
    kv = pl.pallas_call(
        keys_join_kernel,
        out_shape=shaped((LEVELS // 2 + LEVELS, tok, 2 * HD)),
        in_specs=[SMEM] + [VMEM] * 6,
        out_specs=VMEM,
        scratch_shapes=[pltpu.VMEM((all_rows, 2 * HD), jnp.float32)],
        compiler_params=PARAMS,
        cost_estimate=pl.CostEstimate(
            flops=24_000_000_000, bytes_accessed=4_000_000, transcendentals=0
        ),
        name="keys_join",
    )(where, keep, got_keys, old_own, old_next, cosine, sine)
    kv_near, kv_far = to_near(kv), to_far(kv)
    kv_both = permuted(kv, lambda z, p, c: (z, p ^ 3, c))

    kv_near, kv_far, kv_both, out_near, out_pair = lax.optimization_barrier(
        (kv_near, kv_far, kv_both, out_near, out_pair)
    )
    out_far, out_both = to_far(out_pair), to_far(out_near)

    attended = [
        pl.pallas_call(
            functools.partial(attend_kernel, pair),
            out_shape=shaped((LEVELS * tok, 2 * HD)),
            in_specs=[SMEM] + [VMEM] * 9,
            out_specs=VMEM,
            scratch_shapes=[pltpu.VMEM((LEVELS, 2, tok, HD), jnp.bfloat16)],
            compiler_params=PARAMS,
            cost_estimate=pl.CostEstimate(
                flops=4_000_000_000, bytes_accessed=4_000_000, transcendentals=2_400_000
            ),
            name="attend",
        )(where, q_keep, got_near, got_queries, cosine, sine, kv, kv_near, kv_far, kv_both)
        for pair in range(2)
    ]
    attended += [across(each, 1) for each in attended]

    wide_cols = PLANE * w_out.shape[1]
    mine, other = pl.pallas_call(
        output_kernel,
        out_shape=(
            shaped((LEVELS, tok, wide_cols), jnp.float32),
            shaped((LEVELS, tok, wide_cols)),
        ),
        in_specs=[SMEM] + [VMEM] * 8,
        out_specs=(VMEM, VMEM),
        scratch_shapes=[pltpu.VMEM((LEVELS * tok, out_rows), jnp.bfloat16)],
        compiler_params=PARAMS,
        cost_estimate=pl.CostEstimate(
            flops=5_000_000_000, bytes_accessed=4_000_000, transcendentals=0
        ),
        name="output",
    )(where, *attended, out_pair, out_near, out_far, out_both)
    got = other_core(other)
    block = [mine[d] + got[d].astype(jnp.float32) for d in range(LEVELS)]
    shares = [up(block[d].astype(jnp.bfloat16), d) for d in range(1, LEVELS)]
    return pl.pallas_call(
        finish_kernel,
        out_shape=shaped((tok, width)),
        in_specs=[SMEM] + [VMEM] * 4,
        out_specs=VMEM,
        compiler_params=PARAMS,
        name="finish",
    )(where, block[0], *shares)


def solution(mesh):
    def run(*args):
        kv_local = args[5].shape[1] // HD // mesh.shape["head"]
        levels_fit = (
            mesh.shape["seq"] == LEVELS * PLANE
            and mesh.shape["head"] == 2
            and kv_local == LEVELS
            and args[1].shape[0] == 2 * TILE_RUN
            and args[0].shape[0] == 2048
            and args[8].shape[0] == LEVELS * PLANE * CACHED
            and args[10].shape[0] == LEVELS * PLANE * REC
        )
        return jax.shard_map(
            by_levels if levels_fit else on_device,
            mesh=mesh,
            in_specs=(
                P("seq", "head"),
                P("seq", "head"),
                P("seq"),
                P(),
                P("seq", "head"),
                P("seq", "head"),
                P("seq", "head"),
                P("head", "seq"),
                P("seq", "head"),
                P("seq", "head"),
                P("seq", "head"),
                P("seq"),
            ),
            out_specs=P("seq", "head"),
            check_vma=False,
        )(*args)

    return run
```

```python
import functools

import jax
import jax.numpy as jnp
from jax import lax
from jax.experimental import pallas as pl
from jax.experimental.pallas import tpu as pltpu
from jax.sharding import PartitionSpec as P

D = 4096
HD = 128


EPSILON = 1e-05
ROPE_BASE = 1000000.0
NEG_FILL = -1e30


def rotate(values, positions):
    half = values.shape[-1] // 2
    freqs = ROPE_BASE ** (-jnp.arange(half, dtype=jnp.float32) / half)
    angles = positions[:, None] * freqs[None, :]
    cosine = jnp.cos(angles)[:, None, :]
    sine = jnp.sin(angles)[:, None, :]
    first = values[..., :half]
    second = values[..., half:]
    return jnp.concatenate(
        [first * cosine - second * sine, second * cosine + first * sine], axis=-1
    )


def scaled(rows_wide, squares, gain):
    return (rows_wide * lax.rsqrt(squares / D + EPSILON)[:, None] * gain[None, :]).astype(
        jnp.bfloat16
    )


def attend(carry, key_piece, value_piece, queries, allowed):
    best, total, accum = carry
    count = key_piece.shape[0]
    kv_local = queries.shape[0]
    keys_split = key_piece.reshape(count, kv_local, HD)
    values_split = value_piece.reshape(count, kv_local, HD)
    scores = jnp.einsum(
        "kgtd,nkd->kgtn", queries, keys_split, preferred_element_type=jnp.float32
    ) * HD ** (-0.5)
    scores = jnp.where(allowed, scores, NEG_FILL)
    fresh = jnp.maximum(best, jnp.max(scores, axis=-1))
    factor = jnp.exp(best - fresh)
    weights = jnp.where(allowed, jnp.exp(scores - fresh[..., None]), 0.0)
    total = total * factor + jnp.sum(weights, axis=-1)
    accum = accum * factor[..., None] + jnp.einsum(
        "kgtn,nkd->kgtd",
        weights.astype(jnp.bfloat16),
        values_split,
        preferred_element_type=jnp.float32,
    )
    return (fresh, total, accum)


def on_device(
    text_rows,
    picture_rows,
    picture_slots,
    norm_gain,
    w_query,
    w_key,
    w_value,
    w_out,
    cache_keys,
    cache_values,
    recompute_rows,
    recompute_slots,
):
    tok_rows = text_rows.shape[0]
    rec_count = recompute_rows.shape[0]
    cache_rows = cache_keys.shape[0]
    seq_index = lax.axis_index("seq")
    local_pos = seq_index * tok_rows + jnp.arange(tok_rows, dtype=jnp.int32)
    rows_piece = lax.all_gather(picture_rows, "seq", axis=0, tiled=True)
    slots_piece = lax.all_gather(picture_slots, "seq", axis=0, tiled=True)
    select = (slots_piece[None, :] == local_pos[:, None]).astype(jnp.bfloat16)
    placed = jnp.dot(select, rows_piece, preferred_element_type=jnp.float32)
    hits = jnp.sum(select.astype(jnp.float32), axis=1)
    added, hits = (placed, hits)
    stream = jnp.where(hits[:, None] > 0.5, added, text_rows.astype(jnp.float32)).astype(
        jnp.bfloat16
    )
    slice_width = stream.shape[1]
    gain_slice = lax.dynamic_slice_in_dim(
        norm_gain, lax.axis_index("head") * slice_width, slice_width, 0
    )
    stream_wide = stream.astype(jnp.float32)
    rec_wide = recompute_rows.astype(jnp.float32)
    stream_sq, rec_sq = lax.psum(
        (jnp.sum(stream_wide * stream_wide, axis=1), jnp.sum(rec_wide * rec_wide, axis=1)), "head"
    )
    normed, rec_normed = (
        lax.all_gather(scaled(stream_wide, stream_sq, gain_slice), "head", axis=1, tiled=True),
        lax.all_gather(scaled(rec_wide, rec_sq, gain_slice), "head", axis=1, tiled=True),
    )
    stacked = jnp.concatenate([normed, rec_normed], axis=0)
    query_cols = w_query.shape[1]
    key_cols = w_key.shape[1]
    pieces = (
        lax.all_gather(w_query, "seq", axis=0, tiled=True),
        lax.all_gather(w_key, "seq", axis=0, tiled=True),
        lax.all_gather(w_value, "seq", axis=0, tiled=True),
    )
    query_all = jnp.dot(stacked, pieces[0], preferred_element_type=jnp.float32)
    key_all = jnp.dot(stacked, pieces[1], preferred_element_type=jnp.float32)
    value_all = jnp.dot(stacked, pieces[2], preferred_element_type=jnp.float32)
    cache_total = cache_rows * lax.axis_size("seq")
    stream_pos = (cache_total + local_pos).astype(jnp.float32)
    rec_pos = recompute_slots.astype(jnp.float32)
    heads_local = query_cols // HD
    kv_local = key_cols // HD
    group = heads_local // kv_local
    rot_query = rotate(query_all[:tok_rows].reshape(tok_rows, heads_local, HD), stream_pos).astype(
        jnp.bfloat16
    )
    rot_key = (
        rotate(key_all[:tok_rows].reshape(tok_rows, kv_local, HD), stream_pos)
        .astype(jnp.bfloat16)
        .reshape(tok_rows, key_cols)
    )
    values_new = value_all[:tok_rows].astype(jnp.bfloat16)
    rot_rec_key = (
        rotate(key_all[tok_rows:].reshape(rec_count, kv_local, HD), rec_pos)
        .astype(jnp.bfloat16)
        .reshape(rec_count, key_cols)
    )
    rec_values = value_all[tok_rows:].astype(jnp.bfloat16)
    local_slots = recompute_slots - seq_index * cache_rows
    select = local_slots[:, None] == jnp.arange(cache_rows, dtype=jnp.int32)[None, :]
    replaced = jnp.any(select, axis=0)[:, None]
    select_cols = select.astype(jnp.bfloat16).T
    new_keys = jnp.dot(select_cols, rot_rec_key, preferred_element_type=jnp.float32).astype(
        jnp.bfloat16
    )
    new_values = jnp.dot(select_cols, rec_values, preferred_element_type=jnp.float32).astype(
        jnp.bfloat16
    )
    cache_k = jnp.where(replaced, new_keys, cache_keys)
    cache_v = jnp.where(replaced, new_values, cache_values)
    queries = jnp.transpose(rot_query.reshape(tok_rows, kv_local, group, HD), (1, 2, 0, 3))
    carry_start = (
        jnp.full((kv_local, group, tok_rows), NEG_FILL, jnp.float32),
        jnp.zeros((kv_local, group, tok_rows), jnp.float32),
        jnp.zeros((kv_local, group, tok_rows, HD), jnp.float32),
    )
    pieces = (
        lax.all_gather(cache_k, "seq", axis=0, tiled=True),
        lax.all_gather(cache_v, "seq", axis=0, tiled=True),
    )
    allowed = jnp.ones((tok_rows, pieces[0].shape[0]), jnp.bool_)
    carry_mid = attend(carry_start, pieces[0], pieces[1], queries, allowed)
    pieces = (
        lax.all_gather(rot_key, "seq", axis=0, tiled=True),
        lax.all_gather(values_new, "seq", axis=0, tiled=True),
    )
    key_pos = jnp.arange(pieces[0].shape[0], dtype=jnp.int32)
    allowed = key_pos[None, :] <= local_pos[:, None]
    best, total, accum = attend(carry_mid, pieces[0], pieces[1], queries, allowed)
    attended = (
        jnp.transpose(accum / total[..., None], (2, 0, 1, 3))
        .reshape(tok_rows, query_cols)
        .astype(jnp.bfloat16)
    )
    partial_out = jnp.dot(
        attended,
        lax.all_gather(w_out, "seq", axis=1, tiled=True),
        preferred_element_type=jnp.float32,
    )
    return lax.psum_scatter(
        partial_out.astype(jnp.bfloat16), "head", scatter_dimension=1, tiled=True
    )


LEVELS = 4
PLANE = 4
TILE_RUN = 256
CACHED = 64
REC = 8
REC_PAD = 16


def permuted(value, move):
    perm = []
    for level in range(LEVELS):
        for place in range(PLANE):
            for core in range(2):
                target = move(level, place, core)
                if target is not None:
                    to_level, to_place, to_core = target
                    perm.append(
                        (
                            (level * PLANE + place) * 2 + core,
                            (to_level * PLANE + to_place) * 2 + to_core,
                        )
                    )
    return lax.ppermute(value, ("seq", "head"), perm)


def across(value, bit):
    return permuted(value, lambda z, p, c: (z ^ bit, p, c))


def up(value, steps):
    return permuted(value, lambda z, p, c: ((z + steps) % LEVELS, p, c))


def other_core(value):
    return permuted(value, lambda z, p, c: (z, p, 1 - c))


def to_near(value):
    return permuted(value, lambda z, p, c: (z, p ^ (1 + c), c))


def to_far(value):
    return permuted(value, lambda z, p, c: (z, p ^ (2 - c), c))


def place_of(which, place, core):
    if which == 0:
        return place
    if which == 3:
        return place ^ 3
    return place ^ (1 + core) if which == 1 else place ^ (2 - core)


def turned(values, cosine, sine):
    return values * cosine + pltpu.roll(values, HD // 2, 1) * sine


def pack_kernel(where_ref, *refs):
    w_key, w_value, cache_keys, cache_values, slots = refs[:5]
    outs, sems = refs[5:7], refs[7]
    level = where_ref[0]
    depth = w_key.shape[0]
    copies = []

    def copy(source, target):
        copies.append(pltpu.make_async_copy(source, target, sems.at[len(copies)]))
        copies[-1].start()

    for n in range(2):
        keys = outs[n]
        for m in range(2):
            at = jnp.bitwise_xor(level, n + 2 * m)
            small = pl.ds(pl.multiple_of(at * HD, HD), HD)
            for k, (new, old) in enumerate(((w_key, cache_keys), (w_value, cache_values))):
                to = pl.ds((2 * m + k) * HD, HD)
                copy(new.at[:, small], keys.at[0:depth, to])
                copy(old.at[:, small], keys.at[depth : depth + CACHED, to])
        copy(slots, keys.at[depth + CACHED : depth + CACHED + REC_PAD])
    for each in copies:
        each.wait()


PACK_COPIES = 18


def assemble(where_ref, parts, x_ref):
    level, core = where_ref[0], where_ref[2]
    shown = TILE_RUN // 2 // PLANE
    rows = parts[0].shape[0] - shown
    for n, part in enumerate(parts):
        x_ref[n * rows : (n + 1) * rows] = part[0:rows]
    start = where_ref[4] * rows
    for n, part in enumerate(parts):
        which = 2 * lax.rem(level + n % 2, 2) + (core if n < 2 else 1 - core)
        to = pl.multiple_of(start + which * shown, 16)
        x_ref[pl.ds(to, shown)] = part[rows : rows + shown]


def products(where_ref, x_ref, pieces):
    level, place, core = where_ref[0], where_ref[1], where_ref[2]
    total = None
    for i in range(2):
        for j in range(PLANE):
            depth = pieces[i][j].shape[0]
            block = lax.rem(level + i, 2) * PLANE + place_of(j, place, core)
            start = pl.multiple_of(block * depth, depth)
            part = jnp.dot(
                x_ref[:, pl.ds(start, depth)],
                pieces[i][j][...],
                preferred_element_type=jnp.float32,
            )
            total = part if total is None else total + part
    return total


def keys_part_kernel(
    where_ref, x0, x1, x2, x3, own, near, far, old0, old1, keep_ref, send_ref, x_ref
):
    assemble(where_ref, (x0, x1, x2, x3), x_ref)
    pieces = [[own.at[i], near.at[i], far.at[i], far.at[2 + i]] for i in range(2)]
    width = 2 * HD
    total = products(where_ref, x_ref, pieces)
    at = total.shape[0]
    keep_ref[...] = total[:, :width]
    send_ref[0:at] = total[:, width:].astype(jnp.bfloat16)
    for old in (old0, old1):
        send_ref[at : at + CACHED + REC_PAD] = old[:, width:]
        at += CACHED + REC_PAD


def keys_join_kernel(where_ref, keep_ref, got_ref, old0, old1, cos_ref, sin_ref, kv_ref, sum_ref):
    level = where_ref[0]
    rows = sum_ref.shape[0]
    block = rows // LEVELS
    tok = block - REC_PAD
    width = 2 * HD
    sum_ref[...] = keep_ref[...] + got_ref[0:rows].astype(jnp.float32)
    first = where_ref[3]
    span = CACHED + REC_PAD
    for n in range(LEVELS):
        at = jnp.bitwise_xor(level, n)
        start = pl.multiple_of(lax.rem(first + n, LEVELS) * block, 16)
        cosine, sine = cos_ref[at], sin_ref[at]
        fresh = sum_ref[pl.ds(start, tok), :]
        kv_ref[2 + at, :, 0:HD] = turned(fresh[:, :HD], cosine[:tok], sine[:tok]).astype(
            jnp.bfloat16
        )
        kv_ref[2 + at, :, HD:width] = fresh[:, HD:].astype(jnp.bfloat16)
        if n < 2:
            old = (old0, old1)[n][:, 0:width].astype(jnp.float32)
        else:
            old = got_ref[rows + (n - 2) * span : rows + (n - 1) * span].astype(jnp.float32)
        slots = old[CACHED : CACHED + REC].astype(jnp.int32)
        rec = sum_ref[pl.ds(pl.multiple_of(start + tok, 16), REC_PAD), :]
        line = lax.broadcasted_iota(jnp.int32, (CACHED, width), 0)
        found = jnp.zeros((CACHED, width), jnp.float32)
        hit = jnp.zeros((CACHED, width), jnp.int32)
        for r in range(REC):
            same = line == slots[r : r + 1]
            found = jnp.where(same, rec[r : r + 1], found)
            hit = jnp.where(same, 1, hit)
        keys = turned(found[:, :HD], cosine[tok : tok + CACHED], sine[tok : tok + CACHED])
        found = jnp.concatenate([keys, found[:, HD:]], axis=1)
        line_at = pl.multiple_of(lax.rem(at, 2) * CACHED, CACHED)
        kv_ref[at // 2, pl.ds(line_at, CACHED), :] = jnp.where(
            hit == 1, found, old[:CACHED]
        ).astype(jnp.bfloat16)


def queries_part_kernel(where_ref, x0, x1, x2, x3, *refs):
    weights, outs, x_ref = refs[:4], refs[4:8], refs[8]
    level, place, core = where_ref[0], where_ref[1], where_ref[2]
    assemble(where_ref, (x0, x1, x2, x3), x_ref)
    depth = weights[0].shape[0]
    width = 4 * HD
    block = x_ref.shape[0] // LEVELS
    tok = block - REC_PAD
    for m, out_ref in zip((0, 2, 1, 3), outs):
        group = pl.ds(pl.multiple_of(jnp.bitwise_xor(level, m) * width, width), width)
        total = None
        for j in range(PLANE):
            at = lax.rem(level, 2) * PLANE + place_of(j, place, core)
            part = jnp.dot(
                x_ref[:, pl.ds(pl.multiple_of(at * depth, depth), depth)],
                weights[j][:, group],
                preferred_element_type=jnp.float32,
            )
            total = part if total is None else total + part
        for k in range(LEVELS):
            at = jnp.bitwise_xor(level, lax.rem(k + LEVELS - where_ref[3], LEVELS))
            out_ref[at] = total[k * block : k * block + tok].astype(out_ref.dtype)


def attend_kernel(
    pair, where_ref, keep_ref, near_ref, got_ref, cos_ref, sin_ref, kv0, kv1, kv2, kv3, out_ref, query_ref
):
    level, place, core = where_ref[0], where_ref[1], where_ref[2]
    pieces = (kv0, kv1, kv2, kv3)
    tok = keep_ref.shape[1]
    old = LEVELS // 2
    heads = query_ref.shape[1]
    columns = slice(pair * heads * HD, (pair + 1) * heads * HD)
    for at in range(LEVELS):
        total = keep_ref[at, :, columns] + (
            near_ref[at, :, columns].astype(jnp.float32)
            + got_ref[at, :, columns].astype(jnp.float32)
        )
        cosine, sine = cos_ref[at][:tok], sin_ref[at][:tok]
        for h in range(heads):
            head = turned(total[:, h * HD : (h + 1) * HD], cosine, sine)
            query_ref[at, h] = head.astype(jnp.bfloat16)
    row = lax.broadcasted_iota(jnp.int32, (tok, tok), 0)
    col = lax.broadcasted_iota(jnp.int32, (tok, tok), 1)
    scale = HD ** (-0.5) * 1.4426950408889634
    for i in range(LEVELS):
        count = (old + i + 1) * tok
        queries = query_ref[i].reshape(heads * tok, HD)
        scores = []
        best = None
        for j in range(PLANE):
            keys = pieces[j][0 : old + i + 1, :, 0:HD].reshape(count, HD)
            raw = lax.dot_general(
                queries, keys, (((1,), (1,)), ((), ())), preferred_element_type=jnp.float32
            )
            if j == 0:
                allowed = col <= row
            else:
                allowed = jnp.broadcast_to(place_of(j, place, core), (tok, tok)) < place
            allowed = jnp.concatenate([allowed] * heads, axis=0)
            last = jnp.where(allowed, raw[:, count - tok :], NEG_FILL)
            raw = jnp.concatenate([raw[:, : count - tok], last], axis=1)
            top = jnp.max(raw, axis=1, keepdims=True)
            best = top if best is None else jnp.maximum(best, top)
            scores.append(raw)
        total, accum = 0.0, 0.0
        for j in range(PLANE):
            weights = jnp.exp2((scores[j] - best) * scale)
            total = total + jnp.sum(weights, axis=1, keepdims=True)
            values = pieces[j][0 : old + i + 1, :, HD : 2 * HD].reshape(count, HD)
            accum = accum + jnp.dot(
                weights.astype(jnp.bfloat16), values, preferred_element_type=jnp.float32
            )
        result = (accum / total).astype(jnp.bfloat16)
        for h in range(heads):
            out_ref[i * tok : (i + 1) * tok, h * HD : (h + 1) * HD] = result[
                h * tok : (h + 1) * tok
            ]


def output_kernel(where_ref, *refs):
    heads, weights, (mine_ref, other_ref, x_ref) = refs[:4], refs[4:-3], refs[-3:]
    level, core = where_ref[0], where_ref[2]
    depth = heads[0].shape[1]
    width = weights[0].shape[2]
    tok = mine_ref.shape[1]
    for n, ref in enumerate(heads):
        at = 2 * lax.rem(level + n // 2, 2) + n % 2
        x_ref[:, pl.ds(pl.multiple_of(at * depth, depth), depth)] = ref[...]
    swap = jnp.where(core == level // 2, 0, 1)
    for s, out_ref in enumerate((mine_ref, other_ref)):
        i = jnp.bitwise_xor(swap, s)
        for j, piece in enumerate(weights):
            slot = (0, 2, 1, 3)[j] if s else j
            part = jnp.dot(x_ref[...], piece[i], preferred_element_type=jnp.float32)
            for t in range(LEVELS):
                out_ref[
                    lax.rem(t + LEVELS - level, LEVELS), :, slot * width : (slot + 1) * width
                ] = part[t * tok : (t + 1) * tok].astype(out_ref.dtype)


def finish_kernel(where_ref, own, first, second, third, out_ref):
    level, place, core = where_ref[0], where_ref[1], where_ref[2]
    half = out_ref.shape[1] // 2
    width = half // PLANE
    sums = (
        own[...] + second[...].astype(jnp.float32),
        first[...].astype(jnp.float32) + third[...].astype(jnp.float32),
    )
    for steps, total in enumerate(sums):
        for j in range(PLANE):
            at = lax.rem(level + steps, 2) * half + place_of(j, place, core) * width
            out_ref[:, pl.ds(pl.multiple_of(at, width), width)] = total[
                :, j * width : (j + 1) * width
            ].astype(out_ref.dtype)


SMEM = pl.BlockSpec(memory_space=pltpu.SMEM)
VMEM = pl.BlockSpec(memory_space=pltpu.VMEM)
HBM = pl.BlockSpec(memory_space=pltpu.MemorySpace.HBM)
PARAMS = pltpu.CompilerParams(vmem_limit_bytes=48 * 1024 * 1024)


def shaped(shape, dtype=jnp.bfloat16):
    return jax.ShapeDtypeStruct(shape, dtype)


def by_levels(
    text_rows,
    picture_rows,
    picture_slots,
    norm_gain,
    w_query,
    w_key,
    w_value,
    w_out,
    cache_keys,
    cache_values,
    recompute_rows,
    recompute_slots,
):
    seq_index = lax.axis_index("seq")
    core = lax.axis_index("head")
    level, place = seq_index // PLANE, seq_index % PLANE
    half_at = level // 2
    own_first = core == half_at
    tok, width = text_rows.shape
    block_rows = tok + REC_PAD

    stream_len = tok * LEVELS * PLANE
    tile_owners = TILE_RUN // tok
    first = stream_len // 2 // tok
    last = (stream_len - TILE_RUN) // tok
    owners = [first + i for i in range(tile_owners)] + [last + i for i in range(tile_owners)]
    assert [owner % PLANE for owner in owners] == list(range(LEVELS))
    owner_level = jnp.where(place < tile_owners, first // PLANE, last // PLANE)

    first_block = jnp.where(own_first, 0, 2)
    shown_block = (first_block + (level ^ owner_level)) % LEVELS
    where = jnp.stack([level, place, core, first_block, shown_block]).astype(jnp.int32)

    slots = (recompute_slots - seq_index * CACHED).astype(jnp.bfloat16)
    slot_rows = jnp.broadcast_to(jnp.pad(slots, (0, REC_PAD - REC))[:, None], (REC_PAD, 4 * HD))
    depth = w_key.shape[0]
    rows = jnp.concatenate(
        [text_rows, recompute_rows, jnp.zeros((REC_PAD - REC, width), text_rows.dtype)], axis=0
    )
    gain = lax.dynamic_slice_in_dim(norm_gain, core * width, width, 0)
    wide, pictures = rows.astype(jnp.float32), picture_rows.astype(jnp.float32)
    squares, picture_squares = lax.psum(
        (jnp.sum(wide * wide, axis=1), jnp.sum(pictures * pictures, axis=1)), "head"
    )
    normed = scaled(wide, squares, gain)
    pictures = scaled(pictures, picture_squares, gain)

    normed, pictures, slot_rows = lax.optimization_barrier((normed, pictures, slot_rows))
    key_own, key_give = pl.pallas_call(
        pack_kernel,
        out_shape=(shaped((depth + CACHED + REC_PAD, 4 * HD)),) * 2,
        in_specs=[SMEM] + [HBM] * 5,
        out_specs=(HBM,) * 2,
        scratch_shapes=[pltpu.SemaphoreType.DMA((PACK_COPIES,))],
        compiler_params=PARAMS,
        cost_estimate=pl.CostEstimate(
            flops=6_000_000_000, bytes_accessed=4_000_000, transcendentals=0
        ),
        name="pack",
    )(where, w_key, w_value, cache_keys, cache_values, slot_rows)

    out_rows = w_out.shape[0] // 2
    out_own, out_give = (
        lax.dynamic_slice_in_dim(w_out, at * out_rows, out_rows, 0) for at in (half_at, 1 - half_at)
    )

    crossed = permuted(normed, lambda z, p, c: (z ^ 2, p, 1 - c) if c == 1 - z // 2 else None)
    shown = permuted(pictures, lambda z, p, c: (2 * c + p // 2, z, p % 2))
    key_next = across(key_give, 1)
    query_near, query_far = to_near(w_query), to_far(w_query)
    query_near, query_far = lax.optimization_barrier((query_near, query_far))
    query_both = to_far(query_near)
    shown, key_next = lax.optimization_barrier((shown, key_next))
    keys = jnp.stack([key_own[:depth], key_next[:depth]])
    old_own, old_next = key_own[depth:], key_next[depth:]
    keys_near = to_near(keys)
    crossed, shown, out_give = lax.optimization_barrier((crossed, shown, out_give))
    held = jnp.concatenate([jnp.where(own_first, normed, crossed), shown], axis=0)
    next_rows = across(held, 1)
    held_other = other_core(held)
    next_rows, out_got = lax.optimization_barrier((next_rows, across(out_give, 2)))
    next_other = other_core(next_rows)
    keys_far = to_far(jnp.concatenate([keys, keys_near], axis=0))
    next_other, held_other, keys_far, query_both = lax.optimization_barrier(
        (next_other, held_other, keys_far, query_both)
    )
    parts = (held, next_rows, held_other, next_other)

    half = HD // 2
    freqs = ROPE_BASE ** (-jnp.arange(half, dtype=jnp.float32) / half)
    blocks = (jnp.arange(LEVELS, dtype=jnp.int32) * PLANE + place)[:, None]
    stream_pos = (
        CACHED * LEVELS * PLANE + blocks * tok + jnp.arange(tok, dtype=jnp.int32)[None]
    ).astype(jnp.float32)
    cache_pos = (blocks * CACHED + jnp.arange(CACHED, dtype=jnp.int32)[None]).astype(jnp.float32)
    angles = jnp.concatenate([stream_pos, cache_pos], axis=1)[..., None] * freqs
    cosine, sine = jnp.cos(angles), jnp.sin(angles)
    cosine = jnp.concatenate([cosine, cosine], axis=-1)
    sine = jnp.concatenate([-sine, sine], axis=-1)

    all_rows = LEVELS * block_rows
    keep, send = pl.pallas_call(
        keys_part_kernel,
        out_shape=(
            shaped((all_rows, 2 * HD), jnp.float32),
            shaped((all_rows + 2 * (CACHED + REC_PAD), 2 * HD)),
        ),
        in_specs=[SMEM] + [VMEM] * 9,
        out_specs=(VMEM, VMEM),
        scratch_shapes=[pltpu.VMEM((all_rows, width), jnp.bfloat16)],
        compiler_params=PARAMS,
        cost_estimate=pl.CostEstimate(
            flops=3_000_000_000, bytes_accessed=4_000_000, transcendentals=0
        ),
        name="keys_part",
    )(where, *parts, keys, keys_near, keys_far, old_own, old_next)
    send, *parts = lax.optimization_barrier((send, *parts))
    group_shape = (LEVELS, tok, 4 * HD)
    q_keep, q_keep2, q_send, q_send2 = pl.pallas_call(
        queries_part_kernel,
        out_shape=(shaped(group_shape, jnp.float32),) * 2 + (shaped(group_shape),) * 2,
        in_specs=[SMEM] + [VMEM] * 8,
        out_specs=(VMEM,) * 4,
        scratch_shapes=[pltpu.VMEM((all_rows, width), jnp.bfloat16)],
        compiler_params=PARAMS,
        cost_estimate=pl.CostEstimate(
            flops=5_000_000_000, bytes_accessed=4_000_000, transcendentals=0
        ),
        name="queries_part",
    )(where, *parts, w_query, query_near, query_far, query_both)
    got_near2 = across(q_send2, 1)
    got_near = across(q_send, 1)
    got_queries = across((q_keep2 + got_near2.astype(jnp.float32)).astype(jnp.bfloat16), 2)
    out_pair = jnp.stack([out_own, out_got])
    out_pair, q_send2 = lax.optimization_barrier((out_pair, q_send2))
    out_near = to_near(out_pair)
    got_keys, q_send2 = lax.optimization_barrier((across(send, 2), q_send2))
    kv = pl.pallas_call(
        keys_join_kernel,
        out_shape=shaped((LEVELS // 2 + LEVELS, tok, 2 * HD)),
        in_specs=[SMEM] + [VMEM] * 6,
        out_specs=VMEM,
        scratch_shapes=[pltpu.VMEM((all_rows, 2 * HD), jnp.float32)],
        compiler_params=PARAMS,
        cost_estimate=pl.CostEstimate(
            flops=24_000_000_000, bytes_accessed=4_000_000, transcendentals=0
        ),
        name="keys_join",
    )(where, keep, got_keys, old_own, old_next, cosine, sine)
    kv_near, kv_far = to_near(kv), to_far(kv)
    kv_both = permuted(kv, lambda z, p, c: (z, p ^ 3, c))

    kv_far, out_pair = lax.optimization_barrier((kv_far, out_pair))
    out_far = to_far(out_pair)
    kv_near, kv_both, out_near = lax.optimization_barrier((kv_near, kv_both, out_near))
    out_both = to_far(out_near)

    attended = [
        pl.pallas_call(
            functools.partial(attend_kernel, pair),
            out_shape=shaped((LEVELS * tok, 2 * HD)),
            in_specs=[SMEM] + [VMEM] * 9,
            out_specs=VMEM,
            scratch_shapes=[pltpu.VMEM((LEVELS, 2, tok, HD), jnp.bfloat16)],
            compiler_params=PARAMS,
            cost_estimate=pl.CostEstimate(
                flops=4_000_000_000, bytes_accessed=4_000_000, transcendentals=2_400_000
            ),
            name="attend",
        )(where, q_keep, got_near, got_queries, cosine, sine, kv, kv_near, kv_far, kv_both)
        for pair in range(2)
    ]
    attended += [across(each, 1) for each in attended]

    wide_cols = PLANE * w_out.shape[1]
    mine, other = pl.pallas_call(
        output_kernel,
        out_shape=(
            shaped((LEVELS, tok, wide_cols), jnp.float32),
            shaped((LEVELS, tok, wide_cols)),
        ),
        in_specs=[SMEM] + [VMEM] * 8,
        out_specs=(VMEM, VMEM),
        scratch_shapes=[pltpu.VMEM((LEVELS * tok, out_rows), jnp.bfloat16)],
        compiler_params=PARAMS,
        cost_estimate=pl.CostEstimate(
            flops=5_000_000_000, bytes_accessed=4_000_000, transcendentals=0
        ),
        name="output",
    )(where, *attended, out_pair, out_near, out_far, out_both)
    got = other_core(other)
    block = [mine[d] + got[d].astype(jnp.float32) for d in range(LEVELS)]
    shares = [up(block[d].astype(jnp.bfloat16), d) for d in range(1, LEVELS)]
    return pl.pallas_call(
        finish_kernel,
        out_shape=shaped((tok, width)),
        in_specs=[SMEM] + [VMEM] * 4,
        out_specs=VMEM,
        compiler_params=PARAMS,
        name="finish",
    )(where, block[0], *shares)


def solution(mesh):
    def run(*args):
        kv_local = args[5].shape[1] // HD // mesh.shape["head"]
        levels_fit = (
            mesh.shape["seq"] == LEVELS * PLANE
            and mesh.shape["head"] == 2
            and kv_local == LEVELS
            and args[1].shape[0] == 2 * TILE_RUN
            and args[0].shape[0] == 2048
            and args[8].shape[0] == LEVELS * PLANE * CACHED
            and args[10].shape[0] == LEVELS * PLANE * REC
        )
        return jax.shard_map(
            by_levels if levels_fit else on_device,
            mesh=mesh,
            in_specs=(
                P("seq", "head"),
                P("seq", "head"),
                P("seq"),
                P(),
                P("seq", "head"),
                P("seq", "head"),
                P("seq", "head"),
                P("head", "seq"),
                P("seq", "head"),
                P("seq", "head"),
                P("seq", "head"),
                P("seq"),
            ),
            out_specs=P("seq", "head"),
            check_vma=False,
        )(*args)

    return run
```

```python
import functools

import jax
import jax.numpy as jnp
from jax import lax
from jax.experimental import pallas as pl
from jax.experimental.pallas import tpu as pltpu
from jax.sharding import PartitionSpec as P

D = 4096
HD = 128


EPSILON = 1e-05
ROPE_BASE = 1000000.0
NEG_FILL = -1e30


def rotate(values, positions):
    half = values.shape[-1] // 2
    freqs = ROPE_BASE ** (-jnp.arange(half, dtype=jnp.float32) / half)
    angles = positions[:, None] * freqs[None, :]
    cosine = jnp.cos(angles)[:, None, :]
    sine = jnp.sin(angles)[:, None, :]
    first = values[..., :half]
    second = values[..., half:]
    return jnp.concatenate(
        [first * cosine - second * sine, second * cosine + first * sine], axis=-1
    )


def scaled(rows_wide, squares, gain):
    return (rows_wide * lax.rsqrt(squares / D + EPSILON)[:, None] * gain[None, :]).astype(
        jnp.bfloat16
    )


def attend(carry, key_piece, value_piece, queries, allowed):
    best, total, accum = carry
    count = key_piece.shape[0]
    kv_local = queries.shape[0]
    keys_split = key_piece.reshape(count, kv_local, HD)
    values_split = value_piece.reshape(count, kv_local, HD)
    scores = jnp.einsum(
        "kgtd,nkd->kgtn", queries, keys_split, preferred_element_type=jnp.float32
    ) * HD ** (-0.5)
    scores = jnp.where(allowed, scores, NEG_FILL)
    fresh = jnp.maximum(best, jnp.max(scores, axis=-1))
    factor = jnp.exp(best - fresh)
    weights = jnp.where(allowed, jnp.exp(scores - fresh[..., None]), 0.0)
    total = total * factor + jnp.sum(weights, axis=-1)
    accum = accum * factor[..., None] + jnp.einsum(
        "kgtn,nkd->kgtd",
        weights.astype(jnp.bfloat16),
        values_split,
        preferred_element_type=jnp.float32,
    )
    return (fresh, total, accum)


def on_device(
    text_rows,
    picture_rows,
    picture_slots,
    norm_gain,
    w_query,
    w_key,
    w_value,
    w_out,
    cache_keys,
    cache_values,
    recompute_rows,
    recompute_slots,
):
    tok_rows = text_rows.shape[0]
    rec_count = recompute_rows.shape[0]
    cache_rows = cache_keys.shape[0]
    seq_index = lax.axis_index("seq")
    local_pos = seq_index * tok_rows + jnp.arange(tok_rows, dtype=jnp.int32)
    rows_piece = lax.all_gather(picture_rows, "seq", axis=0, tiled=True)
    slots_piece = lax.all_gather(picture_slots, "seq", axis=0, tiled=True)
    select = (slots_piece[None, :] == local_pos[:, None]).astype(jnp.bfloat16)
    placed = jnp.dot(select, rows_piece, preferred_element_type=jnp.float32)
    hits = jnp.sum(select.astype(jnp.float32), axis=1)
    added, hits = (placed, hits)
    stream = jnp.where(hits[:, None] > 0.5, added, text_rows.astype(jnp.float32)).astype(
        jnp.bfloat16
    )
    slice_width = stream.shape[1]
    gain_slice = lax.dynamic_slice_in_dim(
        norm_gain, lax.axis_index("head") * slice_width, slice_width, 0
    )
    stream_wide = stream.astype(jnp.float32)
    rec_wide = recompute_rows.astype(jnp.float32)
    stream_sq, rec_sq = lax.psum(
        (jnp.sum(stream_wide * stream_wide, axis=1), jnp.sum(rec_wide * rec_wide, axis=1)), "head"
    )
    normed, rec_normed = (
        lax.all_gather(scaled(stream_wide, stream_sq, gain_slice), "head", axis=1, tiled=True),
        lax.all_gather(scaled(rec_wide, rec_sq, gain_slice), "head", axis=1, tiled=True),
    )
    stacked = jnp.concatenate([normed, rec_normed], axis=0)
    query_cols = w_query.shape[1]
    key_cols = w_key.shape[1]
    pieces = (
        lax.all_gather(w_query, "seq", axis=0, tiled=True),
        lax.all_gather(w_key, "seq", axis=0, tiled=True),
        lax.all_gather(w_value, "seq", axis=0, tiled=True),
    )
    query_all = jnp.dot(stacked, pieces[0], preferred_element_type=jnp.float32)
    key_all = jnp.dot(stacked, pieces[1], preferred_element_type=jnp.float32)
    value_all = jnp.dot(stacked, pieces[2], preferred_element_type=jnp.float32)
    cache_total = cache_rows * lax.axis_size("seq")
    stream_pos = (cache_total + local_pos).astype(jnp.float32)
    rec_pos = recompute_slots.astype(jnp.float32)
    heads_local = query_cols // HD
    kv_local = key_cols // HD
    group = heads_local // kv_local
    rot_query = rotate(query_all[:tok_rows].reshape(tok_rows, heads_local, HD), stream_pos).astype(
        jnp.bfloat16
    )
    rot_key = (
        rotate(key_all[:tok_rows].reshape(tok_rows, kv_local, HD), stream_pos)
        .astype(jnp.bfloat16)
        .reshape(tok_rows, key_cols)
    )
    values_new = value_all[:tok_rows].astype(jnp.bfloat16)
    rot_rec_key = (
        rotate(key_all[tok_rows:].reshape(rec_count, kv_local, HD), rec_pos)
        .astype(jnp.bfloat16)
        .reshape(rec_count, key_cols)
    )
    rec_values = value_all[tok_rows:].astype(jnp.bfloat16)
    local_slots = recompute_slots - seq_index * cache_rows
    select = local_slots[:, None] == jnp.arange(cache_rows, dtype=jnp.int32)[None, :]
    replaced = jnp.any(select, axis=0)[:, None]
    select_cols = select.astype(jnp.bfloat16).T
    new_keys = jnp.dot(select_cols, rot_rec_key, preferred_element_type=jnp.float32).astype(
        jnp.bfloat16
    )
    new_values = jnp.dot(select_cols, rec_values, preferred_element_type=jnp.float32).astype(
        jnp.bfloat16
    )
    cache_k = jnp.where(replaced, new_keys, cache_keys)
    cache_v = jnp.where(replaced, new_values, cache_values)
    queries = jnp.transpose(rot_query.reshape(tok_rows, kv_local, group, HD), (1, 2, 0, 3))
    carry_start = (
        jnp.full((kv_local, group, tok_rows), NEG_FILL, jnp.float32),
        jnp.zeros((kv_local, group, tok_rows), jnp.float32),
        jnp.zeros((kv_local, group, tok_rows, HD), jnp.float32),
    )
    pieces = (
        lax.all_gather(cache_k, "seq", axis=0, tiled=True),
        lax.all_gather(cache_v, "seq", axis=0, tiled=True),
    )
    allowed = jnp.ones((tok_rows, pieces[0].shape[0]), jnp.bool_)
    carry_mid = attend(carry_start, pieces[0], pieces[1], queries, allowed)
    pieces = (
        lax.all_gather(rot_key, "seq", axis=0, tiled=True),
        lax.all_gather(values_new, "seq", axis=0, tiled=True),
    )
    key_pos = jnp.arange(pieces[0].shape[0], dtype=jnp.int32)
    allowed = key_pos[None, :] <= local_pos[:, None]
    best, total, accum = attend(carry_mid, pieces[0], pieces[1], queries, allowed)
    attended = (
        jnp.transpose(accum / total[..., None], (2, 0, 1, 3))
        .reshape(tok_rows, query_cols)
        .astype(jnp.bfloat16)
    )
    partial_out = jnp.dot(
        attended,
        lax.all_gather(w_out, "seq", axis=1, tiled=True),
        preferred_element_type=jnp.float32,
    )
    return lax.psum_scatter(
        partial_out.astype(jnp.bfloat16), "head", scatter_dimension=1, tiled=True
    )


LEVELS = 4
PLANE = 4
TILE_RUN = 256
CACHED = 64
REC = 8
REC_PAD = 16


def permuted(value, move):
    perm = []
    for level in range(LEVELS):
        for place in range(PLANE):
            for core in range(2):
                target = move(level, place, core)
                if target is not None:
                    to_level, to_place, to_core = target
                    perm.append(
                        (
                            (level * PLANE + place) * 2 + core,
                            (to_level * PLANE + to_place) * 2 + to_core,
                        )
                    )
    return lax.ppermute(value, ("seq", "head"), perm)


def across(value, bit):
    return permuted(value, lambda z, p, c: (z ^ bit, p, c))


def up(value, steps):
    return permuted(value, lambda z, p, c: ((z + steps) % LEVELS, p, c))


def other_core(value):
    return permuted(value, lambda z, p, c: (z, p, 1 - c))


def to_near(value):
    return permuted(value, lambda z, p, c: (z, p ^ (1 + c), c))


def to_far(value):
    return permuted(value, lambda z, p, c: (z, p ^ (2 - c), c))


def place_of(which, place, core):
    if which == 0:
        return place
    if which == 3:
        return place ^ 3
    return place ^ (1 + core) if which == 1 else place ^ (2 - core)


def turned(values, cosine, sine):
    return values * cosine + pltpu.roll(values, HD // 2, 1) * sine


def pack_kernel(where_ref, *refs):
    w_key, w_value, cache_keys, cache_values, slots = refs[:5]
    outs, sems = refs[5:7], refs[7]
    level = where_ref[0]
    depth = w_key.shape[0]
    copies = []

    def copy(source, target):
        copies.append(pltpu.make_async_copy(source, target, sems.at[len(copies)]))
        copies[-1].start()

    for n in range(2):
        keys = outs[n]
        for m in range(2):
            at = jnp.bitwise_xor(level, n + 2 * m)
            small = pl.ds(pl.multiple_of(at * HD, HD), HD)
            for k, (new, old) in enumerate(((w_key, cache_keys), (w_value, cache_values))):
                to = pl.ds((2 * m + k) * HD, HD)
                copy(new.at[:, small], keys.at[0:depth, to])
                copy(old.at[:, small], keys.at[depth : depth + CACHED, to])
        copy(slots, keys.at[depth + CACHED : depth + CACHED + REC_PAD])
    for each in copies:
        each.wait()


PACK_COPIES = 18


def assemble(where_ref, parts, x_ref):
    level, core = where_ref[0], where_ref[2]
    shown = TILE_RUN // 2 // PLANE
    rows = parts[0].shape[0] - shown
    for n, part in enumerate(parts):
        x_ref[n * rows : (n + 1) * rows] = part[0:rows]
    start = where_ref[4] * rows
    for n, part in enumerate(parts):
        which = 2 * lax.rem(level + n % 2, 2) + (core if n < 2 else 1 - core)
        to = pl.multiple_of(start + which * shown, 16)
        x_ref[pl.ds(to, shown)] = part[rows : rows + shown]


def products(where_ref, x_ref, pieces):
    level, place, core = where_ref[0], where_ref[1], where_ref[2]
    total = None
    for i in range(2):
        for j in range(PLANE):
            depth = pieces[i][j].shape[0]
            block = lax.rem(level + i, 2) * PLANE + place_of(j, place, core)
            start = pl.multiple_of(block * depth, depth)
            part = jnp.dot(
                x_ref[:, pl.ds(start, depth)],
                pieces[i][j][...],
                preferred_element_type=jnp.float32,
            )
            total = part if total is None else total + part
    return total


def keys_part_kernel(
    where_ref, x0, x1, x2, x3, own, near, far, old0, old1, keep_ref, send_ref, x_ref
):
    assemble(where_ref, (x0, x1, x2, x3), x_ref)
    pieces = [[own.at[i], near.at[i], far.at[i], far.at[2 + i]] for i in range(2)]
    width = 2 * HD
    total = products(where_ref, x_ref, pieces)
    at = total.shape[0]
    keep_ref[...] = total[:, :width]
    send_ref[0:at] = total[:, width:].astype(jnp.bfloat16)
    for old in (old0, old1):
        send_ref[at : at + CACHED + REC_PAD] = old[:, width:]
        at += CACHED + REC_PAD


def keys_join_kernel(where_ref, keep_ref, got_ref, old0, old1, cos_ref, sin_ref, kv_ref, sum_ref):
    level = where_ref[0]
    rows = sum_ref.shape[0]
    block = rows // LEVELS
    tok = block - REC_PAD
    width = 2 * HD
    sum_ref[...] = keep_ref[...] + got_ref[0:rows].astype(jnp.float32)
    first = where_ref[3]
    span = CACHED + REC_PAD
    for n in range(LEVELS):
        at = jnp.bitwise_xor(level, n)
        start = pl.multiple_of(lax.rem(first + n, LEVELS) * block, 16)
        cosine, sine = cos_ref[at], sin_ref[at]
        fresh = sum_ref[pl.ds(start, tok), :]
        kv_ref[2 + at, :, 0:HD] = turned(fresh[:, :HD], cosine[:tok], sine[:tok]).astype(
            jnp.bfloat16
        )
        kv_ref[2 + at, :, HD:width] = fresh[:, HD:].astype(jnp.bfloat16)
        if n < 2:
            old = (old0, old1)[n][:, 0:width].astype(jnp.float32)
        else:
            old = got_ref[rows + (n - 2) * span : rows + (n - 1) * span].astype(jnp.float32)
        slots = old[CACHED : CACHED + REC].astype(jnp.int32)
        rec = sum_ref[pl.ds(pl.multiple_of(start + tok, 16), REC_PAD), :]
        line = lax.broadcasted_iota(jnp.int32, (CACHED, width), 0)
        found = jnp.zeros((CACHED, width), jnp.float32)
        hit = jnp.zeros((CACHED, width), jnp.int32)
        for r in range(REC):
            same = line == slots[r : r + 1]
            found = jnp.where(same, rec[r : r + 1], found)
            hit = jnp.where(same, 1, hit)
        keys = turned(found[:, :HD], cosine[tok : tok + CACHED], sine[tok : tok + CACHED])
        found = jnp.concatenate([keys, found[:, HD:]], axis=1)
        line_at = pl.multiple_of(lax.rem(at, 2) * CACHED, CACHED)
        kv_ref[at // 2, pl.ds(line_at, CACHED), :] = jnp.where(
            hit == 1, found, old[:CACHED]
        ).astype(jnp.bfloat16)


def queries_part_kernel(where_ref, x0, x1, x2, x3, *refs):
    weights, outs, x_ref = refs[:4], refs[4:8], refs[8]
    level, place, core = where_ref[0], where_ref[1], where_ref[2]
    assemble(where_ref, (x0, x1, x2, x3), x_ref)
    depth = weights[0].shape[0]
    width = 4 * HD
    block = x_ref.shape[0] // LEVELS
    tok = block - REC_PAD
    for m, out_ref in zip((0, 2, 1, 3), outs):
        group = pl.ds(pl.multiple_of(jnp.bitwise_xor(level, m) * width, width), width)
        total = None
        for j in range(PLANE):
            at = lax.rem(level, 2) * PLANE + place_of(j, place, core)
            part = jnp.dot(
                x_ref[:, pl.ds(pl.multiple_of(at * depth, depth), depth)],
                weights[j][:, group],
                preferred_element_type=jnp.float32,
            )
            total = part if total is None else total + part
        for k in range(LEVELS):
            at = jnp.bitwise_xor(level, lax.rem(k + LEVELS - where_ref[3], LEVELS))
            out_ref[at] = total[k * block : k * block + tok].astype(out_ref.dtype)


def attend_kernel(
    pair, where_ref, keep_ref, near_ref, got_ref, cos_ref, sin_ref, kv0, kv1, kv2, kv3, out_ref, query_ref
):
    level, place, core = where_ref[0], where_ref[1], where_ref[2]
    pieces = (kv0, kv1, kv2, kv3)
    tok = keep_ref.shape[1]
    old = LEVELS // 2
    heads = query_ref.shape[1]
    columns = slice(pair * heads * HD, (pair + 1) * heads * HD)
    for at in range(LEVELS):
        total = keep_ref[at, :, columns] + (
            near_ref[at, :, columns].astype(jnp.float32)
            + got_ref[at, :, columns].astype(jnp.float32)
        )
        cosine, sine = cos_ref[at][:tok], sin_ref[at][:tok]
        for h in range(heads):
            head = turned(total[:, h * HD : (h + 1) * HD], cosine, sine)
            query_ref[at, h] = head.astype(jnp.bfloat16)
    row = lax.broadcasted_iota(jnp.int32, (tok, tok), 0)
    col = lax.broadcasted_iota(jnp.int32, (tok, tok), 1)
    scale = HD ** (-0.5) * 1.4426950408889634
    for i in range(LEVELS):
        count = (old + i + 1) * tok
        queries = query_ref[i].reshape(heads * tok, HD)
        scores = []
        best = None
        for j in range(PLANE):
            keys = pieces[j][0 : old + i + 1, :, 0:HD].reshape(count, HD)
            raw = lax.dot_general(
                queries, keys, (((1,), (1,)), ((), ())), preferred_element_type=jnp.float32
            )
            if j == 0:
                allowed = col <= row
            else:
                allowed = jnp.broadcast_to(place_of(j, place, core), (tok, tok)) < place
            allowed = jnp.concatenate([allowed] * heads, axis=0)
            last = jnp.where(allowed, raw[:, count - tok :], NEG_FILL)
            raw = jnp.concatenate([raw[:, : count - tok], last], axis=1)
            top = jnp.max(raw, axis=1, keepdims=True)
            best = top if best is None else jnp.maximum(best, top)
            scores.append(raw)
        total, accum = 0.0, 0.0
        for j in range(PLANE):
            weights = jnp.exp2((scores[j] - best) * scale)
            total = total + jnp.sum(weights, axis=1, keepdims=True)
            values = pieces[j][0 : old + i + 1, :, HD : 2 * HD].reshape(count, HD)
            accum = accum + jnp.dot(
                weights.astype(jnp.bfloat16), values, preferred_element_type=jnp.float32
            )
        result = (accum / total).astype(jnp.bfloat16)
        for h in range(heads):
            out_ref[i * tok : (i + 1) * tok, h * HD : (h + 1) * HD] = result[
                h * tok : (h + 1) * tok
            ]


def output_kernel(where_ref, *refs):
    heads, weights, (mine_ref, other_ref, x_ref) = refs[:4], refs[4:-3], refs[-3:]
    level, core = where_ref[0], where_ref[2]
    depth = heads[0].shape[1]
    width = weights[0].shape[2]
    tok = mine_ref.shape[1]
    for n, ref in enumerate(heads):
        at = 2 * lax.rem(level + n // 2, 2) + n % 2
        x_ref[:, pl.ds(pl.multiple_of(at * depth, depth), depth)] = ref[...]
    swap = jnp.where(core == level // 2, 0, 1)
    for s, out_ref in enumerate((mine_ref, other_ref)):
        i = jnp.bitwise_xor(swap, s)
        for j, piece in enumerate(weights):
            slot = (0, 2, 1, 3)[j] if s else j
            part = jnp.dot(x_ref[...], piece[i], preferred_element_type=jnp.float32)
            for t in range(LEVELS):
                out_ref[
                    lax.rem(t + LEVELS - level, LEVELS), :, slot * width : (slot + 1) * width
                ] = part[t * tok : (t + 1) * tok].astype(out_ref.dtype)


def finish_kernel(where_ref, own, first, second, third, out_ref):
    level, place, core = where_ref[0], where_ref[1], where_ref[2]
    half = out_ref.shape[1] // 2
    width = half // PLANE
    sums = (
        own[...] + second[...].astype(jnp.float32),
        first[...].astype(jnp.float32) + third[...].astype(jnp.float32),
    )
    for steps, total in enumerate(sums):
        for j in range(PLANE):
            at = lax.rem(level + steps, 2) * half + place_of(j, place, core) * width
            out_ref[:, pl.ds(pl.multiple_of(at, width), width)] = total[
                :, j * width : (j + 1) * width
            ].astype(out_ref.dtype)


SMEM = pl.BlockSpec(memory_space=pltpu.SMEM)
VMEM = pl.BlockSpec(memory_space=pltpu.VMEM)
HBM = pl.BlockSpec(memory_space=pltpu.MemorySpace.HBM)
PARAMS = pltpu.CompilerParams(vmem_limit_bytes=48 * 1024 * 1024)


def shaped(shape, dtype=jnp.bfloat16):
    return jax.ShapeDtypeStruct(shape, dtype)


def by_levels(
    text_rows,
    picture_rows,
    picture_slots,
    norm_gain,
    w_query,
    w_key,
    w_value,
    w_out,
    cache_keys,
    cache_values,
    recompute_rows,
    recompute_slots,
):
    seq_index = lax.axis_index("seq")
    core = lax.axis_index("head")
    level, place = seq_index // PLANE, seq_index % PLANE
    half_at = level // 2
    own_first = core == half_at
    tok, width = text_rows.shape
    block_rows = tok + REC_PAD

    stream_len = tok * LEVELS * PLANE
    tile_owners = TILE_RUN // tok
    first = stream_len // 2 // tok
    last = (stream_len - TILE_RUN) // tok
    owners = [first + i for i in range(tile_owners)] + [last + i for i in range(tile_owners)]
    assert [owner % PLANE for owner in owners] == list(range(LEVELS))
    owner_level = jnp.where(place < tile_owners, first // PLANE, last // PLANE)

    first_block = jnp.where(own_first, 0, 2)
    shown_block = (first_block + (level ^ owner_level)) % LEVELS
    where = jnp.stack([level, place, core, first_block, shown_block]).astype(jnp.int32)

    slots = (recompute_slots - seq_index * CACHED).astype(jnp.bfloat16)
    slot_rows = jnp.broadcast_to(jnp.pad(slots, (0, REC_PAD - REC))[:, None], (REC_PAD, 4 * HD))
    depth = w_key.shape[0]
    rows = jnp.concatenate(
        [text_rows, recompute_rows, jnp.zeros((REC_PAD - REC, width), text_rows.dtype)], axis=0
    )
    gain = lax.dynamic_slice_in_dim(norm_gain, core * width, width, 0)
    wide, pictures = rows.astype(jnp.float32), picture_rows.astype(jnp.float32)
    squares, picture_squares = lax.psum(
        (jnp.sum(wide * wide, axis=1), jnp.sum(pictures * pictures, axis=1)), "head"
    )
    normed = scaled(wide, squares, gain)
    pictures = scaled(pictures, picture_squares, gain)

    normed, pictures, slot_rows = lax.optimization_barrier((normed, pictures, slot_rows))
    key_own, key_give = pl.pallas_call(
        pack_kernel,
        out_shape=(shaped((depth + CACHED + REC_PAD, 4 * HD)),) * 2,
        in_specs=[SMEM] + [HBM] * 5,
        out_specs=(HBM,) * 2,
        scratch_shapes=[pltpu.SemaphoreType.DMA((PACK_COPIES,))],
        compiler_params=PARAMS,
        cost_estimate=pl.CostEstimate(
            flops=6_000_000_000, bytes_accessed=4_000_000, transcendentals=0
        ),
        name="pack",
    )(where, w_key, w_value, cache_keys, cache_values, slot_rows)

    out_rows = w_out.shape[0] // 2
    out_own, out_give = (
        lax.dynamic_slice_in_dim(w_out, at * out_rows, out_rows, 0) for at in (half_at, 1 - half_at)
    )

    crossed = permuted(normed, lambda z, p, c: (z ^ 2, p, 1 - c) if c == 1 - z // 2 else None)
    shown = permuted(pictures, lambda z, p, c: (2 * c + p // 2, z, p % 2))
    key_next = across(key_give, 1)
    query_near, query_far = to_near(w_query), to_far(w_query)
    shown, key_next, query_near, query_far = lax.optimization_barrier(
        (shown, key_next, query_near, query_far)
    )
    query_both = to_far(query_near)
    keys = jnp.stack([key_own[:depth], key_next[:depth]])
    old_own, old_next = key_own[depth:], key_next[depth:]
    keys_near = to_near(keys)
    crossed, shown, out_give = lax.optimization_barrier((crossed, shown, out_give))
    held = jnp.concatenate([jnp.where(own_first, normed, crossed), shown], axis=0)
    next_rows = across(held, 1)
    held_other = other_core(held)
    out_first = out_rows * 3 // 4
    next_rows, out_got0, query_both = lax.optimization_barrier(
        (next_rows, across(out_give[:out_first], 2), query_both)
    )
    out_got1 = across(out_give[out_first:], 2)
    next_other = other_core(next_rows)
    keys_far = to_far(jnp.concatenate([keys, keys_near], axis=0))
    next_other, held_other, keys_far = lax.optimization_barrier(
        (next_other, held_other, keys_far)
    )
    parts = (held, next_rows, held_other, next_other)

    half = HD // 2
    freqs = ROPE_BASE ** (-jnp.arange(half, dtype=jnp.float32) / half)
    blocks = (jnp.arange(LEVELS, dtype=jnp.int32) * PLANE + place)[:, None]
    stream_pos = (
        CACHED * LEVELS * PLANE + blocks * tok + jnp.arange(tok, dtype=jnp.int32)[None]
    ).astype(jnp.float32)
    cache_pos = (blocks * CACHED + jnp.arange(CACHED, dtype=jnp.int32)[None]).astype(jnp.float32)
    angles = jnp.concatenate([stream_pos, cache_pos], axis=1)[..., None] * freqs
    cosine, sine = jnp.cos(angles), jnp.sin(angles)
    cosine = jnp.concatenate([cosine, cosine], axis=-1)
    sine = jnp.concatenate([-sine, sine], axis=-1)

    all_rows = LEVELS * block_rows
    keep, send = pl.pallas_call(
        keys_part_kernel,
        out_shape=(
            shaped((all_rows, 2 * HD), jnp.float32),
            shaped((all_rows + 2 * (CACHED + REC_PAD), 2 * HD)),
        ),
        in_specs=[SMEM] + [VMEM] * 9,
        out_specs=(VMEM, VMEM),
        scratch_shapes=[pltpu.VMEM((all_rows, width), jnp.bfloat16)],
        compiler_params=PARAMS,
        cost_estimate=pl.CostEstimate(
            flops=3_000_000_000, bytes_accessed=4_000_000, transcendentals=0
        ),
        name="keys_part",
    )(where, *parts, keys, keys_near, keys_far, old_own, old_next)
    send, *parts = lax.optimization_barrier((send, *parts))
    group_shape = (LEVELS, tok, 4 * HD)
    q_keep, q_keep2, q_send, q_send2 = pl.pallas_call(
        queries_part_kernel,
        out_shape=(shaped(group_shape, jnp.float32),) * 2 + (shaped(group_shape),) * 2,
        in_specs=[SMEM] + [VMEM] * 8,
        out_specs=(VMEM,) * 4,
        scratch_shapes=[pltpu.VMEM((all_rows, width), jnp.bfloat16)],
        compiler_params=PARAMS,
        cost_estimate=pl.CostEstimate(
            flops=5_000_000_000, bytes_accessed=4_000_000, transcendentals=0
        ),
        name="queries_part",
    )(where, *parts, w_query, query_near, query_far, query_both)
    got_near2 = across(q_send2, 1)
    got_near = across(q_send, 1)
    got_queries = across((q_keep2 + got_near2.astype(jnp.float32)).astype(jnp.bfloat16), 2)
    out_got1, q_send2 = lax.optimization_barrier((out_got1, q_send2))
    out_pair = jnp.stack([out_own, jnp.concatenate([out_got0, out_got1], axis=0)])
    out_near = to_near(out_pair)
    got_keys, q_send2 = lax.optimization_barrier((across(send, 2), q_send2))
    kv = pl.pallas_call(
        keys_join_kernel,
        out_shape=shaped((LEVELS // 2 + LEVELS, tok, 2 * HD)),
        in_specs=[SMEM] + [VMEM] * 6,
        out_specs=VMEM,
        scratch_shapes=[pltpu.VMEM((all_rows, 2 * HD), jnp.float32)],
        compiler_params=PARAMS,
        cost_estimate=pl.CostEstimate(
            flops=24_000_000_000, bytes_accessed=4_000_000, transcendentals=0
        ),
        name="keys_join",
    )(where, keep, got_keys, old_own, old_next, cosine, sine)
    kv_near, kv_far = to_near(kv), to_far(kv)
    kv_both = permuted(kv, lambda z, p, c: (z, p ^ 3, c))

    kv_far, out_pair = lax.optimization_barrier((kv_far, out_pair))
    out_far = to_far(out_pair)
    kv_near, kv_both, out_near = lax.optimization_barrier((kv_near, kv_both, out_near))
    out_both = to_far(out_near)

    attended = [
        pl.pallas_call(
            functools.partial(attend_kernel, pair),
            out_shape=shaped((LEVELS * tok, 2 * HD)),
            in_specs=[SMEM] + [VMEM] * 9,
            out_specs=VMEM,
            scratch_shapes=[pltpu.VMEM((LEVELS, 2, tok, HD), jnp.bfloat16)],
            compiler_params=PARAMS,
            cost_estimate=pl.CostEstimate(
                flops=4_000_000_000, bytes_accessed=4_000_000, transcendentals=2_400_000
            ),
            name="attend",
        )(where, q_keep, got_near, got_queries, cosine, sine, kv, kv_near, kv_far, kv_both)
        for pair in range(2)
    ]
    attended += [across(each, 1) for each in attended]

    wide_cols = PLANE * w_out.shape[1]
    mine, other = pl.pallas_call(
        output_kernel,
        out_shape=(
            shaped((LEVELS, tok, wide_cols), jnp.float32),
            shaped((LEVELS, tok, wide_cols)),
        ),
        in_specs=[SMEM] + [VMEM] * 8,
        out_specs=(VMEM, VMEM),
        scratch_shapes=[pltpu.VMEM((LEVELS * tok, out_rows), jnp.bfloat16)],
        compiler_params=PARAMS,
        cost_estimate=pl.CostEstimate(
            flops=5_000_000_000, bytes_accessed=4_000_000, transcendentals=0
        ),
        name="output",
    )(where, *attended, out_pair, out_near, out_far, out_both)
    got = other_core(other)
    block = [mine[d] + got[d].astype(jnp.float32) for d in range(LEVELS)]
    shares = [up(block[d].astype(jnp.bfloat16), d) for d in range(1, LEVELS)]
    return pl.pallas_call(
        finish_kernel,
        out_shape=shaped((tok, width)),
        in_specs=[SMEM] + [VMEM] * 4,
        out_specs=VMEM,
        compiler_params=PARAMS,
        name="finish",
    )(where, block[0], *shares)


def solution(mesh):
    def run(*args):
        kv_local = args[5].shape[1] // HD // mesh.shape["head"]
        levels_fit = (
            mesh.shape["seq"] == LEVELS * PLANE
            and mesh.shape["head"] == 2
            and kv_local == LEVELS
            and args[1].shape[0] == 2 * TILE_RUN
            and args[0].shape[0] == 2048
            and args[8].shape[0] == LEVELS * PLANE * CACHED
            and args[10].shape[0] == LEVELS * PLANE * REC
        )
        return jax.shard_map(
            by_levels if levels_fit else on_device,
            mesh=mesh,
            in_specs=(
                P("seq", "head"),
                P("seq", "head"),
                P("seq"),
                P(),
                P("seq", "head"),
                P("seq", "head"),
                P("seq", "head"),
                P("head", "seq"),
                P("seq", "head"),
                P("seq", "head"),
                P("seq", "head"),
                P("seq"),
            ),
            out_specs=P("seq", "head"),
            check_vma=False,
        )(*args)

    return run
```

```python
import functools

import jax
import jax.numpy as jnp
from jax import lax
from jax.experimental import pallas as pl
from jax.experimental.pallas import tpu as pltpu
from jax.sharding import PartitionSpec as P

D = 4096
HD = 128


EPSILON = 1e-05
ROPE_BASE = 1000000.0
NEG_FILL = -1e30


def rotate(values, positions):
    half = values.shape[-1] // 2
    freqs = ROPE_BASE ** (-jnp.arange(half, dtype=jnp.float32) / half)
    angles = positions[:, None] * freqs[None, :]
    cosine = jnp.cos(angles)[:, None, :]
    sine = jnp.sin(angles)[:, None, :]
    first = values[..., :half]
    second = values[..., half:]
    return jnp.concatenate(
        [first * cosine - second * sine, second * cosine + first * sine], axis=-1
    )


def scaled(rows_wide, squares, gain):
    return (rows_wide * lax.rsqrt(squares / D + EPSILON)[:, None] * gain[None, :]).astype(
        jnp.bfloat16
    )


def attend(carry, key_piece, value_piece, queries, allowed):
    best, total, accum = carry
    count = key_piece.shape[0]
    kv_local = queries.shape[0]
    keys_split = key_piece.reshape(count, kv_local, HD)
    values_split = value_piece.reshape(count, kv_local, HD)
    scores = jnp.einsum(
        "kgtd,nkd->kgtn", queries, keys_split, preferred_element_type=jnp.float32
    ) * HD ** (-0.5)
    scores = jnp.where(allowed, scores, NEG_FILL)
    fresh = jnp.maximum(best, jnp.max(scores, axis=-1))
    factor = jnp.exp(best - fresh)
    weights = jnp.where(allowed, jnp.exp(scores - fresh[..., None]), 0.0)
    total = total * factor + jnp.sum(weights, axis=-1)
    accum = accum * factor[..., None] + jnp.einsum(
        "kgtn,nkd->kgtd",
        weights.astype(jnp.bfloat16),
        values_split,
        preferred_element_type=jnp.float32,
    )
    return (fresh, total, accum)


def on_device(
    text_rows,
    picture_rows,
    picture_slots,
    norm_gain,
    w_query,
    w_key,
    w_value,
    w_out,
    cache_keys,
    cache_values,
    recompute_rows,
    recompute_slots,
):
    tok_rows = text_rows.shape[0]
    rec_count = recompute_rows.shape[0]
    cache_rows = cache_keys.shape[0]
    seq_index = lax.axis_index("seq")
    local_pos = seq_index * tok_rows + jnp.arange(tok_rows, dtype=jnp.int32)
    rows_piece = lax.all_gather(picture_rows, "seq", axis=0, tiled=True)
    slots_piece = lax.all_gather(picture_slots, "seq", axis=0, tiled=True)
    select = (slots_piece[None, :] == local_pos[:, None]).astype(jnp.bfloat16)
    placed = jnp.dot(select, rows_piece, preferred_element_type=jnp.float32)
    hits = jnp.sum(select.astype(jnp.float32), axis=1)
    added, hits = (placed, hits)
    stream = jnp.where(hits[:, None] > 0.5, added, text_rows.astype(jnp.float32)).astype(
        jnp.bfloat16
    )
    slice_width = stream.shape[1]
    gain_slice = lax.dynamic_slice_in_dim(
        norm_gain, lax.axis_index("head") * slice_width, slice_width, 0
    )
    stream_wide = stream.astype(jnp.float32)
    rec_wide = recompute_rows.astype(jnp.float32)
    stream_sq, rec_sq = lax.psum(
        (jnp.sum(stream_wide * stream_wide, axis=1), jnp.sum(rec_wide * rec_wide, axis=1)), "head"
    )
    normed, rec_normed = (
        lax.all_gather(scaled(stream_wide, stream_sq, gain_slice), "head", axis=1, tiled=True),
        lax.all_gather(scaled(rec_wide, rec_sq, gain_slice), "head", axis=1, tiled=True),
    )
    stacked = jnp.concatenate([normed, rec_normed], axis=0)
    query_cols = w_query.shape[1]
    key_cols = w_key.shape[1]
    pieces = (
        lax.all_gather(w_query, "seq", axis=0, tiled=True),
        lax.all_gather(w_key, "seq", axis=0, tiled=True),
        lax.all_gather(w_value, "seq", axis=0, tiled=True),
    )
    query_all = jnp.dot(stacked, pieces[0], preferred_element_type=jnp.float32)
    key_all = jnp.dot(stacked, pieces[1], preferred_element_type=jnp.float32)
    value_all = jnp.dot(stacked, pieces[2], preferred_element_type=jnp.float32)
    cache_total = cache_rows * lax.axis_size("seq")
    stream_pos = (cache_total + local_pos).astype(jnp.float32)
    rec_pos = recompute_slots.astype(jnp.float32)
    heads_local = query_cols // HD
    kv_local = key_cols // HD
    group = heads_local // kv_local
    rot_query = rotate(query_all[:tok_rows].reshape(tok_rows, heads_local, HD), stream_pos).astype(
        jnp.bfloat16
    )
    rot_key = (
        rotate(key_all[:tok_rows].reshape(tok_rows, kv_local, HD), stream_pos)
        .astype(jnp.bfloat16)
        .reshape(tok_rows, key_cols)
    )
    values_new = value_all[:tok_rows].astype(jnp.bfloat16)
    rot_rec_key = (
        rotate(key_all[tok_rows:].reshape(rec_count, kv_local, HD), rec_pos)
        .astype(jnp.bfloat16)
        .reshape(rec_count, key_cols)
    )
    rec_values = value_all[tok_rows:].astype(jnp.bfloat16)
    local_slots = recompute_slots - seq_index * cache_rows
    select = local_slots[:, None] == jnp.arange(cache_rows, dtype=jnp.int32)[None, :]
    replaced = jnp.any(select, axis=0)[:, None]
    select_cols = select.astype(jnp.bfloat16).T
    new_keys = jnp.dot(select_cols, rot_rec_key, preferred_element_type=jnp.float32).astype(
        jnp.bfloat16
    )
    new_values = jnp.dot(select_cols, rec_values, preferred_element_type=jnp.float32).astype(
        jnp.bfloat16
    )
    cache_k = jnp.where(replaced, new_keys, cache_keys)
    cache_v = jnp.where(replaced, new_values, cache_values)
    queries = jnp.transpose(rot_query.reshape(tok_rows, kv_local, group, HD), (1, 2, 0, 3))
    carry_start = (
        jnp.full((kv_local, group, tok_rows), NEG_FILL, jnp.float32),
        jnp.zeros((kv_local, group, tok_rows), jnp.float32),
        jnp.zeros((kv_local, group, tok_rows, HD), jnp.float32),
    )
    pieces = (
        lax.all_gather(cache_k, "seq", axis=0, tiled=True),
        lax.all_gather(cache_v, "seq", axis=0, tiled=True),
    )
    allowed = jnp.ones((tok_rows, pieces[0].shape[0]), jnp.bool_)
    carry_mid = attend(carry_start, pieces[0], pieces[1], queries, allowed)
    pieces = (
        lax.all_gather(rot_key, "seq", axis=0, tiled=True),
        lax.all_gather(values_new, "seq", axis=0, tiled=True),
    )
    key_pos = jnp.arange(pieces[0].shape[0], dtype=jnp.int32)
    allowed = key_pos[None, :] <= local_pos[:, None]
    best, total, accum = attend(carry_mid, pieces[0], pieces[1], queries, allowed)
    attended = (
        jnp.transpose(accum / total[..., None], (2, 0, 1, 3))
        .reshape(tok_rows, query_cols)
        .astype(jnp.bfloat16)
    )
    partial_out = jnp.dot(
        attended,
        lax.all_gather(w_out, "seq", axis=1, tiled=True),
        preferred_element_type=jnp.float32,
    )
    return lax.psum_scatter(
        partial_out.astype(jnp.bfloat16), "head", scatter_dimension=1, tiled=True
    )


LEVELS = 4
PLANE = 4
TILE_RUN = 256
CACHED = 64
REC = 8
REC_PAD = 16


def permuted(value, move):
    perm = []
    for level in range(LEVELS):
        for place in range(PLANE):
            for core in range(2):
                target = move(level, place, core)
                if target is not None:
                    to_level, to_place, to_core = target
                    perm.append(
                        (
                            (level * PLANE + place) * 2 + core,
                            (to_level * PLANE + to_place) * 2 + to_core,
                        )
                    )
    return lax.ppermute(value, ("seq", "head"), perm)


def across(value, bit):
    return permuted(value, lambda z, p, c: (z ^ bit, p, c))


def up(value, steps):
    return permuted(value, lambda z, p, c: ((z + steps) % LEVELS, p, c))


def other_core(value):
    return permuted(value, lambda z, p, c: (z, p, 1 - c))


def to_near(value):
    return permuted(value, lambda z, p, c: (z, p ^ (1 + c), c))


def to_far(value):
    return permuted(value, lambda z, p, c: (z, p ^ (2 - c), c))


def place_of(which, place, core):
    if which == 0:
        return place
    if which == 3:
        return place ^ 3
    return place ^ (1 + core) if which == 1 else place ^ (2 - core)


def turned(values, cosine, sine):
    return values * cosine + pltpu.roll(values, HD // 2, 1) * sine


def pack_kernel(where_ref, *refs):
    w_key, w_value, cache_keys, cache_values, slots = refs[:5]
    outs, sems = refs[5:7], refs[7]
    level = where_ref[0]
    depth = w_key.shape[0]
    copies = []

    def copy(source, target):
        copies.append(pltpu.make_async_copy(source, target, sems.at[len(copies)]))
        copies[-1].start()

    for n in range(2):
        keys = outs[n]
        for m in range(2):
            at = jnp.bitwise_xor(level, n + 2 * m)
            small = pl.ds(pl.multiple_of(at * HD, HD), HD)
            for k, (new, old) in enumerate(((w_key, cache_keys), (w_value, cache_values))):
                to = pl.ds((2 * m + k) * HD, HD)
                copy(new.at[:, small], keys.at[0:depth, to])
                copy(old.at[:, small], keys.at[depth : depth + CACHED, to])
        copy(slots, keys.at[depth + CACHED : depth + CACHED + REC_PAD])
    for each in copies:
        each.wait()


PACK_COPIES = 18


def assemble(where_ref, parts, x_ref):
    level, core = where_ref[0], where_ref[2]
    shown = TILE_RUN // 2 // PLANE
    rows = parts[0].shape[0] - shown
    for n, part in enumerate(parts):
        x_ref[n * rows : (n + 1) * rows] = part[0:rows]
    start = where_ref[4] * rows
    for n, part in enumerate(parts):
        which = 2 * lax.rem(level + n % 2, 2) + (core if n < 2 else 1 - core)
        to = pl.multiple_of(start + which * shown, 16)
        x_ref[pl.ds(to, shown)] = part[rows : rows + shown]


def products(where_ref, x_ref, pieces):
    level, place, core = where_ref[0], where_ref[1], where_ref[2]
    total = None
    for i in range(2):
        for j in range(PLANE):
            depth = pieces[i][j].shape[0]
            block = lax.rem(level + i, 2) * PLANE + place_of(j, place, core)
            start = pl.multiple_of(block * depth, depth)
            part = jnp.dot(
                x_ref[:, pl.ds(start, depth)],
                pieces[i][j][...],
                preferred_element_type=jnp.float32,
            )
            total = part if total is None else total + part
    return total


def keys_part_kernel(
    where_ref, x0, x1, x2, x3, own, near, far, old0, old1, keep_ref, send_ref, x_ref
):
    assemble(where_ref, (x0, x1, x2, x3), x_ref)
    pieces = [[own.at[i], near.at[i], far.at[i], far.at[2 + i]] for i in range(2)]
    width = 2 * HD
    total = products(where_ref, x_ref, pieces)
    at = total.shape[0]
    keep_ref[...] = total[:, :width]
    send_ref[0:at] = total[:, width:].astype(jnp.bfloat16)
    for old in (old0, old1):
        send_ref[at : at + CACHED + REC_PAD] = old[:, width:]
        at += CACHED + REC_PAD


def keys_join_kernel(where_ref, keep_ref, got_ref, old0, old1, cos_ref, sin_ref, kv_ref, sum_ref):
    level = where_ref[0]
    rows = sum_ref.shape[0]
    block = rows // LEVELS
    tok = block - REC_PAD
    width = 2 * HD
    sum_ref[...] = keep_ref[...] + got_ref[0:rows].astype(jnp.float32)
    first = where_ref[3]
    span = CACHED + REC_PAD
    for n in range(LEVELS):
        at = jnp.bitwise_xor(level, n)
        start = pl.multiple_of(lax.rem(first + n, LEVELS) * block, 16)
        cosine, sine = cos_ref[at], sin_ref[at]
        fresh = sum_ref[pl.ds(start, tok), :]
        kv_ref[2 + at, :, 0:HD] = turned(fresh[:, :HD], cosine[:tok], sine[:tok]).astype(
            jnp.bfloat16
        )
        kv_ref[2 + at, :, HD:width] = fresh[:, HD:].astype(jnp.bfloat16)
        if n < 2:
            old = (old0, old1)[n][:, 0:width].astype(jnp.float32)
        else:
            old = got_ref[rows + (n - 2) * span : rows + (n - 1) * span].astype(jnp.float32)
        slots = old[CACHED : CACHED + REC].astype(jnp.int32)
        rec = sum_ref[pl.ds(pl.multiple_of(start + tok, 16), REC_PAD), :]
        line = lax.broadcasted_iota(jnp.int32, (CACHED, width), 0)
        found = jnp.zeros((CACHED, width), jnp.float32)
        hit = jnp.zeros((CACHED, width), jnp.int32)
        for r in range(REC):
            same = line == slots[r : r + 1]
            found = jnp.where(same, rec[r : r + 1], found)
            hit = jnp.where(same, 1, hit)
        keys = turned(found[:, :HD], cosine[tok : tok + CACHED], sine[tok : tok + CACHED])
        found = jnp.concatenate([keys, found[:, HD:]], axis=1)
        line_at = pl.multiple_of(lax.rem(at, 2) * CACHED, CACHED)
        kv_ref[at // 2, pl.ds(line_at, CACHED), :] = jnp.where(
            hit == 1, found, old[:CACHED]
        ).astype(jnp.bfloat16)


def queries_part_kernel(where_ref, x0, x1, x2, x3, *refs):
    weights, outs, x_ref = refs[:4], refs[4:8], refs[8]
    level, place, core = where_ref[0], where_ref[1], where_ref[2]
    assemble(where_ref, (x0, x1, x2, x3), x_ref)
    depth = weights[0].shape[0]
    width = 4 * HD
    block = x_ref.shape[0] // LEVELS
    tok = block - REC_PAD
    for m, out_ref in zip((0, 2, 1, 3), outs):
        group = pl.ds(pl.multiple_of(jnp.bitwise_xor(level, m) * width, width), width)
        total = None
        for j in range(PLANE):
            at = lax.rem(level, 2) * PLANE + place_of(j, place, core)
            part = jnp.dot(
                x_ref[:, pl.ds(pl.multiple_of(at * depth, depth), depth)],
                weights[j][:, group],
                preferred_element_type=jnp.float32,
            )
            total = part if total is None else total + part
        for k in range(LEVELS):
            at = jnp.bitwise_xor(level, lax.rem(k + LEVELS - where_ref[3], LEVELS))
            out_ref[at] = total[k * block : k * block + tok].astype(out_ref.dtype)


def attend_kernel(
    pair, where_ref, keep_ref, near_ref, got_ref, cos_ref, sin_ref, kv0, kv1, kv2, kv3, out_ref, query_ref
):
    level, place, core = where_ref[0], where_ref[1], where_ref[2]
    pieces = (kv0, kv1, kv2, kv3)
    tok = keep_ref.shape[1]
    old = LEVELS // 2
    heads = query_ref.shape[1]
    columns = slice(pair * heads * HD, (pair + 1) * heads * HD)
    for at in range(LEVELS):
        total = keep_ref[at, :, columns] + (
            near_ref[at, :, columns].astype(jnp.float32)
            + got_ref[at, :, columns].astype(jnp.float32)
        )
        cosine, sine = cos_ref[at][:tok], sin_ref[at][:tok]
        for h in range(heads):
            head = turned(total[:, h * HD : (h + 1) * HD], cosine, sine)
            query_ref[at, h] = head.astype(jnp.bfloat16)
    row = lax.broadcasted_iota(jnp.int32, (tok, tok), 0)
    col = lax.broadcasted_iota(jnp.int32, (tok, tok), 1)
    scale = HD ** (-0.5) * 1.4426950408889634
    for i in range(LEVELS):
        count = (old + i + 1) * tok
        queries = query_ref[i].reshape(heads * tok, HD)
        scores = []
        best = None
        for j in range(PLANE):
            keys = pieces[j][0 : old + i + 1, :, 0:HD].reshape(count, HD)
            raw = lax.dot_general(
                queries, keys, (((1,), (1,)), ((), ())), preferred_element_type=jnp.float32
            )
            if j == 0:
                allowed = col <= row
            else:
                allowed = jnp.broadcast_to(place_of(j, place, core), (tok, tok)) < place
            allowed = jnp.concatenate([allowed] * heads, axis=0)
            last = jnp.where(allowed, raw[:, count - tok :], NEG_FILL)
            raw = jnp.concatenate([raw[:, : count - tok], last], axis=1)
            top = jnp.max(raw, axis=1, keepdims=True)
            best = top if best is None else jnp.maximum(best, top)
            scores.append(raw)
        total, accum = 0.0, 0.0
        for j in range(PLANE):
            weights = jnp.exp2((scores[j] - best) * scale)
            total = total + jnp.sum(weights, axis=1, keepdims=True)
            values = pieces[j][0 : old + i + 1, :, HD : 2 * HD].reshape(count, HD)
            accum = accum + jnp.dot(
                weights.astype(jnp.bfloat16), values, preferred_element_type=jnp.float32
            )
        result = (accum / total).astype(jnp.bfloat16)
        for h in range(heads):
            out_ref[i * tok : (i + 1) * tok, h * HD : (h + 1) * HD] = result[
                h * tok : (h + 1) * tok
            ]


def output_kernel(where_ref, *refs):
    heads, weights, (mine_ref, other_ref, x_ref) = refs[:4], refs[4:-3], refs[-3:]
    level, core = where_ref[0], where_ref[2]
    depth = heads[0].shape[1]
    width = weights[0].shape[2]
    tok = mine_ref.shape[1]
    for n, ref in enumerate(heads):
        at = 2 * lax.rem(level + n // 2, 2) + n % 2
        x_ref[:, pl.ds(pl.multiple_of(at * depth, depth), depth)] = ref[...]
    swap = jnp.where(core == level // 2, 0, 1)
    for s, out_ref in enumerate((mine_ref, other_ref)):
        i = jnp.bitwise_xor(swap, s)
        for j, piece in enumerate(weights):
            slot = (0, 2, 1, 3)[j] if s else j
            part = jnp.dot(x_ref[...], piece[i], preferred_element_type=jnp.float32)
            for t in range(LEVELS):
                out_ref[
                    lax.rem(t + LEVELS - level, LEVELS), :, slot * width : (slot + 1) * width
                ] = part[t * tok : (t + 1) * tok].astype(out_ref.dtype)


def finish_kernel(where_ref, own, first, second, third, out_ref):
    level, place, core = where_ref[0], where_ref[1], where_ref[2]
    half = out_ref.shape[1] // 2
    width = half // PLANE
    sums = (
        own[...] + second[...].astype(jnp.float32),
        first[...].astype(jnp.float32) + third[...].astype(jnp.float32),
    )
    for steps, total in enumerate(sums):
        for j in range(PLANE):
            at = lax.rem(level + steps, 2) * half + place_of(j, place, core) * width
            out_ref[:, pl.ds(pl.multiple_of(at, width), width)] = total[
                :, j * width : (j + 1) * width
            ].astype(out_ref.dtype)


SMEM = pl.BlockSpec(memory_space=pltpu.SMEM)
VMEM = pl.BlockSpec(memory_space=pltpu.VMEM)
HBM = pl.BlockSpec(memory_space=pltpu.MemorySpace.HBM)
PARAMS = pltpu.CompilerParams(vmem_limit_bytes=48 * 1024 * 1024)


def shaped(shape, dtype=jnp.bfloat16):
    return jax.ShapeDtypeStruct(shape, dtype)


def by_levels(
    text_rows,
    picture_rows,
    picture_slots,
    norm_gain,
    w_query,
    w_key,
    w_value,
    w_out,
    cache_keys,
    cache_values,
    recompute_rows,
    recompute_slots,
):
    seq_index = lax.axis_index("seq")
    core = lax.axis_index("head")
    level, place = seq_index // PLANE, seq_index % PLANE
    half_at = level // 2
    own_first = core == half_at
    tok, width = text_rows.shape
    block_rows = tok + REC_PAD

    stream_len = tok * LEVELS * PLANE
    tile_owners = TILE_RUN // tok
    first = stream_len // 2 // tok
    last = (stream_len - TILE_RUN) // tok
    owners = [first + i for i in range(tile_owners)] + [last + i for i in range(tile_owners)]
    assert [owner % PLANE for owner in owners] == list(range(LEVELS))
    owner_level = jnp.where(place < tile_owners, first // PLANE, last // PLANE)

    first_block = jnp.where(own_first, 0, 2)
    shown_block = (first_block + (level ^ owner_level)) % LEVELS
    where = jnp.stack([level, place, core, first_block, shown_block]).astype(jnp.int32)

    slots = (recompute_slots - seq_index * CACHED).astype(jnp.bfloat16)
    slot_rows = jnp.broadcast_to(jnp.pad(slots, (0, REC_PAD - REC))[:, None], (REC_PAD, 4 * HD))
    depth = w_key.shape[0]
    rows = jnp.concatenate(
        [text_rows, recompute_rows, jnp.zeros((REC_PAD - REC, width), text_rows.dtype)], axis=0
    )
    gain = lax.dynamic_slice_in_dim(norm_gain, core * width, width, 0)
    wide, pictures = rows.astype(jnp.float32), picture_rows.astype(jnp.float32)
    squares, picture_squares = lax.psum(
        (jnp.sum(wide * wide, axis=1), jnp.sum(pictures * pictures, axis=1)), "head"
    )
    normed = scaled(wide, squares, gain)
    pictures = scaled(pictures, picture_squares, gain)

    normed, pictures, slot_rows = lax.optimization_barrier((normed, pictures, slot_rows))
    key_own, key_give = pl.pallas_call(
        pack_kernel,
        out_shape=(shaped((depth + CACHED + REC_PAD, 4 * HD)),) * 2,
        in_specs=[SMEM] + [HBM] * 5,
        out_specs=(HBM,) * 2,
        scratch_shapes=[pltpu.SemaphoreType.DMA((PACK_COPIES,))],
        compiler_params=PARAMS,
        cost_estimate=pl.CostEstimate(
            flops=6_000_000_000, bytes_accessed=4_000_000, transcendentals=0
        ),
        name="pack",
    )(where, w_key, w_value, cache_keys, cache_values, slot_rows)

    out_rows = w_out.shape[0] // 2
    out_own, out_give = (
        lax.dynamic_slice_in_dim(w_out, at * out_rows, out_rows, 0) for at in (half_at, 1 - half_at)
    )

    crossed = permuted(normed, lambda z, p, c: (z ^ 2, p, 1 - c) if c == 1 - z // 2 else None)
    shown = permuted(pictures, lambda z, p, c: (2 * c + p // 2, z, p % 2))
    key_next = across(key_give, 1)
    query_near, query_far = to_near(w_query), to_far(w_query)
    query_near, query_far = lax.optimization_barrier((query_near, query_far))
    query_both = to_far(query_near)
    shown, key_next = lax.optimization_barrier((shown, key_next))
    keys = jnp.stack([key_own[:depth], key_next[:depth]])
    old_own, old_next = key_own[depth:], key_next[depth:]
    keys_near = to_near(keys)
    crossed, shown, out_give = lax.optimization_barrier((crossed, shown, out_give))
    held = jnp.concatenate([jnp.where(own_first, normed, crossed), shown], axis=0)
    next_rows = across(held, 1)
    held_other = other_core(held)
    next_rows, out_got = lax.optimization_barrier((next_rows, across(out_give, 2)))
    next_other = other_core(next_rows)
    keys_far = to_far(jnp.concatenate([keys, keys_near], axis=0))
    next_other, held_other, keys_far, query_both = lax.optimization_barrier(
        (next_other, held_other, keys_far, query_both)
    )
    parts = (held, next_rows, held_other, next_other)

    half = HD // 2
    freqs = ROPE_BASE ** (-jnp.arange(half, dtype=jnp.float32) / half)
    blocks = (jnp.arange(LEVELS, dtype=jnp.int32) * PLANE + place)[:, None]
    stream_pos = (
        CACHED * LEVELS * PLANE + blocks * tok + jnp.arange(tok, dtype=jnp.int32)[None]
    ).astype(jnp.float32)
    cache_pos = (blocks * CACHED + jnp.arange(CACHED, dtype=jnp.int32)[None]).astype(jnp.float32)
    angles = jnp.concatenate([stream_pos, cache_pos], axis=1)[..., None] * freqs
    cosine, sine = jnp.cos(angles), jnp.sin(angles)
    cosine = jnp.concatenate([cosine, cosine], axis=-1)
    sine = jnp.concatenate([-sine, sine], axis=-1)

    all_rows = LEVELS * block_rows
    keep, send = pl.pallas_call(
        keys_part_kernel,
        out_shape=(
            shaped((all_rows, 2 * HD), jnp.float32),
            shaped((all_rows + 2 * (CACHED + REC_PAD), 2 * HD)),
        ),
        in_specs=[SMEM] + [VMEM] * 9,
        out_specs=(VMEM, VMEM),
        scratch_shapes=[pltpu.VMEM((all_rows, width), jnp.bfloat16)],
        compiler_params=PARAMS,
        cost_estimate=pl.CostEstimate(
            flops=3_000_000_000, bytes_accessed=4_000_000, transcendentals=0
        ),
        name="keys_part",
    )(where, *parts, keys, keys_near, keys_far, old_own, old_next)
    send, *parts = lax.optimization_barrier((send, *parts))
    group_shape = (LEVELS, tok, 4 * HD)
    q_keep, q_keep2, q_send, q_send2 = pl.pallas_call(
        queries_part_kernel,
        out_shape=(shaped(group_shape, jnp.float32),) * 2 + (shaped(group_shape),) * 2,
        in_specs=[SMEM] + [VMEM] * 8,
        out_specs=(VMEM,) * 4,
        scratch_shapes=[pltpu.VMEM((all_rows, width), jnp.bfloat16)],
        compiler_params=PARAMS,
        cost_estimate=pl.CostEstimate(
            flops=5_000_000_000, bytes_accessed=4_000_000, transcendentals=0
        ),
        name="queries_part",
    )(where, *parts, w_query, query_near, query_far, query_both)
    got_near2 = across(q_send2, 1)
    got_near = across(q_send, 1)
    got_queries = across((q_keep2 + got_near2.astype(jnp.float32)).astype(jnp.bfloat16), 2)
    out_pair = jnp.stack([out_own, out_got])
    out_pair, q_send2 = lax.optimization_barrier((out_pair, q_send2))
    out_near = to_near(out_pair)
    got_keys, q_send2 = lax.optimization_barrier((across(send, 2), q_send2))
    kv = pl.pallas_call(
        keys_join_kernel,
        out_shape=shaped((LEVELS // 2 + LEVELS, tok, 2 * HD)),
        in_specs=[SMEM] + [VMEM] * 6,
        out_specs=VMEM,
        scratch_shapes=[pltpu.VMEM((all_rows, 2 * HD), jnp.float32)],
        compiler_params=PARAMS,
        cost_estimate=pl.CostEstimate(
            flops=24_000_000_000, bytes_accessed=4_000_000, transcendentals=0
        ),
        name="keys_join",
    )(where, keep, got_keys, old_own, old_next, cosine, sine)
    kv_near, kv_far = to_near(kv), to_far(kv)
    kv_both = permuted(kv, lambda z, p, c: (z, p ^ 3, c))

    kv_far, out_pair = lax.optimization_barrier((kv_far, out_pair))
    out_far = to_far(out_pair)
    kv_near, out_near = lax.optimization_barrier((kv_near, out_near))
    out_both = to_far(out_near)

    attended = [
        pl.pallas_call(
            functools.partial(attend_kernel, pair),
            out_shape=shaped((LEVELS * tok, 2 * HD)),
            in_specs=[SMEM] + [VMEM] * 9,
            out_specs=VMEM,
            scratch_shapes=[pltpu.VMEM((LEVELS, 2, tok, HD), jnp.bfloat16)],
            compiler_params=PARAMS,
            cost_estimate=pl.CostEstimate(
                flops=4_000_000_000, bytes_accessed=4_000_000, transcendentals=2_400_000
            ),
            name="attend",
        )(where, q_keep, got_near, got_queries, cosine, sine, kv, kv_near, kv_far, kv_both)
        for pair in range(2)
    ]
    attended += [across(each, 1) for each in attended]

    wide_cols = PLANE * w_out.shape[1]
    mine, other = pl.pallas_call(
        output_kernel,
        out_shape=(
            shaped((LEVELS, tok, wide_cols), jnp.float32),
            shaped((LEVELS, tok, wide_cols)),
        ),
        in_specs=[SMEM] + [VMEM] * 8,
        out_specs=(VMEM, VMEM),
        scratch_shapes=[pltpu.VMEM((LEVELS * tok, out_rows), jnp.bfloat16)],
        compiler_params=PARAMS,
        cost_estimate=pl.CostEstimate(
            flops=5_000_000_000, bytes_accessed=4_000_000, transcendentals=0
        ),
        name="output",
    )(where, *attended, out_pair, out_near, out_far, out_both)
    got = other_core(other)
    block = [mine[d] + got[d].astype(jnp.float32) for d in range(LEVELS)]
    shares = [up(block[d].astype(jnp.bfloat16), d) for d in range(1, LEVELS)]
    return pl.pallas_call(
        finish_kernel,
        out_shape=shaped((tok, width)),
        in_specs=[SMEM] + [VMEM] * 4,
        out_specs=VMEM,
        compiler_params=PARAMS,
        name="finish",
    )(where, block[0], *shares)


def solution(mesh):
    def run(*args):
        kv_local = args[5].shape[1] // HD // mesh.shape["head"]
        levels_fit = (
            mesh.shape["seq"] == LEVELS * PLANE
            and mesh.shape["head"] == 2
            and kv_local == LEVELS
            and args[1].shape[0] == 2 * TILE_RUN
            and args[0].shape[0] == 2048
            and args[8].shape[0] == LEVELS * PLANE * CACHED
            and args[10].shape[0] == LEVELS * PLANE * REC
        )
        return jax.shard_map(
            by_levels if levels_fit else on_device,
            mesh=mesh,
            in_specs=(
                P("seq", "head"),
                P("seq", "head"),
                P("seq"),
                P(),
                P("seq", "head"),
                P("seq", "head"),
                P("seq", "head"),
                P("head", "seq"),
                P("seq", "head"),
                P("seq", "head"),
                P("seq", "head"),
                P("seq"),
            ),
            out_specs=P("seq", "head"),
            check_vma=False,
        )(*args)

    return run
```
